32 devices in a mesh: gx: 4 (over x, core), gy: 8 (over z, y).
Axes of the slice: x: 2, y: 2, z: 4, core: 2. Of those that a mesh axis runs over, the one named last changes fastest.
Arguments:
- charges: bfloat16 [65536, 32], P(('gx', 'gy')), may hold values from -6 to 6
- panel_counts: int32 [1024], P(('gx', 'gy')), may hold values from 1 to 64, as said below
- basis: bfloat16 [1024, 64, 64], P(('gx', 'gy')), may hold values from -0.75 to 0.75
- transfer: bfloat16 [1024, 64, 64], P(('gx', 'gy')), may hold values from -0.5 to 0.5
- leaf_coupling: bfloat16 [1024, 16, 64, 64], P(('gx', 'gy')), may hold values from -0.1875 to 0.1875
- leaf_partners: int32 [1024, 16], P(('gx', 'gy')), may hold values from 0 to 1023, as said below
- near_blocks: bfloat16 [1024, 3, 64, 64], P(('gx', 'gy')), may hold values from -0.4375 to 0.4375
- parent_coupling: bfloat16 [512, 16, 64, 64], P(('gx', 'gy')), may hold values from -0.1875 to 0.1875
- parent_partners: int32 [512, 16], P(('gx', 'gy')), may hold values from 0 to 511, as said below
Outputs:
- potential: bfloat16 [65536, 32], P(('gx', 'gy'))
The draws below stay inside these ranges and needn't reach their ends.
Inputs may be any that keep to these rules, and one draw needn't show every extreme that they name: `panel_counts`: every value 1 to 64 occurs; every fifth leaf has all 64 panels live. `leaf_partners`: the partner of leaf g lies among the leaves of g's device, the device before or the device after in the order of the combined index gx * 32 + gy (leaf g is on device g // 32). `parent_partners`: the partner of parent q lies in the same block of 128 parents as q (one index of gx).
All inputs are finite; a program needn't handle non-finite values.
Results may differ from the reference program's by a relative error of at most 0.0054.
Values may be sent and summed in bfloat16 or wider, within the bound.
No kernel may reach another device: no remote copies, remote signals or barrier semaphores. Data moves between devices by JAX's collectives and lax.ppermute only.
A program may use at most 128 MiB of HBM per device.

```python
import jax
import jax.numpy as jnp
from jax import lax

LEAF = 64
K = 64
R = 32
NC = 16
NC2 = 16
LD = 32
LEAVES = 1024
PARENTS = 512
ROWP = 128
PANELS = 65536
DEVICES = 32


def draw_panel_counts(key, part):
    key = jax.random.fold_in(key, 1)
    counts = jax.random.randint(key, (LEAVES,), 1, LEAF + 1)
    counts = counts.at[::5].set(LEAF)
    return counts.astype(jnp.int32)


def draw_leaf_partners(key, part):
    key = jax.random.fold_in(key, 2)
    owner = jnp.arange(LEAVES, dtype=jnp.int32) // LD
    offset = jax.random.randint(key, (LEAVES, NC), -LD, 2 * LD)
    chosen = owner[:, None] * LD + offset
    return jnp.clip(chosen, 0, LEAVES - 1).astype(jnp.int32)


def draw_parent_partners(key, part):
    key = jax.random.fold_in(key, 3)
    block = jnp.arange(PARENTS, dtype=jnp.int32) // ROWP
    offset = jax.random.randint(key, (PARENTS, NC2), 0, ROWP)
    return (block[:, None] * ROWP + offset).astype(jnp.int32)


def shard_levels(key, dims, shards, smallest, top_value):
    level, own = 1.0, jax.random.fold_in(key, 6)
    for position, blocks in shards:
        draws = jnp.exp(jax.random.uniform(jax.random.fold_in(own, position), (blocks,), jnp.float32, smallest / len(shards), top_value / len(shards)))
        level = level * jnp.repeat(draws, dims[position] // blocks).reshape([-1 if axis == position else 1 for axis in range(len(dims))])
    return level


def gaussian(stream_key, shape, scale, bound, cuts=(), held_as=jnp.bfloat16):
    result = scale * jax.random.normal(stream_key, shape, jnp.float32)
    if cuts:
        result = result * shard_levels(stream_key, shape, cuts, -0.22, 0.18)
    return jnp.clip(result, -bound, bound).astype(held_as)


def setup_inputs(seed: int = 0) -> dict:
    key_list = jax.random.split(jax.random.key(seed), 10)
    charges = gaussian(key_list[0], (PANELS, R), 1.0, 6.0, ((0, 32),))
    panel_counts = draw_panel_counts(jax.random.fold_in(key_list[9], 71), 0)
    basis = gaussian(key_list[2], (LEAVES, LEAF, K), LEAF ** -0.5, 0.75, ((0, 32),))
    transfer = gaussian(key_list[3], (LEAVES, K, K), (2 * K) ** -0.5, 0.5, ((0, 32),))
    leaf_coupling = gaussian(key_list[4], (LEAVES, NC, K, K), (NC * K) ** -0.5, 0.1875, ((0, 32),))
    leaf_partners = draw_leaf_partners(jax.random.fold_in(key_list[9], 71), 0)
    near_blocks = gaussian(key_list[6], (LEAVES, 3, LEAF, LEAF), (3 * LEAF) ** -0.5, 0.4375, ((0, 32),))
    parent_coupling = gaussian(key_list[7], (PARENTS, NC2, K, K), (NC2 * K) ** -0.5, 0.1875, ((0, 32),))
    parent_partners = draw_parent_partners(jax.random.fold_in(key_list[9], 71), 0)
    return {"charges": charges, "panel_counts": panel_counts, "basis": basis, "transfer": transfer, "leaf_coupling": leaf_coupling, "leaf_partners": leaf_partners, "near_blocks": near_blocks, "parent_coupling": parent_coupling, "parent_partners": parent_partners}


def reference(charges, panel_counts, basis, transfer, leaf_coupling, leaf_partners, near_blocks, parent_coupling, parent_partners):
    slots = jnp.arange(LEAF, dtype=jnp.int32)
    mask = (slots[None, :] < panel_counts[:, None]).astype(jnp.bfloat16)[:, :, None]
    live = charges.reshape(LEAVES, LEAF, R) * mask
    leaf_coef = jnp.einsum('gpk,gpr->gkr', basis.astype(jnp.float32), live.astype(jnp.float32)).astype(jnp.bfloat16)
    pairs = transfer.reshape(PARENTS, 2, K, K).astype(jnp.float32)
    kids = leaf_coef.reshape(PARENTS, 2, K, R).astype(jnp.float32)
    parent_coef = jnp.einsum('qckl,qckr->qlr', pairs, kids).astype(jnp.bfloat16)

    def parent_block(args):
        blocks, partners = args
        picked = parent_coef[partners].astype(jnp.float32)
        return jnp.einsum('qjkl,qjlr->qkr', blocks.astype(jnp.float32), picked)

    half = LD // 2
    parent_far = lax.map(parent_block, (parent_coupling.reshape(DEVICES, half, NC2, K, K), parent_partners.reshape(DEVICES, half, NC2)))
    parent_far = parent_far.reshape(PARENTS, K, R).astype(jnp.bfloat16)
    spread = jnp.repeat(parent_far, 2, axis=0).astype(jnp.float32)
    zero_leaf = jnp.zeros((1, LEAF, R), jnp.bfloat16)
    padded = jnp.concatenate([zero_leaf, live, zero_leaf], axis=0)

    def leaf_block(args):
        blocks, partners, trans, near_b, bas, down, start = args
        picked = leaf_coef[partners].astype(jnp.float32)
        far = jnp.einsum('gjkl,gjlr->gkr', blocks.astype(jnp.float32), picked)
        local_coef = (far + jnp.einsum('gkl,glr->gkr', trans.astype(jnp.float32), down)).astype(jnp.bfloat16)
        window = lax.dynamic_slice_in_dim(padded, start, LD + 2, 0).astype(jnp.float32)
        near = jnp.zeros((LD, LEAF, R), jnp.float32)
        for n in range(3):
            near = near + jnp.einsum('gpq,gqr->gpr', near_b[:, n].astype(jnp.float32), window[n:n + LD])
        return jnp.einsum('gpk,gkr->gpr', bas.astype(jnp.float32), local_coef.astype(jnp.float32)) + near

    starts = jnp.arange(DEVICES, dtype=jnp.int32) * LD
    total = lax.map(leaf_block, (leaf_coupling.reshape(DEVICES, LD, NC, K, K), leaf_partners.reshape(DEVICES, LD, NC), transfer.reshape(DEVICES, LD, K, K), near_blocks.reshape(DEVICES, LD, 3, LEAF, LEAF), basis.reshape(DEVICES, LD, LEAF, K), spread.reshape(DEVICES, LD, K, R), starts))
    total = total.reshape(LEAVES, LEAF, R) * mask.astype(jnp.float32)
    return total.astype(jnp.bfloat16).reshape(PANELS, R)
```

```python
import jax
import jax.numpy as jnp
from jax import lax
from jax.sharding import PartitionSpec as P


def shifted(array, axis, by):
    length = lax.axis_size(axis)
    pairs = [(i, i + by) for i in range(length) if 0 <= i + by < length]
    return lax.ppermute(array, axis, pairs)


def send_rims(payload, offset):
    return shifted(payload, ("gx", "gy"), offset)


def per_device(
    charges,
    panel_counts,
    basis,
    transfer,
    leaf_coupling,
    leaf_partners,
    near_blocks,
    parent_coupling,
    parent_partners,
):
    leaves, leaf_size, rank = basis.shape
    sides = charges.shape[1]
    half = leaves // 2
    slots = jnp.arange(leaf_size, dtype=jnp.int32)
    mask = (slots[None, :] < panel_counts[:, None]).astype(jnp.bfloat16)[:, :, None]
    live = charges.reshape(leaves, leaf_size, sides) * mask
    leaf_coef = jnp.einsum("gpk,gpr->gkr", basis, live, preferred_element_type=jnp.float32).astype(
        jnp.bfloat16
    )
    pairs = transfer.reshape(half, 2, rank, rank)
    kids = leaf_coef.reshape(half, 2, rank, sides)
    parent_coef = jnp.einsum(
        "qckl,qckr->qlr", pairs, kids, preferred_element_type=jnp.float32
    ).astype(jnp.bfloat16)
    device = lax.axis_index("gx") * lax.axis_size("gy") + lax.axis_index("gy")
    relative = leaf_partners - device * leaves
    cut = leaves * rank
    flat_coef = leaf_coef.reshape(cut, sides)
    received = []
    for offset in (1, -1):
        edge = live[leaves - 1] if offset == 1 else live[0]
        payload = jnp.concatenate([flat_coef, edge], axis=0)
        received.append(send_rims(payload, offset))
    before, after = received
    window_coef = jnp.concatenate([before[:cut], flat_coef, after[:cut]], axis=0).reshape(
        3 * leaves, rank, sides
    )
    picked = window_coef[relative + leaves]
    leaf_far = jnp.einsum(
        "gjkl,gjlr->gkr", leaf_coupling, picked, preferred_element_type=jnp.float32
    )
    row_start = lax.axis_index("gx") * lax.axis_size("gy") * half
    n = lax.axis_size("gy")
    sent = jnp.broadcast_to(parent_coef[None], (n,) + parent_coef.shape)
    row_coef = lax.all_to_all(sent, "gy", 0, 0).reshape((n * half,) + parent_coef.shape[1:])
    chosen = row_coef[parent_partners - row_start]
    parent_far = jnp.einsum(
        "qjkl,qjlr->qkr", parent_coupling, chosen, preferred_element_type=jnp.float32
    )
    parent_far = parent_far.astype(jnp.bfloat16)
    spread = jnp.repeat(parent_far, 2, axis=0)
    local_coef = (
        leaf_far + jnp.einsum("gkl,glr->gkr", transfer, spread, preferred_element_type=jnp.float32)
    ).astype(jnp.bfloat16)
    window = jnp.concatenate([before[cut:][None], live, after[cut:][None]], axis=0)
    near = jnp.zeros((leaves, leaf_size, sides), jnp.float32)
    for n in range(3):
        near = near + jnp.einsum(
            "gpq,gqr->gpr",
            near_blocks[:, n],
            window[n : n + leaves],
            preferred_element_type=jnp.float32,
        )
    total = jnp.einsum("gpk,gkr->gpr", basis, local_coef, preferred_element_type=jnp.float32) + near
    total = total * mask.astype(jnp.float32)
    return total.astype(jnp.bfloat16).reshape(leaves * leaf_size, sides)


def solution(mesh):
    in_specs = (
        P(("gx", "gy"), None),
        P(("gx", "gy")),
        P(("gx", "gy"), None, None),
        P(("gx", "gy"), None, None),
        P(("gx", "gy"), None, None, None),
        P(("gx", "gy"), None),
        P(("gx", "gy"), None, None, None),
        P(("gx", "gy"), None, None, None),
        P(("gx", "gy"), None),
    )
    out_specs = P(("gx", "gy"), None)
    return jax.shard_map(
        per_device, mesh=mesh, in_specs=in_specs, out_specs=out_specs, check_vma=False
    )
```

```python
import functools

import jax
import jax.numpy as jnp
from jax import lax
from jax.experimental import pallas as pl
from jax.experimental.pallas import tpu as pltpu
from jax.sharding import PartitionSpec as P

VMEM = pl.BlockSpec(memory_space=pltpu.VMEM)
SMEM = pl.BlockSpec(memory_space=pltpu.SMEM)
NN = (((1,), (0,)), ((), ()))
NT = (((1,), (1,)), ((), ()))


def dot(a, b, dims):
    return lax.dot_general(a, b, dims, preferred_element_type=jnp.float32)


def left_half(sides, width):
    return lax.broadcasted_iota(jnp.int32, (sides, 2 * width), 1) < width


def pair_mask(counts_ref, pair, sides, width):
    lane = lax.broadcasted_iota(jnp.int32, (sides, 2 * width), 1)
    left = lane < width
    count = jnp.where(left, counts_ref[2 * pair], counts_ref[2 * pair + 1])
    return jnp.where(left, lane, lane - width) < count


def swap(pair, width):
    return jnp.concatenate([pair[:, width:], pair[:, :width]], axis=1)


def up_kernel(copies, counts_ref, charges_ref, basis_ref, transfer_ref, rim_ref, live_ref, parents_ref):
    sides = charges_ref.shape[0]
    leaves, width, rank = basis_ref.shape
    pairs = leaves // 2
    own = pairs // 2
    left = left_half(sides, width)
    sums = []
    for a in range(pairs):
        charge = charges_ref[:, 2 * width * a : 2 * width * (a + 1)]
        live = jnp.where(pair_mask(counts_ref, a, sides, width), charge, jnp.zeros_like(charge))
        live_ref[a] = live
        if a == 0:
            rim_ref[pairs] = live
        if a == pairs - 1:
            rim_ref[pairs + 1] = live
        none = jnp.zeros_like(live)
        both = jnp.concatenate([jnp.where(left, live, none), jnp.where(left, none, live)], axis=0)
        coef = dot(both, basis_ref[2 * a : 2 * a + 2].reshape(2 * width, rank), NN)
        coef = jnp.concatenate([coef[:sides], coef[sides:]], axis=1).astype(jnp.bfloat16)
        rim_ref[a] = coef
        sums.append(dot(coef, transfer_ref[2 * a : 2 * a + 2].reshape(2 * rank, rank), NN))
        if a % 2 == 1:
            parent = jnp.concatenate(sums, axis=1).astype(jnp.bfloat16)
            sums = []
            for c in range(copies):
                parents_ref[c * own + a // 2] = parent


def spread_pair(dup_ref, at, pair, left, width):
    turned = swap(pair, width)
    dup_ref[at] = jnp.where(left, pair, turned)
    dup_ref[at + 1] = jnp.where(left, turned, pair)


def picked_product(dup_ref, partners, blocks, left):
    lhs = [
        jnp.where(left, dup_ref[partners[j]], dup_ref[partners[j + 1]])
        for j in range(0, len(partners), 2)
    ]
    rhs = [
        jnp.concatenate([blocks[j], blocks[j + 1]], axis=1) for j in range(0, len(partners), 2)
    ]
    return dot(jnp.concatenate(lhs, axis=1), jnp.concatenate(rhs, axis=1), NT)


def leaf_kernel(
    start_ref, partners_ref, rim_ref, before_ref, after_ref, live_ref, coupling_ref, near_ref,
    far_ref, near_out_ref, dup_ref,
):
    leaves, many, rank, _ = coupling_ref.shape
    width = near_ref.shape[2]
    pairs = leaves // 2
    sides = live_ref.shape[1]
    left = left_half(sides, rank)
    for b, ref in enumerate((before_ref, rim_ref, after_ref)):
        for a in range(pairs):
            spread_pair(dup_ref, b * leaves + 2 * a, ref[a], left, rank)
    shift = leaves - start_ref[0]

    def step(a, carry):
        fars = []
        for c in range(2):
            g = 2 * a + c
            partners = [partners_ref[j, g] + shift for j in range(many)]
            fars.append(picked_product(dup_ref, partners, [coupling_ref[g, j] for j in range(many)], left))
        far_ref[a] = jnp.concatenate(fars, axis=1)
        here = live_ref[a]
        prev = jnp.where(a == 0, before_ref[pairs + 1], live_ref[jnp.maximum(a - 1, 0)])
        next_ = jnp.where(a == pairs - 1, after_ref[pairs], live_ref[jnp.minimum(a + 1, pairs - 1)])
        even = dot(here, jnp.concatenate([near_ref[2 * a, 1], near_ref[2 * a, 2]], axis=1), NT)
        even = even + dot(prev[:, width:], near_ref[2 * a, 0], NT)
        odd = dot(here, jnp.concatenate([near_ref[2 * a + 1, 0], near_ref[2 * a + 1, 1]], axis=1), NT)
        odd = odd + dot(next_[:, :width], near_ref[2 * a + 1, 2], NT)
        near_out_ref[a] = jnp.concatenate([even, odd], axis=1)
        return carry

    lax.fori_loop(0, pairs, step, 0, unroll=2)


def down_kernel(
    counts_ref, partners_ref, row_ref, coupling_ref, transfer_ref, basis_ref, far_ref, near_ref,
    out_ref, dup_ref,
):
    parents, many, rank, _ = coupling_ref.shape
    width = basis_ref.shape[1]
    sides = row_ref.shape[1]
    row = 2 * row_ref.shape[0]
    left = left_half(sides, rank)

    def spread(a, carry):
        spread_pair(dup_ref, 2 * a, row_ref[a], left, rank)
        return carry

    lax.fori_loop(0, row_ref.shape[0], spread, 0, unroll=8)

    for q in range(parents):
        partners = [lax.rem(partners_ref[q, j], row) for j in range(many)]
        far = picked_product(dup_ref, partners, [coupling_ref[q, j] for j in range(many)], left)
        far = far.astype(jnp.bfloat16)
        local = far_ref[q] + dot(far, transfer_ref[2 * q : 2 * q + 2].reshape(2 * rank, rank), NT)
        local = local.astype(jnp.bfloat16)
        total = jnp.concatenate(
            [dot(local[:, :rank], basis_ref[2 * q], NT), dot(local[:, rank:], basis_ref[2 * q + 1], NT)],
            axis=1,
        )
        total = total + near_ref[q]
        total = jnp.where(pair_mask(counts_ref, q, sides, width), total, jnp.zeros_like(total))
        out_ref[:, 2 * width * q : 2 * width * (q + 1)] = total.astype(out_ref.dtype)


def shifted(array, axis, by):
    length = lax.axis_size(axis)
    pairs = [(i, i + by) for i in range(length) if 0 <= i + by < length]
    return lax.ppermute(array, axis, pairs)


def per_device(
    charges,
    panel_counts,
    basis,
    transfer,
    leaf_coupling,
    leaf_partners,
    near_blocks,
    parent_coupling,
    parent_partners,
):
    leaves, width, rank = basis.shape
    sides = charges.shape[1]
    pairs = leaves // 2
    own = pairs // 2
    n = lax.axis_size("gy")
    bf16, f32 = jnp.bfloat16, jnp.float32
    shape = jax.ShapeDtypeStruct
    params = pltpu.CompilerParams(vmem_limit_bytes=16 * 2**20)
    rim, live, parents = pl.pallas_call(
        functools.partial(up_kernel, n),
        name="up",
        out_shape=[
            shape((pairs + 2, sides, 2 * rank), bf16),
            shape((pairs, sides, 2 * width), bf16),
            shape((n * own, sides, 2 * rank), bf16),
        ],
        in_specs=[SMEM, VMEM, VMEM, VMEM],
        out_specs=[VMEM, VMEM, VMEM],
        compiler_params=params,
    )(panel_counts, charges.T, basis, transfer)
    row = lax.all_to_all(parents, "gy", 0, 0, tiled=True)
    axes = ("gx", "gy")
    before = shifted(rim, axes, 1)
    after = shifted(rim, axes, -1)
    device = lax.axis_index("gx") * n + lax.axis_index("gy")
    far, near = pl.pallas_call(
        leaf_kernel,
        name="leaf",
        out_shape=[shape((pairs, sides, 2 * rank), f32), shape((pairs, sides, 2 * width), f32)],
        in_specs=[SMEM, SMEM] + [VMEM] * 6,
        out_specs=[VMEM, VMEM],
        scratch_shapes=[pltpu.VMEM((3 * leaves, sides, 2 * rank), bf16)],
        compiler_params=params,
    )(
        (device * leaves).astype(jnp.int32).reshape(1), leaf_partners.T, rim, before, after, live,
        leaf_coupling, near_blocks,
    )
    out = pl.pallas_call(
        down_kernel,
        name="down",
        out_shape=shape((sides, leaves * width), bf16),
        in_specs=[SMEM, SMEM] + [VMEM] * 6,
        out_specs=VMEM,
        scratch_shapes=[pltpu.VMEM((n * pairs, sides, 2 * rank), bf16)],
        compiler_params=params,
    )(panel_counts, parent_partners, row, parent_coupling, transfer, basis, far, near)
    return out.T


def solution(mesh):
    in_specs = (
        P(("gx", "gy"), None),
        P(("gx", "gy")),
        P(("gx", "gy"), None, None),
        P(("gx", "gy"), None, None),
        P(("gx", "gy"), None, None, None),
        P(("gx", "gy"), None),
        P(("gx", "gy"), None, None, None),
        P(("gx", "gy"), None, None, None),
        P(("gx", "gy"), None),
    )
    out_specs = P(("gx", "gy"), None)
    return jax.shard_map(
        per_device, mesh=mesh, in_specs=in_specs, out_specs=out_specs, check_vma=False
    )
```

```python
import functools

import jax
import jax.numpy as jnp
from jax import lax
from jax.experimental import pallas as pl
from jax.experimental.pallas import tpu as pltpu
from jax.sharding import PartitionSpec as P

VMEM = pl.BlockSpec(memory_space=pltpu.VMEM)
HBM = pl.BlockSpec(memory_space=pltpu.HBM)
NN = (((1,), (0,)), ((), ()))
NT = (((1,), (1,)), ((), ()))


def dot(a, b, dims):
    return lax.dot_general(a, b, dims, preferred_element_type=jnp.float32)


def left_half(sides, width):
    return lax.broadcasted_iota(jnp.int32, (sides, 2 * width), 1) < width


def swap(pair, width):
    return jnp.concatenate([pair[:, width:], pair[:, :width]], axis=1)


def start_all(copies, sems):
    started = [pltpu.make_async_copy(src, dst, sems.at[i]) for i, (src, dst) in enumerate(copies)]
    for copy in started:
        copy.start()
    return started


def up_kernel(
    copies, counts_hbm, charges_hbm, basis_hbm, transfer_hbm,
    rim_ref, live_ref, parents_ref, mask_ref,
    counts_ref, charges_ref, basis_ref, transfer_ref, sems,
):
    counts_in, charges_in, basis_in, transfer_in = start_all(
        [
            (counts_hbm, counts_ref), (charges_hbm, charges_ref),
            (basis_hbm, basis_ref), (transfer_hbm, transfer_ref),
        ],
        sems,
    )
    sides = charges_ref.shape[0]
    leaves, width, rank = basis_ref.shape
    pairs = leaves // 2
    own = pairs // 2
    left = left_half(sides, width)
    lane = lax.broadcasted_iota(jnp.int32, (sides, 2 * width), 1)
    slot = jnp.where(left, lane, lane - width)
    counts_in.wait()
    charges_in.wait()
    lives = []
    for a in range(pairs):
        charge = charges_ref[:, 2 * width * a : 2 * width * (a + 1)]
        mask = slot < jnp.where(left, counts_ref[2 * a], counts_ref[2 * a + 1])
        mask_ref[a] = mask[:8].astype(jnp.float32)
        live = jnp.where(mask, charge, jnp.zeros_like(charge))
        live_ref[a] = live
        lives.append(live)
    rim_ref[pairs] = lives[0]
    rim_ref[pairs + 1] = lives[-1]
    basis_in.wait()
    none = jnp.zeros_like(lives[0])
    coefs = []
    for a in range(pairs):
        live = lives[a]
        both = jnp.concatenate([jnp.where(left, live, none), jnp.where(left, none, live)], axis=0)
        coef = dot(both, basis_ref[2 * a : 2 * a + 2].reshape(2 * width, rank), NN)
        coef = jnp.concatenate([coef[:sides], coef[sides:]], axis=1).astype(jnp.bfloat16)
        rim_ref[a] = coef
        coefs.append(coef)
    transfer_in.wait()
    sums = [
        dot(coefs[a], transfer_ref[2 * a : 2 * a + 2].reshape(2 * rank, rank), NN)
        for a in range(pairs)
    ]
    for a in range(own):
        parent = jnp.concatenate(sums[2 * a : 2 * a + 2], axis=1).astype(jnp.bfloat16)
        for c in range(copies):
            parents_ref[c * own + a] = parent


def mid_kernel(
    row_ref, live_ref, coupling_hbm, near_hbm, parent_hbm, basis_hbm, transfer_hbm,
    packed_ref, parent_packed_ref, near_out_ref, rim_near_ref, basis_out_ref, transfer_out_ref,
    coupling_ref, near_ref, parent_ref, sems,
):
    leaves, many, rank, _ = coupling_ref.shape
    parents = parent_ref.shape[0]
    width = near_ref.shape[2]
    pairs = leaves // 2
    started = start_all(
        [(near_hbm, near_ref)]
        + [(coupling_hbm.at[pl.ds(4 * i, 4)], coupling_ref.at[pl.ds(4 * i, 4)]) for i in range(leaves // 4)]
        + [(parent_hbm.at[pl.ds(4 * i, 4)], parent_ref.at[pl.ds(4 * i, 4)]) for i in range(parents // 4)]
        + [(basis_hbm, basis_out_ref), (transfer_hbm, transfer_out_ref)],
        sems,
    )
    near_in, basis_in, transfer_in = started[0], started[-2], started[-1]
    coupling_in = started[1 : 1 + leaves // 4]
    parent_in = started[1 + leaves // 4 : -2]
    near_in.wait()
    rim_near_ref[0] = near_ref[0, 0]
    rim_near_ref[1] = near_ref[leaves - 1, 2]
    for a in range(pairs):
        here = live_ref[a]
        even = dot(here, jnp.concatenate([near_ref[2 * a, 1], near_ref[2 * a, 2]], axis=1), NT)
        odd = dot(here, jnp.concatenate([near_ref[2 * a + 1, 0], near_ref[2 * a + 1, 1]], axis=1), NT)
        if a > 0:
            even = even + dot(live_ref[a - 1][:, width:], near_ref[2 * a, 0], NT)
        if a < pairs - 1:
            odd = odd + dot(live_ref[a + 1][:, :width], near_ref[2 * a + 1, 2], NT)
        near_out_ref[a] = jnp.concatenate([even, odd], axis=1)

    def pack(src, dst, g):
        for j in range(0, many, 2):
            dst[g, :, rank * j : rank * (j + 2)] = jnp.concatenate([src[g, j], src[g, j + 1]], axis=1)

    for i, copy in enumerate(coupling_in):
        copy.wait()
        for g in range(4 * i, 4 * i + 4):
            pack(coupling_ref, packed_ref, g)
    for i, copy in enumerate(parent_in):
        copy.wait()
        for q in range(4 * i, 4 * i + 4):
            pack(parent_ref, parent_packed_ref, q)
    basis_in.wait()
    transfer_in.wait()


def spread_pair(dup_ref, at, pair, left, width):
    turned = swap(pair, width)
    dup_ref[at] = jnp.where(left, pair, turned)
    dup_ref[at + 1] = jnp.where(left, turned, pair)


def picked(dup_ref, partners, left):
    return jnp.concatenate(
        [
            jnp.where(left, dup_ref[partners[j]], dup_ref[partners[j + 1]])
            for j in range(0, len(partners), 2)
        ],
        axis=1,
    )


def leaf_kernel(
    axes, partners_hbm, rim_ref, even_ref, odd_ref, packed_ref, rim_near_ref,
    far_ref, edge_ref, dup_ref, partners_ref, sems,
):
    (partners_in,) = start_all([(partners_hbm, partners_ref)], sems)
    many, leaves = partners_ref.shape
    rank = packed_ref.shape[1]
    width = rim_near_ref.shape[1]
    pairs = leaves // 2
    sides = rim_ref.shape[1]
    left = left_half(sides, rank)
    device = lax.axis_index(axes[0]) * lax.axis_size(axes[1]) + lax.axis_index(axes[1])
    parity = lax.rem(device, 2)
    shift = leaves - device * leaves
    for ref, base in (
        (rim_ref, leaves), (even_ref, 2 * leaves * (1 - parity)), (odd_ref, 2 * leaves * parity),
    ):
        for a in range(pairs):
            spread_pair(dup_ref, base + 2 * a, ref[a], left, rank)
    before = jnp.where(parity == 1, even_ref[pairs + 1], odd_ref[pairs + 1])
    after = jnp.where(parity == 1, odd_ref[pairs], even_ref[pairs])
    low = dot(before[:, width:], rim_near_ref[0], NT)
    high = dot(after[:, :width], rim_near_ref[1], NT)
    edge_ref[0] = jnp.concatenate([low, jnp.zeros_like(low)], axis=1)
    edge_ref[1] = jnp.concatenate([jnp.zeros_like(high), high], axis=1)
    partners_in.wait()
    for a in range(pairs):
        fars = []
        for g in (2 * a, 2 * a + 1):
            partners = [partners_ref[j, g] + shift for j in range(many)]
            fars.append(dot(picked(dup_ref, partners, left), packed_ref[g], NT))
        far_ref[a] = jnp.concatenate(fars, axis=1)


def down_kernel(
    axis, partners_hbm, same_ref, other_ref, packed_ref, transfer_ref, basis_ref,
    far_ref, near_ref, edge_ref, mask_ref,
    out_ref, dup_ref, partners_ref, local_ref, down_ref, sems,
):
    (partners_in,) = start_all([(partners_hbm, partners_ref)], sems)
    parents, many = partners_ref.shape
    rank = packed_ref.shape[1]
    width = basis_ref.shape[1]
    sides = same_ref.shape[1]
    half = 2 * same_ref.shape[0]
    left = left_half(sides, rank)
    parity = lax.rem(lax.axis_index(axis), 2)

    def spread(a, carry):
        spread_pair(dup_ref, half * parity + 2 * a, same_ref[a], left, rank)
        spread_pair(dup_ref, half * (1 - parity) + 2 * a, other_ref[a], left, rank)
        return carry

    lax.fori_loop(0, same_ref.shape[0], spread, 0, unroll=8)
    partners_in.wait()

    def place(partner):
        relative = lax.rem(partner, 2 * half)
        source = relative // parents
        return lax.rem(source, 2) * half + source // 2 * parents + lax.rem(relative, parents)

    for q in range(parents):
        partners = [place(partners_ref[q, j]) for j in range(many)]
        far = dot(picked(dup_ref, partners, left), packed_ref[q], NT)
        down_ref[q] = far.astype(jnp.bfloat16)
    for q in range(parents):
        local = far_ref[q] + dot(down_ref[q], transfer_ref[2 * q : 2 * q + 2].reshape(2 * rank, rank), NT)
        local_ref[q] = local.astype(jnp.bfloat16)
    for q in range(parents):
        local = local_ref[q]
        total = jnp.concatenate(
            [dot(local[:, :rank], basis_ref[2 * q], NT), dot(local[:, rank:], basis_ref[2 * q + 1], NT)],
            axis=1,
        )
        total = total + near_ref[q]
        if q == 0:
            total = total + edge_ref[0]
        if q == parents - 1:
            total = total + edge_ref[1]
        total = total * mask_ref[q][:1]
        out_ref[:, 2 * width * q : 2 * width * (q + 1)] = total.astype(out_ref.dtype)


def per_device(
    charges,
    panel_counts,
    basis,
    transfer,
    leaf_coupling,
    leaf_partners,
    near_blocks,
    parent_coupling,
    parent_partners,
):
    leaves, width, rank = basis.shape
    sides = charges.shape[1]
    parents, many = parent_partners.shape
    pairs = leaves // 2
    own = pairs // 2
    n = lax.axis_size("gy")
    total = n * lax.axis_size("gx")
    axes = ("gx", "gy")
    bf16, f32 = jnp.bfloat16, jnp.float32
    keep = lambda *arrays: [pltpu.with_memory_space_constraint(a, pltpu.HBM) for a in arrays]
    shape = pltpu.VMEM
    dma = lambda count: pltpu.SemaphoreType.DMA((count,))
    params = lambda mib: pltpu.CompilerParams(vmem_limit_bytes=mib * 2**20)

    rim, live, sent, mask = pl.pallas_call(
        functools.partial(up_kernel, n // 2),
        name="up",
        out_shape=[
            shape((pairs + 2, sides, 2 * rank), bf16),
            shape((pairs, sides, 2 * width), bf16),
            shape((n // 2 * own, sides, 2 * rank), bf16),
            shape((pairs, 8, 2 * width), f32),
        ],
        in_specs=[HBM] * 4,
        out_specs=[VMEM] * 4,
        scratch_shapes=[
            pltpu.SMEM((leaves,), jnp.int32),
            pltpu.VMEM((sides, leaves * width), bf16),
            pltpu.VMEM((leaves, width, rank), bf16),
            pltpu.VMEM((leaves, rank, rank), bf16),
            dma(4),
        ],
        compiler_params=params(8),
    )(*keep(panel_counts, charges.T, basis, transfer))

    groups = [list(range(c, n, 2)) for c in range(2)]
    same = lax.all_to_all(sent, "gy", 0, 0, axis_index_groups=groups, tiled=True)
    even = lax.ppermute(rim, axes, [(i, i ^ 1) for i in range(total)])
    steps = [(i, i + 1) for i in range(1, total - 1, 2)]
    odd = lax.ppermute(rim, axes, steps + [(b, a) for a, b in steps])
    other = lax.ppermute(same, "gy", [(i, i ^ 1) for i in range(n)])

    packed, parent_packed, near, rim_near, basis_in, transfer_in = pl.pallas_call(
        mid_kernel,
        name="mid",
        out_shape=[
            shape((leaves, rank, many * rank), bf16),
            shape((parents, rank, many * rank), bf16),
            shape((pairs, sides, 2 * width), f32),
            shape((2, width, width), bf16),
            shape(basis.shape, bf16),
            shape(transfer.shape, bf16),
        ],
        in_specs=[VMEM] * 2 + [HBM] * 5,
        out_specs=[VMEM] * 6,
        scratch_shapes=[
            pltpu.VMEM(leaf_coupling.shape, bf16),
            pltpu.VMEM(near_blocks.shape, bf16),
            pltpu.VMEM(parent_coupling.shape, bf16),
            dma(3 + leaves // 4 + parents // 4),
        ],
        compiler_params=params(20),
    )(same, live, *keep(leaf_coupling, near_blocks, parent_coupling, basis, transfer))

    far, edge = pl.pallas_call(
        functools.partial(leaf_kernel, axes),
        name="leaf",
        out_shape=[shape((pairs, sides, 2 * rank), f32), shape((2, sides, 2 * width), f32)],
        in_specs=[HBM] + [VMEM] * 5,
        out_specs=[VMEM, VMEM],
        scratch_shapes=[
            pltpu.VMEM((3 * leaves, sides, 2 * rank), bf16),
            pltpu.SMEM((leaf_partners.shape[1], leaves), jnp.int32),
            dma(1),
        ],
        compiler_params=params(8),
    )(*keep(leaf_partners.T), rim, even, odd, packed, rim_near)

    out = pl.pallas_call(
        functools.partial(down_kernel, "gy"),
        name="down",
        out_shape=jax.ShapeDtypeStruct((sides, leaves * width), bf16),
        in_specs=[HBM] + [VMEM] * 9,
        out_specs=VMEM,
        scratch_shapes=[
            pltpu.VMEM((n * parents, sides, 2 * rank), bf16),
            pltpu.SMEM(parent_partners.shape, jnp.int32),
            pltpu.VMEM((pairs, sides, 2 * rank), bf16),
            pltpu.VMEM((parents, sides, rank), bf16),
            dma(1),
        ],
        compiler_params=params(12),
    )(*keep(parent_partners), same, other, parent_packed, transfer_in, basis_in, far, near, edge, mask)
    return out.T


def solution(mesh):
    in_specs = (
        P(("gx", "gy"), None),
        P(("gx", "gy")),
        P(("gx", "gy"), None, None),
        P(("gx", "gy"), None, None),
        P(("gx", "gy"), None, None, None),
        P(("gx", "gy"), None),
        P(("gx", "gy"), None, None, None),
        P(("gx", "gy"), None, None, None),
        P(("gx", "gy"), None),
    )
    out_specs = P(("gx", "gy"), None)
    return jax.shard_map(
        per_device, mesh=mesh, in_specs=in_specs, out_specs=out_specs, check_vma=False
    )
```

```python
import functools

import jax
import jax.numpy as jnp
from jax import lax
from jax.experimental import pallas as pl
from jax.experimental.pallas import tpu as pltpu
from jax.sharding import PartitionSpec as P

VMEM = pl.BlockSpec(memory_space=pltpu.VMEM)
HBM = pl.BlockSpec(memory_space=pltpu.HBM)
NN = (((1,), (0,)), ((), ()))
NT = (((1,), (1,)), ((), ()))


def dot(a, b, dims):
    return lax.dot_general(a, b, dims, preferred_element_type=jnp.float32)


def left_half(sides, width):
    return lax.broadcasted_iota(jnp.int32, (sides, 2 * width), 1) < width


def swap(pair, width):
    return jnp.concatenate([pair[:, width:], pair[:, :width]], axis=1)


def mod(x, m):
    return x & (m - 1) if m & (m - 1) == 0 else lax.rem(x, m)


def div(x, m):
    return x >> (m.bit_length() - 1) if m & (m - 1) == 0 else x // m


def position(axes):
    index = 0
    for axis in axes:
        index = index * lax.axis_size(axis) + lax.axis_index(axis)
    return index


def start_all(copies, sems):
    started = [pltpu.make_async_copy(src, dst, sems.at[i]) for i, (src, dst) in enumerate(copies)]
    for copy in started:
        copy.start()
    return started


def up_kernel(
    copies, counts_hbm, charges_hbm, basis_hbm, transfer_hbm,
    rim_ref, live_ref, parents_ref, mask_ref,
    counts_ref, charges_ref, basis_ref, transfer_ref, sems,
):
    counts_in, charges_in, basis_in, transfer_in = start_all(
        [
            (counts_hbm, counts_ref), (charges_hbm, charges_ref),
            (basis_hbm, basis_ref), (transfer_hbm, transfer_ref),
        ],
        sems,
    )
    sides = charges_ref.shape[0]
    leaves, width, rank = basis_ref.shape
    pairs = leaves // 2
    own = pairs // 2
    left = left_half(sides, width)
    lane = lax.broadcasted_iota(jnp.int32, (sides, 2 * width), 1)
    slot = jnp.where(left, lane, lane - width)
    counts_in.wait()
    charges_in.wait()
    lives = []
    for a in range(pairs):
        charge = charges_ref[:, 2 * width * a : 2 * width * (a + 1)]
        mask = slot < jnp.where(left, counts_ref[2 * a], counts_ref[2 * a + 1])
        mask_ref[a] = mask[:8].astype(jnp.float32)
        live = jnp.where(mask, charge, jnp.zeros_like(charge))
        live_ref[a] = live
        lives.append(live)
    rim_ref[pairs] = lives[0]
    rim_ref[pairs + 1] = lives[-1]
    basis_in.wait()
    none = jnp.zeros_like(lives[0])
    coefs = []
    for a in range(pairs):
        live = lives[a]
        both = jnp.concatenate([jnp.where(left, live, none), jnp.where(left, none, live)], axis=0)
        coef = dot(both, basis_ref[2 * a : 2 * a + 2].reshape(2 * width, rank), NN)
        coef = jnp.concatenate([coef[:sides], coef[sides:]], axis=1).astype(jnp.bfloat16)
        rim_ref[a] = coef
        coefs.append(coef)
    transfer_in.wait()
    sums = [
        dot(coefs[a], transfer_ref[2 * a : 2 * a + 2].reshape(2 * rank, rank), NN)
        for a in range(pairs)
    ]
    for a in range(own):
        parent = jnp.concatenate(sums[2 * a : 2 * a + 2], axis=1).astype(jnp.bfloat16)
        for c in range(copies):
            parents_ref[c * own + a] = parent


def mid_kernel(
    axes, live_ref, coupling_hbm, near_hbm, parent_hbm, basis_hbm, transfer_hbm, leaf_partners_hbm,
    parent_partners_hbm,
    packed_ref, parent_packed_ref, near_out_ref, rim_near_ref, basis_out_ref, transfer_out_ref,
    leaf_at_ref, parent_at_ref,
    coupling_ref, near_ref, parent_ref, sems,
):
    leaves, many, rank, _ = coupling_ref.shape
    parents = parent_ref.shape[0]
    width = near_ref.shape[2]
    pairs = leaves // 2
    started = start_all(
        [(near_hbm, near_ref)]
        + [(coupling_hbm.at[pl.ds(4 * i, 4)], coupling_ref.at[pl.ds(4 * i, 4)]) for i in range(leaves // 4)]
        + [(parent_hbm.at[pl.ds(4 * i, 4)], parent_ref.at[pl.ds(4 * i, 4)]) for i in range(parents // 4)]
        + [(basis_hbm, basis_out_ref), (transfer_hbm, transfer_out_ref)]
        + [(leaf_partners_hbm, leaf_at_ref), (parent_partners_hbm, parent_at_ref)],
        sems,
    )
    near_in = started[0]
    coupling_in = started[1 : 1 + leaves // 4]
    parent_in = started[1 + leaves // 4 : -4]
    near_in.wait()
    rim_near_ref[0] = near_ref[0, 0]
    rim_near_ref[1] = near_ref[leaves - 1, 2]
    for a in range(pairs):
        here = live_ref[a]
        even = dot(here, jnp.concatenate([near_ref[2 * a, 1], near_ref[2 * a, 2]], axis=1), NT)
        odd = dot(here, jnp.concatenate([near_ref[2 * a + 1, 0], near_ref[2 * a + 1, 1]], axis=1), NT)
        if a > 0:
            even = even + dot(live_ref[a - 1][:, width:], near_ref[2 * a, 0], NT)
        if a < pairs - 1:
            odd = odd + dot(live_ref[a + 1][:, :width], near_ref[2 * a + 1, 2], NT)
        near_out_ref[a] = jnp.concatenate([even, odd], axis=1)

    def pack(src, dst, g):
        for j in range(0, many, 2):
            dst[g, :, rank * j : rank * (j + 2)] = jnp.concatenate([src[g, j], src[g, j + 1]], axis=1)

    for i, copy in enumerate(coupling_in):
        copy.wait()
        for g in range(4 * i, 4 * i + 4):
            pack(coupling_ref, packed_ref, g)
    for i, copy in enumerate(parent_in):
        copy.wait()
        for q in range(4 * i, 4 * i + 4):
            pack(parent_ref, parent_packed_ref, q)
    for copy in started[-4:]:
        copy.wait()
    wanted = leaf_at_ref[...] + (1 - position(axes)) * leaves
    leaf_at_ref[...] = wanted ^ (lax.broadcasted_iota(jnp.int32, wanted.shape, 0) & 1)
    n, inner = lax.axis_size(axes[1]) * lax.axis_size(axes[2]), lax.axis_size(axes[2])
    wanted = mod(parent_at_ref[...], n * parents)
    source = div(wanted, parents)
    wanted = (mod(source, inner) * (n // inner) + div(source, inner)) * parents + mod(wanted, parents)
    parent_at_ref[...] = wanted ^ (lax.broadcasted_iota(jnp.int32, wanted.shape, 1) & 1)


def spread_pair(table_ref, at, pair, width):
    table_ref[at] = pair
    table_ref[at + 1] = swap(pair, width)


def picked(table_ref, rows, left):
    return jnp.concatenate(
        [
            jnp.where(left, table_ref[rows[j]], table_ref[rows[j + 1]])
            for j in range(0, len(rows), 2)
        ],
        axis=1,
    )


def leaf_kernel(
    axes, at_vmem, rim_ref, even_ref, odd_ref, packed_ref, rim_near_ref,
    far_ref, edge_ref, table_ref, at_ref, sems,
):
    (at_in,) = start_all([(at_vmem, at_ref)], sems)
    many, leaves = at_ref.shape
    rank = packed_ref.shape[1]
    width = rim_near_ref.shape[1]
    pairs = leaves // 2
    sides = rim_ref.shape[1]
    left = left_half(sides, rank)
    parity = lax.rem(position(axes), 2)
    for ref, base in (
        (rim_ref, leaves), (even_ref, 2 * leaves * (1 - parity)), (odd_ref, 2 * leaves * parity),
    ):
        for a in range(pairs):
            spread_pair(table_ref, base + 2 * a, ref[a], rank)
    before = jnp.where(parity == 1, even_ref[pairs + 1], odd_ref[pairs + 1])
    after = jnp.where(parity == 1, odd_ref[pairs], even_ref[pairs])
    low = dot(before[:, width:], rim_near_ref[0], NT)
    high = dot(after[:, :width], rim_near_ref[1], NT)
    edge_ref[0] = jnp.concatenate([low, jnp.zeros_like(low)], axis=1)
    edge_ref[1] = jnp.concatenate([jnp.zeros_like(high), high], axis=1)
    at_in.wait()
    for a in range(pairs):
        fars = []
        for g in (2 * a, 2 * a + 1):
            rows = [at_ref[j, g] for j in range(many)]
            fars.append(dot(picked(table_ref, rows, left), packed_ref[g], NT))
        far_ref[a] = jnp.concatenate(fars, axis=1)


def down_kernel(
    axis, at_vmem, same_ref, other_ref, packed_ref, transfer_ref, basis_ref,
    far_ref, near_ref, edge_ref, mask_ref,
    out_ref, table_ref, at_ref, local_ref, down_ref, sems,
):
    (at_in,) = start_all([(at_vmem, at_ref)], sems)
    parents, many = at_ref.shape
    rank = packed_ref.shape[1]
    width = basis_ref.shape[1]
    sides = same_ref.shape[1]
    half = 2 * same_ref.shape[0]
    left = left_half(sides, rank)
    parity = lax.axis_index(axis)

    def spread(a, carry):
        spread_pair(table_ref, half * parity + 2 * a, same_ref[a], rank)
        spread_pair(table_ref, half * (1 - parity) + 2 * a, other_ref[a], rank)
        return carry

    lax.fori_loop(0, same_ref.shape[0], spread, 0, unroll=min(32, same_ref.shape[0]))
    at_in.wait()
    for q in range(parents):
        rows = [at_ref[q, j] for j in range(many)]
        far = dot(picked(table_ref, rows, left), packed_ref[q], NT)
        down_ref[q] = far.astype(jnp.bfloat16)
    for q in range(parents):
        local = far_ref[q] + dot(down_ref[q], transfer_ref[2 * q : 2 * q + 2].reshape(2 * rank, rank), NT)
        local_ref[q] = local.astype(jnp.bfloat16)
    for q in range(parents):
        local = local_ref[q]
        total = jnp.concatenate(
            [dot(local[:, :rank], basis_ref[2 * q], NT), dot(local[:, rank:], basis_ref[2 * q + 1], NT)],
            axis=1,
        )
        total = total + near_ref[q]
        if q == 0:
            total = total + edge_ref[0]
        if q == parents - 1:
            total = total + edge_ref[1]
        total = total * mask_ref[q][:1]
        out_ref[:, 2 * width * q : 2 * width * (q + 1)] = total.astype(out_ref.dtype)


def per_device(
    charges,
    panel_counts,
    basis,
    transfer,
    leaf_coupling,
    leaf_partners,
    near_blocks,
    parent_coupling,
    parent_partners,
):
    leaves, width, rank = basis.shape
    sides = charges.shape[1]
    parents, many = parent_partners.shape
    pairs = leaves // 2
    own = pairs // 2
    axes = ("gx", "gz", "gp")
    n = lax.axis_size("gz") * lax.axis_size("gp")
    total = n * lax.axis_size("gx")
    bf16, f32 = jnp.bfloat16, jnp.float32
    keep = lambda *arrays: [pltpu.with_memory_space_constraint(a, pltpu.HBM) for a in arrays]
    shape = pltpu.VMEM
    dma = lambda count: pltpu.SemaphoreType.DMA((count,))
    params = lambda mib: pltpu.CompilerParams(vmem_limit_bytes=mib * 2**20)

    rim, live, sent, mask = pl.pallas_call(
        functools.partial(up_kernel, n // 2),
        name="up",
        out_shape=[
            shape((pairs + 2, sides, 2 * rank), bf16),
            shape((pairs, sides, 2 * width), bf16),
            shape((n // 2 * own, sides, 2 * rank), bf16),
            shape((pairs, 8, 2 * width), f32),
        ],
        in_specs=[HBM] * 4,
        out_specs=[VMEM] * 4,
        scratch_shapes=[
            pltpu.SMEM((leaves,), jnp.int32),
            pltpu.VMEM((sides, leaves * width), bf16),
            pltpu.VMEM((leaves, width, rank), bf16),
            pltpu.VMEM((leaves, rank, rank), bf16),
            dma(4),
        ],
        compiler_params=params(8),
    )(*keep(panel_counts, charges.T, basis, transfer))

    same = lax.all_to_all(sent, "gz", 0, 0, tiled=True)
    even = lax.ppermute(rim, axes, [(i, i ^ 1) for i in range(total)])
    steps = [(i, i + 1) for i in range(1, total - 1, 2)]
    odd = lax.ppermute(rim, axes, steps + [(b, a) for a, b in steps])
    other = lax.ppermute(same, "gp", [(0, 1), (1, 0)])

    packed, parent_packed, near, rim_near, basis_in, transfer_in, leaf_at, parent_at = pl.pallas_call(
        functools.partial(mid_kernel, axes),
        name="mid",
        out_shape=[
            shape((leaves, rank, many * rank), bf16),
            shape((parents, rank, many * rank), bf16),
            shape((pairs, sides, 2 * width), f32),
            shape((2, width, width), bf16),
            shape(basis.shape, bf16),
            shape(transfer.shape, bf16),
            shape((many, leaves), jnp.int32),
            shape((parents, many), jnp.int32),
        ],
        in_specs=[VMEM] + [HBM] * 7,
        out_specs=[VMEM] * 8,
        scratch_shapes=[
            pltpu.VMEM(leaf_coupling.shape, bf16),
            pltpu.VMEM(near_blocks.shape, bf16),
            pltpu.VMEM(parent_coupling.shape, bf16),
            dma(5 + leaves // 4 + parents // 4),
        ],
        compiler_params=params(20),
    )(
        live,
        *keep(
            leaf_coupling, near_blocks, parent_coupling, basis, transfer, leaf_partners.T, parent_partners
        ),
    )

    far, edge = pl.pallas_call(
        functools.partial(leaf_kernel, axes),
        name="leaf",
        out_shape=[shape((pairs, sides, 2 * rank), f32), shape((2, sides, 2 * width), f32)],
        in_specs=[VMEM] * 6,
        out_specs=[VMEM, VMEM],
        scratch_shapes=[
            pltpu.VMEM((3 * leaves, sides, 2 * rank), bf16),
            pltpu.SMEM((many, leaves), jnp.int32),
            dma(1),
        ],
        compiler_params=params(8),
    )(leaf_at, rim, even, odd, packed, rim_near)

    out = pl.pallas_call(
        functools.partial(down_kernel, "gp"),
        name="down",
        out_shape=jax.ShapeDtypeStruct((sides, leaves * width), bf16),
        in_specs=[VMEM] * 10,
        out_specs=VMEM,
        scratch_shapes=[
            pltpu.VMEM((n * parents, sides, 2 * rank), bf16),
            pltpu.SMEM((parents, many), jnp.int32),
            pltpu.VMEM((pairs, sides, 2 * rank), bf16),
            pltpu.VMEM((parents, sides, rank), bf16),
            dma(1),
        ],
        compiler_params=params(12),
    )(parent_at, same, other, parent_packed, transfer_in, basis_in, far, near, edge, mask)
    return out.T


def solution(mesh):
    outer, inner = mesh.devices.shape
    split = jax.sharding.Mesh(mesh.devices.reshape(outer, inner // 2, 2), ("gx", "gz", "gp"))
    leaves = ("gx", "gz", "gp")
    in_specs = (
        P(leaves, None),
        P(leaves),
        P(leaves, None, None),
        P(leaves, None, None),
        P(leaves, None, None, None),
        P(leaves, None),
        P(leaves, None, None, None),
        P(leaves, None, None, None),
        P(leaves, None),
    )
    return jax.shard_map(
        per_device, mesh=split, in_specs=in_specs, out_specs=P(leaves, None), check_vma=False
    )
```

```python
import functools

import jax
import jax.numpy as jnp
from jax import lax
from jax.experimental import pallas as pl
from jax.experimental.pallas import tpu as pltpu
from jax.sharding import PartitionSpec as P

VMEM = pl.BlockSpec(memory_space=pltpu.VMEM)
HBM = pl.BlockSpec(memory_space=pltpu.HBM)
NN = (((1,), (0,)), ((), ()))
NT = (((1,), (1,)), ((), ()))


def dot(a, b, dims):
    return lax.dot_general(a, b, dims, preferred_element_type=jnp.float32)


def left_half(sides, width):
    return lax.broadcasted_iota(jnp.int32, (sides, 2 * width), 1) < width


def swap(pair, width):
    return jnp.concatenate([pair[:, width:], pair[:, :width]], axis=1)


def mod(x, m):
    return x & (m - 1) if m & (m - 1) == 0 else lax.rem(x, m)


def position(axes):
    index = 0
    for axis in axes:
        index = index * lax.axis_size(axis) + lax.axis_index(axis)
    return index


def start_all(copies, sems):
    started = [pltpu.make_async_copy(src, dst, sems.at[i]) for i, (src, dst) in enumerate(copies)]
    for copy in started:
        copy.start()
    return started


def up_kernel(
    copies, counts_hbm, charges_hbm, basis_hbm, transfer_hbm,
    rim_ref, live_ref, parents_ref, mask_ref,
    counts_ref, charges_ref, basis_ref, transfer_ref, sems,
):
    counts_in, charges_in, basis_in, transfer_in = start_all(
        [
            (counts_hbm, counts_ref), (charges_hbm, charges_ref),
            (basis_hbm, basis_ref), (transfer_hbm, transfer_ref),
        ],
        sems,
    )
    sides = charges_ref.shape[0]
    leaves, width, rank = basis_ref.shape
    pairs = leaves // 2
    own = pairs // 2
    left = left_half(sides, width)
    lane = lax.broadcasted_iota(jnp.int32, (sides, 2 * width), 1)
    slot = jnp.where(left, lane, lane - width)
    counts_in.wait()
    charges_in.wait()
    lives = []
    for a in range(pairs):
        charge = charges_ref[:, 2 * width * a : 2 * width * (a + 1)]
        mask = slot < jnp.where(left, counts_ref[2 * a], counts_ref[2 * a + 1])
        mask_ref[a] = mask[:8].astype(jnp.float32)
        live = jnp.where(mask, charge, jnp.zeros_like(charge))
        live_ref[a] = live
        lives.append(live)
    rim_ref[pairs] = lives[0]
    rim_ref[pairs + 1] = lives[-1]
    basis_in.wait()
    none = jnp.zeros_like(lives[0])
    coefs = []
    for a in range(pairs):
        live = lives[a]
        both = jnp.concatenate([jnp.where(left, live, none), jnp.where(left, none, live)], axis=0)
        coef = dot(both, basis_ref[2 * a : 2 * a + 2].reshape(2 * width, rank), NN)
        coef = jnp.concatenate([coef[:sides], coef[sides:]], axis=1).astype(jnp.bfloat16)
        rim_ref[a] = coef
        coefs.append(coef)
    transfer_in.wait()
    sums = [
        dot(coefs[a], transfer_ref[2 * a : 2 * a + 2].reshape(2 * rank, rank), NN)
        for a in range(pairs)
    ]
    for a in range(own):
        parent = jnp.concatenate(sums[2 * a : 2 * a + 2], axis=1).astype(jnp.bfloat16)
        for c in range(copies):
            parents_ref[c * own + a] = parent


def mid_kernel(
    axes, live_ref, coupling_hbm, near_hbm, parent_hbm, basis_hbm, transfer_hbm, leaf_partners_hbm,
    parent_partners_hbm,
    packed_ref, parent_packed_ref, near_out_ref, rim_near_ref, basis_out_ref, transfer_out_ref,
    leaf_at_ref, parent_at_ref,
    coupling_ref, near_ref, parent_ref, sems,
):
    leaves, many, rank, _ = coupling_ref.shape
    parents = parent_ref.shape[0]
    width = near_ref.shape[2]
    pairs = leaves // 2
    started = start_all(
        [(near_hbm, near_ref)]
        + [(coupling_hbm.at[pl.ds(4 * i, 4)], coupling_ref.at[pl.ds(4 * i, 4)]) for i in range(leaves // 4)]
        + [(parent_hbm.at[pl.ds(4 * i, 4)], parent_ref.at[pl.ds(4 * i, 4)]) for i in range(parents // 4)]
        + [(basis_hbm, basis_out_ref), (transfer_hbm, transfer_out_ref)]
        + [(leaf_partners_hbm, leaf_at_ref), (parent_partners_hbm, parent_at_ref)],
        sems,
    )
    near_in = started[0]
    coupling_in = started[1 : 1 + leaves // 4]
    parent_in = started[1 + leaves // 4 : -4]
    near_in.wait()
    rim_near_ref[0] = near_ref[0, 0]
    rim_near_ref[1] = near_ref[leaves - 1, 2]
    for a in range(pairs):
        here = live_ref[a]
        even = dot(here, jnp.concatenate([near_ref[2 * a, 1], near_ref[2 * a, 2]], axis=1), NT)
        odd = dot(here, jnp.concatenate([near_ref[2 * a + 1, 0], near_ref[2 * a + 1, 1]], axis=1), NT)
        if a > 0:
            even = even + dot(live_ref[a - 1][:, width:], near_ref[2 * a, 0], NT)
        if a < pairs - 1:
            odd = odd + dot(live_ref[a + 1][:, :width], near_ref[2 * a + 1, 2], NT)
        near_out_ref[a] = jnp.concatenate([even, odd], axis=1)

    def pack(src, dst, g):
        for j in range(0, many, 2):
            dst[g, :, rank * j : rank * (j + 2)] = jnp.concatenate([src[g, j], src[g, j + 1]], axis=1)

    for i, copy in enumerate(coupling_in):
        copy.wait()
        for g in range(4 * i, 4 * i + 4):
            pack(coupling_ref, packed_ref, g)
    for i, copy in enumerate(parent_in):
        copy.wait()
        for q in range(4 * i, 4 * i + 4):
            pack(parent_ref, parent_packed_ref, q)
    for copy in started[-4:]:
        copy.wait()
    wanted = leaf_at_ref[...] + (1 - position(axes)) * leaves
    leaf_at_ref[...] = wanted ^ (lax.broadcasted_iota(jnp.int32, wanted.shape, 0) & 1)
    n = lax.axis_size(axes[1])
    wanted = mod(parent_at_ref[...], n * parents)
    parent_at_ref[...] = wanted ^ (lax.broadcasted_iota(jnp.int32, wanted.shape, 1) & 1)


def spread_pair(table_ref, at, pair, width):
    table_ref[at] = pair
    table_ref[at + 1] = swap(pair, width)


def picked(table_ref, rows, left):
    return jnp.concatenate(
        [
            jnp.where(left, table_ref[rows[j]], table_ref[rows[j + 1]])
            for j in range(0, len(rows), 2)
        ],
        axis=1,
    )


def leaf_kernel(
    axes, at_vmem, rim_ref, even_ref, odd_ref, packed_ref, rim_near_ref,
    far_ref, edge_ref, table_ref, at_ref, sems,
):
    (at_in,) = start_all([(at_vmem, at_ref)], sems)
    many, leaves = at_ref.shape
    rank = packed_ref.shape[1]
    width = rim_near_ref.shape[1]
    pairs = leaves // 2
    sides = rim_ref.shape[1]
    left = left_half(sides, rank)
    parity = lax.rem(position(axes), 2)
    for ref, base in (
        (rim_ref, leaves), (even_ref, 2 * leaves * (1 - parity)), (odd_ref, 2 * leaves * parity),
    ):
        for a in range(pairs):
            spread_pair(table_ref, base + 2 * a, ref[a], rank)
    before = jnp.where(parity == 1, even_ref[pairs + 1], odd_ref[pairs + 1])
    after = jnp.where(parity == 1, odd_ref[pairs], even_ref[pairs])
    low = dot(before[:, width:], rim_near_ref[0], NT)
    high = dot(after[:, :width], rim_near_ref[1], NT)
    edge_ref[0] = jnp.concatenate([low, jnp.zeros_like(low)], axis=1)
    edge_ref[1] = jnp.concatenate([jnp.zeros_like(high), high], axis=1)
    at_in.wait()
    for a in range(pairs):
        fars = []
        for g in (2 * a, 2 * a + 1):
            rows = [at_ref[j, g] for j in range(many)]
            fars.append(dot(picked(table_ref, rows, left), packed_ref[g], NT))
        far_ref[a] = jnp.concatenate(fars, axis=1)


def down_kernel(
    at_vmem, row_ref, packed_ref, transfer_ref, basis_ref,
    far_ref, near_ref, edge_ref, mask_ref,
    out_ref, table_ref, at_ref, local_ref, down_ref, sems,
):
    (at_in,) = start_all([(at_vmem, at_ref)], sems)
    parents, many = at_ref.shape
    rank = packed_ref.shape[1]
    width = basis_ref.shape[1]
    sides = row_ref.shape[1]
    left = left_half(sides, rank)

    def spread(a, carry):
        spread_pair(table_ref, 2 * a, row_ref[a], rank)
        return carry

    lax.fori_loop(0, row_ref.shape[0], spread, 0, unroll=min(64, row_ref.shape[0]))
    at_in.wait()
    for q in range(parents):
        rows = [at_ref[q, j] for j in range(many)]
        far = dot(picked(table_ref, rows, left), packed_ref[q], NT)
        down_ref[q] = far.astype(jnp.bfloat16)
    for q in range(parents):
        local = far_ref[q] + dot(down_ref[q], transfer_ref[2 * q : 2 * q + 2].reshape(2 * rank, rank), NT)
        local_ref[q] = local.astype(jnp.bfloat16)
    for q in range(parents):
        local = local_ref[q]
        total = jnp.concatenate(
            [dot(local[:, :rank], basis_ref[2 * q], NT), dot(local[:, rank:], basis_ref[2 * q + 1], NT)],
            axis=1,
        )
        total = total + near_ref[q]
        if q == 0:
            total = total + edge_ref[0]
        if q == parents - 1:
            total = total + edge_ref[1]
        total = total * mask_ref[q][:1]
        out_ref[:, 2 * width * q : 2 * width * (q + 1)] = total.astype(out_ref.dtype)


def per_device(
    charges,
    panel_counts,
    basis,
    transfer,
    leaf_coupling,
    leaf_partners,
    near_blocks,
    parent_coupling,
    parent_partners,
):
    leaves, width, rank = basis.shape
    sides = charges.shape[1]
    parents, many = parent_partners.shape
    pairs = leaves // 2
    own = pairs // 2
    axes = ("gx", "gy")
    n = lax.axis_size("gy")
    total = n * lax.axis_size("gx")
    bf16, f32 = jnp.bfloat16, jnp.float32
    keep = lambda *arrays: [pltpu.with_memory_space_constraint(a, pltpu.HBM) for a in arrays]
    shape = pltpu.VMEM
    dma = lambda count: pltpu.SemaphoreType.DMA((count,))
    params = lambda mib: pltpu.CompilerParams(vmem_limit_bytes=mib * 2**20)

    rim, live, sent, mask = pl.pallas_call(
        functools.partial(up_kernel, n),
        name="up",
        out_shape=[
            shape((pairs + 2, sides, 2 * rank), bf16),
            shape((pairs, sides, 2 * width), bf16),
            shape((n * own, sides, 2 * rank), bf16),
            shape((pairs, 8, 2 * width), f32),
        ],
        in_specs=[HBM] * 4,
        out_specs=[VMEM] * 4,
        scratch_shapes=[
            pltpu.SMEM((leaves,), jnp.int32),
            pltpu.VMEM((sides, leaves * width), bf16),
            pltpu.VMEM((leaves, width, rank), bf16),
            pltpu.VMEM((leaves, rank, rank), bf16),
            dma(4),
        ],
        compiler_params=params(8),
    )(*keep(panel_counts, charges.T, basis, transfer))

    row = lax.all_to_all(sent, "gy", 0, 0, tiled=True)
    even = lax.ppermute(rim, axes, [(i, i ^ 1) for i in range(total)])
    steps = [(i, i + 1) for i in range(1, total - 1, 2)]
    odd = lax.ppermute(rim, axes, steps + [(b, a) for a, b in steps])

    packed, parent_packed, near, rim_near, basis_in, transfer_in, leaf_at, parent_at = pl.pallas_call(
        functools.partial(mid_kernel, axes),
        name="mid",
        out_shape=[
            shape((leaves, rank, many * rank), bf16),
            shape((parents, rank, many * rank), bf16),
            shape((pairs, sides, 2 * width), f32),
            shape((2, width, width), bf16),
            shape(basis.shape, bf16),
            shape(transfer.shape, bf16),
            shape((many, leaves), jnp.int32),
            shape((parents, many), jnp.int32),
        ],
        in_specs=[VMEM] + [HBM] * 7,
        out_specs=[VMEM] * 8,
        scratch_shapes=[
            pltpu.VMEM(leaf_coupling.shape, bf16),
            pltpu.VMEM(near_blocks.shape, bf16),
            pltpu.VMEM(parent_coupling.shape, bf16),
            dma(5 + leaves // 4 + parents // 4),
        ],
        compiler_params=params(20),
    )(
        live,
        *keep(
            leaf_coupling, near_blocks, parent_coupling, basis, transfer, leaf_partners.T, parent_partners
        ),
    )

    far, edge = pl.pallas_call(
        functools.partial(leaf_kernel, axes),
        name="leaf",
        out_shape=[shape((pairs, sides, 2 * rank), f32), shape((2, sides, 2 * width), f32)],
        in_specs=[VMEM] * 6,
        out_specs=[VMEM, VMEM],
        scratch_shapes=[
            pltpu.VMEM((3 * leaves, sides, 2 * rank), bf16),
            pltpu.SMEM((many, leaves), jnp.int32),
            dma(1),
        ],
        compiler_params=params(8),
    )(leaf_at, rim, even, odd, packed, rim_near)

    out = pl.pallas_call(
        down_kernel,
        name="down",
        out_shape=jax.ShapeDtypeStruct((sides, leaves * width), bf16),
        in_specs=[VMEM] * 9,
        out_specs=VMEM,
        scratch_shapes=[
            pltpu.VMEM((n * parents, sides, 2 * rank), bf16),
            pltpu.SMEM((parents, many), jnp.int32),
            pltpu.VMEM((pairs, sides, 2 * rank), bf16),
            pltpu.VMEM((parents, sides, rank), bf16),
            dma(1),
        ],
        compiler_params=params(12),
    )(parent_at, row, parent_packed, transfer_in, basis_in, far, near, edge, mask)
    return out.T


def solution(mesh):
    leaves = ("gx", "gy")
    in_specs = (
        P(leaves, None),
        P(leaves),
        P(leaves, None, None),
        P(leaves, None, None),
        P(leaves, None, None, None),
        P(leaves, None),
        P(leaves, None, None, None),
        P(leaves, None, None, None),
        P(leaves, None),
    )
    return jax.shard_map(
        per_device, mesh=mesh, in_specs=in_specs, out_specs=P(leaves, None), check_vma=False
    )
```

```python
import functools

import jax
import jax.numpy as jnp
from jax import lax
from jax.experimental import pallas as pl
from jax.experimental.pallas import tpu as pltpu
from jax.sharding import PartitionSpec as P

VMEM = pl.BlockSpec(memory_space=pltpu.VMEM)
HBM = pl.BlockSpec(memory_space=pltpu.HBM)
NN = (((1,), (0,)), ((), ()))
NT = (((1,), (1,)), ((), ()))


def dot(a, b, dims):
    return lax.dot_general(a, b, dims, preferred_element_type=jnp.float32)


def left_half(sides, width):
    return lax.broadcasted_iota(jnp.int32, (sides, 2 * width), 1) < width


def pair_mask(counts_ref, pair, sides, width):
    lane = lax.broadcasted_iota(jnp.int32, (sides, 2 * width), 1)
    left = lane < width
    count = jnp.where(left, counts_ref[2 * pair], counts_ref[2 * pair + 1])
    return jnp.where(left, lane, lane - width) < count


def swap(pair, width):
    return jnp.concatenate([pair[:, width:], pair[:, :width]], axis=1)


def mod(x, m):
    return x & (m - 1) if m & (m - 1) == 0 else lax.rem(x, m)


def position(axes):
    index = 0
    for axis in axes:
        index = index * lax.axis_size(axis) + lax.axis_index(axis)
    return index


def start_all(copies, sems):
    started = [pltpu.make_async_copy(src, dst, sems.at[i]) for i, (src, dst) in enumerate(copies)]
    for copy in started:
        copy.start()
    return started


def up_kernel(
    copies, counts_hbm, charges_hbm, basis_hbm, transfer_hbm,
    rim_ref, live_ref, parents_ref,
    counts_ref, charges_ref, basis_ref, transfer_ref, sems,
):
    counts_in, charges_in, basis_in, transfer_in = start_all(
        [
            (counts_hbm, counts_ref), (charges_hbm, charges_ref),
            (basis_hbm, basis_ref), (transfer_hbm, transfer_ref),
        ],
        sems,
    )
    sides = charges_ref.shape[0]
    leaves, width, rank = basis_ref.shape
    pairs = leaves // 2
    own = pairs // 2
    left = left_half(sides, width)
    counts_in.wait()
    charges_in.wait()
    lives = []
    for a in range(pairs):
        charge = charges_ref[:, 2 * width * a : 2 * width * (a + 1)]
        live = jnp.where(pair_mask(counts_ref, a, sides, width), charge, jnp.zeros_like(charge))
        live_ref[a] = live
        lives.append(live)
    rim_ref[pairs] = lives[0]
    rim_ref[pairs + 1] = lives[-1]
    basis_in.wait()
    none = jnp.zeros_like(lives[0])
    coefs = []
    for a in range(pairs):
        live = lives[a]
        both = jnp.concatenate([jnp.where(left, live, none), jnp.where(left, none, live)], axis=0)
        coef = dot(both, basis_ref[2 * a : 2 * a + 2].reshape(2 * width, rank), NN)
        coef = jnp.concatenate([coef[:sides], coef[sides:]], axis=1).astype(jnp.bfloat16)
        rim_ref[a] = coef
        coefs.append(coef)
    transfer_in.wait()
    sums = [
        dot(coefs[a], transfer_ref[2 * a : 2 * a + 2].reshape(2 * rank, rank), NN)
        for a in range(pairs)
    ]
    for a in range(own):
        parent = jnp.concatenate(sums[2 * a : 2 * a + 2], axis=1).astype(jnp.bfloat16)
        for c in range(copies):
            parents_ref[c * own + a] = parent


def mid_kernel(
    axes, live_ref, coupling_hbm, near_hbm, parent_hbm, leaf_partners_hbm, parent_partners_hbm,
    packed_ref, first_ref, second_hbm, near_out_ref, rim_near_ref, leaf_at_ref, parent_at_ref,
    coupling_ref, near_ref, parent_ref, second_ref, sems,
):
    leaves, many, rank, _ = coupling_ref.shape
    parents = parent_ref.shape[0]
    width = near_ref.shape[2]
    pairs = leaves // 2
    started = start_all(
        [(near_hbm, near_ref)]
        + [(parent_hbm.at[pl.ds(4 * i, 4)], parent_ref.at[pl.ds(4 * i, 4)]) for i in reversed(range(parents // 4))]
        + [(coupling_hbm.at[pl.ds(4 * i, 4)], coupling_ref.at[pl.ds(4 * i, 4)]) for i in range(leaves // 4)]
        + [(leaf_partners_hbm, leaf_at_ref), (parent_partners_hbm, parent_at_ref)],
        sems,
    )
    near_in = started[0]
    parent_in = started[1 : 1 + parents // 4][::-1]
    coupling_in = started[1 + parents // 4 : -2]
    near_in.wait()
    rim_near_ref[0] = near_ref[0, 0]
    rim_near_ref[1] = near_ref[leaves - 1, 2]
    for a in range(pairs):
        here = live_ref[a]
        even = dot(here, jnp.concatenate([near_ref[2 * a, 1], near_ref[2 * a, 2]], axis=1), NT)
        odd = dot(here, jnp.concatenate([near_ref[2 * a + 1, 0], near_ref[2 * a + 1, 1]], axis=1), NT)
        if a > 0:
            even = even + dot(live_ref[a - 1][:, width:], near_ref[2 * a, 0], NT)
        if a < pairs - 1:
            odd = odd + dot(live_ref[a + 1][:, :width], near_ref[2 * a + 1, 2], NT)
        near_out_ref[a] = jnp.concatenate([even, odd], axis=1)

    def pack(src, dst, g, to):
        for j in range(0, many, 2):
            dst[to, :, rank * j : rank * (j + 2)] = jnp.concatenate([src[g, j], src[g, j + 1]], axis=1)

    half = first_ref.shape[0]
    for i, copy in reversed(list(enumerate(parent_in))):
        copy.wait()
        for q in range(4 * i, 4 * i + 4):
            if q < half:
                pack(parent_ref, first_ref, q, q)
            else:
                pack(parent_ref, second_ref, q, q - half)
        if 4 * i == half:
            out = pltpu.make_async_copy(second_ref, second_hbm, sems.at[len(started)])
            out.start()
    for i, copy in enumerate(coupling_in):
        copy.wait()
        for g in range(4 * i, 4 * i + 4):
            pack(coupling_ref, packed_ref, g, g)
    for copy in started[-2:]:
        copy.wait()
    out.wait()
    wanted = leaf_at_ref[...] + (1 - position(axes)) * leaves
    leaf_at_ref[...] = wanted ^ (lax.broadcasted_iota(jnp.int32, wanted.shape, 0) & 1)
    n = lax.axis_size(axes[1])
    wanted = mod(parent_at_ref[...], n * parents)
    parent_at_ref[...] = wanted ^ (lax.broadcasted_iota(jnp.int32, wanted.shape, 1) & 1)


def spread_pair(table_ref, at, pair, width):
    table_ref[at] = pair
    table_ref[at + 1] = swap(pair, width)


def picked(table_ref, rows, left):
    return jnp.concatenate(
        [
            jnp.where(left, table_ref[rows[j]], table_ref[rows[j + 1]])
            for j in range(0, len(rows), 2)
        ],
        axis=1,
    )


def leaf_kernel(
    axes, at_vmem, rim_ref, even_ref, odd_ref, packed_ref, rim_near_ref,
    far_ref, edge_ref, table_ref, at_ref, sems,
):
    (at_in,) = start_all([(at_vmem, at_ref)], sems)
    many, leaves = at_ref.shape
    rank = packed_ref.shape[1]
    width = rim_near_ref.shape[1]
    pairs = leaves // 2
    sides = rim_ref.shape[1]
    left = left_half(sides, rank)
    parity = lax.rem(position(axes), 2)
    for ref, base in (
        (rim_ref, leaves), (even_ref, 2 * leaves * (1 - parity)), (odd_ref, 2 * leaves * parity),
    ):
        for a in range(pairs):
            spread_pair(table_ref, base + 2 * a, ref[a], rank)
    before = jnp.where(parity == 1, even_ref[pairs + 1], odd_ref[pairs + 1])
    after = jnp.where(parity == 1, odd_ref[pairs], even_ref[pairs])
    low = dot(before[:, width:], rim_near_ref[0], NT)
    high = dot(after[:, :width], rim_near_ref[1], NT)
    edge_ref[0] = jnp.concatenate([low, jnp.zeros_like(low)], axis=1)
    edge_ref[1] = jnp.concatenate([jnp.zeros_like(high), high], axis=1)
    at_in.wait()
    for a in range(pairs):
        fars = []
        for g in (2 * a, 2 * a + 1):
            rows = [at_ref[j, g] for j in range(many)]
            fars.append(dot(picked(table_ref, rows, left), packed_ref[g], NT))
        far_ref[a] = jnp.concatenate(fars, axis=1)


def down_kernel(
    at_vmem, row_ref, first_ref, second_hbm, transfer_hbm, basis_hbm, counts_hbm,
    far_ref, near_ref, edge_ref,
    out_ref, table_ref, at_ref, local_ref, down_ref, second_ref, transfer_ref, basis_ref, counts_ref, sems,
):
    at_in, second_in, transfer_in, basis_in, counts_in = start_all(
        [
            (at_vmem, at_ref), (second_hbm, second_ref), (transfer_hbm, transfer_ref),
            (basis_hbm, basis_ref), (counts_hbm, counts_ref),
        ],
        sems,
    )
    parents, many = at_ref.shape
    rank = first_ref.shape[1]
    half = first_ref.shape[0]
    width = basis_ref.shape[1]
    sides = row_ref.shape[1]
    left = left_half(sides, rank)

    def spread(a, carry):
        spread_pair(table_ref, 2 * a, row_ref[a], rank)
        return carry

    lax.fori_loop(0, row_ref.shape[0], spread, 0, unroll=min(64, row_ref.shape[0]))
    at_in.wait()
    for q in range(parents):
        if q == half:
            second_in.wait()
        rows = [at_ref[q, j] for j in range(many)]
        packed = first_ref[q] if q < half else second_ref[q - half]
        far = dot(picked(table_ref, rows, left), packed, NT)
        down_ref[q] = far.astype(jnp.bfloat16)
    transfer_in.wait()
    for q in range(parents):
        local = far_ref[q] + dot(down_ref[q], transfer_ref[2 * q : 2 * q + 2].reshape(2 * rank, rank), NT)
        local_ref[q] = local.astype(jnp.bfloat16)
    basis_in.wait()
    counts_in.wait()
    for q in range(parents):
        local = local_ref[q]
        total = jnp.concatenate(
            [dot(local[:, :rank], basis_ref[2 * q], NT), dot(local[:, rank:], basis_ref[2 * q + 1], NT)],
            axis=1,
        )
        total = total + near_ref[q]
        if q == 0:
            total = total + edge_ref[0]
        if q == parents - 1:
            total = total + edge_ref[1]
        total = jnp.where(pair_mask(counts_ref, q, sides, width), total, jnp.zeros_like(total))
        out_ref[:, 2 * width * q : 2 * width * (q + 1)] = total.astype(out_ref.dtype)


def per_device(
    charges,
    panel_counts,
    basis,
    transfer,
    leaf_coupling,
    leaf_partners,
    near_blocks,
    parent_coupling,
    parent_partners,
):
    leaves, width, rank = basis.shape
    sides = charges.shape[1]
    parents, many = parent_partners.shape
    pairs = leaves // 2
    own = pairs // 2
    axes = ("gx", "gy")
    n = lax.axis_size("gy")
    total = n * lax.axis_size("gx")
    bf16, f32 = jnp.bfloat16, jnp.float32
    keep = lambda *arrays: [pltpu.with_memory_space_constraint(a, pltpu.HBM) for a in arrays]
    shape = pltpu.VMEM
    dma = lambda count: pltpu.SemaphoreType.DMA((count,))
    params = lambda mib: pltpu.CompilerParams(vmem_limit_bytes=mib * 2**20)

    rim, live, sent = pl.pallas_call(
        functools.partial(up_kernel, n),
        name="up",
        out_shape=[
            shape((pairs + 2, sides, 2 * rank), bf16),
            shape((pairs, sides, 2 * width), bf16),
            shape((n * own, sides, 2 * rank), bf16),
        ],
        in_specs=[HBM] * 4,
        out_specs=[VMEM] * 3,
        scratch_shapes=[
            pltpu.SMEM((leaves,), jnp.int32),
            pltpu.VMEM((sides, leaves * width), bf16),
            pltpu.VMEM((leaves, width, rank), bf16),
            pltpu.VMEM((leaves, rank, rank), bf16),
            dma(4),
        ],
        compiler_params=params(8),
    )(*keep(panel_counts, charges.T, basis, transfer))

    row = lax.all_to_all(sent, "gy", 0, 0, tiled=True)
    even = lax.ppermute(rim, axes, [(i, i ^ 1) for i in range(total)])
    steps = [(i, i + 1) for i in range(1, total - 1, 2)]
    odd = lax.ppermute(rim, axes, steps + [(b, a) for a, b in steps])

    half = parents // 8 * 4
    packed, first, second, near, rim_near, leaf_at, parent_at = pl.pallas_call(
        functools.partial(mid_kernel, axes),
        name="mid",
        out_shape=[
            shape((leaves, rank, many * rank), bf16),
            shape((half, rank, many * rank), bf16),
            pltpu.HBM((parents - half, rank, many * rank), bf16),
            shape((pairs, sides, 2 * width), f32),
            shape((2, width, width), bf16),
            shape((many, leaves), jnp.int32),
            shape((parents, many), jnp.int32),
        ],
        in_specs=[VMEM] + [HBM] * 5,
        out_specs=[VMEM] * 2 + [HBM] + [VMEM] * 4,
        scratch_shapes=[
            pltpu.VMEM(leaf_coupling.shape, bf16),
            pltpu.VMEM(near_blocks.shape, bf16),
            pltpu.VMEM(parent_coupling.shape, bf16),
            pltpu.VMEM((parents - half, rank, many * rank), bf16),
            dma(4 + leaves // 4 + parents // 4),
        ],
        compiler_params=params(20),
    )(live, *keep(leaf_coupling, near_blocks, parent_coupling, leaf_partners.T, parent_partners))

    far, edge = pl.pallas_call(
        functools.partial(leaf_kernel, axes),
        name="leaf",
        out_shape=[shape((pairs, sides, 2 * rank), f32), shape((2, sides, 2 * width), f32)],
        in_specs=[VMEM] * 6,
        out_specs=[VMEM, VMEM],
        scratch_shapes=[
            pltpu.VMEM((3 * leaves, sides, 2 * rank), bf16),
            pltpu.SMEM((many, leaves), jnp.int32),
            dma(1),
        ],
        compiler_params=params(8),
    )(leaf_at, rim, even, odd, packed, rim_near)

    out = pl.pallas_call(
        down_kernel,
        name="down",
        out_shape=jax.ShapeDtypeStruct((sides, leaves * width), bf16),
        in_specs=[VMEM] * 3 + [HBM] * 4 + [VMEM] * 3,
        out_specs=VMEM,
        scratch_shapes=[
            pltpu.VMEM((n * parents, sides, 2 * rank), bf16),
            pltpu.SMEM((parents, many), jnp.int32),
            pltpu.VMEM((pairs, sides, 2 * rank), bf16),
            pltpu.VMEM((parents, sides, rank), bf16),
            pltpu.VMEM((parents - half, rank, many * rank), bf16),
            pltpu.VMEM(transfer.shape, bf16),
            pltpu.VMEM(basis.shape, bf16),
            pltpu.SMEM((leaves,), jnp.int32),
            dma(5),
        ],
        compiler_params=params(12),
    )(parent_at, row, first, *keep(second, transfer, basis, panel_counts), far, near, edge)
    return out.T


def solution(mesh):
    leaves = ("gx", "gy")
    in_specs = (
        P(leaves, None),
        P(leaves),
        P(leaves, None, None),
        P(leaves, None, None),
        P(leaves, None, None, None),
        P(leaves, None),
        P(leaves, None, None, None),
        P(leaves, None, None, None),
        P(leaves, None),
    )
    return jax.shard_map(
        per_device, mesh=mesh, in_specs=in_specs, out_specs=P(leaves, None), check_vma=False
    )
```

```python
import functools

import jax
import jax.numpy as jnp
from jax import lax
from jax.experimental import pallas as pl
from jax.experimental.pallas import tpu as pltpu
from jax.sharding import PartitionSpec as P

VMEM = pl.BlockSpec(memory_space=pltpu.VMEM)
HBM = pl.BlockSpec(memory_space=pltpu.HBM)
NN = (((1,), (0,)), ((), ()))
NT = (((1,), (1,)), ((), ()))


def dot(a, b, dims):
    return lax.dot_general(a, b, dims, preferred_element_type=jnp.float32)


def left_half(sides, width):
    return lax.broadcasted_iota(jnp.int32, (sides, 2 * width), 1) < width


def pair_mask(counts_ref, pair, sides, width):
    lane = lax.broadcasted_iota(jnp.int32, (sides, 2 * width), 1)
    left = lane < width
    count = jnp.where(left, counts_ref[2 * pair], counts_ref[2 * pair + 1])
    return jnp.where(left, lane, lane - width) < count


def swap(pair, width):
    return jnp.concatenate([pair[:, width:], pair[:, :width]], axis=1)


def mod(x, m):
    return x & (m - 1) if m & (m - 1) == 0 else lax.rem(x, m)


def position(axes):
    index = 0
    for axis in axes:
        index = index * lax.axis_size(axis) + lax.axis_index(axis)
    return index


def start_all(copies, sems):
    started = [pltpu.make_async_copy(src, dst, sems.at[i]) for i, (src, dst) in enumerate(copies)]
    for copy in started:
        copy.start()
    return started


def up_kernel(
    counts_hbm, charges_hbm, basis_hbm, transfer_hbm,
    rim_ref, live_ref, parents_ref,
    counts_ref, charges_ref, basis_ref, transfer_ref, sems,
):
    counts_in, charges_in, basis_in, transfer_in = start_all(
        [
            (counts_hbm, counts_ref), (charges_hbm, charges_ref),
            (basis_hbm, basis_ref), (transfer_hbm, transfer_ref),
        ],
        sems,
    )
    sides = charges_ref.shape[0]
    leaves, width, rank = basis_ref.shape
    pairs = leaves // 2
    own = pairs // 2
    left = left_half(sides, width)
    counts_in.wait()
    charges_in.wait()
    lives = []
    for a in range(pairs):
        charge = charges_ref[:, 2 * width * a : 2 * width * (a + 1)]
        live = jnp.where(pair_mask(counts_ref, a, sides, width), charge, jnp.zeros_like(charge))
        live_ref[a] = live
        lives.append(live)
    rim_ref[pairs] = lives[0]
    rim_ref[pairs + 1] = lives[-1]
    basis_in.wait()
    none = jnp.zeros_like(lives[0])
    coefs = []
    for a in range(pairs):
        live = lives[a]
        both = jnp.concatenate([jnp.where(left, live, none), jnp.where(left, none, live)], axis=0)
        coef = dot(both, basis_ref[2 * a : 2 * a + 2].reshape(2 * width, rank), NN)
        coef = jnp.concatenate([coef[:sides], coef[sides:]], axis=1).astype(jnp.bfloat16)
        rim_ref[a] = coef
        coefs.append(coef)
    transfer_in.wait()
    sums = [
        dot(coefs[a], transfer_ref[2 * a : 2 * a + 2].reshape(2 * rank, rank), NN)
        for a in range(pairs)
    ]
    for a in range(own):
        parents_ref[a] = jnp.concatenate(sums[2 * a : 2 * a + 2], axis=1).astype(jnp.bfloat16)


def copies_kernel(parents_ref, sent_hbm, sems):
    own = parents_ref.shape[0]
    copies = sent_hbm.shape[0] // own
    for copy in start_all([(parents_ref, sent_hbm.at[pl.ds(own * c, own)]) for c in range(copies)], sems):
        copy.wait()


def mid_kernel(
    axes, live_ref, coupling_hbm, near_hbm, parent_hbm, leaf_partners_hbm, parent_partners_hbm,
    packed_ref, first_ref, second_hbm, near_out_ref, rim_near_ref, leaf_at_ref, parent_at_ref,
    coupling_ref, near_ref, parent_ref, second_ref, sems,
):
    leaves, many, rank, _ = coupling_ref.shape
    parents = parent_ref.shape[0]
    width = near_ref.shape[2]
    pairs = leaves // 2
    started = start_all(
        [(near_hbm, near_ref)]
        + [(parent_hbm.at[pl.ds(4 * i, 4)], parent_ref.at[pl.ds(4 * i, 4)]) for i in reversed(range(parents // 4))]
        + [(coupling_hbm.at[pl.ds(4 * i, 4)], coupling_ref.at[pl.ds(4 * i, 4)]) for i in range(leaves // 4)]
        + [(leaf_partners_hbm, leaf_at_ref), (parent_partners_hbm, parent_at_ref)],
        sems,
    )
    near_in = started[0]
    parent_in = started[1 : 1 + parents // 4][::-1]
    coupling_in = started[1 + parents // 4 : -2]
    near_in.wait()
    rim_near_ref[0] = near_ref[0, 0]
    rim_near_ref[1] = near_ref[leaves - 1, 2]
    for a in range(pairs):
        here = live_ref[a]
        even = dot(here, jnp.concatenate([near_ref[2 * a, 1], near_ref[2 * a, 2]], axis=1), NT)
        odd = dot(here, jnp.concatenate([near_ref[2 * a + 1, 0], near_ref[2 * a + 1, 1]], axis=1), NT)
        if a > 0:
            even = even + dot(live_ref[a - 1][:, width:], near_ref[2 * a, 0], NT)
        if a < pairs - 1:
            odd = odd + dot(live_ref[a + 1][:, :width], near_ref[2 * a + 1, 2], NT)
        near_out_ref[a] = jnp.concatenate([even, odd], axis=1)

    def pack(src, dst, g, to):
        for j in range(0, many, 2):
            dst[to, :, rank * j : rank * (j + 2)] = jnp.concatenate([src[g, j], src[g, j + 1]], axis=1)

    half = first_ref.shape[0]
    for i, copy in reversed(list(enumerate(parent_in))):
        copy.wait()
        for q in range(4 * i, 4 * i + 4):
            if q < half:
                pack(parent_ref, first_ref, q, q)
            else:
                pack(parent_ref, second_ref, q, q - half)
        if 4 * i == half:
            out = pltpu.make_async_copy(second_ref, second_hbm, sems.at[len(started)])
            out.start()
    for i, copy in enumerate(coupling_in):
        copy.wait()
        for g in range(4 * i, 4 * i + 4):
            pack(coupling_ref, packed_ref, g, g)
    for copy in started[-2:]:
        copy.wait()
    out.wait()
    wanted = leaf_at_ref[...] + (1 - position(axes)) * leaves
    leaf_at_ref[...] = wanted ^ (lax.broadcasted_iota(jnp.int32, wanted.shape, 0) & 1)
    n = lax.axis_size(axes[1])
    wanted = mod(parent_at_ref[...], n * parents)
    parent_at_ref[...] = wanted ^ (lax.broadcasted_iota(jnp.int32, wanted.shape, 1) & 1)


def spread_pair(table_ref, at, pair, width):
    table_ref[at] = pair
    table_ref[at + 1] = swap(pair, width)


def picked(table_ref, rows, left):
    return jnp.concatenate(
        [
            jnp.where(left, table_ref[rows[j]], table_ref[rows[j + 1]])
            for j in range(0, len(rows), 2)
        ],
        axis=1,
    )


def leaf_kernel(
    axes, at_vmem, rim_ref, even_ref, odd_ref, packed_ref, rim_near_ref, transfer_hbm,
    far_ref, edge_ref, transfer_ref, table_ref, at_ref, sems,
):
    at_in, transfer_in = start_all([(at_vmem, at_ref), (transfer_hbm, transfer_ref)], sems)
    many, leaves = at_ref.shape
    rank = packed_ref.shape[1]
    width = rim_near_ref.shape[1]
    pairs = leaves // 2
    sides = rim_ref.shape[1]
    left = left_half(sides, rank)
    parity = lax.rem(position(axes), 2)
    for ref, base in (
        (rim_ref, leaves), (even_ref, 2 * leaves * (1 - parity)), (odd_ref, 2 * leaves * parity),
    ):
        for a in range(pairs):
            spread_pair(table_ref, base + 2 * a, ref[a], rank)
    before = jnp.where(parity == 1, even_ref[pairs + 1], odd_ref[pairs + 1])
    after = jnp.where(parity == 1, odd_ref[pairs], even_ref[pairs])
    low = dot(before[:, width:], rim_near_ref[0], NT)
    high = dot(after[:, :width], rim_near_ref[1], NT)
    edge_ref[0] = jnp.concatenate([low, jnp.zeros_like(low)], axis=1)
    edge_ref[1] = jnp.concatenate([jnp.zeros_like(high), high], axis=1)
    at_in.wait()
    for a in range(pairs):
        fars = []
        for g in (2 * a, 2 * a + 1):
            rows = [at_ref[j, g] for j in range(many)]
            fars.append(dot(picked(table_ref, rows, left), packed_ref[g], NT))
        far_ref[a] = jnp.concatenate(fars, axis=1)
    transfer_in.wait()


def down_kernel(
    at_vmem, row_ref, first_ref, second_hbm, basis_hbm, counts_hbm,
    far_ref, near_ref, edge_ref, transfer_ref,
    out_ref, table_ref, at_ref, local_ref, down_ref, second_ref, basis_ref, counts_ref, sems,
):
    at_in, second_in, basis_in, counts_in = start_all(
        [
            (at_vmem, at_ref), (second_hbm, second_ref), (basis_hbm, basis_ref), (counts_hbm, counts_ref),
        ],
        sems,
    )
    parents, many = at_ref.shape
    rank = first_ref.shape[1]
    half = first_ref.shape[0]
    width = basis_ref.shape[1]
    sides = row_ref.shape[1]
    left = left_half(sides, rank)

    def spread(a, carry):
        spread_pair(table_ref, 2 * a, row_ref[a], rank)
        return carry

    lax.fori_loop(0, row_ref.shape[0], spread, 0, unroll=min(64, row_ref.shape[0]))
    at_in.wait()
    for q in range(parents):
        if q == half:
            second_in.wait()
        rows = [at_ref[q, j] for j in range(many)]
        packed = first_ref[q] if q < half else second_ref[q - half]
        far = dot(picked(table_ref, rows, left), packed, NT)
        down_ref[q] = far.astype(jnp.bfloat16)
    for q in range(parents):
        local = far_ref[q] + dot(down_ref[q], transfer_ref[2 * q : 2 * q + 2].reshape(2 * rank, rank), NT)
        local_ref[q] = local.astype(jnp.bfloat16)
    basis_in.wait()
    counts_in.wait()
    for q in range(parents):
        local = local_ref[q]
        total = jnp.concatenate(
            [dot(local[:, :rank], basis_ref[2 * q], NT), dot(local[:, rank:], basis_ref[2 * q + 1], NT)],
            axis=1,
        )
        total = total + near_ref[q]
        if q == 0:
            total = total + edge_ref[0]
        if q == parents - 1:
            total = total + edge_ref[1]
        total = jnp.where(pair_mask(counts_ref, q, sides, width), total, jnp.zeros_like(total))
        out_ref[:, 2 * width * q : 2 * width * (q + 1)] = total.astype(out_ref.dtype)


def per_device(
    charges,
    panel_counts,
    basis,
    transfer,
    leaf_coupling,
    leaf_partners,
    near_blocks,
    parent_coupling,
    parent_partners,
):
    leaves, width, rank = basis.shape
    sides = charges.shape[1]
    parents, many = parent_partners.shape
    pairs = leaves // 2
    own = pairs // 2
    axes = ("gx", "gy")
    n = lax.axis_size("gy")
    total = n * lax.axis_size("gx")
    bf16, f32 = jnp.bfloat16, jnp.float32
    keep = lambda *arrays: [pltpu.with_memory_space_constraint(a, pltpu.HBM) for a in arrays]
    shape = pltpu.VMEM
    dma = lambda count: pltpu.SemaphoreType.DMA((count,))
    params = lambda mib: pltpu.CompilerParams(vmem_limit_bytes=mib * 2**20)

    rim, live, parent_coef = pl.pallas_call(
        up_kernel,
        name="up",
        out_shape=[
            shape((pairs + 2, sides, 2 * rank), bf16),
            shape((pairs, sides, 2 * width), bf16),
            shape((own, sides, 2 * rank), bf16),
        ],
        in_specs=[HBM] * 4,
        out_specs=[VMEM] * 3,
        scratch_shapes=[
            pltpu.SMEM((leaves,), jnp.int32),
            pltpu.VMEM((sides, leaves * width), bf16),
            pltpu.VMEM((leaves, width, rank), bf16),
            pltpu.VMEM((leaves, rank, rank), bf16),
            dma(4),
        ],
        compiler_params=params(8),
    )(*keep(panel_counts, charges.T, basis, transfer))

    sent = pl.pallas_call(
        copies_kernel,
        name="copies",
        out_shape=pltpu.HBM((n * own, sides, 2 * rank), bf16),
        in_specs=[VMEM],
        out_specs=HBM,
        scratch_shapes=[dma(n)],
        compiler_params=params(4),
    )(parent_coef)
    row = lax.all_to_all(sent, "gy", 0, 0, tiled=True)
    even = lax.ppermute(rim, axes, [(i, i ^ 1) for i in range(total)])
    steps = [(i, i + 1) for i in range(1, total - 1, 2)]
    odd = lax.ppermute(rim, axes, steps + [(b, a) for a, b in steps])

    half = parents // 8 * 4
    packed, first, second, near, rim_near, leaf_at, parent_at = pl.pallas_call(
        functools.partial(mid_kernel, axes),
        name="mid",
        out_shape=[
            shape((leaves, rank, many * rank), bf16),
            shape((half, rank, many * rank), bf16),
            pltpu.HBM((parents - half, rank, many * rank), bf16),
            shape((pairs, sides, 2 * width), f32),
            shape((2, width, width), bf16),
            shape((many, leaves), jnp.int32),
            shape((parents, many), jnp.int32),
        ],
        in_specs=[VMEM] + [HBM] * 5,
        out_specs=[VMEM] * 2 + [HBM] + [VMEM] * 4,
        scratch_shapes=[
            pltpu.VMEM(leaf_coupling.shape, bf16),
            pltpu.VMEM(near_blocks.shape, bf16),
            pltpu.VMEM(parent_coupling.shape, bf16),
            pltpu.VMEM((parents - half, rank, many * rank), bf16),
            dma(4 + leaves // 4 + parents // 4),
        ],
        compiler_params=params(20),
    )(live, *keep(leaf_coupling, near_blocks, parent_coupling, leaf_partners.T, parent_partners))

    far, edge, transfer_in = pl.pallas_call(
        functools.partial(leaf_kernel, axes),
        name="leaf",
        out_shape=[
            shape((pairs, sides, 2 * rank), f32),
            shape((2, sides, 2 * width), f32),
            shape(transfer.shape, bf16),
        ],
        in_specs=[VMEM] * 6 + [HBM],
        out_specs=[VMEM] * 3,
        scratch_shapes=[
            pltpu.VMEM((3 * leaves, sides, 2 * rank), bf16),
            pltpu.SMEM((many, leaves), jnp.int32),
            dma(2),
        ],
        compiler_params=params(8),
    )(leaf_at, rim, even, odd, packed, rim_near, *keep(transfer))

    out = pl.pallas_call(
        down_kernel,
        name="down",
        out_shape=jax.ShapeDtypeStruct((sides, leaves * width), bf16),
        in_specs=[VMEM] * 3 + [HBM] * 3 + [VMEM] * 4,
        out_specs=VMEM,
        scratch_shapes=[
            pltpu.VMEM((n * parents, sides, 2 * rank), bf16),
            pltpu.SMEM((parents, many), jnp.int32),
            pltpu.VMEM((pairs, sides, 2 * rank), bf16),
            pltpu.VMEM((parents, sides, rank), bf16),
            pltpu.VMEM((parents - half, rank, many * rank), bf16),
            pltpu.VMEM(basis.shape, bf16),
            pltpu.SMEM((leaves,), jnp.int32),
            dma(4),
        ],
        compiler_params=params(12),
    )(parent_at, row, first, *keep(second, basis, panel_counts), far, near, edge, transfer_in)
    return out.T


def solution(mesh):
    leaves = ("gx", "gy")
    in_specs = (
        P(leaves, None),
        P(leaves),
        P(leaves, None, None),
        P(leaves, None, None),
        P(leaves, None, None, None),
        P(leaves, None),
        P(leaves, None, None, None),
        P(leaves, None, None, None),
        P(leaves, None),
    )
    return jax.shard_map(
        per_device, mesh=mesh, in_specs=in_specs, out_specs=P(leaves, None), check_vma=False
    )
```

```python
import functools

import jax
import jax.numpy as jnp
from jax import lax
from jax.experimental import pallas as pl
from jax.experimental.pallas import tpu as pltpu
from jax.sharding import PartitionSpec as P

VMEM = pl.BlockSpec(memory_space=pltpu.VMEM)
HBM = pl.BlockSpec(memory_space=pltpu.HBM)
NN = (((1,), (0,)), ((), ()))
NT = (((1,), (1,)), ((), ()))


def dot(a, b, dims):
    return lax.dot_general(a, b, dims, preferred_element_type=jnp.float32)


def left_half(sides, width):
    return lax.broadcasted_iota(jnp.int32, (sides, 2 * width), 1) < width


def pair_mask(counts_ref, pair, sides, width):
    lane = lax.broadcasted_iota(jnp.int32, (sides, 2 * width), 1)
    left = lane < width
    count = jnp.where(left, counts_ref[2 * pair], counts_ref[2 * pair + 1])
    return jnp.where(left, lane, lane - width) < count


def swap(pair, width):
    return jnp.concatenate([pair[:, width:], pair[:, :width]], axis=1)


def mod(x, m):
    return x & (m - 1) if m & (m - 1) == 0 else lax.rem(x, m)


def position(axes):
    index = 0
    for axis in axes:
        index = index * lax.axis_size(axis) + lax.axis_index(axis)
    return index


def start_all(copies, sems):
    started = [pltpu.make_async_copy(src, dst, sems.at[i]) for i, (src, dst) in enumerate(copies)]
    for copy in started:
        copy.start()
    return started


def up_kernel(
    counts_hbm, charges_hbm, basis_hbm, transfer_hbm,
    rim_ref, live_ref, parents_ref,
    counts_ref, charges_ref, basis_ref, transfer_ref, sems,
):
    counts_in, charges_in, basis_in, transfer_in = start_all(
        [
            (counts_hbm, counts_ref), (charges_hbm, charges_ref),
            (basis_hbm, basis_ref), (transfer_hbm, transfer_ref),
        ],
        sems,
    )
    sides = charges_ref.shape[0]
    leaves, width, rank = basis_ref.shape
    pairs = leaves // 2
    own = pairs // 2
    left = left_half(sides, width)
    counts_in.wait()
    charges_in.wait()
    lives = []
    for a in range(pairs):
        charge = charges_ref[:, 2 * width * a : 2 * width * (a + 1)]
        live = jnp.where(pair_mask(counts_ref, a, sides, width), charge, jnp.zeros_like(charge))
        live_ref[a] = live
        lives.append(live)
    rim_ref[pairs] = lives[0]
    rim_ref[pairs + 1] = lives[-1]
    basis_in.wait()
    none = jnp.zeros_like(lives[0])
    coefs = []
    for a in range(pairs):
        live = lives[a]
        both = jnp.concatenate([jnp.where(left, live, none), jnp.where(left, none, live)], axis=0)
        coef = dot(both, basis_ref[2 * a : 2 * a + 2].reshape(2 * width, rank), NN)
        coef = jnp.concatenate([coef[:sides], coef[sides:]], axis=1).astype(jnp.bfloat16)
        rim_ref[a] = coef
        coefs.append(coef)
    transfer_in.wait()
    sums = [
        dot(coefs[a], transfer_ref[2 * a : 2 * a + 2].reshape(2 * rank, rank), NN)
        for a in range(pairs)
    ]
    for a in range(own):
        parents_ref[a] = jnp.concatenate(sums[2 * a : 2 * a + 2], axis=1).astype(jnp.bfloat16)


def copies_kernel(parents_ref, rim_ref, sent_hbm, sems):
    del rim_ref
    own = parents_ref.shape[0]
    copies = sent_hbm.shape[0] // own
    for copy in start_all([(parents_ref, sent_hbm.at[pl.ds(own * c, own)]) for c in range(copies)], sems):
        copy.wait()


def mid_kernel(
    axes, sent_hbm, live_ref, coupling_hbm, near_hbm, parent_hbm, leaf_partners_hbm, parent_partners_hbm,
    packed_ref, first_ref, second_hbm, near_out_ref, rim_near_ref, leaf_at_ref, parent_at_ref,
    coupling_ref, near_ref, parent_ref, second_ref, sems,
):
    del sent_hbm
    leaves, many, rank, _ = coupling_ref.shape
    parents = parent_ref.shape[0]
    width = near_ref.shape[2]
    pairs = leaves // 2
    started = start_all(
        [(near_hbm, near_ref)]
        + [(parent_hbm.at[pl.ds(4 * i, 4)], parent_ref.at[pl.ds(4 * i, 4)]) for i in reversed(range(parents // 4))]
        + [(coupling_hbm.at[pl.ds(4 * i, 4)], coupling_ref.at[pl.ds(4 * i, 4)]) for i in range(leaves // 4)]
        + [(leaf_partners_hbm, leaf_at_ref), (parent_partners_hbm, parent_at_ref)],
        sems,
    )
    near_in = started[0]
    parent_in = started[1 : 1 + parents // 4][::-1]
    coupling_in = started[1 + parents // 4 : -2]
    near_in.wait()
    rim_near_ref[0] = near_ref[0, 0]
    rim_near_ref[1] = near_ref[leaves - 1, 2]
    for a in range(pairs):
        here = live_ref[a]
        even = dot(here, jnp.concatenate([near_ref[2 * a, 1], near_ref[2 * a, 2]], axis=1), NT)
        odd = dot(here, jnp.concatenate([near_ref[2 * a + 1, 0], near_ref[2 * a + 1, 1]], axis=1), NT)
        if a > 0:
            even = even + dot(live_ref[a - 1][:, width:], near_ref[2 * a, 0], NT)
        if a < pairs - 1:
            odd = odd + dot(live_ref[a + 1][:, :width], near_ref[2 * a + 1, 2], NT)
        near_out_ref[a] = jnp.concatenate([even, odd], axis=1)

    def pack(src, dst, g, to):
        for j in range(0, many, 2):
            dst[to, :, rank * j : rank * (j + 2)] = jnp.concatenate([src[g, j], src[g, j + 1]], axis=1)

    half = first_ref.shape[0]
    for i, copy in reversed(list(enumerate(parent_in))):
        copy.wait()
        for q in range(4 * i, 4 * i + 4):
            if q < half:
                pack(parent_ref, first_ref, q, q)
            else:
                pack(parent_ref, second_ref, q, q - half)
        if 4 * i == half:
            out = pltpu.make_async_copy(second_ref, second_hbm, sems.at[len(started)])
            out.start()
    for i, copy in enumerate(coupling_in):
        copy.wait()
        for g in range(4 * i, 4 * i + 4):
            pack(coupling_ref, packed_ref, g, g)
    for copy in started[-2:]:
        copy.wait()
    out.wait()
    wanted = leaf_at_ref[...] + (1 - position(axes)) * leaves
    leaf_at_ref[...] = wanted ^ (lax.broadcasted_iota(jnp.int32, wanted.shape, 0) & 1)
    n = lax.axis_size(axes[1])
    wanted = mod(parent_at_ref[...], n * parents)
    parent_at_ref[...] = wanted ^ (lax.broadcasted_iota(jnp.int32, wanted.shape, 1) & 1)


def spread_pair(table_ref, at, pair, width):
    table_ref[at] = pair
    table_ref[at + 1] = swap(pair, width)


def picked(table_ref, rows, left):
    return jnp.concatenate(
        [
            jnp.where(left, table_ref[rows[j]], table_ref[rows[j + 1]])
            for j in range(0, len(rows), 2)
        ],
        axis=1,
    )


def leaf_kernel(
    axes, at_vmem, rim_ref, even_ref, odd_ref, packed_ref, rim_near_ref, transfer_hbm, basis_hbm,
    far_ref, edge_ref, transfer_ref, basis_packed_ref, table_ref, at_ref, basis_ref, sems,
):
    at_in, transfer_in, basis_in = start_all(
        [(at_vmem, at_ref), (transfer_hbm, transfer_ref), (basis_hbm, basis_ref)], sems
    )
    many, leaves = at_ref.shape
    rank = packed_ref.shape[1]
    width = rim_near_ref.shape[1]
    pairs = leaves // 2
    sides = rim_ref.shape[1]
    left = left_half(sides, rank)
    parity = lax.rem(position(axes), 2)
    for ref, base in (
        (rim_ref, leaves), (even_ref, 2 * leaves * (1 - parity)), (odd_ref, 2 * leaves * parity),
    ):
        for a in range(pairs):
            spread_pair(table_ref, base + 2 * a, ref[a], rank)
    before = jnp.where(parity == 1, even_ref[pairs + 1], odd_ref[pairs + 1])
    after = jnp.where(parity == 1, odd_ref[pairs], even_ref[pairs])
    low = dot(before[:, width:], rim_near_ref[0], NT)
    high = dot(after[:, :width], rim_near_ref[1], NT)
    edge_ref[0] = jnp.concatenate([low, jnp.zeros_like(low)], axis=1)
    edge_ref[1] = jnp.concatenate([jnp.zeros_like(high), high], axis=1)
    at_in.wait()
    for a in range(pairs):
        fars = []
        for g in (2 * a, 2 * a + 1):
            rows = [at_ref[j, g] for j in range(many)]
            fars.append(dot(picked(table_ref, rows, left), packed_ref[g], NT))
        far_ref[a] = jnp.concatenate(fars, axis=1)
    basis_in.wait()
    for a in range(pairs):
        basis_packed_ref[a] = jnp.concatenate([basis_ref[2 * a], basis_ref[2 * a + 1]], axis=1)
    transfer_in.wait()


def down_kernel(
    at_vmem, row_ref, first_ref, second_hbm, counts_hbm,
    far_ref, near_ref, edge_ref, transfer_ref, basis_ref,
    out_ref, table_ref, at_ref, local_ref, down_ref, second_ref, counts_ref, sems,
):
    at_in, second_in, counts_in = start_all(
        [(at_vmem, at_ref), (second_hbm, second_ref), (counts_hbm, counts_ref)], sems
    )
    parents, many = at_ref.shape
    rank = first_ref.shape[1]
    half = first_ref.shape[0]
    width = basis_ref.shape[1]
    sides = row_ref.shape[1]
    left = left_half(sides, rank)

    def spread(a, carry):
        spread_pair(table_ref, 2 * a, row_ref[a], rank)
        return carry

    lax.fori_loop(0, row_ref.shape[0], spread, 0, unroll=min(64, row_ref.shape[0]))
    at_in.wait()
    for q in range(parents):
        if q == half:
            second_in.wait()
        rows = [at_ref[q, j] for j in range(many)]
        packed = first_ref[q] if q < half else second_ref[q - half]
        far = dot(picked(table_ref, rows, left), packed, NT)
        down_ref[q] = far.astype(jnp.bfloat16)
    for q in range(parents):
        local = far_ref[q] + dot(down_ref[q], transfer_ref[2 * q : 2 * q + 2].reshape(2 * rank, rank), NT)
        local_ref[q] = local.astype(jnp.bfloat16)
    counts_in.wait()
    for q in range(parents):
        local = local_ref[q]
        none = jnp.zeros_like(local)
        both = jnp.concatenate([jnp.where(left, local, none), jnp.where(left, none, local)], axis=0)
        total = dot(both, basis_ref[q], NT)
        total = jnp.concatenate([total[:sides], total[sides:]], axis=1) + near_ref[q]
        if q == 0:
            total = total + edge_ref[0]
        if q == parents - 1:
            total = total + edge_ref[1]
        total = jnp.where(pair_mask(counts_ref, q, sides, width), total, jnp.zeros_like(total))
        out_ref[:, 2 * width * q : 2 * width * (q + 1)] = total.astype(out_ref.dtype)


def per_device(
    charges,
    panel_counts,
    basis,
    transfer,
    leaf_coupling,
    leaf_partners,
    near_blocks,
    parent_coupling,
    parent_partners,
):
    leaves, width, rank = basis.shape
    sides = charges.shape[1]
    parents, many = parent_partners.shape
    pairs = leaves // 2
    own = pairs // 2
    axes = ("gx", "gy")
    n = lax.axis_size("gy")
    total = n * lax.axis_size("gx")
    bf16, f32 = jnp.bfloat16, jnp.float32
    keep = lambda *arrays: [pltpu.with_memory_space_constraint(a, pltpu.HBM) for a in arrays]
    shape = pltpu.VMEM
    dma = lambda count: pltpu.SemaphoreType.DMA((count,))
    params = lambda mib: pltpu.CompilerParams(vmem_limit_bytes=mib * 2**20)

    rim, live, parent_coef = pl.pallas_call(
        up_kernel,
        name="up",
        out_shape=[
            shape((pairs + 2, sides, 2 * rank), bf16),
            shape((pairs, sides, 2 * width), bf16),
            shape((own, sides, 2 * rank), bf16),
        ],
        in_specs=[HBM] * 4,
        out_specs=[VMEM] * 3,
        scratch_shapes=[
            pltpu.SMEM((leaves,), jnp.int32),
            pltpu.VMEM((sides, leaves * width), bf16),
            pltpu.VMEM((leaves, width, rank), bf16),
            pltpu.VMEM((leaves, rank, rank), bf16),
            dma(4),
        ],
        compiler_params=params(8),
    )(*keep(panel_counts, charges.T, basis, transfer))

    even = lax.ppermute(rim, axes, [(i, i ^ 1) for i in range(total)])
    steps = [(i, i + 1) for i in range(1, total - 1, 2)]
    odd = lax.ppermute(rim, axes, steps + [(b, a) for a, b in steps])
    sent = pl.pallas_call(
        copies_kernel,
        name="copies",
        out_shape=pltpu.HBM((n * own, sides, 2 * rank), bf16),
        in_specs=[VMEM, VMEM],
        out_specs=HBM,
        scratch_shapes=[dma(n)],
        compiler_params=params(4),
    )(parent_coef, even)
    row = lax.all_to_all(sent, "gy", 0, 0, tiled=True)

    held = parents // 16 * 12
    packed, first, second, near, rim_near, leaf_at, parent_at = pl.pallas_call(
        functools.partial(mid_kernel, axes),
        name="mid",
        out_shape=[
            shape((leaves, rank, many * rank), bf16),
            shape((held, rank, many * rank), bf16),
            pltpu.HBM((parents - held, rank, many * rank), bf16),
            shape((pairs, sides, 2 * width), f32),
            shape((2, width, width), bf16),
            shape((many, leaves), jnp.int32),
            shape((parents, many), jnp.int32),
        ],
        in_specs=[HBM, VMEM] + [HBM] * 5,
        out_specs=[VMEM] * 2 + [HBM] + [VMEM] * 4,
        scratch_shapes=[
            pltpu.VMEM(leaf_coupling.shape, bf16),
            pltpu.VMEM(near_blocks.shape, bf16),
            pltpu.VMEM(parent_coupling.shape, bf16),
            pltpu.VMEM((parents - held, rank, many * rank), bf16),
            dma(4 + leaves // 4 + parents // 4),
        ],
        compiler_params=params(20),
    )(*keep(sent), live, *keep(leaf_coupling, near_blocks, parent_coupling, leaf_partners.T, parent_partners))

    far, edge, transfer_in, basis_in = pl.pallas_call(
        functools.partial(leaf_kernel, axes),
        name="leaf",
        out_shape=[
            shape((pairs, sides, 2 * rank), f32),
            shape((2, sides, 2 * width), f32),
            shape(transfer.shape, bf16),
            shape((pairs, width, 2 * rank), bf16),
        ],
        in_specs=[VMEM] * 6 + [HBM] * 2,
        out_specs=[VMEM] * 4,
        scratch_shapes=[
            pltpu.VMEM((3 * leaves, sides, 2 * rank), bf16),
            pltpu.SMEM((many, leaves), jnp.int32),
            pltpu.VMEM(basis.shape, bf16),
            dma(3),
        ],
        compiler_params=params(8),
    )(leaf_at, rim, even, odd, packed, rim_near, *keep(transfer, basis))

    out = pl.pallas_call(
        down_kernel,
        name="down",
        out_shape=jax.ShapeDtypeStruct((sides, leaves * width), bf16),
        in_specs=[VMEM] * 3 + [HBM] * 2 + [VMEM] * 5,
        out_specs=VMEM,
        scratch_shapes=[
            pltpu.VMEM((n * parents, sides, 2 * rank), bf16),
            pltpu.SMEM((parents, many), jnp.int32),
            pltpu.VMEM((pairs, sides, 2 * rank), bf16),
            pltpu.VMEM((parents, sides, rank), bf16),
            pltpu.VMEM((parents - held, rank, many * rank), bf16),
            pltpu.SMEM((leaves,), jnp.int32),
            dma(3),
        ],
        compiler_params=params(12),
    )(parent_at, row, first, *keep(second, panel_counts), far, near, edge, transfer_in, basis_in)
    return out.T


def solution(mesh):
    leaves = ("gx", "gy")
    in_specs = (
        P(leaves, None),
        P(leaves),
        P(leaves, None, None),
        P(leaves, None, None),
        P(leaves, None, None, None),
        P(leaves, None),
        P(leaves, None, None, None),
        P(leaves, None, None, None),
        P(leaves, None),
    )
    return jax.shard_map(
        per_device, mesh=mesh, in_specs=in_specs, out_specs=P(leaves, None), check_vma=False
    )
```

```python
import functools

import jax
import jax.numpy as jnp
from jax import lax
from jax.experimental import pallas as pl
from jax.experimental.pallas import tpu as pltpu
from jax.sharding import PartitionSpec as P

VMEM = pl.BlockSpec(memory_space=pltpu.VMEM)
HBM = pl.BlockSpec(memory_space=pltpu.HBM)
NN = (((1,), (0,)), ((), ()))
NT = (((1,), (1,)), ((), ()))


def dot(a, b, dims):
    return lax.dot_general(a, b, dims, preferred_element_type=jnp.float32)


def left_half(sides, width):
    return lax.broadcasted_iota(jnp.int32, (sides, 2 * width), 1) < width


def pair_mask(counts_ref, pair, sides, width):
    lane = lax.broadcasted_iota(jnp.int32, (sides, 2 * width), 1)
    left = lane < width
    count = jnp.where(left, counts_ref[2 * pair], counts_ref[2 * pair + 1])
    return jnp.where(left, lane, lane - width) < count


def swap(pair, width):
    return jnp.concatenate([pair[:, width:], pair[:, :width]], axis=1)


def mod(x, m):
    return x & (m - 1) if m & (m - 1) == 0 else lax.rem(x, m)


def position(axes):
    index = 0
    for axis in axes:
        index = index * lax.axis_size(axis) + lax.axis_index(axis)
    return index


def start_all(copies, sems):
    started = [pltpu.make_async_copy(src, dst, sems.at[i]) for i, (src, dst) in enumerate(copies)]
    for copy in started:
        copy.start()
    return started


def up_kernel(
    counts_hbm, charges_hbm, basis_hbm, transfer_hbm,
    rim_ref, live_ref, parents_ref,
    counts_ref, charges_ref, basis_ref, transfer_ref, sems,
):
    counts_in, charges_in, basis_in, transfer_in = start_all(
        [
            (counts_hbm, counts_ref), (charges_hbm, charges_ref),
            (basis_hbm, basis_ref), (transfer_hbm, transfer_ref),
        ],
        sems,
    )
    sides = charges_ref.shape[0]
    leaves, width, rank = basis_ref.shape
    pairs = leaves // 2
    own = pairs // 2
    left = left_half(sides, width)
    counts_in.wait()
    charges_in.wait()
    lives = []
    for a in range(pairs):
        charge = charges_ref[:, 2 * width * a : 2 * width * (a + 1)]
        live = jnp.where(pair_mask(counts_ref, a, sides, width), charge, jnp.zeros_like(charge))
        live_ref[a] = live
        lives.append(live)
    rim_ref[pairs] = lives[0]
    rim_ref[pairs + 1] = lives[-1]
    basis_in.wait()
    none = jnp.zeros_like(lives[0])
    coefs = []
    for a in range(pairs):
        live = lives[a]
        both = jnp.concatenate([jnp.where(left, live, none), jnp.where(left, none, live)], axis=0)
        coef = dot(both, basis_ref[2 * a : 2 * a + 2].reshape(2 * width, rank), NN)
        coef = jnp.concatenate([coef[:sides], coef[sides:]], axis=1).astype(jnp.bfloat16)
        rim_ref[a] = coef
        coefs.append(coef)
    transfer_in.wait()
    sums = [
        dot(coefs[a], transfer_ref[2 * a : 2 * a + 2].reshape(2 * rank, rank), NN)
        for a in range(pairs)
    ]
    for a in range(own):
        parents_ref[a] = jnp.concatenate(sums[2 * a : 2 * a + 2], axis=1).astype(jnp.bfloat16)


def copies_kernel(parents_ref, sent_hbm, sems):
    own = parents_ref.shape[0]
    copies = sent_hbm.shape[0] // own
    for copy in start_all([(parents_ref, sent_hbm.at[pl.ds(own * c, own)]) for c in range(copies)], sems):
        copy.wait()


def mid_kernel(
    axes, live_ref, coupling_hbm, near_hbm, parent_hbm, leaf_partners_hbm, parent_partners_hbm,
    packed_ref, first_ref, second_hbm, near_out_ref, rim_near_ref, leaf_at_ref, parent_at_ref,
    coupling_ref, near_ref, parent_ref, second_ref, sems,
):
    leaves, many, rank, _ = coupling_ref.shape
    parents = parent_ref.shape[0]
    width = near_ref.shape[2]
    pairs = leaves // 2
    started = start_all(
        [(near_hbm, near_ref)]
        + [(parent_hbm.at[pl.ds(4 * i, 4)], parent_ref.at[pl.ds(4 * i, 4)]) for i in reversed(range(parents // 4))]
        + [(coupling_hbm.at[pl.ds(4 * i, 4)], coupling_ref.at[pl.ds(4 * i, 4)]) for i in range(leaves // 4)]
        + [(leaf_partners_hbm, leaf_at_ref), (parent_partners_hbm, parent_at_ref)],
        sems,
    )
    near_in = started[0]
    parent_in = started[1 : 1 + parents // 4][::-1]
    coupling_in = started[1 + parents // 4 : -2]
    near_in.wait()
    rim_near_ref[0] = near_ref[0, 0]
    rim_near_ref[1] = near_ref[leaves - 1, 2]
    for a in range(pairs):
        here = live_ref[a]
        even = dot(here, jnp.concatenate([near_ref[2 * a, 1], near_ref[2 * a, 2]], axis=1), NT)
        odd = dot(here, jnp.concatenate([near_ref[2 * a + 1, 0], near_ref[2 * a + 1, 1]], axis=1), NT)
        if a > 0:
            even = even + dot(live_ref[a - 1][:, width:], near_ref[2 * a, 0], NT)
        if a < pairs - 1:
            odd = odd + dot(live_ref[a + 1][:, :width], near_ref[2 * a + 1, 2], NT)
        near_out_ref[a] = jnp.concatenate([even, odd], axis=1)

    def pack(src, dst, g, to):
        for j in range(0, many, 2):
            dst[to, :, rank * j : rank * (j + 2)] = jnp.concatenate([src[g, j], src[g, j + 1]], axis=1)

    half = first_ref.shape[0]
    for i, copy in reversed(list(enumerate(parent_in))):
        copy.wait()
        for q in range(4 * i, 4 * i + 4):
            if q < half:
                pack(parent_ref, first_ref, q, q)
            else:
                pack(parent_ref, second_ref, q, q - half)
        if 4 * i == half:
            out = pltpu.make_async_copy(second_ref, second_hbm, sems.at[len(started)])
            out.start()
    for i, copy in enumerate(coupling_in):
        copy.wait()
        for g in range(4 * i, 4 * i + 4):
            pack(coupling_ref, packed_ref, g, g)
    for copy in started[-2:]:
        copy.wait()
    out.wait()
    wanted = leaf_at_ref[...] + (1 - position(axes)) * leaves
    leaf_at_ref[...] = wanted ^ (lax.broadcasted_iota(jnp.int32, wanted.shape, 0) & 1)
    n = lax.axis_size(axes[1])
    wanted = mod(parent_at_ref[...], n * parents)
    parent_at_ref[...] = wanted ^ (lax.broadcasted_iota(jnp.int32, wanted.shape, 1) & 1)


def spread_pair(table_ref, at, pair, width):
    table_ref[at] = pair
    table_ref[at + 1] = swap(pair, width)


def picked(table_ref, rows, left):
    return jnp.concatenate(
        [
            jnp.where(left, table_ref[rows[j]], table_ref[rows[j + 1]])
            for j in range(0, len(rows), 2)
        ],
        axis=1,
    )


def leaf_kernel(
    axes, at_vmem, rim_ref, even_ref, odd_ref, packed_ref, rim_near_ref, transfer_hbm, basis_hbm,
    far_ref, edge_ref, transfer_ref, basis_packed_ref, table_ref, at_ref, basis_ref, sems,
):
    at_in, transfer_in, basis_in = start_all(
        [(at_vmem, at_ref), (transfer_hbm, transfer_ref), (basis_hbm, basis_ref)], sems
    )
    many, leaves = at_ref.shape
    rank = packed_ref.shape[1]
    width = rim_near_ref.shape[1]
    pairs = leaves // 2
    sides = rim_ref.shape[1]
    left = left_half(sides, rank)
    parity = lax.rem(position(axes), 2)
    for ref, base in (
        (rim_ref, leaves), (even_ref, 2 * leaves * (1 - parity)), (odd_ref, 2 * leaves * parity),
    ):
        for a in range(pairs):
            spread_pair(table_ref, base + 2 * a, ref[a], rank)
    before = jnp.where(parity == 1, even_ref[pairs + 1], odd_ref[pairs + 1])
    after = jnp.where(parity == 1, odd_ref[pairs], even_ref[pairs])
    low = dot(before[:, width:], rim_near_ref[0], NT)
    high = dot(after[:, :width], rim_near_ref[1], NT)
    edge_ref[0] = jnp.concatenate([low, jnp.zeros_like(low)], axis=1)
    edge_ref[1] = jnp.concatenate([jnp.zeros_like(high), high], axis=1)
    at_in.wait()
    for a in range(pairs):
        fars = []
        for g in (2 * a, 2 * a + 1):
            rows = [at_ref[j, g] for j in range(many)]
            fars.append(dot(picked(table_ref, rows, left), packed_ref[g], NT))
        far_ref[a] = jnp.concatenate(fars, axis=1)
    basis_in.wait()
    for a in range(pairs):
        basis_packed_ref[a] = jnp.concatenate([basis_ref[2 * a], basis_ref[2 * a + 1]], axis=1)
    transfer_in.wait()


def down_kernel(
    at_vmem, row_ref, first_ref, second_hbm, counts_hbm,
    far_ref, near_ref, edge_ref, transfer_ref, basis_ref,
    out_ref, table_ref, at_ref, local_ref, down_ref, second_ref, counts_ref, sems,
):
    at_in, second_in, counts_in = start_all(
        [(at_vmem, at_ref), (second_hbm, second_ref), (counts_hbm, counts_ref)], sems
    )
    parents, many = at_ref.shape
    rank = first_ref.shape[1]
    half = first_ref.shape[0]
    width = basis_ref.shape[1]
    sides = row_ref.shape[1]
    left = left_half(sides, rank)

    def spread(a, carry):
        spread_pair(table_ref, 2 * a, row_ref[a], rank)
        return carry

    lax.fori_loop(0, row_ref.shape[0], spread, 0, unroll=min(64, row_ref.shape[0]))
    at_in.wait()
    for q in range(parents):
        if q == half:
            second_in.wait()
        rows = [at_ref[q, j] for j in range(many)]
        packed = first_ref[q] if q < half else second_ref[q - half]
        far = dot(picked(table_ref, rows, left), packed, NT)
        down_ref[q] = far.astype(jnp.bfloat16)
    for q in range(parents):
        local = far_ref[q] + dot(down_ref[q], transfer_ref[2 * q : 2 * q + 2].reshape(2 * rank, rank), NT)
        local_ref[q] = local.astype(jnp.bfloat16)
    counts_in.wait()
    for q in range(parents):
        local = local_ref[q]
        none = jnp.zeros_like(local)
        both = jnp.concatenate([jnp.where(left, local, none), jnp.where(left, none, local)], axis=0)
        total = dot(both, basis_ref[q], NT)
        total = jnp.concatenate([total[:sides], total[sides:]], axis=1) + near_ref[q]
        if q == 0:
            total = total + edge_ref[0]
        if q == parents - 1:
            total = total + edge_ref[1]
        total = jnp.where(pair_mask(counts_ref, q, sides, width), total, jnp.zeros_like(total))
        out_ref[:, 2 * width * q : 2 * width * (q + 1)] = total.astype(out_ref.dtype)


def per_device(
    charges,
    panel_counts,
    basis,
    transfer,
    leaf_coupling,
    leaf_partners,
    near_blocks,
    parent_coupling,
    parent_partners,
):
    leaves, width, rank = basis.shape
    sides = charges.shape[1]
    parents, many = parent_partners.shape
    pairs = leaves // 2
    own = pairs // 2
    axes = ("gx", "gy")
    n = lax.axis_size("gy")
    total = n * lax.axis_size("gx")
    bf16, f32 = jnp.bfloat16, jnp.float32
    keep = lambda *arrays: [pltpu.with_memory_space_constraint(a, pltpu.HBM) for a in arrays]
    shape = pltpu.VMEM
    dma = lambda count: pltpu.SemaphoreType.DMA((count,))
    params = lambda mib: pltpu.CompilerParams(vmem_limit_bytes=mib * 2**20)
    cost = lambda mib: pl.CostEstimate(flops=0, transcendentals=0, bytes_accessed=mib * 2**20)

    rim, live, parent_coef = pl.pallas_call(
        up_kernel,
        name="up",
        out_shape=[
            shape((pairs + 2, sides, 2 * rank), bf16),
            shape((pairs, sides, 2 * width), bf16),
            shape((own, sides, 2 * rank), bf16),
        ],
        in_specs=[HBM] * 4,
        out_specs=[VMEM] * 3,
        scratch_shapes=[
            pltpu.SMEM((leaves,), jnp.int32),
            pltpu.VMEM((sides, leaves * width), bf16),
            pltpu.VMEM((leaves, width, rank), bf16),
            pltpu.VMEM((leaves, rank, rank), bf16),
            dma(4),
        ],
        compiler_params=params(8),
    )(*keep(panel_counts, charges.T, basis, transfer))

    even = lax.ppermute(rim, axes, [(i, i ^ 1) for i in range(total)])
    steps = [(i, i + 1) for i in range(1, total - 1, 2)]
    odd = lax.ppermute(rim, axes, steps + [(b, a) for a, b in steps])
    sent = pl.pallas_call(
        copies_kernel,
        name="copies",
        out_shape=pltpu.HBM((n * own, sides, 2 * rank), bf16),
        in_specs=[VMEM],
        out_specs=HBM,
        scratch_shapes=[dma(n)],
        compiler_params=params(4),
    )(parent_coef)
    row = lax.all_to_all(sent, "gy", 0, 0, tiled=True)

    held = parents // 8 * 4
    packed, first, second, near, rim_near, leaf_at, parent_at = pl.pallas_call(
        functools.partial(mid_kernel, axes),
        name="mid",
        out_shape=[
            shape((leaves, rank, many * rank), bf16),
            shape((held, rank, many * rank), bf16),
            pltpu.HBM((parents - held, rank, many * rank), bf16),
            shape((pairs, sides, 2 * width), f32),
            shape((2, width, width), bf16),
            shape((many, leaves), jnp.int32),
            shape((parents, many), jnp.int32),
        ],
        in_specs=[VMEM] + [HBM] * 5,
        out_specs=[VMEM] * 2 + [HBM] + [VMEM] * 4,
        scratch_shapes=[
            pltpu.VMEM(leaf_coupling.shape, bf16),
            pltpu.VMEM(near_blocks.shape, bf16),
            pltpu.VMEM(parent_coupling.shape, bf16),
            pltpu.VMEM((parents - held, rank, many * rank), bf16),
            dma(4 + leaves // 4 + parents // 4),
        ],
        compiler_params=params(20),
        cost_estimate=cost(16),
    )(live, *keep(leaf_coupling, near_blocks, parent_coupling, leaf_partners.T, parent_partners))

    far, edge, transfer_in, basis_in = pl.pallas_call(
        functools.partial(leaf_kernel, axes),
        name="leaf",
        out_shape=[
            shape((pairs, sides, 2 * rank), f32),
            shape((2, sides, 2 * width), f32),
            shape(transfer.shape, bf16),
            shape((pairs, width, 2 * rank), bf16),
        ],
        in_specs=[VMEM] * 6 + [HBM] * 2,
        out_specs=[VMEM] * 4,
        scratch_shapes=[
            pltpu.VMEM((3 * leaves, sides, 2 * rank), bf16),
            pltpu.SMEM((many, leaves), jnp.int32),
            pltpu.VMEM(basis.shape, bf16),
            dma(3),
        ],
        compiler_params=params(8),
        cost_estimate=cost(64),
    )(leaf_at, rim, even, odd, packed, rim_near, *keep(transfer, basis))

    out = pl.pallas_call(
        down_kernel,
        name="down",
        out_shape=jax.ShapeDtypeStruct((sides, leaves * width), bf16),
        in_specs=[VMEM] * 3 + [HBM] * 2 + [VMEM] * 5,
        out_specs=VMEM,
        scratch_shapes=[
            pltpu.VMEM((n * parents, sides, 2 * rank), bf16),
            pltpu.SMEM((parents, many), jnp.int32),
            pltpu.VMEM((pairs, sides, 2 * rank), bf16),
            pltpu.VMEM((parents, sides, rank), bf16),
            pltpu.VMEM((parents - held, rank, many * rank), bf16),
            pltpu.SMEM((leaves,), jnp.int32),
            dma(3),
        ],
        compiler_params=params(12),
    )(parent_at, row, first, *keep(second, panel_counts), far, near, edge, transfer_in, basis_in)
    return out.T


def solution(mesh):
    leaves = ("gx", "gy")
    in_specs = (
        P(leaves, None),
        P(leaves),
        P(leaves, None, None),
        P(leaves, None, None),
        P(leaves, None, None, None),
        P(leaves, None),
        P(leaves, None, None, None),
        P(leaves, None, None, None),
        P(leaves, None),
    )
    return jax.shard_map(
        per_device, mesh=mesh, in_specs=in_specs, out_specs=P(leaves, None), check_vma=False
    )
```

```python
import functools

import jax
import jax.numpy as jnp
from jax import lax
from jax.experimental import pallas as pl
from jax.experimental.pallas import tpu as pltpu
from jax.sharding import PartitionSpec as P

VMEM = pl.BlockSpec(memory_space=pltpu.VMEM)
HBM = pl.BlockSpec(memory_space=pltpu.HBM)
NN = (((1,), (0,)), ((), ()))
NT = (((1,), (1,)), ((), ()))


def dot(a, b, dims):
    return lax.dot_general(a, b, dims, preferred_element_type=jnp.float32)


def left_half(sides, width):
    return lax.broadcasted_iota(jnp.int32, (sides, 2 * width), 1) < width


def pair_mask(counts_ref, pair, sides, width):
    lane = lax.broadcasted_iota(jnp.int32, (sides, 2 * width), 1)
    left = lane < width
    count = jnp.where(left, counts_ref[2 * pair], counts_ref[2 * pair + 1])
    return jnp.where(left, lane, lane - width) < count


def swap(pair, width):
    return jnp.concatenate([pair[:, width:], pair[:, :width]], axis=1)


def mod(x, m):
    return x & (m - 1) if m & (m - 1) == 0 else lax.rem(x, m)


def position(axes):
    index = 0
    for axis in axes:
        index = index * lax.axis_size(axis) + lax.axis_index(axis)
    return index


def start_all(copies, sems):
    started = [pltpu.make_async_copy(src, dst, sems.at[i]) for i, (src, dst) in enumerate(copies)]
    for copy in started:
        copy.start()
    return started


def up_kernel(
    counts_hbm, charges_hbm, basis_hbm, transfer_hbm,
    rim_ref, live_ref, parents_ref,
    counts_ref, charges_ref, basis_ref, transfer_ref, sems,
):
    counts_in, charges_in, basis_in, transfer_in = start_all(
        [
            (counts_hbm, counts_ref), (charges_hbm, charges_ref),
            (basis_hbm, basis_ref), (transfer_hbm, transfer_ref),
        ],
        sems,
    )
    sides = charges_ref.shape[0]
    leaves, width, rank = basis_ref.shape
    pairs = leaves // 2
    own = pairs // 2
    left = left_half(sides, width)
    counts_in.wait()
    charges_in.wait()
    lives = []
    for a in range(pairs):
        charge = charges_ref[:, 2 * width * a : 2 * width * (a + 1)]
        live = jnp.where(pair_mask(counts_ref, a, sides, width), charge, jnp.zeros_like(charge))
        live_ref[a] = live
        lives.append(live)
    rim_ref[pairs] = lives[0]
    rim_ref[pairs + 1] = lives[-1]
    basis_in.wait()
    none = jnp.zeros_like(lives[0])
    coefs = []
    for a in range(pairs):
        live = lives[a]
        both = jnp.concatenate([jnp.where(left, live, none), jnp.where(left, none, live)], axis=0)
        coef = dot(both, basis_ref[2 * a : 2 * a + 2].reshape(2 * width, rank), NN)
        coef = jnp.concatenate([coef[:sides], coef[sides:]], axis=1).astype(jnp.bfloat16)
        rim_ref[a] = coef
        coefs.append(coef)
    transfer_in.wait()
    sums = [
        dot(coefs[a], transfer_ref[2 * a : 2 * a + 2].reshape(2 * rank, rank), NN)
        for a in range(pairs)
    ]
    for a in range(own):
        parents_ref[a] = jnp.concatenate(sums[2 * a : 2 * a + 2], axis=1).astype(jnp.bfloat16)


def copies_kernel(parents_ref, sent_hbm, sems):
    own = parents_ref.shape[0]
    copies = sent_hbm.shape[0] // own
    for copy in start_all([(parents_ref, sent_hbm.at[pl.ds(own * c, own)]) for c in range(copies)], sems):
        copy.wait()


def mid_kernel(
    axes, live_ref, coupling_hbm, near_hbm, parent_hbm, leaf_partners_hbm, parent_partners_hbm,
    packed_ref, first_ref, second_hbm, near_out_ref, rim_near_ref, leaf_at_ref, parent_at_ref,
    coupling_ref, near_ref, parent_ref, second_ref, sems,
):
    leaves, many, rank, _ = coupling_ref.shape
    parents = parent_ref.shape[0]
    width = near_ref.shape[2]
    pairs = leaves // 2
    started = start_all(
        [(near_hbm, near_ref)]
        + [(parent_hbm.at[pl.ds(4 * i, 4)], parent_ref.at[pl.ds(4 * i, 4)]) for i in reversed(range(parents // 4))]
        + [(coupling_hbm.at[pl.ds(4 * i, 4)], coupling_ref.at[pl.ds(4 * i, 4)]) for i in range(leaves // 4)]
        + [(leaf_partners_hbm, leaf_at_ref), (parent_partners_hbm, parent_at_ref)],
        sems,
    )
    near_in = started[0]
    parent_in = started[1 : 1 + parents // 4][::-1]
    coupling_in = started[1 + parents // 4 : -2]
    near_in.wait()
    rim_near_ref[0] = near_ref[0, 0]
    rim_near_ref[1] = near_ref[leaves - 1, 2]
    for a in range(pairs):
        here = live_ref[a]
        even = dot(here, jnp.concatenate([near_ref[2 * a, 1], near_ref[2 * a, 2]], axis=1), NT)
        odd = dot(here, jnp.concatenate([near_ref[2 * a + 1, 0], near_ref[2 * a + 1, 1]], axis=1), NT)
        if a > 0:
            even = even + dot(live_ref[a - 1][:, width:], near_ref[2 * a, 0], NT)
        if a < pairs - 1:
            odd = odd + dot(live_ref[a + 1][:, :width], near_ref[2 * a + 1, 2], NT)
        near_out_ref[a] = jnp.concatenate([even, odd], axis=1)

    def pack(src, dst, g, to):
        for j in range(0, many, 2):
            dst[to, :, rank * j : rank * (j + 2)] = jnp.concatenate([src[g, j], src[g, j + 1]], axis=1)

    half = first_ref.shape[0]
    for i, copy in reversed(list(enumerate(parent_in))):
        copy.wait()
        for q in range(4 * i, 4 * i + 4):
            if q < half:
                pack(parent_ref, first_ref, q, q)
            else:
                pack(parent_ref, second_ref, q, q - half)
        if 4 * i == half:
            out = pltpu.make_async_copy(second_ref, second_hbm, sems.at[len(started)])
            out.start()
    for i, copy in enumerate(coupling_in):
        copy.wait()
        for g in range(4 * i, 4 * i + 4):
            pack(coupling_ref, packed_ref, g, g)
    for copy in started[-2:]:
        copy.wait()
    out.wait()
    wanted = leaf_at_ref[...] + (1 - position(axes)) * leaves
    leaf_at_ref[...] = wanted ^ (lax.broadcasted_iota(jnp.int32, wanted.shape, 0) & 1)
    n = lax.axis_size(axes[1])
    wanted = mod(parent_at_ref[...], n * parents)
    parent_at_ref[...] = wanted ^ (lax.broadcasted_iota(jnp.int32, wanted.shape, 1) & 1)


def spread_pair(table_ref, at, pair, width):
    table_ref[at] = pair
    table_ref[at + 1] = swap(pair, width)


def picked(table_ref, rows, left):
    return jnp.concatenate(
        [
            jnp.where(left, table_ref[rows[j]], table_ref[rows[j + 1]])
            for j in range(0, len(rows), 2)
        ],
        axis=1,
    )


def leaf_kernel(
    axes, at_vmem, rim_ref, even_ref, odd_ref, packed_ref, rim_near_ref, transfer_hbm, basis_hbm,
    far_ref, edge_ref, transfer_ref, basis_packed_ref, table_ref, at_ref, basis_ref, sems,
):
    at_in, transfer_in, basis_in = start_all(
        [(at_vmem, at_ref), (transfer_hbm, transfer_ref), (basis_hbm, basis_ref)], sems
    )
    many, leaves = at_ref.shape
    rank = packed_ref.shape[1]
    width = rim_near_ref.shape[1]
    pairs = leaves // 2
    sides = rim_ref.shape[1]
    left = left_half(sides, rank)
    parity = lax.rem(position(axes), 2)
    for ref, base in (
        (rim_ref, leaves), (even_ref, 2 * leaves * (1 - parity)), (odd_ref, 2 * leaves * parity),
    ):
        for a in range(pairs):
            spread_pair(table_ref, base + 2 * a, ref[a], rank)
    before = jnp.where(parity == 1, even_ref[pairs + 1], odd_ref[pairs + 1])
    after = jnp.where(parity == 1, odd_ref[pairs], even_ref[pairs])
    low = dot(before[:, width:], rim_near_ref[0], NT)
    high = dot(after[:, :width], rim_near_ref[1], NT)
    edge_ref[0] = jnp.concatenate([low, jnp.zeros_like(low)], axis=1)
    edge_ref[1] = jnp.concatenate([jnp.zeros_like(high), high], axis=1)
    at_in.wait()
    for a in range(pairs):
        fars = []
        for g in (2 * a, 2 * a + 1):
            rows = [at_ref[j, g] for j in range(many)]
            fars.append(dot(picked(table_ref, rows, left), packed_ref[g], NT))
        far_ref[a] = jnp.concatenate(fars, axis=1)
    basis_in.wait()
    for a in range(pairs):
        basis_packed_ref[a] = jnp.concatenate([basis_ref[2 * a], basis_ref[2 * a + 1]], axis=1)
    transfer_in.wait()


def down_kernel(
    at_vmem, row_ref, first_ref, second_hbm, counts_hbm,
    far_ref, near_ref, edge_ref, transfer_ref, basis_ref,
    out_ref, table_ref, at_ref, local_ref, down_ref, second_ref, counts_ref, sems,
):
    at_in, second_in, counts_in = start_all(
        [(at_vmem, at_ref), (second_hbm, second_ref), (counts_hbm, counts_ref)], sems
    )
    parents, many = at_ref.shape
    rank = first_ref.shape[1]
    half = first_ref.shape[0]
    width = basis_ref.shape[1]
    sides = row_ref.shape[1]
    left = left_half(sides, rank)

    def spread(a, carry):
        spread_pair(table_ref, 2 * a, row_ref[a], rank)
        return carry

    lax.fori_loop(0, row_ref.shape[0], spread, 0, unroll=min(64, row_ref.shape[0]))
    at_in.wait()
    for q in range(parents):
        if q == half:
            second_in.wait()
        rows = [at_ref[q, j] for j in range(many)]
        packed = first_ref[q] if q < half else second_ref[q - half]
        far = dot(picked(table_ref, rows, left), packed, NT)
        down_ref[q] = far.astype(jnp.bfloat16)
    for q in range(parents):
        local = far_ref[q] + dot(down_ref[q], transfer_ref[2 * q : 2 * q + 2].reshape(2 * rank, rank), NT)
        local_ref[q] = local.astype(jnp.bfloat16)
    counts_in.wait()
    for q in range(parents):
        local = local_ref[q]
        none = jnp.zeros_like(local)
        both = jnp.concatenate([jnp.where(left, local, none), jnp.where(left, none, local)], axis=0)
        total = dot(both, basis_ref[q], NT)
        total = jnp.concatenate([total[:sides], total[sides:]], axis=1) + near_ref[q]
        if q == 0:
            total = total + edge_ref[0]
        if q == parents - 1:
            total = total + edge_ref[1]
        total = jnp.where(pair_mask(counts_ref, q, sides, width), total, jnp.zeros_like(total))
        out_ref[:, 2 * width * q : 2 * width * (q + 1)] = total.astype(out_ref.dtype)


def per_device(
    charges,
    panel_counts,
    basis,
    transfer,
    leaf_coupling,
    leaf_partners,
    near_blocks,
    parent_coupling,
    parent_partners,
):
    leaves, width, rank = basis.shape
    sides = charges.shape[1]
    parents, many = parent_partners.shape
    pairs = leaves // 2
    own = pairs // 2
    axes = ("gx", "gy")
    n = lax.axis_size("gy")
    total = n * lax.axis_size("gx")
    bf16, f32 = jnp.bfloat16, jnp.float32
    keep = lambda *arrays: [pltpu.with_memory_space_constraint(a, pltpu.HBM) for a in arrays]
    shape = pltpu.VMEM
    dma = lambda count: pltpu.SemaphoreType.DMA((count,))
    params = lambda mib: pltpu.CompilerParams(vmem_limit_bytes=mib * 2**20)
    cost = lambda mib: pl.CostEstimate(flops=0, transcendentals=0, bytes_accessed=mib * 2**20)

    rim, live, parent_coef = pl.pallas_call(
        up_kernel,
        name="up",
        out_shape=[
            shape((pairs + 2, sides, 2 * rank), bf16),
            shape((pairs, sides, 2 * width), bf16),
            shape((own, sides, 2 * rank), bf16),
        ],
        in_specs=[HBM] * 4,
        out_specs=[VMEM] * 3,
        scratch_shapes=[
            pltpu.SMEM((leaves,), jnp.int32),
            pltpu.VMEM((sides, leaves * width), bf16),
            pltpu.VMEM((leaves, width, rank), bf16),
            pltpu.VMEM((leaves, rank, rank), bf16),
            dma(4),
        ],
        compiler_params=params(8),
    )(*keep(panel_counts, charges.T, basis, transfer))

    even = lax.ppermute(rim, axes, [(i, i ^ 1) for i in range(total)])
    steps = [(i, i + 1) for i in range(1, total - 1, 2)]
    odd = lax.ppermute(rim, axes, steps + [(b, a) for a, b in steps])
    sent = pl.pallas_call(
        copies_kernel,
        name="copies",
        out_shape=pltpu.HBM((n * own, sides, 2 * rank), bf16),
        in_specs=[VMEM],
        out_specs=HBM,
        scratch_shapes=[dma(n)],
        compiler_params=params(4),
    )(parent_coef)
    row = lax.all_to_all(sent, "gy", 0, 0, tiled=True)

    held = parents // 8 * 4
    packed, first, second, near, rim_near, leaf_at, parent_at = pl.pallas_call(
        functools.partial(mid_kernel, axes),
        name="mid",
        out_shape=[
            shape((leaves, rank, many * rank), bf16),
            shape((held, rank, many * rank), bf16),
            pltpu.HBM((parents - held, rank, many * rank), bf16),
            shape((pairs, sides, 2 * width), f32),
            shape((2, width, width), bf16),
            shape((many, leaves), jnp.int32),
            shape((parents, many), jnp.int32),
        ],
        in_specs=[VMEM] + [HBM] * 5,
        out_specs=[VMEM] * 2 + [HBM] + [VMEM] * 4,
        scratch_shapes=[
            pltpu.VMEM(leaf_coupling.shape, bf16),
            pltpu.VMEM(near_blocks.shape, bf16),
            pltpu.VMEM(parent_coupling.shape, bf16),
            pltpu.VMEM((parents - held, rank, many * rank), bf16),
            dma(4 + leaves // 4 + parents // 4),
        ],
        compiler_params=params(20),
        cost_estimate=cost(256),
    )(live, *keep(leaf_coupling, near_blocks, parent_coupling, leaf_partners.T, parent_partners))

    far, edge, transfer_in, basis_in = pl.pallas_call(
        functools.partial(leaf_kernel, axes),
        name="leaf",
        out_shape=[
            shape((pairs, sides, 2 * rank), f32),
            shape((2, sides, 2 * width), f32),
            shape(transfer.shape, bf16),
            shape((pairs, width, 2 * rank), bf16),
        ],
        in_specs=[VMEM] * 6 + [HBM] * 2,
        out_specs=[VMEM] * 4,
        scratch_shapes=[
            pltpu.VMEM((3 * leaves, sides, 2 * rank), bf16),
            pltpu.SMEM((many, leaves), jnp.int32),
            pltpu.VMEM(basis.shape, bf16),
            dma(3),
        ],
        compiler_params=params(8),
        cost_estimate=cost(4096),
    )(leaf_at, rim, even, odd, packed, rim_near, *keep(transfer, basis))

    out = pl.pallas_call(
        down_kernel,
        name="down",
        out_shape=jax.ShapeDtypeStruct((sides, leaves * width), bf16),
        in_specs=[VMEM] * 3 + [HBM] * 2 + [VMEM] * 5,
        out_specs=VMEM,
        scratch_shapes=[
            pltpu.VMEM((n * parents, sides, 2 * rank), bf16),
            pltpu.SMEM((parents, many), jnp.int32),
            pltpu.VMEM((pairs, sides, 2 * rank), bf16),
            pltpu.VMEM((parents, sides, rank), bf16),
            pltpu.VMEM((parents - held, rank, many * rank), bf16),
            pltpu.SMEM((leaves,), jnp.int32),
            dma(3),
        ],
        compiler_params=params(12),
    )(parent_at, row, first, *keep(second, panel_counts), far, near, edge, transfer_in, basis_in)
    return out.T


def solution(mesh):
    leaves = ("gx", "gy")
    in_specs = (
        P(leaves, None),
        P(leaves),
        P(leaves, None, None),
        P(leaves, None, None),
        P(leaves, None, None, None),
        P(leaves, None),
        P(leaves, None, None, None),
        P(leaves, None, None, None),
        P(leaves, None),
    )
    return jax.shard_map(
        per_device, mesh=mesh, in_specs=in_specs, out_specs=P(leaves, None), check_vma=False
    )
```

```python
import functools

import jax
import jax.numpy as jnp
from jax import lax
from jax.experimental import pallas as pl
from jax.experimental.pallas import tpu as pltpu
from jax.sharding import PartitionSpec as P

VMEM = pl.BlockSpec(memory_space=pltpu.VMEM)
HBM = pl.BlockSpec(memory_space=pltpu.HBM)
NN = (((1,), (0,)), ((), ()))
NT = (((1,), (1,)), ((), ()))


def dot(a, b, dims):
    return lax.dot_general(a, b, dims, preferred_element_type=jnp.float32)


def left_half(sides, width):
    return lax.broadcasted_iota(jnp.int32, (sides, 2 * width), 1) < width


def pair_mask(counts_ref, pair, sides, width):
    lane = lax.broadcasted_iota(jnp.int32, (sides, 2 * width), 1)
    left = lane < width
    count = jnp.where(left, counts_ref[2 * pair], counts_ref[2 * pair + 1])
    return jnp.where(left, lane, lane - width) < count


def swap(pair, width):
    return jnp.concatenate([pair[:, width:], pair[:, :width]], axis=1)


def mod(x, m):
    return x & (m - 1) if m & (m - 1) == 0 else lax.rem(x, m)


def position(axes):
    index = 0
    for axis in axes:
        index = index * lax.axis_size(axis) + lax.axis_index(axis)
    return index


def start_all(copies, sems):
    started = [pltpu.make_async_copy(src, dst, sems.at[i]) for i, (src, dst) in enumerate(copies)]
    for copy in started:
        copy.start()
    return started


def up_kernel(
    counts_hbm, charges_hbm, basis_hbm, transfer_hbm,
    rim_ref, live_ref, parents_ref,
    counts_ref, charges_ref, basis_ref, transfer_ref, sems,
):
    counts_in, charges_in, basis_in, transfer_in = start_all(
        [
            (counts_hbm, counts_ref), (charges_hbm, charges_ref),
            (basis_hbm, basis_ref), (transfer_hbm, transfer_ref),
        ],
        sems,
    )
    sides = charges_ref.shape[0]
    leaves, width, rank = basis_ref.shape
    pairs = leaves // 2
    own = pairs // 2
    left = left_half(sides, width)
    counts_in.wait()
    charges_in.wait()
    lives = []
    for a in range(pairs):
        charge = charges_ref[:, 2 * width * a : 2 * width * (a + 1)]
        live = jnp.where(pair_mask(counts_ref, a, sides, width), charge, jnp.zeros_like(charge))
        live_ref[a] = live
        lives.append(live)
    rim_ref[pairs] = lives[0]
    rim_ref[pairs + 1] = lives[-1]
    basis_in.wait()
    none = jnp.zeros_like(lives[0])
    coefs = []
    for a in range(pairs):
        live = lives[a]
        both = jnp.concatenate([jnp.where(left, live, none), jnp.where(left, none, live)], axis=0)
        coef = dot(both, basis_ref[2 * a : 2 * a + 2].reshape(2 * width, rank), NN)
        coef = jnp.concatenate([coef[:sides], coef[sides:]], axis=1).astype(jnp.bfloat16)
        rim_ref[a] = coef
        coefs.append(coef)
    transfer_in.wait()
    sums = [
        dot(coefs[a], transfer_ref[2 * a : 2 * a + 2].reshape(2 * rank, rank), NN)
        for a in range(pairs)
    ]
    for a in range(own):
        parents_ref[a] = jnp.concatenate(sums[2 * a : 2 * a + 2], axis=1).astype(jnp.bfloat16)


def copies_kernel(parents_ref, sent_hbm, sems):
    own = parents_ref.shape[0]
    copies = sent_hbm.shape[0] // own
    for copy in start_all([(parents_ref, sent_hbm.at[pl.ds(own * c, own)]) for c in range(copies)], sems):
        copy.wait()


def mid_kernel(
    axes, live_ref, coupling_hbm, near_hbm, parent_hbm, leaf_partners_hbm, parent_partners_hbm,
    packed_ref, first_ref, second_hbm, near_out_ref, rim_near_ref, leaf_at_ref, parent_at_ref,
    coupling_ref, near_ref, parent_ref, second_ref, sems,
):
    leaves, many, rank, _ = coupling_ref.shape
    parents = parent_ref.shape[0]
    width = near_ref.shape[2]
    pairs = leaves // 2
    started = start_all(
        [(near_hbm, near_ref)]
        + [(parent_hbm.at[pl.ds(4 * i, 4)], parent_ref.at[pl.ds(4 * i, 4)]) for i in reversed(range(parents // 4))]
        + [(coupling_hbm.at[pl.ds(4 * i, 4)], coupling_ref.at[pl.ds(4 * i, 4)]) for i in range(leaves // 4)]
        + [(leaf_partners_hbm, leaf_at_ref), (parent_partners_hbm, parent_at_ref)],
        sems,
    )
    near_in = started[0]
    parent_in = started[1 : 1 + parents // 4][::-1]
    coupling_in = started[1 + parents // 4 : -2]
    near_in.wait()
    rim_near_ref[0] = near_ref[0, 0]
    rim_near_ref[1] = near_ref[leaves - 1, 2]
    for a in range(pairs):
        here = live_ref[a]
        even = dot(here, jnp.concatenate([near_ref[2 * a, 1], near_ref[2 * a, 2]], axis=1), NT)
        odd = dot(here, jnp.concatenate([near_ref[2 * a + 1, 0], near_ref[2 * a + 1, 1]], axis=1), NT)
        if a > 0:
            even = even + dot(live_ref[a - 1][:, width:], near_ref[2 * a, 0], NT)
        if a < pairs - 1:
            odd = odd + dot(live_ref[a + 1][:, :width], near_ref[2 * a + 1, 2], NT)
        near_out_ref[a] = jnp.concatenate([even, odd], axis=1)

    def pack(src, dst, g, to):
        for j in range(0, many, 2):
            dst[to, :, rank * j : rank * (j + 2)] = jnp.concatenate([src[g, j], src[g, j + 1]], axis=1)

    half = first_ref.shape[0]
    for i, copy in reversed(list(enumerate(parent_in))):
        copy.wait()
        for q in range(4 * i, 4 * i + 4):
            if q < half:
                pack(parent_ref, first_ref, q, q)
            else:
                pack(parent_ref, second_ref, q, q - half)
        if 4 * i == half:
            out = pltpu.make_async_copy(second_ref, second_hbm, sems.at[len(started)])
            out.start()
    for i, copy in enumerate(coupling_in):
        copy.wait()
        for g in range(4 * i, 4 * i + 4):
            pack(coupling_ref, packed_ref, g, g)
    for copy in started[-2:]:
        copy.wait()
    out.wait()
    wanted = leaf_at_ref[...] + (1 - position(axes)) * leaves
    leaf_at_ref[...] = wanted ^ (lax.broadcasted_iota(jnp.int32, wanted.shape, 0) & 1)
    n = lax.axis_size(axes[1])
    wanted = mod(parent_at_ref[...], n * parents)
    parent_at_ref[...] = wanted ^ (lax.broadcasted_iota(jnp.int32, wanted.shape, 1) & 1)


def spread_pair(table_ref, at, pair, width):
    table_ref[at] = pair
    table_ref[at + 1] = swap(pair, width)


def picked(table_ref, rows, left):
    return jnp.concatenate(
        [
            jnp.where(left, table_ref[rows[j]], table_ref[rows[j + 1]])
            for j in range(0, len(rows), 2)
        ],
        axis=1,
    )


def leaf_kernel(
    axes, at_vmem, rim_ref, even_ref, odd_ref, packed_ref, rim_near_ref, transfer_hbm, basis_hbm,
    far_ref, edge_ref, transfer_ref, basis_packed_ref, table_ref, at_ref, basis_ref, sems,
):
    at_in, transfer_in, basis_in = start_all(
        [(at_vmem, at_ref), (transfer_hbm, transfer_ref), (basis_hbm, basis_ref)], sems
    )
    many, leaves = at_ref.shape
    rank = packed_ref.shape[1]
    width = rim_near_ref.shape[1]
    pairs = leaves // 2
    sides = rim_ref.shape[1]
    left = left_half(sides, rank)
    parity = lax.rem(position(axes), 2)
    for ref, base in (
        (rim_ref, leaves), (even_ref, 2 * leaves * (1 - parity)), (odd_ref, 2 * leaves * parity),
    ):
        for a in range(pairs):
            spread_pair(table_ref, base + 2 * a, ref[a], rank)
    before = jnp.where(parity == 1, even_ref[pairs + 1], odd_ref[pairs + 1])
    after = jnp.where(parity == 1, odd_ref[pairs], even_ref[pairs])
    low = dot(before[:, width:], rim_near_ref[0], NT)
    high = dot(after[:, :width], rim_near_ref[1], NT)
    edge_ref[0] = jnp.concatenate([low, jnp.zeros_like(low)], axis=1)
    edge_ref[1] = jnp.concatenate([jnp.zeros_like(high), high], axis=1)
    at_in.wait()
    for a in range(pairs):
        fars = []
        for g in (2 * a, 2 * a + 1):
            rows = [at_ref[j, g] for j in range(many)]
            fars.append(dot(picked(table_ref, rows, left), packed_ref[g], NT))
        far_ref[a] = jnp.concatenate(fars, axis=1)
    basis_in.wait()
    for a in range(pairs):
        basis_packed_ref[a] = jnp.concatenate([basis_ref[2 * a], basis_ref[2 * a + 1]], axis=1)
    transfer_in.wait()


def down_kernel(
    at_vmem, row_ref, first_ref, second_hbm, counts_hbm,
    far_ref, near_ref, edge_ref, transfer_ref, basis_ref,
    out_ref, table_ref, at_ref, local_ref, down_ref, second_ref, counts_ref, sems,
):
    at_in, second_in, counts_in = start_all(
        [(at_vmem, at_ref), (second_hbm, second_ref), (counts_hbm, counts_ref)], sems
    )
    parents, many = at_ref.shape
    rank = first_ref.shape[1]
    half = first_ref.shape[0]
    width = basis_ref.shape[1]
    sides = row_ref.shape[1]
    left = left_half(sides, rank)

    def spread(a, carry):
        spread_pair(table_ref, 2 * a, row_ref[a], rank)
        return carry

    lax.fori_loop(0, row_ref.shape[0], spread, 0, unroll=min(64, row_ref.shape[0]))
    at_in.wait()
    for q in range(parents):
        if q == half:
            second_in.wait()
        rows = [at_ref[q, j] for j in range(many)]
        packed = first_ref[q] if q < half else second_ref[q - half]
        far = dot(picked(table_ref, rows, left), packed, NT)
        down_ref[q] = far.astype(jnp.bfloat16)
    for q in range(parents):
        local = far_ref[q] + dot(down_ref[q], transfer_ref[2 * q : 2 * q + 2].reshape(2 * rank, rank), NT)
        local_ref[q] = local.astype(jnp.bfloat16)
    counts_in.wait()
    for q in range(parents):
        local = local_ref[q]
        none = jnp.zeros_like(local)
        both = jnp.concatenate([jnp.where(left, local, none), jnp.where(left, none, local)], axis=0)
        total = dot(both, basis_ref[q], NT)
        total = jnp.concatenate([total[:sides], total[sides:]], axis=1) + near_ref[q]
        if q == 0:
            total = total + edge_ref[0]
        if q == parents - 1:
            total = total + edge_ref[1]
        total = jnp.where(pair_mask(counts_ref, q, sides, width), total, jnp.zeros_like(total))
        out_ref[:, 2 * width * q : 2 * width * (q + 1)] = total.astype(out_ref.dtype)


def per_device(
    charges,
    panel_counts,
    basis,
    transfer,
    leaf_coupling,
    leaf_partners,
    near_blocks,
    parent_coupling,
    parent_partners,
):
    leaves, width, rank = basis.shape
    sides = charges.shape[1]
    parents, many = parent_partners.shape
    pairs = leaves // 2
    own = pairs // 2
    axes = ("gx", "gy")
    n = lax.axis_size("gy")
    total = n * lax.axis_size("gx")
    bf16, f32 = jnp.bfloat16, jnp.float32
    keep = lambda *arrays: [pltpu.with_memory_space_constraint(a, pltpu.HBM) for a in arrays]
    shape = pltpu.VMEM
    dma = lambda count: pltpu.SemaphoreType.DMA((count,))
    params = lambda mib: pltpu.CompilerParams(vmem_limit_bytes=mib * 2**20)
    cost = lambda mib: pl.CostEstimate(flops=0, transcendentals=0, bytes_accessed=mib * 2**20)

    rim, live, parent_coef = pl.pallas_call(
        up_kernel,
        name="up",
        out_shape=[
            shape((pairs + 2, sides, 2 * rank), bf16),
            shape((pairs, sides, 2 * width), bf16),
            shape((own, sides, 2 * rank), bf16),
        ],
        in_specs=[HBM] * 4,
        out_specs=[VMEM] * 3,
        scratch_shapes=[
            pltpu.SMEM((leaves,), jnp.int32),
            pltpu.VMEM((sides, leaves * width), bf16),
            pltpu.VMEM((leaves, width, rank), bf16),
            pltpu.VMEM((leaves, rank, rank), bf16),
            dma(4),
        ],
        compiler_params=params(8),
    )(*keep(panel_counts, charges.T, basis, transfer))

    even = lax.ppermute(rim, axes, [(i, i ^ 1) for i in range(total)])
    steps = [(i, i + 1) for i in range(1, total - 1, 2)]
    odd = lax.ppermute(rim, axes, steps + [(b, a) for a, b in steps])
    sent = pl.pallas_call(
        copies_kernel,
        name="copies",
        out_shape=pltpu.HBM((n * own, sides, 2 * rank), bf16),
        in_specs=[VMEM],
        out_specs=HBM,
        scratch_shapes=[dma(n)],
        compiler_params=params(4),
    )(parent_coef)
    row = lax.all_to_all(sent, "gy", 0, 0, tiled=True)

    held = parents // 8 * 4
    packed, first, second, near, rim_near, leaf_at, parent_at = pl.pallas_call(
        functools.partial(mid_kernel, axes),
        name="mid",
        out_shape=[
            shape((leaves, rank, many * rank), bf16),
            shape((held, rank, many * rank), bf16),
            pltpu.HBM((parents - held, rank, many * rank), bf16),
            shape((pairs, sides, 2 * width), f32),
            shape((2, width, width), bf16),
            shape((many, leaves), jnp.int32),
            shape((parents, many), jnp.int32),
        ],
        in_specs=[VMEM] + [HBM] * 5,
        out_specs=[VMEM] * 2 + [HBM] + [VMEM] * 4,
        scratch_shapes=[
            pltpu.VMEM(leaf_coupling.shape, bf16),
            pltpu.VMEM(near_blocks.shape, bf16),
            pltpu.VMEM(parent_coupling.shape, bf16),
            pltpu.VMEM((parents - held, rank, many * rank), bf16),
            dma(4 + leaves // 4 + parents // 4),
        ],
        compiler_params=params(20),
        cost_estimate=cost(0),
    )(live, *keep(leaf_coupling, near_blocks, parent_coupling, leaf_partners.T, parent_partners))

    far, edge, transfer_in, basis_in = pl.pallas_call(
        functools.partial(leaf_kernel, axes),
        name="leaf",
        out_shape=[
            shape((pairs, sides, 2 * rank), f32),
            shape((2, sides, 2 * width), f32),
            shape(transfer.shape, bf16),
            shape((pairs, width, 2 * rank), bf16),
        ],
        in_specs=[VMEM] * 6 + [HBM] * 2,
        out_specs=[VMEM] * 4,
        scratch_shapes=[
            pltpu.VMEM((3 * leaves, sides, 2 * rank), bf16),
            pltpu.SMEM((many, leaves), jnp.int32),
            pltpu.VMEM(basis.shape, bf16),
            dma(3),
        ],
        compiler_params=params(8),
        cost_estimate=cost(512),
    )(leaf_at, rim, even, odd, packed, rim_near, *keep(transfer, basis))

    out = pl.pallas_call(
        down_kernel,
        name="down",
        out_shape=jax.ShapeDtypeStruct((sides, leaves * width), bf16),
        in_specs=[VMEM] * 3 + [HBM] * 2 + [VMEM] * 5,
        out_specs=VMEM,
        scratch_shapes=[
            pltpu.VMEM((n * parents, sides, 2 * rank), bf16),
            pltpu.SMEM((parents, many), jnp.int32),
            pltpu.VMEM((pairs, sides, 2 * rank), bf16),
            pltpu.VMEM((parents, sides, rank), bf16),
            pltpu.VMEM((parents - held, rank, many * rank), bf16),
            pltpu.SMEM((leaves,), jnp.int32),
            dma(3),
        ],
        compiler_params=params(12),
    )(parent_at, row, first, *keep(second, panel_counts), far, near, edge, transfer_in, basis_in)
    return out.T


def solution(mesh):
    leaves = ("gx", "gy")
    in_specs = (
        P(leaves, None),
        P(leaves),
        P(leaves, None, None),
        P(leaves, None, None),
        P(leaves, None, None, None),
        P(leaves, None),
        P(leaves, None, None, None),
        P(leaves, None, None, None),
        P(leaves, None),
    )
    return jax.shard_map(
        per_device, mesh=mesh, in_specs=in_specs, out_specs=P(leaves, None), check_vma=False
    )
```

```python
import functools

import jax
import jax.numpy as jnp
from jax import lax
from jax.experimental import pallas as pl
from jax.experimental.pallas import tpu as pltpu
from jax.sharding import PartitionSpec as P

VMEM = pl.BlockSpec(memory_space=pltpu.VMEM)
HBM = pl.BlockSpec(memory_space=pltpu.HBM)
NN = (((1,), (0,)), ((), ()))
NT = (((1,), (1,)), ((), ()))


def dot(a, b, dims):
    return lax.dot_general(a, b, dims, preferred_element_type=jnp.float32)


def left_half(sides, width):
    return lax.broadcasted_iota(jnp.int32, (sides, 2 * width), 1) < width


def pair_mask(counts_ref, pair, sides, width):
    lane = lax.broadcasted_iota(jnp.int32, (sides, 2 * width), 1)
    left = lane < width
    count = jnp.where(left, counts_ref[2 * pair], counts_ref[2 * pair + 1])
    return jnp.where(left, lane, lane - width) < count


def swap(pair, width):
    return jnp.concatenate([pair[:, width:], pair[:, :width]], axis=1)


def mod(x, m):
    return x & (m - 1) if m & (m - 1) == 0 else lax.rem(x, m)


def position(axes):
    index = 0
    for axis in axes:
        index = index * lax.axis_size(axis) + lax.axis_index(axis)
    return index


def start_all(copies, sems):
    started = [pltpu.make_async_copy(src, dst, sems.at[i]) for i, (src, dst) in enumerate(copies)]
    for copy in started:
        copy.start()
    return started


def up_kernel(
    counts_hbm, charges_hbm, basis_hbm, transfer_hbm,
    rim_ref, live_ref, parents_ref,
    counts_ref, charges_ref, basis_ref, transfer_ref, sems,
):
    counts_in, charges_in, basis_in, transfer_in = start_all(
        [
            (counts_hbm, counts_ref), (charges_hbm, charges_ref),
            (basis_hbm, basis_ref), (transfer_hbm, transfer_ref),
        ],
        sems,
    )
    sides = charges_ref.shape[0]
    leaves, width, rank = basis_ref.shape
    pairs = leaves // 2
    own = pairs // 2
    left = left_half(sides, width)
    counts_in.wait()
    charges_in.wait()
    lives = []
    for a in range(pairs):
        charge = charges_ref[:, 2 * width * a : 2 * width * (a + 1)]
        live = jnp.where(pair_mask(counts_ref, a, sides, width), charge, jnp.zeros_like(charge))
        live_ref[a] = live
        lives.append(live)
    rim_ref[pairs] = lives[0]
    rim_ref[pairs + 1] = lives[-1]
    basis_in.wait()
    none = jnp.zeros_like(lives[0])
    coefs = []
    for a in range(pairs):
        live = lives[a]
        both = jnp.concatenate([jnp.where(left, live, none), jnp.where(left, none, live)], axis=0)
        coef = dot(both, basis_ref[2 * a : 2 * a + 2].reshape(2 * width, rank), NN)
        coef = jnp.concatenate([coef[:sides], coef[sides:]], axis=1).astype(jnp.bfloat16)
        rim_ref[a] = coef
        coefs.append(coef)
    transfer_in.wait()
    sums = [
        dot(coefs[a], transfer_ref[2 * a : 2 * a + 2].reshape(2 * rank, rank), NN)
        for a in range(pairs)
    ]
    for a in range(own):
        parents_ref[a] = jnp.concatenate(sums[2 * a : 2 * a + 2], axis=1).astype(jnp.bfloat16)


def copies_kernel(parents_ref, sent_hbm, sems):
    own = parents_ref.shape[0]
    copies = sent_hbm.shape[0] // own
    for copy in start_all([(parents_ref, sent_hbm.at[pl.ds(own * c, own)]) for c in range(copies)], sems):
        copy.wait()


def mid_kernel(
    axes, live_ref, coupling_hbm, near_hbm, parent_hbm, leaf_partners_hbm, parent_partners_hbm,
    packed_ref, first_ref, second_hbm, near_out_ref, rim_near_ref, leaf_at_ref, parent_at_ref,
    coupling_ref, near_ref, parent_ref, second_ref, sems,
):
    leaves, many, rank, _ = coupling_ref.shape
    parents = parent_ref.shape[0]
    width = near_ref.shape[2]
    pairs = leaves // 2
    started = start_all(
        [(near_hbm, near_ref)]
        + [(parent_hbm.at[pl.ds(4 * i, 4)], parent_ref.at[pl.ds(4 * i, 4)]) for i in reversed(range(parents // 4))]
        + [(coupling_hbm.at[pl.ds(4 * i, 4)], coupling_ref.at[pl.ds(4 * i, 4)]) for i in range(leaves // 4)]
        + [(leaf_partners_hbm, leaf_at_ref), (parent_partners_hbm, parent_at_ref)],
        sems,
    )
    near_in = started[0]
    parent_in = started[1 : 1 + parents // 4][::-1]
    coupling_in = started[1 + parents // 4 : -2]
    near_in.wait()
    rim_near_ref[0] = near_ref[0, 0]
    rim_near_ref[1] = near_ref[leaves - 1, 2]
    for a in range(pairs):
        here = live_ref[a]
        even = dot(here, jnp.concatenate([near_ref[2 * a, 1], near_ref[2 * a, 2]], axis=1), NT)
        odd = dot(here, jnp.concatenate([near_ref[2 * a + 1, 0], near_ref[2 * a + 1, 1]], axis=1), NT)
        if a > 0:
            even = even + dot(live_ref[a - 1][:, width:], near_ref[2 * a, 0], NT)
        if a < pairs - 1:
            odd = odd + dot(live_ref[a + 1][:, :width], near_ref[2 * a + 1, 2], NT)
        near_out_ref[a] = jnp.concatenate([even, odd], axis=1)

    def pack(src, dst, g, to):
        for j in range(0, many, 2):
            dst[to, :, rank * j : rank * (j + 2)] = jnp.concatenate([src[g, j], src[g, j + 1]], axis=1)

    half = first_ref.shape[0]
    for i, copy in reversed(list(enumerate(parent_in))):
        copy.wait()
        for q in range(4 * i, 4 * i + 4):
            if q < half:
                pack(parent_ref, first_ref, q, q)
            else:
                pack(parent_ref, second_ref, q, q - half)
        if 4 * i == half:
            out = pltpu.make_async_copy(second_ref, second_hbm, sems.at[len(started)])
            out.start()
    for i, copy in enumerate(coupling_in):
        copy.wait()
        for g in range(4 * i, 4 * i + 4):
            pack(coupling_ref, packed_ref, g, g)
    for copy in started[-2:]:
        copy.wait()
    out.wait()
    wanted = leaf_at_ref[...] + (1 - position(axes)) * leaves
    leaf_at_ref[...] = wanted ^ (lax.broadcasted_iota(jnp.int32, wanted.shape, 0) & 1)
    n = lax.axis_size(axes[1])
    wanted = mod(parent_at_ref[...], n * parents)
    parent_at_ref[...] = wanted ^ (lax.broadcasted_iota(jnp.int32, wanted.shape, 1) & 1)


def spread_pair(table_ref, at, pair, width):
    table_ref[at] = pair
    table_ref[at + 1] = swap(pair, width)


def picked(table_ref, rows, left):
    return jnp.concatenate(
        [
            jnp.where(left, table_ref[rows[j]], table_ref[rows[j + 1]])
            for j in range(0, len(rows), 2)
        ],
        axis=1,
    )


def leaf_kernel(
    axes, at_vmem, rim_ref, even_ref, odd_ref, packed_ref, rim_near_ref, transfer_hbm, basis_hbm,
    far_ref, edge_ref, transfer_ref, basis_packed_ref, table_ref, at_ref, basis_ref, sems,
):
    at_in, transfer_in, basis_in = start_all(
        [(at_vmem, at_ref), (transfer_hbm, transfer_ref), (basis_hbm, basis_ref)], sems
    )
    many, leaves = at_ref.shape
    rank = packed_ref.shape[1]
    width = rim_near_ref.shape[1]
    pairs = leaves // 2
    sides = rim_ref.shape[1]
    left = left_half(sides, rank)
    parity = lax.rem(position(axes), 2)
    for ref, base in (
        (rim_ref, leaves), (even_ref, 2 * leaves * (1 - parity)), (odd_ref, 2 * leaves * parity),
    ):
        for a in range(pairs):
            spread_pair(table_ref, base + 2 * a, ref[a], rank)
    before = jnp.where(parity == 1, even_ref[pairs + 1], odd_ref[pairs + 1])
    after = jnp.where(parity == 1, odd_ref[pairs], even_ref[pairs])
    low = dot(before[:, width:], rim_near_ref[0], NT)
    high = dot(after[:, :width], rim_near_ref[1], NT)
    edge_ref[0] = jnp.concatenate([low, jnp.zeros_like(low)], axis=1)
    edge_ref[1] = jnp.concatenate([jnp.zeros_like(high), high], axis=1)
    at_in.wait()
    for a in range(pairs):
        fars = []
        for g in (2 * a, 2 * a + 1):
            rows = [at_ref[j, g] for j in range(many)]
            fars.append(dot(picked(table_ref, rows, left), packed_ref[g], NT))
        far_ref[a] = jnp.concatenate(fars, axis=1)
    basis_in.wait()
    for a in range(pairs):
        basis_packed_ref[a] = jnp.concatenate([basis_ref[2 * a], basis_ref[2 * a + 1]], axis=1)
    transfer_in.wait()


def down_kernel(
    at_vmem, row_ref, first_ref, second_hbm, counts_hbm,
    far_ref, near_ref, edge_ref, transfer_ref, basis_ref,
    out_ref, table_ref, at_ref, local_ref, down_ref, second_ref, counts_ref, sems,
):
    at_in, second_in, counts_in = start_all(
        [(at_vmem, at_ref), (second_hbm, second_ref), (counts_hbm, counts_ref)], sems
    )
    parents, many = at_ref.shape
    rank = first_ref.shape[1]
    half = first_ref.shape[0]
    width = basis_ref.shape[1]
    sides = row_ref.shape[1]
    left = left_half(sides, rank)

    def spread(a, carry):
        spread_pair(table_ref, 2 * a, row_ref[a], rank)
        return carry

    lax.fori_loop(0, row_ref.shape[0], spread, 0, unroll=min(64, row_ref.shape[0]))
    at_in.wait()
    for q in range(parents):
        if q == half:
            second_in.wait()
        rows = [at_ref[q, j] for j in range(many)]
        packed = first_ref[q] if q < half else second_ref[q - half]
        far = dot(picked(table_ref, rows, left), packed, NT)
        down_ref[q] = far.astype(jnp.bfloat16)
    for q in range(parents):
        local = far_ref[q] + dot(down_ref[q], transfer_ref[2 * q : 2 * q + 2].reshape(2 * rank, rank), NT)
        local_ref[q] = local.astype(jnp.bfloat16)
    counts_in.wait()
    for q in range(parents):
        local = local_ref[q]
        none = jnp.zeros_like(local)
        both = jnp.concatenate([jnp.where(left, local, none), jnp.where(left, none, local)], axis=0)
        total = dot(both, basis_ref[q], NT)
        total = jnp.concatenate([total[:sides], total[sides:]], axis=1) + near_ref[q]
        if q == 0:
            total = total + edge_ref[0]
        if q == parents - 1:
            total = total + edge_ref[1]
        total = jnp.where(pair_mask(counts_ref, q, sides, width), total, jnp.zeros_like(total))
        out_ref[:, 2 * width * q : 2 * width * (q + 1)] = total.astype(out_ref.dtype)


def per_device(
    charges,
    panel_counts,
    basis,
    transfer,
    leaf_coupling,
    leaf_partners,
    near_blocks,
    parent_coupling,
    parent_partners,
):
    leaves, width, rank = basis.shape
    sides = charges.shape[1]
    parents, many = parent_partners.shape
    pairs = leaves // 2
    own = pairs // 2
    axes = ("gx", "gy")
    n = lax.axis_size("gy")
    total = n * lax.axis_size("gx")
    bf16, f32 = jnp.bfloat16, jnp.float32
    keep = lambda *arrays: [pltpu.with_memory_space_constraint(a, pltpu.HBM) for a in arrays]
    shape = pltpu.VMEM
    dma = lambda count: pltpu.SemaphoreType.DMA((count,))
    params = lambda mib: pltpu.CompilerParams(vmem_limit_bytes=mib * 2**20)
    cost = lambda mib: pl.CostEstimate(flops=0, transcendentals=0, bytes_accessed=mib * 2**20)

    rim, live, parent_coef = pl.pallas_call(
        up_kernel,
        name="up",
        out_shape=[
            shape((pairs + 2, sides, 2 * rank), bf16),
            shape((pairs, sides, 2 * width), bf16),
            shape((own, sides, 2 * rank), bf16),
        ],
        in_specs=[HBM] * 4,
        out_specs=[VMEM] * 3,
        scratch_shapes=[
            pltpu.SMEM((leaves,), jnp.int32),
            pltpu.VMEM((sides, leaves * width), bf16),
            pltpu.VMEM((leaves, width, rank), bf16),
            pltpu.VMEM((leaves, rank, rank), bf16),
            dma(4),
        ],
        compiler_params=params(8),
    )(*keep(panel_counts, charges.T, basis, transfer))

    even = lax.ppermute(rim, axes, [(i, i ^ 1) for i in range(total)])
    steps = [(i, i + 1) for i in range(1, total - 1, 2)]
    odd = lax.ppermute(rim, axes, steps + [(b, a) for a, b in steps])
    sent = pl.pallas_call(
        copies_kernel,
        name="copies",
        out_shape=pltpu.HBM((n * own, sides, 2 * rank), bf16),
        in_specs=[VMEM],
        out_specs=HBM,
        scratch_shapes=[dma(n)],
        compiler_params=params(4),
        cost_estimate=cost(512),
    )(parent_coef)
    row = lax.all_to_all(sent, "gy", 0, 0, tiled=True)

    held = parents // 8 * 4
    packed, first, second, near, rim_near, leaf_at, parent_at = pl.pallas_call(
        functools.partial(mid_kernel, axes),
        name="mid",
        out_shape=[
            shape((leaves, rank, many * rank), bf16),
            shape((held, rank, many * rank), bf16),
            pltpu.HBM((parents - held, rank, many * rank), bf16),
            shape((pairs, sides, 2 * width), f32),
            shape((2, width, width), bf16),
            shape((many, leaves), jnp.int32),
            shape((parents, many), jnp.int32),
        ],
        in_specs=[VMEM] + [HBM] * 5,
        out_specs=[VMEM] * 2 + [HBM] + [VMEM] * 4,
        scratch_shapes=[
            pltpu.VMEM(leaf_coupling.shape, bf16),
            pltpu.VMEM(near_blocks.shape, bf16),
            pltpu.VMEM(parent_coupling.shape, bf16),
            pltpu.VMEM((parents - held, rank, many * rank), bf16),
            dma(4 + leaves // 4 + parents // 4),
        ],
        compiler_params=params(20),
        cost_estimate=cost(16),
    )(live, *keep(leaf_coupling, near_blocks, parent_coupling, leaf_partners.T, parent_partners))

    far, edge, transfer_in, basis_in = pl.pallas_call(
        functools.partial(leaf_kernel, axes),
        name="leaf",
        out_shape=[
            shape((pairs, sides, 2 * rank), f32),
            shape((2, sides, 2 * width), f32),
            shape(transfer.shape, bf16),
            shape((pairs, width, 2 * rank), bf16),
        ],
        in_specs=[VMEM] * 6 + [HBM] * 2,
        out_specs=[VMEM] * 4,
        scratch_shapes=[
            pltpu.VMEM((3 * leaves, sides, 2 * rank), bf16),
            pltpu.SMEM((many, leaves), jnp.int32),
            pltpu.VMEM(basis.shape, bf16),
            dma(3),
        ],
        compiler_params=params(8),
        cost_estimate=cost(512),
    )(leaf_at, rim, even, odd, packed, rim_near, *keep(transfer, basis))

    out = pl.pallas_call(
        down_kernel,
        name="down",
        out_shape=jax.ShapeDtypeStruct((sides, leaves * width), bf16),
        in_specs=[VMEM] * 3 + [HBM] * 2 + [VMEM] * 5,
        out_specs=VMEM,
        scratch_shapes=[
            pltpu.VMEM((n * parents, sides, 2 * rank), bf16),
            pltpu.SMEM((parents, many), jnp.int32),
            pltpu.VMEM((pairs, sides, 2 * rank), bf16),
            pltpu.VMEM((parents, sides, rank), bf16),
            pltpu.VMEM((parents - held, rank, many * rank), bf16),
            pltpu.SMEM((leaves,), jnp.int32),
            dma(3),
        ],
        compiler_params=params(12),
    )(parent_at, row, first, *keep(second, panel_counts), far, near, edge, transfer_in, basis_in)
    return out.T


def solution(mesh):
    leaves = ("gx", "gy")
    in_specs = (
        P(leaves, None),
        P(leaves),
        P(leaves, None, None),
        P(leaves, None, None),
        P(leaves, None, None, None),
        P(leaves, None),
        P(leaves, None, None, None),
        P(leaves, None, None, None),
        P(leaves, None),
    )
    return jax.shard_map(
        per_device, mesh=mesh, in_specs=in_specs, out_specs=P(leaves, None), check_vma=False
    )
```

```python
import functools

import jax
import jax.numpy as jnp
from jax import lax
from jax.experimental import pallas as pl
from jax.experimental.pallas import tpu as pltpu
from jax.sharding import PartitionSpec as P

VMEM = pl.BlockSpec(memory_space=pltpu.VMEM)
HBM = pl.BlockSpec(memory_space=pltpu.HBM)
NN = (((1,), (0,)), ((), ()))
NT = (((1,), (1,)), ((), ()))


def dot(a, b, dims):
    return lax.dot_general(a, b, dims, preferred_element_type=jnp.float32)


def left_half(sides, width):
    return lax.broadcasted_iota(jnp.int32, (sides, 2 * width), 1) < width


def pair_mask(counts_ref, pair, sides, width):
    lane = lax.broadcasted_iota(jnp.int32, (sides, 2 * width), 1)
    left = lane < width
    count = jnp.where(left, counts_ref[2 * pair], counts_ref[2 * pair + 1])
    return jnp.where(left, lane, lane - width) < count


def swap(pair, width):
    return jnp.concatenate([pair[:, width:], pair[:, :width]], axis=1)


def mod(x, m):
    return x & (m - 1) if m & (m - 1) == 0 else lax.rem(x, m)


def position(axes):
    index = 0
    for axis in axes:
        index = index * lax.axis_size(axis) + lax.axis_index(axis)
    return index


def start_all(copies, sems):
    started = [pltpu.make_async_copy(src, dst, sems.at[i]) for i, (src, dst) in enumerate(copies)]
    for copy in started:
        copy.start()
    return started


def up_kernel(
    counts_hbm, charges_hbm, basis_hbm, transfer_hbm,
    rim_ref, live_ref, parents_ref,
    counts_ref, charges_ref, basis_ref, transfer_ref, sems,
):
    counts_in, charges_in, basis_in, transfer_in = start_all(
        [
            (counts_hbm, counts_ref), (charges_hbm, charges_ref),
            (basis_hbm, basis_ref), (transfer_hbm, transfer_ref),
        ],
        sems,
    )
    sides = charges_ref.shape[0]
    leaves, width, rank = basis_ref.shape
    pairs = leaves // 2
    own = pairs // 2
    left = left_half(sides, width)
    counts_in.wait()
    charges_in.wait()
    lives = []
    for a in range(pairs):
        charge = charges_ref[:, 2 * width * a : 2 * width * (a + 1)]
        live = jnp.where(pair_mask(counts_ref, a, sides, width), charge, jnp.zeros_like(charge))
        live_ref[a] = live
        lives.append(live)
    rim_ref[pairs] = lives[0]
    rim_ref[pairs + 1] = lives[-1]
    basis_in.wait()
    none = jnp.zeros_like(lives[0])
    coefs = []
    for a in range(pairs):
        live = lives[a]
        both = jnp.concatenate([jnp.where(left, live, none), jnp.where(left, none, live)], axis=0)
        coef = dot(both, basis_ref[2 * a : 2 * a + 2].reshape(2 * width, rank), NN)
        coef = jnp.concatenate([coef[:sides], coef[sides:]], axis=1).astype(jnp.bfloat16)
        rim_ref[a] = coef
        coefs.append(coef)
    transfer_in.wait()
    sums = [
        dot(coefs[a], transfer_ref[2 * a : 2 * a + 2].reshape(2 * rank, rank), NN)
        for a in range(pairs)
    ]
    for a in range(own):
        parents_ref[a] = jnp.concatenate(sums[2 * a : 2 * a + 2], axis=1).astype(jnp.bfloat16)


def copies_kernel(parents_ref, sent_hbm, sems):
    own = parents_ref.shape[0]
    copies = sent_hbm.shape[0] // own
    for copy in start_all([(parents_ref, sent_hbm.at[pl.ds(own * c, own)]) for c in range(copies)], sems):
        copy.wait()


def mid_kernel(
    axes, live_ref, coupling_hbm, near_hbm, parent_hbm, leaf_partners_hbm, parent_partners_hbm,
    packed_ref, first_ref, second_hbm, near_out_ref, rim_near_ref, leaf_at_ref, parent_at_ref,
    coupling_ref, near_ref, parent_ref, second_ref, sems,
):
    leaves, many, rank, _ = coupling_ref.shape
    parents = parent_ref.shape[0]
    width = near_ref.shape[2]
    pairs = leaves // 2
    started = start_all(
        [(near_hbm, near_ref)]
        + [(parent_hbm.at[pl.ds(4 * i, 4)], parent_ref.at[pl.ds(4 * i, 4)]) for i in reversed(range(parents // 4))]
        + [(coupling_hbm.at[pl.ds(4 * i, 4)], coupling_ref.at[pl.ds(4 * i, 4)]) for i in range(leaves // 4)]
        + [(leaf_partners_hbm, leaf_at_ref), (parent_partners_hbm, parent_at_ref)],
        sems,
    )
    near_in = started[0]
    parent_in = started[1 : 1 + parents // 4][::-1]
    coupling_in = started[1 + parents // 4 : -2]
    near_in.wait()
    rim_near_ref[0] = near_ref[0, 0]
    rim_near_ref[1] = near_ref[leaves - 1, 2]
    for a in range(pairs):
        here = live_ref[a]
        even = dot(here, jnp.concatenate([near_ref[2 * a, 1], near_ref[2 * a, 2]], axis=1), NT)
        odd = dot(here, jnp.concatenate([near_ref[2 * a + 1, 0], near_ref[2 * a + 1, 1]], axis=1), NT)
        if a > 0:
            even = even + dot(live_ref[a - 1][:, width:], near_ref[2 * a, 0], NT)
        if a < pairs - 1:
            odd = odd + dot(live_ref[a + 1][:, :width], near_ref[2 * a + 1, 2], NT)
        near_out_ref[a] = jnp.concatenate([even, odd], axis=1)

    def pack(src, dst, g, to):
        for j in range(0, many, 2):
            dst[to, :, rank * j : rank * (j + 2)] = jnp.concatenate([src[g, j], src[g, j + 1]], axis=1)

    half = first_ref.shape[0]
    for i, copy in reversed(list(enumerate(parent_in))):
        copy.wait()
        for q in range(4 * i, 4 * i + 4):
            if q < half:
                pack(parent_ref, first_ref, q, q)
            else:
                pack(parent_ref, second_ref, q, q - half)
        if 4 * i == half:
            out = pltpu.make_async_copy(second_ref, second_hbm, sems.at[len(started)])
            out.start()
    for i, copy in enumerate(coupling_in):
        copy.wait()
        for g in range(4 * i, 4 * i + 4):
            pack(coupling_ref, packed_ref, g, g)
    for copy in started[-2:]:
        copy.wait()
    out.wait()
    wanted = leaf_at_ref[...] + (1 - position(axes)) * leaves
    leaf_at_ref[...] = wanted ^ (lax.broadcasted_iota(jnp.int32, wanted.shape, 0) & 1)
    n = lax.axis_size(axes[1])
    wanted = mod(parent_at_ref[...], n * parents)
    parent_at_ref[...] = wanted ^ (lax.broadcasted_iota(jnp.int32, wanted.shape, 1) & 1)


def spread_pair(table_ref, at, pair, width):
    table_ref[at] = pair
    table_ref[at + 1] = swap(pair, width)


def picked(table_ref, rows, left):
    return jnp.concatenate(
        [
            jnp.where(left, table_ref[rows[j]], table_ref[rows[j + 1]])
            for j in range(0, len(rows), 2)
        ],
        axis=1,
    )


def leaf_kernel(
    axes, at_vmem, rim_ref, even_ref, odd_ref, packed_ref, rim_near_ref, transfer_hbm, basis_hbm,
    far_ref, edge_ref, transfer_ref, basis_packed_ref, table_ref, at_ref, basis_ref, sems,
):
    at_in, transfer_in, basis_in = start_all(
        [(at_vmem, at_ref), (transfer_hbm, transfer_ref), (basis_hbm, basis_ref)], sems
    )
    many, leaves = at_ref.shape
    rank = packed_ref.shape[1]
    width = rim_near_ref.shape[1]
    pairs = leaves // 2
    sides = rim_ref.shape[1]
    left = left_half(sides, rank)
    parity = lax.rem(position(axes), 2)
    for ref, base in (
        (rim_ref, leaves), (even_ref, 2 * leaves * (1 - parity)), (odd_ref, 2 * leaves * parity),
    ):
        for a in range(pairs):
            spread_pair(table_ref, base + 2 * a, ref[a], rank)
    before = jnp.where(parity == 1, even_ref[pairs + 1], odd_ref[pairs + 1])
    after = jnp.where(parity == 1, odd_ref[pairs], even_ref[pairs])
    low = dot(before[:, width:], rim_near_ref[0], NT)
    high = dot(after[:, :width], rim_near_ref[1], NT)
    edge_ref[0] = jnp.concatenate([low, jnp.zeros_like(low)], axis=1)
    edge_ref[1] = jnp.concatenate([jnp.zeros_like(high), high], axis=1)
    at_in.wait()
    for a in range(pairs):
        fars = []
        for g in (2 * a, 2 * a + 1):
            rows = [at_ref[j, g] for j in range(many)]
            fars.append(dot(picked(table_ref, rows, left), packed_ref[g], NT))
        far_ref[a] = jnp.concatenate(fars, axis=1)
    basis_in.wait()
    for a in range(pairs):
        basis_packed_ref[a] = jnp.concatenate([basis_ref[2 * a], basis_ref[2 * a + 1]], axis=1)
    transfer_in.wait()


def down_kernel(
    at_vmem, row_ref, first_ref, second_hbm, counts_hbm,
    far_ref, near_ref, edge_ref, transfer_ref, basis_ref,
    out_ref, table_ref, at_ref, local_ref, down_ref, second_ref, counts_ref, sems,
):
    at_in, second_in, counts_in = start_all(
        [(at_vmem, at_ref), (second_hbm, second_ref), (counts_hbm, counts_ref)], sems
    )
    parents, many = at_ref.shape
    rank = first_ref.shape[1]
    half = first_ref.shape[0]
    width = basis_ref.shape[1]
    sides = row_ref.shape[1]
    left = left_half(sides, rank)

    def spread(a, carry):
        spread_pair(table_ref, 2 * a, row_ref[a], rank)
        return carry

    lax.fori_loop(0, row_ref.shape[0], spread, 0, unroll=min(64, row_ref.shape[0]))
    at_in.wait()
    for q in range(parents):
        if q == half:
            second_in.wait()
        rows = [at_ref[q, j] for j in range(many)]
        packed = first_ref[q] if q < half else second_ref[q - half]
        far = dot(picked(table_ref, rows, left), packed, NT)
        down_ref[q] = far.astype(jnp.bfloat16)
    for q in range(parents):
        local = far_ref[q] + dot(down_ref[q], transfer_ref[2 * q : 2 * q + 2].reshape(2 * rank, rank), NT)
        local_ref[q] = local.astype(jnp.bfloat16)
    counts_in.wait()
    for q in range(parents):
        local = local_ref[q]
        none = jnp.zeros_like(local)
        both = jnp.concatenate([jnp.where(left, local, none), jnp.where(left, none, local)], axis=0)
        total = dot(both, basis_ref[q], NT)
        total = jnp.concatenate([total[:sides], total[sides:]], axis=1) + near_ref[q]
        if q == 0:
            total = total + edge_ref[0]
        if q == parents - 1:
            total = total + edge_ref[1]
        total = jnp.where(pair_mask(counts_ref, q, sides, width), total, jnp.zeros_like(total))
        out_ref[:, 2 * width * q : 2 * width * (q + 1)] = total.astype(out_ref.dtype)


def per_device(
    charges,
    panel_counts,
    basis,
    transfer,
    leaf_coupling,
    leaf_partners,
    near_blocks,
    parent_coupling,
    parent_partners,
):
    leaves, width, rank = basis.shape
    sides = charges.shape[1]
    parents, many = parent_partners.shape
    pairs = leaves // 2
    own = pairs // 2
    axes = ("gx", "gy")
    n = lax.axis_size("gy")
    total = n * lax.axis_size("gx")
    bf16, f32 = jnp.bfloat16, jnp.float32
    keep = lambda *arrays: [pltpu.with_memory_space_constraint(a, pltpu.HBM) for a in arrays]
    shape = pltpu.VMEM
    dma = lambda count: pltpu.SemaphoreType.DMA((count,))
    params = lambda mib: pltpu.CompilerParams(vmem_limit_bytes=mib * 2**20)
    cost = lambda kib: pl.CostEstimate(flops=kib * 2**10, transcendentals=0, bytes_accessed=kib * 2**10)

    rim, live, parent_coef = pl.pallas_call(
        up_kernel,
        name="up",
        out_shape=[
            shape((pairs + 2, sides, 2 * rank), bf16),
            shape((pairs, sides, 2 * width), bf16),
            shape((own, sides, 2 * rank), bf16),
        ],
        in_specs=[HBM] * 4,
        out_specs=[VMEM] * 3,
        scratch_shapes=[
            pltpu.SMEM((leaves,), jnp.int32),
            pltpu.VMEM((sides, leaves * width), bf16),
            pltpu.VMEM((leaves, width, rank), bf16),
            pltpu.VMEM((leaves, rank, rank), bf16),
            dma(4),
        ],
        compiler_params=params(8),
    )(*keep(panel_counts, charges.T, basis, transfer))

    even = lax.ppermute(rim, axes, [(i, i ^ 1) for i in range(total)])
    steps = [(i, i + 1) for i in range(1, total - 1, 2)]
    odd = lax.ppermute(rim, axes, steps + [(b, a) for a, b in steps])
    sent = pl.pallas_call(
        copies_kernel,
        name="copies",
        out_shape=pltpu.HBM((n * own, sides, 2 * rank), bf16),
        in_specs=[VMEM],
        out_specs=HBM,
        scratch_shapes=[dma(n)],
        compiler_params=params(4),
        cost_estimate=cost(16),
    )(parent_coef)
    row = lax.all_to_all(sent, "gy", 0, 0, tiled=True)

    held = parents // 8 * 4
    packed, first, second, near, rim_near, leaf_at, parent_at = pl.pallas_call(
        functools.partial(mid_kernel, axes),
        name="mid",
        out_shape=[
            shape((leaves, rank, many * rank), bf16),
            shape((held, rank, many * rank), bf16),
            pltpu.HBM((parents - held, rank, many * rank), bf16),
            shape((pairs, sides, 2 * width), f32),
            shape((2, width, width), bf16),
            shape((many, leaves), jnp.int32),
            shape((parents, many), jnp.int32),
        ],
        in_specs=[VMEM] + [HBM] * 5,
        out_specs=[VMEM] * 2 + [HBM] + [VMEM] * 4,
        scratch_shapes=[
            pltpu.VMEM(leaf_coupling.shape, bf16),
            pltpu.VMEM(near_blocks.shape, bf16),
            pltpu.VMEM(parent_coupling.shape, bf16),
            pltpu.VMEM((parents - held, rank, many * rank), bf16),
            dma(4 + leaves // 4 + parents // 4),
        ],
        compiler_params=params(20),
        cost_estimate=cost(16),
    )(live, *keep(leaf_coupling, near_blocks, parent_coupling, leaf_partners.T, parent_partners))

    far, edge, transfer_in, basis_in = pl.pallas_call(
        functools.partial(leaf_kernel, axes),
        name="leaf",
        out_shape=[
            shape((pairs, sides, 2 * rank), f32),
            shape((2, sides, 2 * width), f32),
            shape(transfer.shape, bf16),
            shape((pairs, width, 2 * rank), bf16),
        ],
        in_specs=[VMEM] * 6 + [HBM] * 2,
        out_specs=[VMEM] * 4,
        scratch_shapes=[
            pltpu.VMEM((3 * leaves, sides, 2 * rank), bf16),
            pltpu.SMEM((many, leaves), jnp.int32),
            pltpu.VMEM(basis.shape, bf16),
            dma(3),
        ],
        compiler_params=params(8),
        cost_estimate=cost(512 * 1024),
    )(leaf_at, rim, even, odd, packed, rim_near, *keep(transfer, basis))

    out = pl.pallas_call(
        down_kernel,
        name="down",
        out_shape=jax.ShapeDtypeStruct((sides, leaves * width), bf16),
        in_specs=[VMEM] * 3 + [HBM] * 2 + [VMEM] * 5,
        out_specs=VMEM,
        scratch_shapes=[
            pltpu.VMEM((n * parents, sides, 2 * rank), bf16),
            pltpu.SMEM((parents, many), jnp.int32),
            pltpu.VMEM((pairs, sides, 2 * rank), bf16),
            pltpu.VMEM((parents, sides, rank), bf16),
            pltpu.VMEM((parents - held, rank, many * rank), bf16),
            pltpu.SMEM((leaves,), jnp.int32),
            dma(3),
        ],
        compiler_params=params(12),
    )(parent_at, row, first, *keep(second, panel_counts), far, near, edge, transfer_in, basis_in)
    return out.T


def solution(mesh):
    leaves = ("gx", "gy")
    in_specs = (
        P(leaves, None),
        P(leaves),
        P(leaves, None, None),
        P(leaves, None, None),
        P(leaves, None, None, None),
        P(leaves, None),
        P(leaves, None, None, None),
        P(leaves, None, None, None),
        P(leaves, None),
    )
    return jax.shard_map(
        per_device, mesh=mesh, in_specs=in_specs, out_specs=P(leaves, None), check_vma=False
    )
```

```python
import functools

import jax
import jax.numpy as jnp
from jax import lax
from jax.experimental import pallas as pl
from jax.experimental.pallas import tpu as pltpu
from jax.sharding import PartitionSpec as P

VMEM = pl.BlockSpec(memory_space=pltpu.VMEM)
HBM = pl.BlockSpec(memory_space=pltpu.HBM)
NN = (((1,), (0,)), ((), ()))
NT = (((1,), (1,)), ((), ()))


def dot(a, b, dims):
    return lax.dot_general(a, b, dims, preferred_element_type=jnp.float32)


def left_half(sides, width):
    return lax.broadcasted_iota(jnp.int32, (sides, 2 * width), 1) < width


def pair_mask(counts_ref, pair, sides, width):
    lane = lax.broadcasted_iota(jnp.int32, (sides, 2 * width), 1)
    left = lane < width
    count = jnp.where(left, counts_ref[2 * pair], counts_ref[2 * pair + 1])
    return jnp.where(left, lane, lane - width) < count


def swap(pair, width):
    return jnp.concatenate([pair[:, width:], pair[:, :width]], axis=1)


def mod(x, m):
    return x & (m - 1) if m & (m - 1) == 0 else lax.rem(x, m)


def div(x, m):
    return x >> (m.bit_length() - 1) if m & (m - 1) == 0 else x // m


def position(axes):
    index = 0
    for axis in axes:
        index = index * lax.axis_size(axis) + lax.axis_index(axis)
    return index


def start_all(copies, sems):
    started = [pltpu.make_async_copy(src, dst, sems.at[i]) for i, (src, dst) in enumerate(copies)]
    for copy in started:
        copy.start()
    return started


def up_kernel(
    counts_hbm, charges_hbm, basis_hbm, transfer_hbm,
    rim_ref, live_ref, parents_ref,
    counts_ref, charges_ref, basis_ref, transfer_ref, sems,
):
    counts_in, charges_in, basis_in, transfer_in = start_all(
        [
            (counts_hbm, counts_ref), (charges_hbm, charges_ref),
            (basis_hbm, basis_ref), (transfer_hbm, transfer_ref),
        ],
        sems,
    )
    sides = charges_ref.shape[0]
    leaves, width, rank = basis_ref.shape
    pairs = leaves // 2
    own = pairs // 2
    left = left_half(sides, width)
    counts_in.wait()
    charges_in.wait()
    lives = []
    for a in range(pairs):
        charge = charges_ref[:, 2 * width * a : 2 * width * (a + 1)]
        live = jnp.where(pair_mask(counts_ref, a, sides, width), charge, jnp.zeros_like(charge))
        live_ref[a] = live
        lives.append(live)
    rim_ref[pairs] = lives[0]
    rim_ref[pairs + 1] = lives[-1]
    basis_in.wait()
    none = jnp.zeros_like(lives[0])
    coefs = []
    for a in range(pairs):
        live = lives[a]
        both = jnp.concatenate([jnp.where(left, live, none), jnp.where(left, none, live)], axis=0)
        coef = dot(both, basis_ref[2 * a : 2 * a + 2].reshape(2 * width, rank), NN)
        coef = jnp.concatenate([coef[:sides], coef[sides:]], axis=1).astype(jnp.bfloat16)
        rim_ref[a] = coef
        coefs.append(coef)
    transfer_in.wait()
    sums = [
        dot(coefs[a], transfer_ref[2 * a : 2 * a + 2].reshape(2 * rank, rank), NN)
        for a in range(pairs)
    ]
    for a in range(own):
        parents_ref[a] = jnp.concatenate(sums[2 * a : 2 * a + 2], axis=1).astype(jnp.bfloat16)


def copies_kernel(parents_ref, sent_hbm, sems):
    own = parents_ref.shape[0]
    copies = sent_hbm.shape[0] // own
    for copy in start_all([(parents_ref, sent_hbm.at[pl.ds(own * c, own)]) for c in range(copies)], sems):
        copy.wait()


def mid_kernel(
    axes, live_ref, coupling_hbm, near_hbm, parent_hbm, leaf_partners_hbm, parent_partners_hbm,
    packed_ref, parent_packed_ref, near_out_ref, rim_near_ref, leaf_at_ref, parent_at_ref,
    coupling_ref, near_ref, parent_ref, sems,
):
    leaves, many, rank, _ = coupling_ref.shape
    parents = parent_ref.shape[0]
    width = near_ref.shape[2]
    pairs = leaves // 2
    started = start_all(
        [(near_hbm, near_ref)]
        + [(parent_hbm.at[pl.ds(4 * i, 4)], parent_ref.at[pl.ds(4 * i, 4)]) for i in range(parents // 4)]
        + [(coupling_hbm.at[pl.ds(4 * i, 4)], coupling_ref.at[pl.ds(4 * i, 4)]) for i in range(leaves // 4)]
        + [(leaf_partners_hbm, leaf_at_ref), (parent_partners_hbm, parent_at_ref)],
        sems,
    )
    near_in = started[0]
    parent_in = started[1 : 1 + parents // 4]
    coupling_in = started[1 + parents // 4 : -2]
    near_in.wait()
    rim_near_ref[0] = near_ref[0, 0]
    rim_near_ref[1] = near_ref[leaves - 1, 2]
    for a in range(pairs):
        here = live_ref[a]
        even = dot(here, jnp.concatenate([near_ref[2 * a, 1], near_ref[2 * a, 2]], axis=1), NT)
        odd = dot(here, jnp.concatenate([near_ref[2 * a + 1, 0], near_ref[2 * a + 1, 1]], axis=1), NT)
        if a > 0:
            even = even + dot(live_ref[a - 1][:, width:], near_ref[2 * a, 0], NT)
        if a < pairs - 1:
            odd = odd + dot(live_ref[a + 1][:, :width], near_ref[2 * a + 1, 2], NT)
        near_out_ref[a] = jnp.concatenate([even, odd], axis=1)

    def pack(src, dst, g):
        for j in range(0, many, 2):
            dst[g, :, rank * j : rank * (j + 2)] = jnp.concatenate([src[g, j], src[g, j + 1]], axis=1)

    for i, copy in enumerate(parent_in):
        copy.wait()
        for q in range(4 * i, 4 * i + 4):
            pack(parent_ref, parent_packed_ref, q)
    for i, copy in enumerate(coupling_in):
        copy.wait()
        for g in range(4 * i, 4 * i + 4):
            pack(coupling_ref, packed_ref, g)
    for copy in started[-2:]:
        copy.wait()
    wanted = leaf_at_ref[...] + (1 - position(axes)) * leaves
    leaf_at_ref[...] = wanted ^ (lax.broadcasted_iota(jnp.int32, wanted.shape, 0) & 1)
    inner = lax.axis_size(axes[2])
    outer = lax.axis_size(axes[1])
    wanted = mod(parent_at_ref[...], outer * inner * parents)
    source = div(wanted, parents)
    wanted = (mod(source, inner) * outer + div(source, inner)) * parents + mod(wanted, parents)
    parent_at_ref[...] = wanted ^ (lax.broadcasted_iota(jnp.int32, wanted.shape, 1) & 1)


def halves_kernel(whole_ref, first_ref, second_ref):
    half = first_ref.shape[0]
    first_ref[...] = whole_ref[:half]
    second_ref[...] = whole_ref[half:]


def spread_pair(table_ref, at, pair, width):
    table_ref[at] = pair
    table_ref[at + 1] = swap(pair, width)


def picked(table_ref, rows, left):
    return jnp.concatenate(
        [
            jnp.where(left, table_ref[rows[j]], table_ref[rows[j + 1]])
            for j in range(0, len(rows), 2)
        ],
        axis=1,
    )


def leaf_kernel(
    axes, at_vmem, rim_ref, even_ref, odd_ref, packed_ref, rim_near_ref, transfer_hbm, basis_hbm,
    far_ref, edge_ref, transfer_ref, basis_packed_ref, table_ref, at_ref, basis_ref, sems,
):
    at_in, transfer_in, basis_in = start_all(
        [(at_vmem, at_ref), (transfer_hbm, transfer_ref), (basis_hbm, basis_ref)], sems
    )
    many, leaves = at_ref.shape
    rank = packed_ref.shape[1]
    width = rim_near_ref.shape[1]
    pairs = leaves // 2
    sides = rim_ref.shape[1]
    left = left_half(sides, rank)
    parity = lax.rem(position(axes), 2)
    for ref, base in (
        (rim_ref, leaves), (even_ref, 2 * leaves * (1 - parity)), (odd_ref, 2 * leaves * parity),
    ):
        for a in range(pairs):
            spread_pair(table_ref, base + 2 * a, ref[a], rank)
    before = jnp.where(parity == 1, even_ref[pairs + 1], odd_ref[pairs + 1])
    after = jnp.where(parity == 1, odd_ref[pairs], even_ref[pairs])
    low = dot(before[:, width:], rim_near_ref[0], NT)
    high = dot(after[:, :width], rim_near_ref[1], NT)
    edge_ref[0] = jnp.concatenate([low, jnp.zeros_like(low)], axis=1)
    edge_ref[1] = jnp.concatenate([jnp.zeros_like(high), high], axis=1)
    at_in.wait()
    for a in range(pairs):
        fars = []
        for g in (2 * a, 2 * a + 1):
            rows = [at_ref[j, g] for j in range(many)]
            fars.append(dot(picked(table_ref, rows, left), packed_ref[g], NT))
        far_ref[a] = jnp.concatenate(fars, axis=1)
    basis_in.wait()
    for a in range(pairs):
        basis_packed_ref[a] = jnp.concatenate([basis_ref[2 * a], basis_ref[2 * a + 1]], axis=1)
    transfer_in.wait()


def down_kernel(
    axis, at_vmem, same_ref, other_refs, packed_ref, counts_hbm,
    far_ref, near_ref, edge_ref, transfer_ref, basis_ref,
    out_ref, table_ref, at_ref, local_ref, down_ref, counts_ref, sems,
):
    at_in, counts_in = start_all([(at_vmem, at_ref), (counts_hbm, counts_ref)], sems)
    parents, many = at_ref.shape
    rank = packed_ref.shape[1]
    width = basis_ref.shape[1]
    sides = same_ref.shape[1]
    half = 2 * same_ref.shape[0]
    left = left_half(sides, rank)
    parity = lax.axis_index(axis)
    quarter = other_refs[0].shape[0]

    def spread(a, carry):
        for b, ref in enumerate(other_refs):
            spread_pair(table_ref, half * (1 - parity) + 2 * (quarter * b + a), ref[a], rank)
            spread_pair(table_ref, half * parity + 2 * (quarter * b + a), same_ref[quarter * b + a], rank)
        return carry

    lax.fori_loop(0, quarter, spread, 0, unroll=min(16, quarter))
    at_in.wait()
    for q in range(parents):
        rows = [at_ref[q, j] for j in range(many)]
        far = dot(picked(table_ref, rows, left), packed_ref[q], NT)
        down_ref[q] = far.astype(jnp.bfloat16)
    for q in range(parents):
        local = far_ref[q] + dot(down_ref[q], transfer_ref[2 * q : 2 * q + 2].reshape(2 * rank, rank), NT)
        local_ref[q] = local.astype(jnp.bfloat16)
    counts_in.wait()
    for q in range(parents):
        local = local_ref[q]
        none = jnp.zeros_like(local)
        both = jnp.concatenate([jnp.where(left, local, none), jnp.where(left, none, local)], axis=0)
        total = dot(both, basis_ref[q], NT)
        total = jnp.concatenate([total[:sides], total[sides:]], axis=1) + near_ref[q]
        if q == 0:
            total = total + edge_ref[0]
        if q == parents - 1:
            total = total + edge_ref[1]
        total = jnp.where(pair_mask(counts_ref, q, sides, width), total, jnp.zeros_like(total))
        out_ref[:, 2 * width * q : 2 * width * (q + 1)] = total.astype(out_ref.dtype)


def per_device(
    charges,
    panel_counts,
    basis,
    transfer,
    leaf_coupling,
    leaf_partners,
    near_blocks,
    parent_coupling,
    parent_partners,
):
    leaves, width, rank = basis.shape
    sides = charges.shape[1]
    parents, many = parent_partners.shape
    pairs = leaves // 2
    own = pairs // 2
    axes = ("gx", "gz", "gp")
    n = lax.axis_size("gz") * lax.axis_size("gp")
    total = n * lax.axis_size("gx")
    bf16, f32 = jnp.bfloat16, jnp.float32
    keep = lambda *arrays: [pltpu.with_memory_space_constraint(a, pltpu.HBM) for a in arrays]
    shape = pltpu.VMEM
    dma = lambda count: pltpu.SemaphoreType.DMA((count,))
    params = lambda mib: pltpu.CompilerParams(vmem_limit_bytes=mib * 2**20)

    rim, live, parent_coef = pl.pallas_call(
        up_kernel,
        name="up",
        out_shape=[
            shape((pairs + 2, sides, 2 * rank), bf16),
            shape((pairs, sides, 2 * width), bf16),
            shape((own, sides, 2 * rank), bf16),
        ],
        in_specs=[HBM] * 4,
        out_specs=[VMEM] * 3,
        scratch_shapes=[
            pltpu.SMEM((leaves,), jnp.int32),
            pltpu.VMEM((sides, leaves * width), bf16),
            pltpu.VMEM((leaves, width, rank), bf16),
            pltpu.VMEM((leaves, rank, rank), bf16),
            dma(4),
        ],
        compiler_params=params(8),
    )(*keep(panel_counts, charges.T, basis, transfer))

    even = lax.ppermute(rim, axes, [(i, i ^ 1) for i in range(total)])
    steps = [(i, i + 1) for i in range(1, total - 1, 2)]
    odd = lax.ppermute(rim, axes, steps + [(b, a) for a, b in steps])
    sent = pl.pallas_call(
        copies_kernel,
        name="copies",
        out_shape=pltpu.HBM((n // 2 * own, sides, 2 * rank), bf16),
        in_specs=[VMEM],
        out_specs=HBM,
        scratch_shapes=[dma(n // 2)],
        compiler_params=params(4),
    )(parent_coef)
    same = lax.all_to_all(sent, "gz", 0, 0, tiled=True)
    quarter = shape((n // 4 * own, sides, 2 * rank), bf16)
    pieces = pl.pallas_call(
        halves_kernel,
        name="halves",
        out_shape=[quarter, quarter],
        in_specs=[VMEM],
        out_specs=[VMEM, VMEM],
        compiler_params=params(4),
    )(same)
    other = [lax.ppermute(piece, "gp", [(0, 1), (1, 0)]) for piece in pieces]

    packed, parent_packed, near, rim_near, leaf_at, parent_at = pl.pallas_call(
        functools.partial(mid_kernel, axes),
        name="mid",
        out_shape=[
            shape((leaves, rank, many * rank), bf16),
            shape((parents, rank, many * rank), bf16),
            shape((pairs, sides, 2 * width), f32),
            shape((2, width, width), bf16),
            shape((many, leaves), jnp.int32),
            shape((parents, many), jnp.int32),
        ],
        in_specs=[VMEM] + [HBM] * 5,
        out_specs=[VMEM] * 6,
        scratch_shapes=[
            pltpu.VMEM(leaf_coupling.shape, bf16),
            pltpu.VMEM(near_blocks.shape, bf16),
            pltpu.VMEM(parent_coupling.shape, bf16),
            dma(3 + leaves // 4 + parents // 4),
        ],
        compiler_params=params(20),
    )(live, *keep(leaf_coupling, near_blocks, parent_coupling, leaf_partners.T, parent_partners))

    far, edge, transfer_in, basis_in = pl.pallas_call(
        functools.partial(leaf_kernel, axes),
        name="leaf",
        out_shape=[
            shape((pairs, sides, 2 * rank), f32),
            shape((2, sides, 2 * width), f32),
            shape(transfer.shape, bf16),
            shape((pairs, width, 2 * rank), bf16),
        ],
        in_specs=[VMEM] * 6 + [HBM] * 2,
        out_specs=[VMEM] * 4,
        scratch_shapes=[
            pltpu.VMEM((3 * leaves, sides, 2 * rank), bf16),
            pltpu.SMEM((many, leaves), jnp.int32),
            pltpu.VMEM(basis.shape, bf16),
            dma(3),
        ],
        compiler_params=params(8),
    )(leaf_at, rim, even, odd, packed, rim_near, *keep(transfer, basis))

    out = pl.pallas_call(
        functools.partial(down_kernel, "gp"),
        name="down",
        out_shape=jax.ShapeDtypeStruct((sides, leaves * width), bf16),
        in_specs=[VMEM, VMEM, [VMEM] * 2, VMEM, HBM] + [VMEM] * 5,
        out_specs=VMEM,
        scratch_shapes=[
            pltpu.VMEM((n * parents, sides, 2 * rank), bf16),
            pltpu.SMEM((parents, many), jnp.int32),
            pltpu.VMEM((pairs, sides, 2 * rank), bf16),
            pltpu.VMEM((parents, sides, rank), bf16),
            pltpu.SMEM((leaves,), jnp.int32),
            dma(2),
        ],
        compiler_params=params(12),
    )(parent_at, same, other, parent_packed, *keep(panel_counts), far, near, edge, transfer_in, basis_in)
    return out.T


def solution(mesh):
    outer, inner = mesh.devices.shape
    split = jax.sharding.Mesh(mesh.devices.reshape(outer, inner // 2, 2), ("gx", "gz", "gp"))
    leaves = ("gx", "gz", "gp")
    in_specs = (
        P(leaves, None),
        P(leaves),
        P(leaves, None, None),
        P(leaves, None, None),
        P(leaves, None, None, None),
        P(leaves, None),
        P(leaves, None, None, None),
        P(leaves, None, None, None),
        P(leaves, None),
    )
    return jax.shard_map(
        per_device, mesh=split, in_specs=in_specs, out_specs=P(leaves, None), check_vma=False
    )
```

```python
import functools

import jax
import jax.numpy as jnp
from jax import lax
from jax.experimental import pallas as pl
from jax.experimental.pallas import tpu as pltpu
from jax.sharding import PartitionSpec as P

VMEM = pl.BlockSpec(memory_space=pltpu.VMEM)
HBM = pl.BlockSpec(memory_space=pltpu.HBM)
NN = (((1,), (0,)), ((), ()))
NT = (((1,), (1,)), ((), ()))


def dot(a, b, dims):
    return lax.dot_general(a, b, dims, preferred_element_type=jnp.float32)


def left_half(sides, width):
    return lax.broadcasted_iota(jnp.int32, (sides, 2 * width), 1) < width


def pair_mask(counts_ref, pair, sides, width):
    lane = lax.broadcasted_iota(jnp.int32, (sides, 2 * width), 1)
    left = lane < width
    count = jnp.where(left, counts_ref[2 * pair], counts_ref[2 * pair + 1])
    return jnp.where(left, lane, lane - width) < count


def swap(pair, width):
    return jnp.concatenate([pair[:, width:], pair[:, :width]], axis=1)


def mod(x, m):
    return x & (m - 1) if m & (m - 1) == 0 else lax.rem(x, m)


def div(x, m):
    return x >> (m.bit_length() - 1) if m & (m - 1) == 0 else x // m


def position(axes):
    index = 0
    for axis in axes:
        index = index * lax.axis_size(axis) + lax.axis_index(axis)
    return index


def start_all(copies, sems):
    started = [pltpu.make_async_copy(src, dst, sems.at[i]) for i, (src, dst) in enumerate(copies)]
    for copy in started:
        copy.start()
    return started


def up_kernel(
    counts_hbm, charges_hbm, basis_hbm, transfer_hbm,
    rim_ref, live_ref, parents_ref,
    counts_ref, charges_ref, basis_ref, transfer_ref, sems,
):
    counts_in, charges_in, basis_in, transfer_in = start_all(
        [
            (counts_hbm, counts_ref), (charges_hbm, charges_ref),
            (basis_hbm, basis_ref), (transfer_hbm, transfer_ref),
        ],
        sems,
    )
    sides = charges_ref.shape[0]
    leaves, width, rank = basis_ref.shape
    pairs = leaves // 2
    own = pairs // 2
    left = left_half(sides, width)
    counts_in.wait()
    charges_in.wait()
    lives = []
    for a in range(pairs):
        charge = charges_ref[:, 2 * width * a : 2 * width * (a + 1)]
        live = jnp.where(pair_mask(counts_ref, a, sides, width), charge, jnp.zeros_like(charge))
        live_ref[a] = live
        lives.append(live)
    rim_ref[pairs] = lives[0]
    rim_ref[pairs + 1] = lives[-1]
    basis_in.wait()
    none = jnp.zeros_like(lives[0])
    coefs = []
    for a in range(pairs):
        live = lives[a]
        both = jnp.concatenate([jnp.where(left, live, none), jnp.where(left, none, live)], axis=0)
        coef = dot(both, basis_ref[2 * a : 2 * a + 2].reshape(2 * width, rank), NN)
        coef = jnp.concatenate([coef[:sides], coef[sides:]], axis=1).astype(jnp.bfloat16)
        rim_ref[a] = coef
        coefs.append(coef)
    transfer_in.wait()
    sums = [
        dot(coefs[a], transfer_ref[2 * a : 2 * a + 2].reshape(2 * rank, rank), NN)
        for a in range(pairs)
    ]
    for a in range(own):
        parents_ref[a] = jnp.concatenate(sums[2 * a : 2 * a + 2], axis=1).astype(jnp.bfloat16)


def copies_kernel(parents_ref, sent_hbm, sems):
    own = parents_ref.shape[0]
    copies = sent_hbm.shape[0] // own
    for copy in start_all([(parents_ref, sent_hbm.at[pl.ds(own * c, own)]) for c in range(copies)], sems):
        copy.wait()


def side_by_side(blocks_ref, g):
    return jnp.concatenate([blocks_ref[g, j] for j in range(blocks_ref.shape[1])], axis=1)


def mid_kernel(
    axes, live_ref, near_hbm, parent_hbm, leaf_partners_hbm, parent_partners_hbm,
    parent_packed_ref, near_out_ref, rim_near_ref, leaf_at_ref, parent_at_ref,
    near_ref, parent_ref, sems,
):
    parents, many, rank, _ = parent_ref.shape
    leaves = near_ref.shape[0]
    width = near_ref.shape[2]
    pairs = leaves // 2
    started = start_all(
        [(near_hbm, near_ref)]
        + [(parent_hbm.at[pl.ds(4 * i, 4)], parent_ref.at[pl.ds(4 * i, 4)]) for i in range(parents // 4)]
        + [(leaf_partners_hbm, leaf_at_ref), (parent_partners_hbm, parent_at_ref)],
        sems,
    )
    near_in = started[0]
    parent_in = started[1:-2]
    near_in.wait()
    rim_near_ref[0] = near_ref[0, 0]
    rim_near_ref[1] = near_ref[leaves - 1, 2]
    for a in range(pairs):
        here = live_ref[a]
        even = dot(here, jnp.concatenate([near_ref[2 * a, 1], near_ref[2 * a, 2]], axis=1), NT)
        odd = dot(here, jnp.concatenate([near_ref[2 * a + 1, 0], near_ref[2 * a + 1, 1]], axis=1), NT)
        if a > 0:
            even = even + dot(live_ref[a - 1][:, width:], near_ref[2 * a, 0], NT)
        if a < pairs - 1:
            odd = odd + dot(live_ref[a + 1][:, :width], near_ref[2 * a + 1, 2], NT)
        near_out_ref[a] = jnp.concatenate([even, odd], axis=1)

    for i, copy in enumerate(parent_in):
        copy.wait()
        for q in range(4 * i, 4 * i + 4):
            parent_packed_ref[q] = side_by_side(parent_ref, q)
    for copy in started[-2:]:
        copy.wait()
    wanted = leaf_at_ref[...] + (1 - position(axes)) * leaves
    leaf_at_ref[...] = wanted ^ (lax.broadcasted_iota(jnp.int32, wanted.shape, 0) & 1)
    inner = lax.axis_size(axes[2])
    outer = lax.axis_size(axes[1])
    wanted = mod(parent_at_ref[...], outer * inner * parents)
    source = div(wanted, parents)
    wanted = (mod(source, inner) * outer + div(source, inner)) * parents + mod(wanted, parents)
    parent_at_ref[...] = wanted ^ (lax.broadcasted_iota(jnp.int32, wanted.shape, 1) & 1)


def halves_kernel(whole_ref, at_ref, first_ref, second_ref):
    del at_ref
    half = first_ref.shape[0]
    first_ref[...] = whole_ref[:half]
    second_ref[...] = whole_ref[half:]


def spread_pair(table_ref, at, pair, width):
    table_ref[at] = pair
    table_ref[at + 1] = swap(pair, width)


def picked(table_ref, rows, left):
    return jnp.concatenate(
        [
            jnp.where(left, table_ref[rows[j]], table_ref[rows[j + 1]])
            for j in range(0, len(rows), 2)
        ],
        axis=1,
    )


def leaf_kernel(
    axes, at_vmem, rim_ref, even_ref, odd_ref, rim_near_ref, coupling_hbm, transfer_hbm, basis_hbm,
    far_ref, edge_ref, transfer_ref, basis_packed_ref, table_ref, at_ref, coupling_ref, basis_ref, sems,
):
    leaves, many, rank, _ = coupling_ref.shape
    at_in, *coupling_in, transfer_in, basis_in = start_all(
        [(at_vmem, at_ref)]
        + [(coupling_hbm.at[pl.ds(2 * i, 2)], coupling_ref.at[pl.ds(2 * i, 2)]) for i in range(leaves // 2)]
        + [(transfer_hbm, transfer_ref), (basis_hbm, basis_ref)],
        sems,
    )
    width = rim_near_ref.shape[1]
    pairs = leaves // 2
    sides = rim_ref.shape[1]
    left = left_half(sides, rank)
    parity = lax.rem(position(axes), 2)
    for ref, base in (
        (rim_ref, leaves), (even_ref, 2 * leaves * (1 - parity)), (odd_ref, 2 * leaves * parity),
    ):
        for a in range(pairs):
            spread_pair(table_ref, base + 2 * a, ref[a], rank)
    before = jnp.where(parity == 1, even_ref[pairs + 1], odd_ref[pairs + 1])
    after = jnp.where(parity == 1, odd_ref[pairs], even_ref[pairs])
    low = dot(before[:, width:], rim_near_ref[0], NT)
    high = dot(after[:, :width], rim_near_ref[1], NT)
    edge_ref[0] = jnp.concatenate([low, jnp.zeros_like(low)], axis=1)
    edge_ref[1] = jnp.concatenate([jnp.zeros_like(high), high], axis=1)
    at_in.wait()
    for a in range(pairs):
        fars = []
        coupling_in[a].wait()
        for g in (2 * a, 2 * a + 1):
            rows = [at_ref[j, g] for j in range(many)]
            fars.append(dot(picked(table_ref, rows, left), side_by_side(coupling_ref, g), NT))
        far_ref[a] = jnp.concatenate(fars, axis=1)
    basis_in.wait()
    for a in range(pairs):
        basis_packed_ref[a] = jnp.concatenate([basis_ref[2 * a], basis_ref[2 * a + 1]], axis=1)
    transfer_in.wait()


def down_kernel(
    axis, at_vmem, same_ref, other_refs, packed_ref, counts_hbm,
    far_ref, near_ref, edge_ref, transfer_ref, basis_ref,
    out_ref, table_ref, at_ref, local_ref, down_ref, counts_ref, sems,
):
    at_in, counts_in = start_all([(at_vmem, at_ref), (counts_hbm, counts_ref)], sems)
    parents, many = at_ref.shape
    rank = packed_ref.shape[1]
    width = basis_ref.shape[1]
    sides = same_ref.shape[1]
    half = 2 * same_ref.shape[0]
    left = left_half(sides, rank)
    parity = lax.axis_index(axis)
    quarter = other_refs[0].shape[0]

    def spread(a, carry):
        for b, ref in enumerate(other_refs):
            spread_pair(table_ref, half * (1 - parity) + 2 * (quarter * b + a), ref[a], rank)
            spread_pair(table_ref, half * parity + 2 * (quarter * b + a), same_ref[quarter * b + a], rank)
        return carry

    lax.fori_loop(0, quarter, spread, 0, unroll=min(16, quarter))
    at_in.wait()
    for q in range(parents):
        rows = [at_ref[q, j] for j in range(many)]
        far = dot(picked(table_ref, rows, left), packed_ref[q], NT)
        down_ref[q] = far.astype(jnp.bfloat16)
    for q in range(parents):
        local = far_ref[q] + dot(down_ref[q], transfer_ref[2 * q : 2 * q + 2].reshape(2 * rank, rank), NT)
        local_ref[q] = local.astype(jnp.bfloat16)
    counts_in.wait()
    for q in range(parents):
        local = local_ref[q]
        none = jnp.zeros_like(local)
        both = jnp.concatenate([jnp.where(left, local, none), jnp.where(left, none, local)], axis=0)
        total = dot(both, basis_ref[q], NT)
        total = jnp.concatenate([total[:sides], total[sides:]], axis=1) + near_ref[q]
        if q == 0:
            total = total + edge_ref[0]
        if q == parents - 1:
            total = total + edge_ref[1]
        total = jnp.where(pair_mask(counts_ref, q, sides, width), total, jnp.zeros_like(total))
        out_ref[:, 2 * width * q : 2 * width * (q + 1)] = total.astype(out_ref.dtype)


def per_device(
    charges,
    panel_counts,
    basis,
    transfer,
    leaf_coupling,
    leaf_partners,
    near_blocks,
    parent_coupling,
    parent_partners,
):
    leaves, width, rank = basis.shape
    sides = charges.shape[1]
    parents, many = parent_partners.shape
    pairs = leaves // 2
    own = pairs // 2
    axes = ("gx", "gz", "gp")
    n = lax.axis_size("gz") * lax.axis_size("gp")
    total = n * lax.axis_size("gx")
    bf16, f32 = jnp.bfloat16, jnp.float32
    keep = lambda *arrays: [pltpu.with_memory_space_constraint(a, pltpu.HBM) for a in arrays]
    shape = pltpu.VMEM
    dma = lambda count: pltpu.SemaphoreType.DMA((count,))
    params = lambda mib: pltpu.CompilerParams(vmem_limit_bytes=mib * 2**20)

    rim, live, parent_coef = pl.pallas_call(
        up_kernel,
        name="up",
        out_shape=[
            shape((pairs + 2, sides, 2 * rank), bf16),
            shape((pairs, sides, 2 * width), bf16),
            shape((own, sides, 2 * rank), bf16),
        ],
        in_specs=[HBM] * 4,
        out_specs=[VMEM] * 3,
        scratch_shapes=[
            pltpu.SMEM((leaves,), jnp.int32),
            pltpu.VMEM((sides, leaves * width), bf16),
            pltpu.VMEM((leaves, width, rank), bf16),
            pltpu.VMEM((leaves, rank, rank), bf16),
            dma(4),
        ],
        compiler_params=params(8),
    )(*keep(panel_counts, charges.T, basis, transfer))

    even = lax.ppermute(rim, axes, [(i, i ^ 1) for i in range(total)])
    steps = [(i, i + 1) for i in range(1, total - 1, 2)]
    odd = lax.ppermute(rim, axes, steps + [(b, a) for a, b in steps])
    sent = pl.pallas_call(
        copies_kernel,
        name="copies",
        out_shape=pltpu.HBM((n // 2 * own, sides, 2 * rank), bf16),
        in_specs=[VMEM],
        out_specs=HBM,
        scratch_shapes=[dma(n // 2)],
        compiler_params=params(4),
    )(parent_coef)
    same = lax.all_to_all(sent, "gz", 0, 0, tiled=True)

    parent_packed, near, rim_near, leaf_at, parent_at = pl.pallas_call(
        functools.partial(mid_kernel, axes),
        name="mid",
        out_shape=[
            shape((parents, rank, many * rank), bf16),
            shape((pairs, sides, 2 * width), f32),
            shape((2, width, width), bf16),
            shape((many, leaves), jnp.int32),
            shape((parents, many), jnp.int32),
        ],
        in_specs=[VMEM] + [HBM] * 4,
        out_specs=[VMEM] * 5,
        scratch_shapes=[
            pltpu.VMEM(near_blocks.shape, bf16),
            pltpu.VMEM(parent_coupling.shape, bf16),
            dma(3 + parents // 4),
        ],
        compiler_params=params(12),
    )(live, *keep(near_blocks, parent_coupling, leaf_partners.T, parent_partners))

    quarter = shape((n // 4 * own, sides, 2 * rank), bf16)
    pieces = pl.pallas_call(
        halves_kernel,
        name="halves",
        out_shape=[quarter, quarter],
        in_specs=[VMEM, VMEM],
        out_specs=[VMEM, VMEM],
        compiler_params=params(4),
    )(same, parent_at)
    other = [lax.ppermute(piece, "gp", [(0, 1), (1, 0)]) for piece in pieces]

    far, edge, transfer_in, basis_in = pl.pallas_call(
        functools.partial(leaf_kernel, axes),
        name="leaf",
        out_shape=[
            shape((pairs, sides, 2 * rank), f32),
            shape((2, sides, 2 * width), f32),
            shape(transfer.shape, bf16),
            shape((pairs, width, 2 * rank), bf16),
        ],
        in_specs=[VMEM] * 5 + [HBM] * 3,
        out_specs=[VMEM] * 4,
        scratch_shapes=[
            pltpu.VMEM((3 * leaves, sides, 2 * rank), bf16),
            pltpu.SMEM((many, leaves), jnp.int32),
            pltpu.VMEM(leaf_coupling.shape, bf16),
            pltpu.VMEM(basis.shape, bf16),
            dma(3 + leaves // 2),
        ],
        compiler_params=params(16),
    )(leaf_at, rim, even, odd, rim_near, *keep(leaf_coupling, transfer, basis))

    out = pl.pallas_call(
        functools.partial(down_kernel, "gp"),
        name="down",
        out_shape=jax.ShapeDtypeStruct((sides, leaves * width), bf16),
        in_specs=[VMEM, VMEM, [VMEM] * 2, VMEM, HBM] + [VMEM] * 5,
        out_specs=VMEM,
        scratch_shapes=[
            pltpu.VMEM((n * parents, sides, 2 * rank), bf16),
            pltpu.SMEM((parents, many), jnp.int32),
            pltpu.VMEM((pairs, sides, 2 * rank), bf16),
            pltpu.VMEM((parents, sides, rank), bf16),
            pltpu.SMEM((leaves,), jnp.int32),
            dma(2),
        ],
        compiler_params=params(12),
    )(parent_at, same, other, parent_packed, *keep(panel_counts), far, near, edge, transfer_in, basis_in)
    return out.T


def solution(mesh):
    outer, inner = mesh.devices.shape
    split = jax.sharding.Mesh(mesh.devices.reshape(outer, inner // 2, 2), ("gx", "gz", "gp"))
    leaves = ("gx", "gz", "gp")
    in_specs = (
        P(leaves, None),
        P(leaves),
        P(leaves, None, None),
        P(leaves, None, None),
        P(leaves, None, None, None),
        P(leaves, None),
        P(leaves, None, None, None),
        P(leaves, None, None, None),
        P(leaves, None),
    )
    return jax.shard_map(
        per_device, mesh=split, in_specs=in_specs, out_specs=P(leaves, None), check_vma=False
    )
```

```python
import functools

import jax
import jax.numpy as jnp
from jax import lax
from jax.experimental import pallas as pl
from jax.experimental.pallas import tpu as pltpu
from jax.sharding import PartitionSpec as P

VMEM = pl.BlockSpec(memory_space=pltpu.VMEM)
HBM = pl.BlockSpec(memory_space=pltpu.HBM)
NN = (((1,), (0,)), ((), ()))
NT = (((1,), (1,)), ((), ()))


def dot(a, b, dims):
    return lax.dot_general(a, b, dims, preferred_element_type=jnp.float32)


def left_half(sides, width):
    return lax.broadcasted_iota(jnp.int32, (sides, 2 * width), 1) < width


def pair_mask(counts_ref, pair, sides, width):
    lane = lax.broadcasted_iota(jnp.int32, (sides, 2 * width), 1)
    left = lane < width
    count = jnp.where(left, counts_ref[2 * pair], counts_ref[2 * pair + 1])
    return jnp.where(left, lane, lane - width) < count


def swap(pair, width):
    return jnp.concatenate([pair[:, width:], pair[:, :width]], axis=1)


def mod(x, m):
    return x & (m - 1) if m & (m - 1) == 0 else lax.rem(x, m)


def div(x, m):
    return x >> (m.bit_length() - 1) if m & (m - 1) == 0 else x // m


def position(axes):
    index = 0
    for axis in axes:
        index = index * lax.axis_size(axis) + lax.axis_index(axis)
    return index


def start_all(copies, sems):
    started = [pltpu.make_async_copy(src, dst, sems.at[i]) for i, (src, dst) in enumerate(copies)]
    for copy in started:
        copy.start()
    return started


def up_kernel(
    counts_hbm, charges_hbm, basis_hbm, transfer_hbm,
    rim_ref, live_ref, parents_ref,
    counts_ref, charges_ref, basis_ref, transfer_ref, sems,
):
    counts_in, charges_in, basis_in, transfer_in = start_all(
        [
            (counts_hbm, counts_ref), (charges_hbm, charges_ref),
            (basis_hbm, basis_ref), (transfer_hbm, transfer_ref),
        ],
        sems,
    )
    sides = charges_ref.shape[0]
    leaves, width, rank = basis_ref.shape
    pairs = leaves // 2
    own = pairs // 2
    left = left_half(sides, width)
    counts_in.wait()
    charges_in.wait()
    lives = []
    for a in range(pairs):
        charge = charges_ref[:, 2 * width * a : 2 * width * (a + 1)]
        live = jnp.where(pair_mask(counts_ref, a, sides, width), charge, jnp.zeros_like(charge))
        live_ref[a] = live
        lives.append(live)
    rim_ref[pairs] = lives[0]
    rim_ref[pairs + 1] = lives[-1]
    basis_in.wait()
    none = jnp.zeros_like(lives[0])
    coefs = []
    for a in range(pairs):
        live = lives[a]
        both = jnp.concatenate([jnp.where(left, live, none), jnp.where(left, none, live)], axis=0)
        coef = dot(both, basis_ref[2 * a : 2 * a + 2].reshape(2 * width, rank), NN)
        coef = jnp.concatenate([coef[:sides], coef[sides:]], axis=1).astype(jnp.bfloat16)
        rim_ref[a] = coef
        coefs.append(coef)
    transfer_in.wait()
    sums = [
        dot(coefs[a], transfer_ref[2 * a : 2 * a + 2].reshape(2 * rank, rank), NN)
        for a in range(pairs)
    ]
    for a in range(own):
        parents_ref[a] = jnp.concatenate(sums[2 * a : 2 * a + 2], axis=1).astype(jnp.bfloat16)


def copies_kernel(parents_ref, sent_hbm, sems):
    own = parents_ref.shape[0]
    copies = sent_hbm.shape[0] // own
    for copy in start_all([(parents_ref, sent_hbm.at[pl.ds(own * c, own)]) for c in range(copies)], sems):
        copy.wait()


def side_by_side(blocks_ref, g):
    return jnp.concatenate([blocks_ref[g, j] for j in range(blocks_ref.shape[1])], axis=1)


def mid_kernel(
    axes, live_ref, near_hbm, parent_hbm, leaf_partners_hbm, parent_partners_hbm,
    parent_packed_ref, near_out_ref, rim_near_ref, leaf_at_ref, parent_at_ref,
    near_ref, parent_ref, sems,
):
    parents, many, rank, _ = parent_ref.shape
    leaves = near_ref.shape[0]
    width = near_ref.shape[2]
    pairs = leaves // 2
    started = start_all(
        [(near_hbm, near_ref)]
        + [(parent_hbm.at[pl.ds(4 * i, 4)], parent_ref.at[pl.ds(4 * i, 4)]) for i in range(parents // 4)]
        + [(leaf_partners_hbm, leaf_at_ref), (parent_partners_hbm, parent_at_ref)],
        sems,
    )
    near_in = started[0]
    parent_in = started[1:-2]
    near_in.wait()
    rim_near_ref[0] = near_ref[0, 0]
    rim_near_ref[1] = near_ref[leaves - 1, 2]
    for a in range(pairs):
        here = live_ref[a]
        even = dot(here, jnp.concatenate([near_ref[2 * a, 1], near_ref[2 * a, 2]], axis=1), NT)
        odd = dot(here, jnp.concatenate([near_ref[2 * a + 1, 0], near_ref[2 * a + 1, 1]], axis=1), NT)
        if a > 0:
            even = even + dot(live_ref[a - 1][:, width:], near_ref[2 * a, 0], NT)
        if a < pairs - 1:
            odd = odd + dot(live_ref[a + 1][:, :width], near_ref[2 * a + 1, 2], NT)
        near_out_ref[a] = jnp.concatenate([even, odd], axis=1)

    for i, copy in enumerate(parent_in):
        copy.wait()
        for q in range(4 * i, 4 * i + 4):
            parent_packed_ref[q] = side_by_side(parent_ref, q)
    for copy in started[-2:]:
        copy.wait()
    leaf_at_ref[...] = leaf_at_ref[...] + (1 - position(axes)) * leaves
    inner = lax.axis_size(axes[2])
    outer = lax.axis_size(axes[1])
    wanted = mod(parent_at_ref[...], outer * inner * parents)
    source = div(wanted, parents)
    wanted = (mod(source, inner) * outer + div(source, inner)) * parents + mod(wanted, parents)
    parent_at_ref[...] = wanted ^ (lax.broadcasted_iota(jnp.int32, wanted.shape, 1) & 1)


def halves_kernel(whole_ref, at_ref, first_ref, second_ref):
    del at_ref
    half = first_ref.shape[0]
    first_ref[...] = whole_ref[:half]
    second_ref[...] = whole_ref[half:]


def spread_pair(table_ref, at, pair, width):
    table_ref[at] = pair
    table_ref[at + 1] = swap(pair, width)


def picked(table_ref, rows, left):
    return jnp.concatenate(
        [
            jnp.where(left, table_ref[rows[j]], table_ref[rows[j + 1]])
            for j in range(0, len(rows), 2)
        ],
        axis=1,
    )


def leaf_kernel(
    axes, at_vmem, rim_ref, even_ref, odd_ref, rim_near_ref, coupling_hbm, transfer_hbm, basis_hbm,
    far_ref, edge_ref, transfer_ref, basis_packed_ref, table_ref, at_ref, coupling_ref, basis_ref, sems,
):
    leaves, many, rank, _ = coupling_ref.shape
    at_in, *coupling_in, transfer_in, basis_in = start_all(
        [(at_vmem, at_ref)]
        + [(coupling_hbm.at[pl.ds(2 * i, 2)], coupling_ref.at[pl.ds(2 * i, 2)]) for i in range(leaves // 2)]
        + [(transfer_hbm, transfer_ref), (basis_hbm, basis_ref)],
        sems,
    )
    width = rim_near_ref.shape[1]
    pairs = leaves // 2
    sides = rim_ref.shape[1]
    parity = lax.rem(position(axes), 2)
    for ref, base in (
        (rim_ref, leaves), (even_ref, 2 * leaves * (1 - parity)), (odd_ref, 2 * leaves * parity),
    ):
        for a in range(pairs):
            spread_pair(table_ref, base + 2 * a, ref[a], rank)
    before = jnp.where(parity == 1, even_ref[pairs + 1], odd_ref[pairs + 1])
    after = jnp.where(parity == 1, odd_ref[pairs], even_ref[pairs])
    low = dot(before[:, width:], rim_near_ref[0], NT)
    high = dot(after[:, :width], rim_near_ref[1], NT)
    edge_ref[0] = jnp.concatenate([low, jnp.zeros_like(low)], axis=1)
    edge_ref[1] = jnp.concatenate([jnp.zeros_like(high), high], axis=1)
    at_in.wait()
    for a in range(pairs):
        fars = []
        coupling_in[a].wait()
        for g in (2 * a, 2 * a + 1):
            far = jnp.zeros((sides, rank), jnp.float32)
            for j in range(many):
                far = far + dot(table_ref[at_ref[j, g], :, :rank], coupling_ref[g, j], NT)
            fars.append(far)
        far_ref[a] = jnp.concatenate(fars, axis=1)
    basis_in.wait()
    for a in range(pairs):
        basis_packed_ref[a] = jnp.concatenate([basis_ref[2 * a], basis_ref[2 * a + 1]], axis=1)
    transfer_in.wait()


def down_kernel(
    axis, at_vmem, same_ref, other_refs, packed_ref, counts_hbm,
    far_ref, near_ref, edge_ref, transfer_ref, basis_ref,
    out_ref, table_ref, at_ref, local_ref, down_ref, counts_ref, sems,
):
    at_in, counts_in = start_all([(at_vmem, at_ref), (counts_hbm, counts_ref)], sems)
    parents, many = at_ref.shape
    rank = packed_ref.shape[1]
    width = basis_ref.shape[1]
    sides = same_ref.shape[1]
    half = 2 * same_ref.shape[0]
    left = left_half(sides, rank)
    parity = lax.axis_index(axis)
    quarter = other_refs[0].shape[0]

    def spread(a, carry):
        for b, ref in enumerate(other_refs):
            spread_pair(table_ref, half * (1 - parity) + 2 * (quarter * b + a), ref[a], rank)
            spread_pair(table_ref, half * parity + 2 * (quarter * b + a), same_ref[quarter * b + a], rank)
        return carry

    lax.fori_loop(0, quarter, spread, 0, unroll=min(16, quarter))
    at_in.wait()
    for q in range(parents):
        rows = [at_ref[q, j] for j in range(many)]
        far = dot(picked(table_ref, rows, left), packed_ref[q], NT)
        down_ref[q] = far.astype(jnp.bfloat16)
    for q in range(parents):
        local = far_ref[q] + dot(down_ref[q], transfer_ref[2 * q : 2 * q + 2].reshape(2 * rank, rank), NT)
        local_ref[q] = local.astype(jnp.bfloat16)
    counts_in.wait()
    for q in range(parents):
        local = local_ref[q]
        none = jnp.zeros_like(local)
        both = jnp.concatenate([jnp.where(left, local, none), jnp.where(left, none, local)], axis=0)
        total = dot(both, basis_ref[q], NT)
        total = jnp.concatenate([total[:sides], total[sides:]], axis=1) + near_ref[q]
        if q == 0:
            total = total + edge_ref[0]
        if q == parents - 1:
            total = total + edge_ref[1]
        total = jnp.where(pair_mask(counts_ref, q, sides, width), total, jnp.zeros_like(total))
        out_ref[:, 2 * width * q : 2 * width * (q + 1)] = total.astype(out_ref.dtype)


def per_device(
    charges,
    panel_counts,
    basis,
    transfer,
    leaf_coupling,
    leaf_partners,
    near_blocks,
    parent_coupling,
    parent_partners,
):
    leaves, width, rank = basis.shape
    sides = charges.shape[1]
    parents, many = parent_partners.shape
    pairs = leaves // 2
    own = pairs // 2
    axes = ("gx", "gz", "gp")
    n = lax.axis_size("gz") * lax.axis_size("gp")
    total = n * lax.axis_size("gx")
    bf16, f32 = jnp.bfloat16, jnp.float32
    keep = lambda *arrays: [pltpu.with_memory_space_constraint(a, pltpu.HBM) for a in arrays]
    shape = pltpu.VMEM
    dma = lambda count: pltpu.SemaphoreType.DMA((count,))
    params = lambda mib: pltpu.CompilerParams(vmem_limit_bytes=mib * 2**20)

    rim, live, parent_coef = pl.pallas_call(
        up_kernel,
        name="up",
        out_shape=[
            shape((pairs + 2, sides, 2 * rank), bf16),
            shape((pairs, sides, 2 * width), bf16),
            shape((own, sides, 2 * rank), bf16),
        ],
        in_specs=[HBM] * 4,
        out_specs=[VMEM] * 3,
        scratch_shapes=[
            pltpu.SMEM((leaves,), jnp.int32),
            pltpu.VMEM((sides, leaves * width), bf16),
            pltpu.VMEM((leaves, width, rank), bf16),
            pltpu.VMEM((leaves, rank, rank), bf16),
            dma(4),
        ],
        compiler_params=params(8),
    )(*keep(panel_counts, charges.T, basis, transfer))

    even = lax.ppermute(rim, axes, [(i, i ^ 1) for i in range(total)])
    steps = [(i, i + 1) for i in range(1, total - 1, 2)]
    odd = lax.ppermute(rim, axes, steps + [(b, a) for a, b in steps])
    sent = pl.pallas_call(
        copies_kernel,
        name="copies",
        out_shape=pltpu.HBM((n // 2 * own, sides, 2 * rank), bf16),
        in_specs=[VMEM],
        out_specs=HBM,
        scratch_shapes=[dma(n // 2)],
        compiler_params=params(4),
    )(parent_coef)
    same = lax.all_to_all(sent, "gz", 0, 0, tiled=True)

    parent_packed, near, rim_near, leaf_at, parent_at = pl.pallas_call(
        functools.partial(mid_kernel, axes),
        name="mid",
        out_shape=[
            shape((parents, rank, many * rank), bf16),
            shape((pairs, sides, 2 * width), f32),
            shape((2, width, width), bf16),
            shape((many, leaves), jnp.int32),
            shape((parents, many), jnp.int32),
        ],
        in_specs=[VMEM] + [HBM] * 4,
        out_specs=[VMEM] * 5,
        scratch_shapes=[
            pltpu.VMEM(near_blocks.shape, bf16),
            pltpu.VMEM(parent_coupling.shape, bf16),
            dma(3 + parents // 4),
        ],
        compiler_params=params(12),
    )(live, *keep(near_blocks, parent_coupling, leaf_partners.T, parent_partners))

    quarter = shape((n // 4 * own, sides, 2 * rank), bf16)
    pieces = pl.pallas_call(
        halves_kernel,
        name="halves",
        out_shape=[quarter, quarter],
        in_specs=[VMEM, VMEM],
        out_specs=[VMEM, VMEM],
        compiler_params=params(4),
    )(same, parent_at)
    other = [lax.ppermute(piece, "gp", [(0, 1), (1, 0)]) for piece in pieces]

    far, edge, transfer_in, basis_in = pl.pallas_call(
        functools.partial(leaf_kernel, axes),
        name="leaf",
        out_shape=[
            shape((pairs, sides, 2 * rank), f32),
            shape((2, sides, 2 * width), f32),
            shape(transfer.shape, bf16),
            shape((pairs, width, 2 * rank), bf16),
        ],
        in_specs=[VMEM] * 5 + [HBM] * 3,
        out_specs=[VMEM] * 4,
        scratch_shapes=[
            pltpu.VMEM((3 * leaves, sides, 2 * rank), bf16),
            pltpu.SMEM((many, leaves), jnp.int32),
            pltpu.VMEM(leaf_coupling.shape, bf16),
            pltpu.VMEM(basis.shape, bf16),
            dma(3 + leaves // 2),
        ],
        compiler_params=params(16),
    )(leaf_at, rim, even, odd, rim_near, *keep(leaf_coupling, transfer, basis))

    out = pl.pallas_call(
        functools.partial(down_kernel, "gp"),
        name="down",
        out_shape=jax.ShapeDtypeStruct((sides, leaves * width), bf16),
        in_specs=[VMEM, VMEM, [VMEM] * 2, VMEM, HBM] + [VMEM] * 5,
        out_specs=VMEM,
        scratch_shapes=[
            pltpu.VMEM((n * parents, sides, 2 * rank), bf16),
            pltpu.SMEM((parents, many), jnp.int32),
            pltpu.VMEM((pairs, sides, 2 * rank), bf16),
            pltpu.VMEM((parents, sides, rank), bf16),
            pltpu.SMEM((leaves,), jnp.int32),
            dma(2),
        ],
        compiler_params=params(12),
    )(parent_at, same, other, parent_packed, *keep(panel_counts), far, near, edge, transfer_in, basis_in)
    return out.T


def solution(mesh):
    outer, inner = mesh.devices.shape
    split = jax.sharding.Mesh(mesh.devices.reshape(outer, inner // 2, 2), ("gx", "gz", "gp"))
    leaves = ("gx", "gz", "gp")
    in_specs = (
        P(leaves, None),
        P(leaves),
        P(leaves, None, None),
        P(leaves, None, None),
        P(leaves, None, None, None),
        P(leaves, None),
        P(leaves, None, None, None),
        P(leaves, None, None, None),
        P(leaves, None),
    )
    return jax.shard_map(
        per_device, mesh=split, in_specs=in_specs, out_specs=P(leaves, None), check_vma=False
    )
```

```python
import functools

import jax
import jax.numpy as jnp
from jax import lax
from jax.experimental import pallas as pl
from jax.experimental.pallas import tpu as pltpu
from jax.sharding import PartitionSpec as P

VMEM = pl.BlockSpec(memory_space=pltpu.VMEM)
HBM = pl.BlockSpec(memory_space=pltpu.HBM)
NN = (((1,), (0,)), ((), ()))
NT = (((1,), (1,)), ((), ()))


def dot(a, b, dims):
    return lax.dot_general(a, b, dims, preferred_element_type=jnp.float32)


def left_half(sides, width):
    return lax.broadcasted_iota(jnp.int32, (sides, 2 * width), 1) < width


def pair_mask(counts_ref, pair, sides, width):
    lane = lax.broadcasted_iota(jnp.int32, (sides, 2 * width), 1)
    left = lane < width
    count = jnp.where(left, counts_ref[2 * pair], counts_ref[2 * pair + 1])
    return jnp.where(left, lane, lane - width) < count


def swap(pair, width):
    return jnp.concatenate([pair[:, width:], pair[:, :width]], axis=1)


def mod(x, m):
    return x & (m - 1) if m & (m - 1) == 0 else lax.rem(x, m)


def div(x, m):
    return x >> (m.bit_length() - 1) if m & (m - 1) == 0 else x // m


def position(axes):
    index = 0
    for axis in axes:
        index = index * lax.axis_size(axis) + lax.axis_index(axis)
    return index


def start_all(copies, sems):
    started = [pltpu.make_async_copy(src, dst, sems.at[i]) for i, (src, dst) in enumerate(copies)]
    for copy in started:
        copy.start()
    return started


def up_kernel(
    counts_hbm, charges_hbm, basis_hbm, transfer_hbm,
    rim_ref, live_ref, sent_hbm,
    counts_ref, charges_ref, basis_ref, transfer_ref, parents_ref, sems, sent_sems,
):
    counts_in, charges_in, basis_in, transfer_in = start_all(
        [
            (counts_hbm, counts_ref), (charges_hbm, charges_ref),
            (basis_hbm, basis_ref), (transfer_hbm, transfer_ref),
        ],
        sems,
    )
    sides = charges_ref.shape[0]
    leaves, width, rank = basis_ref.shape
    pairs = leaves // 2
    own = pairs // 2
    left = left_half(sides, width)
    counts_in.wait()
    charges_in.wait()
    lives = []
    for a in range(pairs):
        charge = charges_ref[:, 2 * width * a : 2 * width * (a + 1)]
        live = jnp.where(pair_mask(counts_ref, a, sides, width), charge, jnp.zeros_like(charge))
        live_ref[a] = live
        lives.append(live)
    rim_ref[pairs] = lives[0]
    rim_ref[pairs + 1] = lives[-1]
    basis_in.wait()
    none = jnp.zeros_like(lives[0])
    coefs = []
    for a in range(pairs):
        live = lives[a]
        both = jnp.concatenate([jnp.where(left, live, none), jnp.where(left, none, live)], axis=0)
        coef = dot(both, basis_ref[2 * a : 2 * a + 2].reshape(2 * width, rank), NN)
        coef = jnp.concatenate([coef[:sides], coef[sides:]], axis=1).astype(jnp.bfloat16)
        rim_ref[a] = coef
        coefs.append(coef)
    transfer_in.wait()
    sums = [
        dot(coefs[a], transfer_ref[2 * a : 2 * a + 2].reshape(2 * rank, rank), NN)
        for a in range(pairs)
    ]
    for a in range(own):
        parents_ref[a] = jnp.concatenate(sums[2 * a : 2 * a + 2], axis=1).astype(jnp.bfloat16)
    copies = sent_hbm.shape[0] // own
    for copy in start_all([(parents_ref, sent_hbm.at[pl.ds(own * c, own)]) for c in range(copies)], sent_sems):
        copy.wait()


def side_by_side(blocks_ref, g):
    return jnp.concatenate([blocks_ref[g, j] for j in range(blocks_ref.shape[1])], axis=1)


def mid_kernel(
    axes, live_ref, near_hbm, parent_hbm, leaf_partners_hbm, parent_partners_hbm,
    parent_packed_ref, near_out_ref, rim_near_ref, leaf_at_ref, parent_at_ref,
    near_ref, parent_ref, sems,
):
    parents, many, rank, _ = parent_ref.shape
    leaves = near_ref.shape[0]
    width = near_ref.shape[2]
    pairs = leaves // 2
    started = start_all(
        [(near_hbm, near_ref)]
        + [(parent_hbm.at[pl.ds(4 * i, 4)], parent_ref.at[pl.ds(4 * i, 4)]) for i in range(parents // 4)]
        + [(leaf_partners_hbm, leaf_at_ref), (parent_partners_hbm, parent_at_ref)],
        sems,
    )
    near_in = started[0]
    parent_in = started[1:-2]
    near_in.wait()
    rim_near_ref[0] = near_ref[0, 0]
    rim_near_ref[1] = near_ref[leaves - 1, 2]
    for a in range(pairs):
        here = live_ref[a]
        even = dot(here, jnp.concatenate([near_ref[2 * a, 1], near_ref[2 * a, 2]], axis=1), NT)
        odd = dot(here, jnp.concatenate([near_ref[2 * a + 1, 0], near_ref[2 * a + 1, 1]], axis=1), NT)
        if a > 0:
            even = even + dot(live_ref[a - 1][:, width:], near_ref[2 * a, 0], NT)
        if a < pairs - 1:
            odd = odd + dot(live_ref[a + 1][:, :width], near_ref[2 * a + 1, 2], NT)
        near_out_ref[a] = jnp.concatenate([even, odd], axis=1)

    for i, copy in enumerate(parent_in):
        copy.wait()
        for q in range(4 * i, 4 * i + 4):
            parent_packed_ref[q] = side_by_side(parent_ref, q)
    for copy in started[-2:]:
        copy.wait()
    wanted = leaf_at_ref[...] + (1 - position(axes)) * leaves
    leaf_at_ref[...] = wanted ^ (lax.broadcasted_iota(jnp.int32, wanted.shape, 0) & 1)
    inner = lax.axis_size(axes[2])
    outer = lax.axis_size(axes[1])
    wanted = mod(parent_at_ref[...], outer * inner * parents)
    source = div(wanted, parents)
    wanted = (mod(source, inner) * outer + div(source, inner)) * parents + mod(wanted, parents)
    parent_at_ref[...] = wanted ^ (lax.broadcasted_iota(jnp.int32, wanted.shape, 1) & 1)


def halves_kernel(whole_ref, at_ref, first_ref, second_ref):
    del at_ref
    half = first_ref.shape[0]
    first_ref[...] = whole_ref[:half]
    second_ref[...] = whole_ref[half:]


def spread_pair(table_ref, at, pair, width):
    table_ref[at] = pair
    table_ref[at + 1] = swap(pair, width)


def picked(table_ref, rows, left):
    return jnp.concatenate(
        [
            jnp.where(left, table_ref[rows[j]], table_ref[rows[j + 1]])
            for j in range(0, len(rows), 2)
        ],
        axis=1,
    )


def leaf_kernel(
    axes, at_vmem, rim_ref, even_ref, odd_ref, rim_near_ref, coupling_hbm, transfer_hbm, basis_hbm,
    far_ref, edge_ref, transfer_ref, basis_packed_ref, table_ref, at_ref, coupling_ref, packed_ref, basis_ref, sems,
):
    leaves, many, rank, _ = coupling_ref.shape
    at_in, *coupling_in, transfer_in, basis_in = start_all(
        [(at_vmem, at_ref)]
        + [(coupling_hbm.at[pl.ds(4 * i, 4)], coupling_ref.at[pl.ds(4 * i, 4)]) for i in range(leaves // 4)]
        + [(transfer_hbm, transfer_ref), (basis_hbm, basis_ref)],
        sems,
    )
    width = rim_near_ref.shape[1]
    pairs = leaves // 2
    sides = rim_ref.shape[1]
    left = left_half(sides, rank)
    parity = lax.rem(position(axes), 2)
    for ref, base in (
        (rim_ref, leaves), (even_ref, 2 * leaves * (1 - parity)), (odd_ref, 2 * leaves * parity),
    ):
        for a in range(pairs):
            spread_pair(table_ref, base + 2 * a, ref[a], rank)
    before = jnp.where(parity == 1, even_ref[pairs + 1], odd_ref[pairs + 1])
    after = jnp.where(parity == 1, odd_ref[pairs], even_ref[pairs])
    low = dot(before[:, width:], rim_near_ref[0], NT)
    high = dot(after[:, :width], rim_near_ref[1], NT)
    edge_ref[0] = jnp.concatenate([low, jnp.zeros_like(low)], axis=1)
    edge_ref[1] = jnp.concatenate([jnp.zeros_like(high), high], axis=1)
    at_in.wait()
    for i in range(leaves // 4 + 1):
        if i < leaves // 4:
            coupling_in[i].wait()
            for g in range(4 * i, 4 * i + 4):
                packed_ref[g] = side_by_side(coupling_ref, g)
        fars = []
        for g in range(4 * i - 4, 4 * i) if i else ():
            rows = [at_ref[j, g] for j in range(many)]
            fars.append(dot(picked(table_ref, rows, left), packed_ref[g], NT))
            if g % 2 == 1:
                far_ref[g // 2] = jnp.concatenate(fars[-2:], axis=1)
    basis_in.wait()
    for a in range(pairs):
        basis_packed_ref[a] = jnp.concatenate([basis_ref[2 * a], basis_ref[2 * a + 1]], axis=1)
    transfer_in.wait()


def down_kernel(
    axis, at_vmem, same_ref, other_refs, packed_ref, counts_hbm,
    far_ref, near_ref, edge_ref, transfer_ref, basis_ref,
    out_ref, table_ref, at_ref, local_ref, down_ref, counts_ref, sems,
):
    at_in, counts_in = start_all([(at_vmem, at_ref), (counts_hbm, counts_ref)], sems)
    parents, many = at_ref.shape
    rank = packed_ref.shape[1]
    width = basis_ref.shape[1]
    sides = same_ref.shape[1]
    half = 2 * same_ref.shape[0]
    left = left_half(sides, rank)
    parity = lax.axis_index(axis)
    quarter = other_refs[0].shape[0]

    def spread(a, carry):
        for b, ref in enumerate(other_refs):
            spread_pair(table_ref, half * (1 - parity) + 2 * (quarter * b + a), ref[a], rank)
            spread_pair(table_ref, half * parity + 2 * (quarter * b + a), same_ref[quarter * b + a], rank)
        return carry

    lax.fori_loop(0, quarter, spread, 0, unroll=min(16, quarter))
    at_in.wait()
    for q in range(parents):
        rows = [at_ref[q, j] for j in range(many)]
        far = dot(picked(table_ref, rows, left), packed_ref[q], NT)
        down_ref[q] = far.astype(jnp.bfloat16)
    for q in range(parents):
        local = far_ref[q] + dot(down_ref[q], transfer_ref[2 * q : 2 * q + 2].reshape(2 * rank, rank), NT)
        local_ref[q] = local.astype(jnp.bfloat16)
    counts_in.wait()
    for q in range(parents):
        local = local_ref[q]
        none = jnp.zeros_like(local)
        both = jnp.concatenate([jnp.where(left, local, none), jnp.where(left, none, local)], axis=0)
        total = dot(both, basis_ref[q], NT)
        total = jnp.concatenate([total[:sides], total[sides:]], axis=1) + near_ref[q]
        if q == 0:
            total = total + edge_ref[0]
        if q == parents - 1:
            total = total + edge_ref[1]
        total = jnp.where(pair_mask(counts_ref, q, sides, width), total, jnp.zeros_like(total))
        out_ref[:, 2 * width * q : 2 * width * (q + 1)] = total.astype(out_ref.dtype)


def per_device(
    charges,
    panel_counts,
    basis,
    transfer,
    leaf_coupling,
    leaf_partners,
    near_blocks,
    parent_coupling,
    parent_partners,
):
    leaves, width, rank = basis.shape
    sides = charges.shape[1]
    parents, many = parent_partners.shape
    pairs = leaves // 2
    own = pairs // 2
    axes = ("gx", "gz", "gp")
    n = lax.axis_size("gz") * lax.axis_size("gp")
    total = n * lax.axis_size("gx")
    bf16, f32 = jnp.bfloat16, jnp.float32
    keep = lambda *arrays: [pltpu.with_memory_space_constraint(a, pltpu.HBM) for a in arrays]
    shape = pltpu.VMEM
    dma = lambda count: pltpu.SemaphoreType.DMA((count,))
    params = lambda mib: pltpu.CompilerParams(vmem_limit_bytes=mib * 2**20)

    rim, live, sent = pl.pallas_call(
        up_kernel,
        name="up",
        out_shape=[
            shape((pairs + 2, sides, 2 * rank), bf16),
            shape((pairs, sides, 2 * width), bf16),
            pltpu.HBM((n // 2 * own, sides, 2 * rank), bf16),
        ],
        in_specs=[HBM] * 4,
        out_specs=[VMEM, VMEM, HBM],
        scratch_shapes=[
            pltpu.SMEM((leaves,), jnp.int32),
            pltpu.VMEM((sides, leaves * width), bf16),
            pltpu.VMEM((leaves, width, rank), bf16),
            pltpu.VMEM((leaves, rank, rank), bf16),
            pltpu.VMEM((own, sides, 2 * rank), bf16),
            dma(4),
            dma(n // 2),
        ],
        compiler_params=params(8),
    )(*keep(panel_counts, charges.T, basis, transfer))

    even = lax.ppermute(rim, axes, [(i, i ^ 1) for i in range(total)])
    steps = [(i, i + 1) for i in range(1, total - 1, 2)]
    odd = lax.ppermute(rim, axes, steps + [(b, a) for a, b in steps])
    same = lax.all_to_all(sent, "gz", 0, 0, tiled=True)

    parent_packed, near, rim_near, leaf_at, parent_at = pl.pallas_call(
        functools.partial(mid_kernel, axes),
        name="mid",
        out_shape=[
            shape((parents, rank, many * rank), bf16),
            shape((pairs, sides, 2 * width), f32),
            shape((2, width, width), bf16),
            shape((many, leaves), jnp.int32),
            shape((parents, many), jnp.int32),
        ],
        in_specs=[VMEM] + [HBM] * 4,
        out_specs=[VMEM] * 5,
        scratch_shapes=[
            pltpu.VMEM(near_blocks.shape, bf16),
            pltpu.VMEM(parent_coupling.shape, bf16),
            dma(3 + parents // 4),
        ],
        compiler_params=params(12),
    )(live, *keep(near_blocks, parent_coupling, leaf_partners.T, parent_partners))

    quarter = shape((n // 4 * own, sides, 2 * rank), bf16)
    pieces = pl.pallas_call(
        halves_kernel,
        name="halves",
        out_shape=[quarter, quarter],
        in_specs=[VMEM, VMEM],
        out_specs=[VMEM, VMEM],
        compiler_params=params(4),
    )(same, parent_at)
    other = [lax.ppermute(piece, "gp", [(0, 1), (1, 0)]) for piece in pieces]

    far, edge, transfer_in, basis_in = pl.pallas_call(
        functools.partial(leaf_kernel, axes),
        name="leaf",
        out_shape=[
            shape((pairs, sides, 2 * rank), f32),
            shape((2, sides, 2 * width), f32),
            shape(transfer.shape, bf16),
            shape((pairs, width, 2 * rank), bf16),
        ],
        in_specs=[VMEM] * 5 + [HBM] * 3,
        out_specs=[VMEM] * 4,
        scratch_shapes=[
            pltpu.VMEM((3 * leaves, sides, 2 * rank), bf16),
            pltpu.SMEM((many, leaves), jnp.int32),
            pltpu.VMEM(leaf_coupling.shape, bf16),
            pltpu.VMEM((leaves, rank, many * rank), bf16),
            pltpu.VMEM(basis.shape, bf16),
            dma(3 + leaves // 4),
        ],
        compiler_params=params(20),
    )(leaf_at, rim, even, odd, rim_near, *keep(leaf_coupling, transfer, basis))

    out = pl.pallas_call(
        functools.partial(down_kernel, "gp"),
        name="down",
        out_shape=jax.ShapeDtypeStruct((sides, leaves * width), bf16),
        in_specs=[VMEM, VMEM, [VMEM] * 2, VMEM, HBM] + [VMEM] * 5,
        out_specs=VMEM,
        scratch_shapes=[
            pltpu.VMEM((n * parents, sides, 2 * rank), bf16),
            pltpu.SMEM((parents, many), jnp.int32),
            pltpu.VMEM((pairs, sides, 2 * rank), bf16),
            pltpu.VMEM((parents, sides, rank), bf16),
            pltpu.SMEM((leaves,), jnp.int32),
            dma(2),
        ],
        compiler_params=params(12),
    )(parent_at, same, other, parent_packed, *keep(panel_counts), far, near, edge, transfer_in, basis_in)
    return out.T


def solution(mesh):
    outer, inner = mesh.devices.shape
    split = jax.sharding.Mesh(mesh.devices.reshape(outer, inner // 2, 2), ("gx", "gz", "gp"))
    leaves = ("gx", "gz", "gp")
    in_specs = (
        P(leaves, None),
        P(leaves),
        P(leaves, None, None),
        P(leaves, None, None),
        P(leaves, None, None, None),
        P(leaves, None),
        P(leaves, None, None, None),
        P(leaves, None, None, None),
        P(leaves, None),
    )
    return jax.shard_map(
        per_device, mesh=split, in_specs=in_specs, out_specs=P(leaves, None), check_vma=False
    )
```

```python
import functools

import jax
import jax.numpy as jnp
from jax import lax
from jax.experimental import pallas as pl
from jax.experimental.pallas import tpu as pltpu
from jax.sharding import PartitionSpec as P

VMEM = pl.BlockSpec(memory_space=pltpu.VMEM)
HBM = pl.BlockSpec(memory_space=pltpu.HBM)
NN = (((1,), (0,)), ((), ()))
NT = (((1,), (1,)), ((), ()))


def dot(a, b, dims):
    return lax.dot_general(a, b, dims, preferred_element_type=jnp.float32)


def left_half(sides, width):
    return lax.broadcasted_iota(jnp.int32, (sides, 2 * width), 1) < width


def pair_mask(counts_ref, pair, sides, width):
    lane = lax.broadcasted_iota(jnp.int32, (sides, 2 * width), 1)
    left = lane < width
    count = jnp.where(left, counts_ref[2 * pair], counts_ref[2 * pair + 1])
    return jnp.where(left, lane, lane - width) < count


def swap(pair, width):
    return jnp.concatenate([pair[:, width:], pair[:, :width]], axis=1)


def mod(x, m):
    return x & (m - 1) if m & (m - 1) == 0 else lax.rem(x, m)


def div(x, m):
    return x >> (m.bit_length() - 1) if m & (m - 1) == 0 else x // m


def position(axes):
    index = 0
    for axis in axes:
        index = index * lax.axis_size(axis) + lax.axis_index(axis)
    return index


def start_all(copies, sems):
    started = [pltpu.make_async_copy(src, dst, sems.at[i]) for i, (src, dst) in enumerate(copies)]
    for copy in started:
        copy.start()
    return started


def up_kernel(
    axes, counts_hbm, charges_hbm, basis_hbm, transfer_hbm, near_hbm,
    rim_ref, even_rim_ref, live_ref, sent_hbm, near_ref,
    counts_ref, charges_ref, basis_ref, transfer_ref, parents_ref, sems, sent_sems,
):
    counts_in, charges_in, basis_in, transfer_in, near_in = start_all(
        [
            (counts_hbm, counts_ref), (charges_hbm, charges_ref),
            (basis_hbm, basis_ref), (transfer_hbm, transfer_ref), (near_hbm, near_ref),
        ],
        sems,
    )
    sides = charges_ref.shape[0]
    leaves, width, rank = basis_ref.shape
    pairs = leaves // 2
    own = pairs // 2
    left = left_half(sides, width)
    counts_in.wait()
    charges_in.wait()
    lives = []
    for a in range(pairs):
        charge = charges_ref[:, 2 * width * a : 2 * width * (a + 1)]
        live = jnp.where(pair_mask(counts_ref, a, sides, width), charge, jnp.zeros_like(charge))
        live_ref[a] = live
        lives.append(live)
    rim_ref[pairs] = lives[0]
    rim_ref[pairs + 1] = lives[-1]
    even_rim_ref[pairs] = jnp.where(lax.rem(position(axes), 2) == 0, lives[-1], lives[0])
    basis_in.wait()
    none = jnp.zeros_like(lives[0])
    coefs = []
    for a in range(pairs):
        live = lives[a]
        both = jnp.concatenate([jnp.where(left, live, none), jnp.where(left, none, live)], axis=0)
        coef = dot(both, basis_ref[2 * a : 2 * a + 2].reshape(2 * width, rank), NN)
        coef = jnp.concatenate([coef[:sides], coef[sides:]], axis=1).astype(jnp.bfloat16)
        rim_ref[a] = coef
        even_rim_ref[a] = coef
        coefs.append(coef)
    transfer_in.wait()
    sums = [
        dot(coefs[a], transfer_ref[2 * a : 2 * a + 2].reshape(2 * rank, rank), NN)
        for a in range(pairs)
    ]
    for a in range(own):
        parents_ref[a] = jnp.concatenate(sums[2 * a : 2 * a + 2], axis=1).astype(jnp.bfloat16)
    copies = sent_hbm.shape[0] // own
    for copy in start_all([(parents_ref, sent_hbm.at[pl.ds(own * c, own)]) for c in range(copies)], sent_sems):
        copy.wait()
    near_in.wait()


def side_by_side(blocks_ref, g):
    return jnp.concatenate([blocks_ref[g, j] for j in range(blocks_ref.shape[1])], axis=1)


def mid_kernel(
    axes, live_ref, near_ref, parent_hbm, leaf_partners_hbm, parent_partners_hbm,
    parent_packed_ref, near_out_ref, rim_near_ref, leaf_at_ref, parent_at_ref,
    parent_ref, sems,
):
    parents, many, rank, _ = parent_ref.shape
    leaves = near_ref.shape[0]
    width = near_ref.shape[2]
    pairs = leaves // 2
    started = start_all(
        [(parent_hbm.at[pl.ds(4 * i, 4)], parent_ref.at[pl.ds(4 * i, 4)]) for i in range(parents // 4)]
        + [(leaf_partners_hbm, leaf_at_ref), (parent_partners_hbm, parent_at_ref)],
        sems,
    )
    parent_in = started[:-2]
    rim_near_ref[0] = near_ref[0, 0]
    rim_near_ref[1] = near_ref[leaves - 1, 2]
    for a in range(pairs):
        here = live_ref[a]
        even = dot(here, jnp.concatenate([near_ref[2 * a, 1], near_ref[2 * a, 2]], axis=1), NT)
        odd = dot(here, jnp.concatenate([near_ref[2 * a + 1, 0], near_ref[2 * a + 1, 1]], axis=1), NT)
        if a > 0:
            even = even + dot(live_ref[a - 1][:, width:], near_ref[2 * a, 0], NT)
        if a < pairs - 1:
            odd = odd + dot(live_ref[a + 1][:, :width], near_ref[2 * a + 1, 2], NT)
        near_out_ref[a] = jnp.concatenate([even, odd], axis=1)

    for i, copy in enumerate(parent_in):
        copy.wait()
        for q in range(4 * i, 4 * i + 4):
            parent_packed_ref[q] = side_by_side(parent_ref, q)
    for copy in started[-2:]:
        copy.wait()
    wanted = leaf_at_ref[...] + (1 - position(axes)) * leaves
    leaf_at_ref[...] = wanted ^ (lax.broadcasted_iota(jnp.int32, wanted.shape, 0) & 1)
    inner = lax.axis_size(axes[2])
    outer = lax.axis_size(axes[1])
    wanted = mod(parent_at_ref[...], outer * inner * parents)
    source = div(wanted, parents)
    wanted = (mod(source, inner) * outer + div(source, inner)) * parents + mod(wanted, parents)
    parent_at_ref[...] = wanted ^ (lax.broadcasted_iota(jnp.int32, wanted.shape, 1) & 1)


def halves_kernel(whole_ref, at_ref, first_ref, second_ref):
    del at_ref
    half = first_ref.shape[0]
    first_ref[...] = whole_ref[:half]
    second_ref[...] = whole_ref[half:]


def spread_pair(table_ref, at, pair, width):
    table_ref[at] = pair
    table_ref[at + 1] = swap(pair, width)


def picked(table_ref, rows, left):
    return jnp.concatenate(
        [
            jnp.where(left, table_ref[rows[j]], table_ref[rows[j + 1]])
            for j in range(0, len(rows), 2)
        ],
        axis=1,
    )


def leaf_kernel(
    axes, at_vmem, rim_ref, even_ref, odd_ref, rim_near_ref, coupling_hbm, transfer_hbm, basis_hbm,
    far_ref, edge_ref, transfer_ref, basis_packed_ref, table_ref, at_ref, coupling_ref, packed_ref, basis_ref, sems,
):
    leaves, many, rank, _ = coupling_ref.shape
    at_in, *coupling_in, transfer_in, basis_in = start_all(
        [(at_vmem, at_ref)]
        + [(coupling_hbm.at[pl.ds(4 * i, 4)], coupling_ref.at[pl.ds(4 * i, 4)]) for i in range(leaves // 4)]
        + [(transfer_hbm, transfer_ref), (basis_hbm, basis_ref)],
        sems,
    )
    width = rim_near_ref.shape[1]
    pairs = leaves // 2
    sides = rim_ref.shape[1]
    left = left_half(sides, rank)
    parity = lax.rem(position(axes), 2)
    for ref, base in (
        (rim_ref, leaves), (even_ref, 2 * leaves * (1 - parity)), (odd_ref, 2 * leaves * parity),
    ):
        for a in range(pairs):
            spread_pair(table_ref, base + 2 * a, ref[a], rank)
    before = jnp.where(parity == 1, even_ref[pairs], odd_ref[pairs + 1])
    after = jnp.where(parity == 1, odd_ref[pairs], even_ref[pairs])
    low = dot(before[:, width:], rim_near_ref[0], NT)
    high = dot(after[:, :width], rim_near_ref[1], NT)
    edge_ref[0] = jnp.concatenate([low, jnp.zeros_like(low)], axis=1)
    edge_ref[1] = jnp.concatenate([jnp.zeros_like(high), high], axis=1)
    at_in.wait()
    for i in range(leaves // 4 + 1):
        if i < leaves // 4:
            coupling_in[i].wait()
            for g in range(4 * i, 4 * i + 4):
                packed_ref[g] = side_by_side(coupling_ref, g)
        fars = []
        for g in range(4 * i - 4, 4 * i) if i else ():
            rows = [at_ref[j, g] for j in range(many)]
            fars.append(dot(picked(table_ref, rows, left), packed_ref[g], NT))
            if g % 2 == 1:
                far_ref[g // 2] = jnp.concatenate(fars[-2:], axis=1)
    basis_in.wait()
    for a in range(pairs):
        basis_packed_ref[a] = jnp.concatenate([basis_ref[2 * a], basis_ref[2 * a + 1]], axis=1)
    transfer_in.wait()


def down_kernel(
    axis, at_vmem, same_ref, other_refs, packed_ref, counts_hbm,
    far_ref, near_ref, edge_ref, transfer_ref, basis_ref,
    out_ref, table_ref, at_ref, local_ref, down_ref, counts_ref, sems,
):
    at_in, counts_in = start_all([(at_vmem, at_ref), (counts_hbm, counts_ref)], sems)
    parents, many = at_ref.shape
    rank = packed_ref.shape[1]
    width = basis_ref.shape[1]
    sides = same_ref.shape[1]
    half = 2 * same_ref.shape[0]
    left = left_half(sides, rank)
    parity = lax.axis_index(axis)
    quarter = other_refs[0].shape[0]

    def spread(a, carry):
        for b, ref in enumerate(other_refs):
            spread_pair(table_ref, half * (1 - parity) + 2 * (quarter * b + a), ref[a], rank)
            spread_pair(table_ref, half * parity + 2 * (quarter * b + a), same_ref[quarter * b + a], rank)
        return carry

    lax.fori_loop(0, quarter, spread, 0, unroll=min(16, quarter))
    at_in.wait()
    for q in range(parents):
        rows = [at_ref[q, j] for j in range(many)]
        far = dot(picked(table_ref, rows, left), packed_ref[q], NT)
        down_ref[q] = far.astype(jnp.bfloat16)
    for q in range(parents):
        local = far_ref[q] + dot(down_ref[q], transfer_ref[2 * q : 2 * q + 2].reshape(2 * rank, rank), NT)
        local_ref[q] = local.astype(jnp.bfloat16)
    counts_in.wait()
    for q in range(parents):
        local = local_ref[q]
        none = jnp.zeros_like(local)
        both = jnp.concatenate([jnp.where(left, local, none), jnp.where(left, none, local)], axis=0)
        total = dot(both, basis_ref[q], NT)
        total = jnp.concatenate([total[:sides], total[sides:]], axis=1) + near_ref[q]
        if q == 0:
            total = total + edge_ref[0]
        if q == parents - 1:
            total = total + edge_ref[1]
        total = jnp.where(pair_mask(counts_ref, q, sides, width), total, jnp.zeros_like(total))
        out_ref[:, 2 * width * q : 2 * width * (q + 1)] = total.astype(out_ref.dtype)


def per_device(
    charges,
    panel_counts,
    basis,
    transfer,
    leaf_coupling,
    leaf_partners,
    near_blocks,
    parent_coupling,
    parent_partners,
):
    leaves, width, rank = basis.shape
    sides = charges.shape[1]
    parents, many = parent_partners.shape
    pairs = leaves // 2
    own = pairs // 2
    axes = ("gx", "gz", "gp")
    n = lax.axis_size("gz") * lax.axis_size("gp")
    total = n * lax.axis_size("gx")
    bf16, f32 = jnp.bfloat16, jnp.float32
    keep = lambda *arrays: [pltpu.with_memory_space_constraint(a, pltpu.HBM) for a in arrays]
    shape = pltpu.VMEM
    dma = lambda count: pltpu.SemaphoreType.DMA((count,))
    params = lambda mib: pltpu.CompilerParams(vmem_limit_bytes=mib * 2**20)

    rim, even_rim, live, sent, near_held = pl.pallas_call(
        functools.partial(up_kernel, axes),
        name="up",
        out_shape=[
            shape((pairs + 2, sides, 2 * rank), bf16),
            shape((pairs + 1, sides, 2 * rank), bf16),
            shape((pairs, sides, 2 * width), bf16),
            pltpu.HBM((n // 2 * own, sides, 2 * rank), bf16),
            shape(near_blocks.shape, bf16),
        ],
        in_specs=[HBM] * 5,
        out_specs=[VMEM, VMEM, VMEM, HBM, VMEM],
        scratch_shapes=[
            pltpu.SMEM((leaves,), jnp.int32),
            pltpu.VMEM((sides, leaves * width), bf16),
            pltpu.VMEM((leaves, width, rank), bf16),
            pltpu.VMEM((leaves, rank, rank), bf16),
            pltpu.VMEM((own, sides, 2 * rank), bf16),
            dma(5),
            dma(n // 2),
        ],
        compiler_params=params(8),
    )(*keep(panel_counts, charges.T, basis, transfer, near_blocks))

    even = lax.ppermute(even_rim, axes, [(i, i ^ 1) for i in range(total)])
    steps = [(i, i + 1) for i in range(1, total - 1, 2)]
    odd = lax.ppermute(rim, axes, steps + [(b, a) for a, b in steps])
    same = lax.all_to_all(sent, "gz", 0, 0, tiled=True)

    parent_packed, near, rim_near, leaf_at, parent_at = pl.pallas_call(
        functools.partial(mid_kernel, axes),
        name="mid",
        out_shape=[
            shape((parents, rank, many * rank), bf16),
            shape((pairs, sides, 2 * width), f32),
            shape((2, width, width), bf16),
            shape((many, leaves), jnp.int32),
            shape((parents, many), jnp.int32),
        ],
        in_specs=[VMEM, VMEM] + [HBM] * 3,
        out_specs=[VMEM] * 5,
        scratch_shapes=[
            pltpu.VMEM(parent_coupling.shape, bf16),
            dma(2 + parents // 4),
        ],
        compiler_params=params(12),
    )(live, near_held, *keep(parent_coupling, leaf_partners.T, parent_partners))

    quarter = shape((n // 4 * own, sides, 2 * rank), bf16)
    pieces = pl.pallas_call(
        halves_kernel,
        name="halves",
        out_shape=[quarter, quarter],
        in_specs=[VMEM, VMEM],
        out_specs=[VMEM, VMEM],
        compiler_params=params(4),
    )(same, parent_at)
    other = [lax.ppermute(piece, "gp", [(0, 1), (1, 0)]) for piece in pieces]

    far, edge, transfer_in, basis_in = pl.pallas_call(
        functools.partial(leaf_kernel, axes),
        name="leaf",
        out_shape=[
            shape((pairs, sides, 2 * rank), f32),
            shape((2, sides, 2 * width), f32),
            shape(transfer.shape, bf16),
            shape((pairs, width, 2 * rank), bf16),
        ],
        in_specs=[VMEM] * 5 + [HBM] * 3,
        out_specs=[VMEM] * 4,
        scratch_shapes=[
            pltpu.VMEM((3 * leaves, sides, 2 * rank), bf16),
            pltpu.SMEM((many, leaves), jnp.int32),
            pltpu.VMEM(leaf_coupling.shape, bf16),
            pltpu.VMEM((leaves, rank, many * rank), bf16),
            pltpu.VMEM(basis.shape, bf16),
            dma(3 + leaves // 4),
        ],
        compiler_params=params(20),
    )(leaf_at, rim, even, odd, rim_near, *keep(leaf_coupling, transfer, basis))

    out = pl.pallas_call(
        functools.partial(down_kernel, "gp"),
        name="down",
        out_shape=jax.ShapeDtypeStruct((sides, leaves * width), bf16),
        in_specs=[VMEM, VMEM, [VMEM] * 2, VMEM, HBM] + [VMEM] * 5,
        out_specs=VMEM,
        scratch_shapes=[
            pltpu.VMEM((n * parents, sides, 2 * rank), bf16),
            pltpu.SMEM((parents, many), jnp.int32),
            pltpu.VMEM((pairs, sides, 2 * rank), bf16),
            pltpu.VMEM((parents, sides, rank), bf16),
            pltpu.SMEM((leaves,), jnp.int32),
            dma(2),
        ],
        compiler_params=params(12),
    )(parent_at, same, other, parent_packed, *keep(panel_counts), far, near, edge, transfer_in, basis_in)
    return out.T


def solution(mesh):
    outer, inner = mesh.devices.shape
    split = jax.sharding.Mesh(mesh.devices.reshape(outer, inner // 2, 2), ("gx", "gz", "gp"))
    leaves = ("gx", "gz", "gp")
    in_specs = (
        P(leaves, None),
        P(leaves),
        P(leaves, None, None),
        P(leaves, None, None),
        P(leaves, None, None, None),
        P(leaves, None),
        P(leaves, None, None, None),
        P(leaves, None, None, None),
        P(leaves, None),
    )
    return jax.shard_map(
        per_device, mesh=split, in_specs=in_specs, out_specs=P(leaves, None), check_vma=False
    )
```

```python
import functools

import jax
import jax.numpy as jnp
from jax import lax
from jax.experimental import pallas as pl
from jax.experimental.pallas import tpu as pltpu
from jax.sharding import PartitionSpec as P

VMEM = pl.BlockSpec(memory_space=pltpu.VMEM)
HBM = pl.BlockSpec(memory_space=pltpu.HBM)
NN = (((1,), (0,)), ((), ()))
NT = (((1,), (1,)), ((), ()))


def dot(a, b, dims):
    return lax.dot_general(a, b, dims, preferred_element_type=jnp.float32)


def left_half(sides, width):
    return lax.broadcasted_iota(jnp.int32, (sides, 2 * width), 1) < width


def pair_mask(counts_ref, pair, sides, width):
    lane = lax.broadcasted_iota(jnp.int32, (sides, 2 * width), 1)
    left = lane < width
    count = jnp.where(left, counts_ref[2 * pair], counts_ref[2 * pair + 1])
    return jnp.where(left, lane, lane - width) < count


def swap(pair, width):
    return jnp.concatenate([pair[:, width:], pair[:, :width]], axis=1)


def mod(x, m):
    return x & (m - 1) if m & (m - 1) == 0 else lax.rem(x, m)


def div(x, m):
    return x >> (m.bit_length() - 1) if m & (m - 1) == 0 else x // m


def position(axes):
    index = 0
    for axis in axes:
        index = index * lax.axis_size(axis) + lax.axis_index(axis)
    return index


def start_all(copies, sems):
    started = [pltpu.make_async_copy(src, dst, sems.at[i]) for i, (src, dst) in enumerate(copies)]
    for copy in started:
        copy.start()
    return started


def up_kernel(
    counts_hbm, charges_hbm, basis_hbm, transfer_hbm,
    rim_ref, live_ref, parents_ref, sent_hbm,
    counts_ref, charges_ref, basis_ref, transfer_ref, sems, sent_sems,
):
    counts_in, charges_in, basis_in, transfer_in = start_all(
        [
            (counts_hbm, counts_ref), (charges_hbm, charges_ref),
            (basis_hbm, basis_ref), (transfer_hbm, transfer_ref),
        ],
        sems,
    )
    sides = charges_ref.shape[0]
    leaves, width, rank = basis_ref.shape
    pairs = leaves // 2
    own = pairs // 2
    left = left_half(sides, width)
    counts_in.wait()
    charges_in.wait()
    lives = []
    for a in range(pairs):
        charge = charges_ref[:, 2 * width * a : 2 * width * (a + 1)]
        live = jnp.where(pair_mask(counts_ref, a, sides, width), charge, jnp.zeros_like(charge))
        live_ref[a] = live
        lives.append(live)
    rim_ref[pairs] = lives[0]
    rim_ref[pairs + 1] = lives[-1]
    basis_in.wait()
    none = jnp.zeros_like(lives[0])
    coefs = []
    for a in range(pairs):
        live = lives[a]
        both = jnp.concatenate([jnp.where(left, live, none), jnp.where(left, none, live)], axis=0)
        coef = dot(both, basis_ref[2 * a : 2 * a + 2].reshape(2 * width, rank), NN)
        coef = jnp.concatenate([coef[:sides], coef[sides:]], axis=1).astype(jnp.bfloat16)
        rim_ref[a] = coef
        coefs.append(coef)
    transfer_in.wait()
    sums = [
        dot(coefs[a], transfer_ref[2 * a : 2 * a + 2].reshape(2 * rank, rank), NN)
        for a in range(pairs)
    ]
    for a in range(own):
        parents_ref[a] = jnp.concatenate(sums[2 * a : 2 * a + 2], axis=1).astype(jnp.bfloat16)
    copies = sent_hbm.shape[0] // own
    for copy in start_all([(parents_ref, sent_hbm.at[pl.ds(own * c, own)]) for c in range(copies)], sent_sems):
        copy.wait()


def side_by_side(blocks_ref, g):
    return jnp.concatenate([blocks_ref[g, j] for j in range(blocks_ref.shape[1])], axis=1)


def mid_kernel(
    axes, live_ref, near_hbm, parent_hbm, leaf_partners_hbm, parent_partners_hbm,
    parent_packed_ref, near_out_ref, rim_near_ref, leaf_at_ref, parent_at_ref,
    near_ref, parent_ref, sems,
):
    parents, many, rank, _ = parent_ref.shape
    leaves = near_ref.shape[0]
    width = near_ref.shape[2]
    pairs = leaves // 2
    started = start_all(
        [(near_hbm, near_ref)]
        + [(parent_hbm.at[pl.ds(4 * i, 4)], parent_ref.at[pl.ds(4 * i, 4)]) for i in range(parents // 4)]
        + [(leaf_partners_hbm, leaf_at_ref), (parent_partners_hbm, parent_at_ref)],
        sems,
    )
    near_in = started[0]
    parent_in = started[1:-2]
    near_in.wait()
    rim_near_ref[0] = near_ref[0, 0]
    rim_near_ref[1] = near_ref[leaves - 1, 2]
    for a in range(pairs):
        here = live_ref[a]
        even = dot(here, jnp.concatenate([near_ref[2 * a, 1], near_ref[2 * a, 2]], axis=1), NT)
        odd = dot(here, jnp.concatenate([near_ref[2 * a + 1, 0], near_ref[2 * a + 1, 1]], axis=1), NT)
        if a > 0:
            even = even + dot(live_ref[a - 1][:, width:], near_ref[2 * a, 0], NT)
        if a < pairs - 1:
            odd = odd + dot(live_ref[a + 1][:, :width], near_ref[2 * a + 1, 2], NT)
        near_out_ref[a] = jnp.concatenate([even, odd], axis=1)

    for i, copy in enumerate(parent_in):
        copy.wait()
        for q in range(4 * i, 4 * i + 4):
            parent_packed_ref[q] = side_by_side(parent_ref, q)
    for copy in started[-2:]:
        copy.wait()
    wanted = leaf_at_ref[...] + (1 - position(axes)) * leaves
    leaf_at_ref[...] = wanted ^ (lax.broadcasted_iota(jnp.int32, wanted.shape, 0) & 1)
    inner = lax.axis_size(axes[2])
    outer = lax.axis_size(axes[1])
    wanted = mod(parent_at_ref[...], outer * inner * parents)
    source = div(wanted, parents)
    wanted = (mod(source, inner) * outer + div(source, inner)) * parents + mod(wanted, parents)
    parent_at_ref[...] = wanted ^ (lax.broadcasted_iota(jnp.int32, wanted.shape, 1) & 1)


def halves_kernel(axis, whole_ref, own_ref, at_ref, first_ref, second_ref):
    del at_ref
    own, half = own_ref.shape[0], first_ref.shape[0]
    count = lax.axis_size(axis)
    for t in range(2 * half):
        source = lax.rem(lax.axis_index(axis) + 1 + t // own, count) * own + t % own
        (first_ref if t < half else second_ref)[t % half] = whole_ref[source]


def spread_pair(table_ref, at, pair, width):
    table_ref[at] = pair
    table_ref[at + 1] = swap(pair, width)


def picked(table_ref, rows, left):
    return jnp.concatenate(
        [
            jnp.where(left, table_ref[rows[j]], table_ref[rows[j + 1]])
            for j in range(0, len(rows), 2)
        ],
        axis=1,
    )


def leaf_kernel(
    axes, at_vmem, rim_ref, even_ref, odd_ref, rim_near_ref, coupling_hbm, transfer_hbm, basis_hbm,
    far_ref, edge_ref, transfer_ref, basis_packed_ref, table_ref, at_ref, coupling_ref, packed_ref, basis_ref, sems,
):
    leaves, many, rank, _ = coupling_ref.shape
    chunks = [(at, 4) for at in range(0, leaves - 4, 4)] + [(leaves - 4, 2), (leaves - 2, 2)]
    at_in, *coupling_in, transfer_in, basis_in = start_all(
        [(at_vmem, at_ref)]
        + [(coupling_hbm.at[pl.ds(at, size)], coupling_ref.at[pl.ds(at, size)]) for at, size in chunks]
        + [(transfer_hbm, transfer_ref), (basis_hbm, basis_ref)],
        sems,
    )
    width = rim_near_ref.shape[1]
    pairs = leaves // 2
    sides = rim_ref.shape[1]
    left = left_half(sides, rank)
    parity = lax.rem(position(axes), 2)
    for ref, base in (
        (rim_ref, leaves), (even_ref, 2 * leaves * (1 - parity)), (odd_ref, 2 * leaves * parity),
    ):
        for a in range(pairs):
            spread_pair(table_ref, base + 2 * a, ref[a], rank)
    before = jnp.where(parity == 1, even_ref[pairs + 1], odd_ref[pairs + 1])
    after = jnp.where(parity == 1, odd_ref[pairs], even_ref[pairs])
    low = dot(before[:, width:], rim_near_ref[0], NT)
    high = dot(after[:, :width], rim_near_ref[1], NT)
    edge_ref[0] = jnp.concatenate([low, jnp.zeros_like(low)], axis=1)
    edge_ref[1] = jnp.concatenate([jnp.zeros_like(high), high], axis=1)
    at_in.wait()
    ready = []
    for i in range(len(chunks) + 1):
        now, ready = ready, []
        if i < len(chunks):
            coupling_in[i].wait()
            ready = range(chunks[i][0], sum(chunks[i]))
            for g in ready:
                packed_ref[g] = side_by_side(coupling_ref, g)
        fars = []
        for g in now:
            rows = [at_ref[j, g] for j in range(many)]
            fars.append(dot(picked(table_ref, rows, left), packed_ref[g], NT))
            if g % 2 == 1:
                far_ref[g // 2] = jnp.concatenate(fars[-2:], axis=1)
    basis_in.wait()
    for a in range(pairs):
        basis_packed_ref[a] = jnp.concatenate([basis_ref[2 * a], basis_ref[2 * a + 1]], axis=1)
    transfer_in.wait()


def down_kernel(
    axes, at_vmem, same_ref, other_own_ref, other_refs, packed_ref, counts_hbm,
    far_ref, near_ref, edge_ref, transfer_ref, basis_ref,
    out_hbm, table_ref, at_ref, local_ref, down_ref, counts_ref, out_ref, sems, out_sems,
):
    at_in, counts_in = start_all([(at_vmem, at_ref), (counts_hbm, counts_ref)], sems)
    parents, many = at_ref.shape
    rank = packed_ref.shape[1]
    width = basis_ref.shape[1]
    sides = same_ref.shape[1]
    half = 2 * same_ref.shape[0]
    left = left_half(sides, rank)
    parity, mine, count = lax.axis_index(axes[1]), lax.axis_index(axes[0]), lax.axis_size(axes[0])
    own, piece = other_own_ref.shape[0], other_refs[0].shape[0]
    for t in range(count * own):
        spread_pair(table_ref, half * parity + 2 * t, same_ref[t], rank)
    for t in range(own):
        spread_pair(table_ref, half * (1 - parity) + 2 * (mine * own + t), other_own_ref[t], rank)
    for t in range(2 * piece):
        place = lax.rem(mine + 1 + t // own, count) * own + t % own
        spread_pair(table_ref, half * (1 - parity) + 2 * place, other_refs[t // piece][t % piece], rank)
    at_in.wait()
    for q in range(parents):
        rows = [at_ref[q, j] for j in range(many)]
        far = dot(picked(table_ref, rows, left), packed_ref[q], NT)
        down_ref[q] = far.astype(jnp.bfloat16)
    for q in range(parents):
        local = far_ref[q] + dot(down_ref[q], transfer_ref[2 * q : 2 * q + 2].reshape(2 * rank, rank), NT)
        local_ref[q] = local.astype(jnp.bfloat16)
    counts_in.wait()
    sent = []
    for q in range(parents):
        local = local_ref[q]
        none = jnp.zeros_like(local)
        both = jnp.concatenate([jnp.where(left, local, none), jnp.where(left, none, local)], axis=0)
        total = dot(both, basis_ref[q], NT)
        total = jnp.concatenate([total[:sides], total[sides:]], axis=1) + near_ref[q]
        if q == 0:
            total = total + edge_ref[0]
        if q == parents - 1:
            total = total + edge_ref[1]
        total = jnp.where(pair_mask(counts_ref, q, sides, width), total, jnp.zeros_like(total))
        out_ref[:, 2 * width * q : 2 * width * (q + 1)] = total.astype(out_ref.dtype)
        if (q + 1) % 4 == 0:
            lanes = pl.ds(2 * width * (q - 3), 8 * width)
            sent.append(pltpu.make_async_copy(out_ref.at[:, lanes], out_hbm.at[:, lanes], out_sems.at[q // 4]))
            sent[-1].start()
    for copy in sent:
        copy.wait()


def per_device(
    charges,
    panel_counts,
    basis,
    transfer,
    leaf_coupling,
    leaf_partners,
    near_blocks,
    parent_coupling,
    parent_partners,
):
    leaves, width, rank = basis.shape
    sides = charges.shape[1]
    parents, many = parent_partners.shape
    pairs = leaves // 2
    own = pairs // 2
    axes = ("gx", "gz", "gp")
    n = lax.axis_size("gz") * lax.axis_size("gp")
    total = n * lax.axis_size("gx")
    bf16, f32 = jnp.bfloat16, jnp.float32
    keep = lambda *arrays: [pltpu.with_memory_space_constraint(a, pltpu.HBM) for a in arrays]
    shape = pltpu.VMEM
    dma = lambda count: pltpu.SemaphoreType.DMA((count,))
    params = lambda mib: pltpu.CompilerParams(vmem_limit_bytes=mib * 2**20)

    rim, live, parent_coef, sent = pl.pallas_call(
        up_kernel,
        name="up",
        out_shape=[
            shape((pairs + 2, sides, 2 * rank), bf16),
            shape((pairs, sides, 2 * width), bf16),
            shape((own, sides, 2 * rank), bf16),
            pltpu.HBM((n // 2 * own, sides, 2 * rank), bf16),
        ],
        in_specs=[HBM] * 4,
        out_specs=[VMEM, VMEM, VMEM, HBM],
        scratch_shapes=[
            pltpu.SMEM((leaves,), jnp.int32),
            pltpu.VMEM((sides, leaves * width), bf16),
            pltpu.VMEM((leaves, width, rank), bf16),
            pltpu.VMEM((leaves, rank, rank), bf16),
            dma(4),
            dma(n // 2),
        ],
        compiler_params=params(8),
    )(*keep(panel_counts, charges.T, basis, transfer))

    even = lax.ppermute(rim, axes, [(i, i ^ 1) for i in range(total)])
    steps = [(i, i + 1) for i in range(1, total - 1, 2)]
    odd = lax.ppermute(rim, axes, steps + [(b, a) for a, b in steps])
    same = lax.all_to_all(sent, "gz", 0, 0, tiled=True)

    parent_packed, near, rim_near, leaf_at, parent_at = pl.pallas_call(
        functools.partial(mid_kernel, axes),
        name="mid",
        out_shape=[
            shape((parents, rank, many * rank), bf16),
            shape((pairs, sides, 2 * width), f32),
            shape((2, width, width), bf16),
            shape((many, leaves), jnp.int32),
            shape((parents, many), jnp.int32),
        ],
        in_specs=[VMEM] + [HBM] * 4,
        out_specs=[VMEM] * 5,
        scratch_shapes=[
            pltpu.VMEM(near_blocks.shape, bf16),
            pltpu.VMEM(parent_coupling.shape, bf16),
            dma(3 + parents // 4),
        ],
        compiler_params=params(12),
    )(live, *keep(near_blocks, parent_coupling, leaf_partners.T, parent_partners))

    other_own = lax.ppermute(parent_coef, "gp", [(0, 1), (1, 0)])
    piece = shape(((n // 2 - 1) * own // 2, sides, 2 * rank), bf16)
    pieces = pl.pallas_call(
        functools.partial(halves_kernel, "gz"),
        name="halves",
        out_shape=[piece, piece],
        in_specs=[VMEM, VMEM, VMEM],
        out_specs=[VMEM, VMEM],
        compiler_params=params(4),
    )(same, other_own, parent_at)
    other = [lax.ppermute(piece, "gp", [(0, 1), (1, 0)]) for piece in pieces]

    far, edge, transfer_in, basis_in = pl.pallas_call(
        functools.partial(leaf_kernel, axes),
        name="leaf",
        out_shape=[
            shape((pairs, sides, 2 * rank), f32),
            shape((2, sides, 2 * width), f32),
            shape(transfer.shape, bf16),
            shape((pairs, width, 2 * rank), bf16),
        ],
        in_specs=[VMEM] * 5 + [HBM] * 3,
        out_specs=[VMEM] * 4,
        scratch_shapes=[
            pltpu.VMEM((3 * leaves, sides, 2 * rank), bf16),
            pltpu.SMEM((many, leaves), jnp.int32),
            pltpu.VMEM(leaf_coupling.shape, bf16),
            pltpu.VMEM((leaves, rank, many * rank), bf16),
            pltpu.VMEM(basis.shape, bf16),
            dma(4 + leaves // 4),
        ],
        compiler_params=params(20),
    )(leaf_at, rim, even, odd, rim_near, *keep(leaf_coupling, transfer, basis))

    out = pl.pallas_call(
        functools.partial(down_kernel, axes[1:]),
        name="down",
        out_shape=pltpu.HBM((sides, leaves * width), bf16),
        in_specs=[VMEM, VMEM, VMEM, [VMEM] * 2, VMEM, HBM] + [VMEM] * 5,
        out_specs=HBM,
        scratch_shapes=[
            pltpu.VMEM((n * parents, sides, 2 * rank), bf16),
            pltpu.SMEM((parents, many), jnp.int32),
            pltpu.VMEM((pairs, sides, 2 * rank), bf16),
            pltpu.VMEM((parents, sides, rank), bf16),
            pltpu.SMEM((leaves,), jnp.int32),
            pltpu.VMEM((sides, leaves * width), bf16),
            dma(2),
            dma(parents // 4),
        ],
        compiler_params=params(12),
    )(parent_at, same, other_own, other, parent_packed, *keep(panel_counts), far, near, edge, transfer_in, basis_in)
    return out.T


def solution(mesh):
    outer, inner = mesh.devices.shape
    split = jax.sharding.Mesh(mesh.devices.reshape(outer, inner // 2, 2), ("gx", "gz", "gp"))
    leaves = ("gx", "gz", "gp")
    in_specs = (
        P(leaves, None),
        P(leaves),
        P(leaves, None, None),
        P(leaves, None, None),
        P(leaves, None, None, None),
        P(leaves, None),
        P(leaves, None, None, None),
        P(leaves, None, None, None),
        P(leaves, None),
    )
    return jax.shard_map(
        per_device, mesh=split, in_specs=in_specs, out_specs=P(leaves, None), check_vma=False
    )
```

```python
import functools

import jax
import jax.numpy as jnp
from jax import lax
from jax.experimental import pallas as pl
from jax.experimental.pallas import tpu as pltpu
from jax.sharding import PartitionSpec as P

VMEM = pl.BlockSpec(memory_space=pltpu.VMEM)
HBM = pl.BlockSpec(memory_space=pltpu.HBM)
NN = (((1,), (0,)), ((), ()))
NT = (((1,), (1,)), ((), ()))


def dot(a, b, dims):
    return lax.dot_general(a, b, dims, preferred_element_type=jnp.float32)


def left_half(sides, width):
    return lax.broadcasted_iota(jnp.int32, (sides, 2 * width), 1) < width


def pair_mask(counts_ref, pair, sides, width):
    lane = lax.broadcasted_iota(jnp.int32, (sides, 2 * width), 1)
    left = lane < width
    count = jnp.where(left, counts_ref[2 * pair], counts_ref[2 * pair + 1])
    return jnp.where(left, lane, lane - width) < count


def swap(pair, width):
    return jnp.concatenate([pair[:, width:], pair[:, :width]], axis=1)


def mod(x, m):
    return x & (m - 1) if m & (m - 1) == 0 else lax.rem(x, m)


def div(x, m):
    return x >> (m.bit_length() - 1) if m & (m - 1) == 0 else x // m


def position(axes):
    index = 0
    for axis in axes:
        index = index * lax.axis_size(axis) + lax.axis_index(axis)
    return index


def start_all(copies, sems):
    started = [pltpu.make_async_copy(src, dst, sems.at[i]) for i, (src, dst) in enumerate(copies)]
    for copy in started:
        copy.start()
    return started


def up_kernel(
    axes, counts_hbm, charges_hbm, basis_hbm, transfer_hbm,
    rim_ref, even_rim_ref, live_ref, parents_ref, sent_hbm,
    counts_ref, charges_ref, basis_ref, transfer_ref, sems, sent_sems,
):
    counts_in, charges_in, basis_in, transfer_in = start_all(
        [
            (counts_hbm, counts_ref), (charges_hbm, charges_ref),
            (basis_hbm, basis_ref), (transfer_hbm, transfer_ref),
        ],
        sems,
    )
    sides = charges_ref.shape[0]
    leaves, width, rank = basis_ref.shape
    pairs = leaves // 2
    own = pairs // 2
    left = left_half(sides, width)
    counts_in.wait()
    charges_in.wait()
    lives = []
    for a in range(pairs):
        charge = charges_ref[:, 2 * width * a : 2 * width * (a + 1)]
        live = jnp.where(pair_mask(counts_ref, a, sides, width), charge, jnp.zeros_like(charge))
        live_ref[a] = live
        lives.append(live)
    rim_ref[pairs] = lives[0]
    rim_ref[pairs + 1] = lives[-1]
    even_rim_ref[pairs] = jnp.where(lax.rem(position(axes), 2) == 0, lives[-1], lives[0])
    basis_in.wait()
    none = jnp.zeros_like(lives[0])
    coefs = []
    for a in range(pairs):
        live = lives[a]
        both = jnp.concatenate([jnp.where(left, live, none), jnp.where(left, none, live)], axis=0)
        coef = dot(both, basis_ref[2 * a : 2 * a + 2].reshape(2 * width, rank), NN)
        coef = jnp.concatenate([coef[:sides], coef[sides:]], axis=1).astype(jnp.bfloat16)
        rim_ref[a] = coef
        even_rim_ref[a] = coef
        coefs.append(coef)
    transfer_in.wait()
    sums = [
        dot(coefs[a], transfer_ref[2 * a : 2 * a + 2].reshape(2 * rank, rank), NN)
        for a in range(pairs)
    ]
    for a in range(own):
        parents_ref[a] = jnp.concatenate(sums[2 * a : 2 * a + 2], axis=1).astype(jnp.bfloat16)
    copies = sent_hbm.shape[0] // own
    for copy in start_all([(parents_ref, sent_hbm.at[pl.ds(own * c, own)]) for c in range(copies)], sent_sems):
        copy.wait()


def side_by_side(blocks_ref, g):
    return jnp.concatenate([blocks_ref[g, j] for j in range(blocks_ref.shape[1])], axis=1)


def mid_kernel(
    axes, live_ref, near_hbm, parent_hbm, leaf_partners_hbm, parent_partners_hbm,
    parent_packed_ref, near_out_ref, rim_near_ref, leaf_at_ref, parent_at_ref,
    near_ref, parent_ref, sems,
):
    parents, many, rank, _ = parent_ref.shape
    leaves = near_ref.shape[0]
    width = near_ref.shape[2]
    pairs = leaves // 2
    started = start_all(
        [(near_hbm, near_ref)]
        + [(parent_hbm.at[pl.ds(4 * i, 4)], parent_ref.at[pl.ds(4 * i, 4)]) for i in range(parents // 4)]
        + [(leaf_partners_hbm, leaf_at_ref), (parent_partners_hbm, parent_at_ref)],
        sems,
    )
    near_in = started[0]
    parent_in = started[1:-2]
    near_in.wait()
    rim_near_ref[0] = near_ref[0, 0]
    rim_near_ref[1] = near_ref[leaves - 1, 2]
    for a in range(pairs):
        here = live_ref[a]
        even = dot(here, jnp.concatenate([near_ref[2 * a, 1], near_ref[2 * a, 2]], axis=1), NT)
        odd = dot(here, jnp.concatenate([near_ref[2 * a + 1, 0], near_ref[2 * a + 1, 1]], axis=1), NT)
        if a > 0:
            even = even + dot(live_ref[a - 1][:, width:], near_ref[2 * a, 0], NT)
        if a < pairs - 1:
            odd = odd + dot(live_ref[a + 1][:, :width], near_ref[2 * a + 1, 2], NT)
        near_out_ref[a] = jnp.concatenate([even, odd], axis=1)

    for i, copy in enumerate(parent_in):
        copy.wait()
        for q in range(4 * i, 4 * i + 4):
            parent_packed_ref[q] = side_by_side(parent_ref, q)
    for copy in started[-2:]:
        copy.wait()
    wanted = leaf_at_ref[...] + (1 - position(axes)) * leaves
    leaf_at_ref[...] = wanted ^ (lax.broadcasted_iota(jnp.int32, wanted.shape, 0) & 1)
    inner = lax.axis_size(axes[2])
    outer = lax.axis_size(axes[1])
    wanted = mod(parent_at_ref[...], outer * inner * parents)
    source = div(wanted, parents)
    wanted = (mod(source, inner) * outer + div(source, inner)) * parents + mod(wanted, parents)
    parent_at_ref[...] = wanted ^ (lax.broadcasted_iota(jnp.int32, wanted.shape, 1) & 1)


def halves_kernel(axis, whole_ref, own_ref, at_ref, first_ref, second_ref):
    del at_ref
    own, half = own_ref.shape[0], first_ref.shape[0]
    count = lax.axis_size(axis)
    for t in range(2 * half):
        source = lax.rem(lax.axis_index(axis) + 1 + t // own, count) * own + t % own
        (first_ref if t < half else second_ref)[t % half] = whole_ref[source]


def spread_pair(table_ref, at, pair, width):
    table_ref[at] = pair
    table_ref[at + 1] = swap(pair, width)


def picked(table_ref, rows, left):
    return jnp.concatenate(
        [
            jnp.where(left, table_ref[rows[j]], table_ref[rows[j + 1]])
            for j in range(0, len(rows), 2)
        ],
        axis=1,
    )


def leaf_kernel(
    axes, at_vmem, rim_ref, even_ref, odd_ref, rim_near_ref, coupling_hbm, transfer_hbm, basis_hbm,
    far_ref, edge_ref, transfer_ref, basis_packed_ref, table_ref, at_ref, coupling_ref, packed_ref, basis_ref, sems,
):
    leaves, many, rank, _ = coupling_ref.shape
    chunks = [(at, 4) for at in range(0, leaves - 4, 4)] + [(leaves - 4, 2), (leaves - 2, 2)]
    at_in, *coupling_in, transfer_in, basis_in = start_all(
        [(at_vmem, at_ref)]
        + [(coupling_hbm.at[pl.ds(at, size)], coupling_ref.at[pl.ds(at, size)]) for at, size in chunks]
        + [(transfer_hbm, transfer_ref), (basis_hbm, basis_ref)],
        sems,
    )
    width = rim_near_ref.shape[1]
    pairs = leaves // 2
    sides = rim_ref.shape[1]
    left = left_half(sides, rank)
    parity = lax.rem(position(axes), 2)
    for ref, base in (
        (rim_ref, leaves), (even_ref, 2 * leaves * (1 - parity)), (odd_ref, 2 * leaves * parity),
    ):
        for a in range(pairs):
            spread_pair(table_ref, base + 2 * a, ref[a], rank)
    before = jnp.where(parity == 1, even_ref[pairs], odd_ref[pairs + 1])
    after = jnp.where(parity == 1, odd_ref[pairs], even_ref[pairs])
    low = dot(before[:, width:], rim_near_ref[0], NT)
    high = dot(after[:, :width], rim_near_ref[1], NT)
    edge_ref[0] = jnp.concatenate([low, jnp.zeros_like(low)], axis=1)
    edge_ref[1] = jnp.concatenate([jnp.zeros_like(high), high], axis=1)
    at_in.wait()
    ready = []
    for i in range(len(chunks) + 1):
        now, ready = ready, []
        if i < len(chunks):
            coupling_in[i].wait()
            ready = range(chunks[i][0], sum(chunks[i]))
            for g in ready:
                packed_ref[g] = side_by_side(coupling_ref, g)
        fars = []
        for g in now:
            rows = [at_ref[j, g] for j in range(many)]
            fars.append(dot(picked(table_ref, rows, left), packed_ref[g], NT))
            if g % 2 == 1:
                far_ref[g // 2] = jnp.concatenate(fars[-2:], axis=1)
    basis_in.wait()
    for a in range(pairs):
        basis_packed_ref[a] = jnp.concatenate([basis_ref[2 * a], basis_ref[2 * a + 1]], axis=1)
    transfer_in.wait()


def down_kernel(
    axes, at_vmem, same_ref, other_own_ref, other_refs, packed_ref, counts_hbm,
    far_ref, near_ref, edge_ref, transfer_ref, basis_ref,
    out_hbm, table_ref, at_ref, local_ref, down_ref, counts_ref, out_ref, sems, out_sems,
):
    at_in, counts_in = start_all([(at_vmem, at_ref), (counts_hbm, counts_ref)], sems)
    parents, many = at_ref.shape
    rank = packed_ref.shape[1]
    width = basis_ref.shape[1]
    sides = same_ref.shape[1]
    half = 2 * same_ref.shape[0]
    left = left_half(sides, rank)
    parity, mine, count = lax.axis_index(axes[1]), lax.axis_index(axes[0]), lax.axis_size(axes[0])
    own, piece = other_own_ref.shape[0], other_refs[0].shape[0]
    for t in range(count * own):
        spread_pair(table_ref, half * parity + 2 * t, same_ref[t], rank)
    for t in range(own):
        spread_pair(table_ref, half * (1 - parity) + 2 * (mine * own + t), other_own_ref[t], rank)
    for t in range(2 * piece):
        place = lax.rem(mine + 1 + t // own, count) * own + t % own
        spread_pair(table_ref, half * (1 - parity) + 2 * place, other_refs[t // piece][t % piece], rank)
    at_in.wait()
    for q in range(parents):
        rows = [at_ref[q, j] for j in range(many)]
        far = dot(picked(table_ref, rows, left), packed_ref[q], NT)
        down_ref[q] = far.astype(jnp.bfloat16)
    for q in range(parents):
        local = far_ref[q] + dot(down_ref[q], transfer_ref[2 * q : 2 * q + 2].reshape(2 * rank, rank), NT)
        local_ref[q] = local.astype(jnp.bfloat16)
    counts_in.wait()
    sent = []
    for q in range(parents):
        local = local_ref[q]
        none = jnp.zeros_like(local)
        both = jnp.concatenate([jnp.where(left, local, none), jnp.where(left, none, local)], axis=0)
        total = dot(both, basis_ref[q], NT)
        total = jnp.concatenate([total[:sides], total[sides:]], axis=1) + near_ref[q]
        if q == 0:
            total = total + edge_ref[0]
        if q == parents - 1:
            total = total + edge_ref[1]
        total = jnp.where(pair_mask(counts_ref, q, sides, width), total, jnp.zeros_like(total))
        out_ref[:, 2 * width * q : 2 * width * (q + 1)] = total.astype(out_ref.dtype)
        if (q + 1) % 4 == 0:
            lanes = pl.ds(2 * width * (q - 3), 8 * width)
            sent.append(pltpu.make_async_copy(out_ref.at[:, lanes], out_hbm.at[:, lanes], out_sems.at[q // 4]))
            sent[-1].start()
    for copy in sent:
        copy.wait()


def per_device(
    charges,
    panel_counts,
    basis,
    transfer,
    leaf_coupling,
    leaf_partners,
    near_blocks,
    parent_coupling,
    parent_partners,
):
    leaves, width, rank = basis.shape
    sides = charges.shape[1]
    parents, many = parent_partners.shape
    pairs = leaves // 2
    own = pairs // 2
    axes = ("gx", "gz", "gp")
    n = lax.axis_size("gz") * lax.axis_size("gp")
    total = n * lax.axis_size("gx")
    bf16, f32 = jnp.bfloat16, jnp.float32
    keep = lambda *arrays: [pltpu.with_memory_space_constraint(a, pltpu.HBM) for a in arrays]
    shape = pltpu.VMEM
    dma = lambda count: pltpu.SemaphoreType.DMA((count,))
    params = lambda mib: pltpu.CompilerParams(vmem_limit_bytes=mib * 2**20)

    rim, even_rim, live, parent_coef, sent = pl.pallas_call(
        functools.partial(up_kernel, axes),
        name="up",
        out_shape=[
            shape((pairs + 2, sides, 2 * rank), bf16),
            shape((pairs + 1, sides, 2 * rank), bf16),
            shape((pairs, sides, 2 * width), bf16),
            shape((own, sides, 2 * rank), bf16),
            pltpu.HBM((n // 2 * own, sides, 2 * rank), bf16),
        ],
        in_specs=[HBM] * 4,
        out_specs=[VMEM] * 4 + [HBM],
        scratch_shapes=[
            pltpu.SMEM((leaves,), jnp.int32),
            pltpu.VMEM((sides, leaves * width), bf16),
            pltpu.VMEM((leaves, width, rank), bf16),
            pltpu.VMEM((leaves, rank, rank), bf16),
            dma(4),
            dma(n // 2),
        ],
        compiler_params=params(8),
    )(*keep(panel_counts, charges.T, basis, transfer))

    even = lax.ppermute(even_rim, axes, [(i, i ^ 1) for i in range(total)])
    steps = [(i, i + 1) for i in range(1, total - 1, 2)]
    odd = lax.ppermute(rim, axes, steps + [(b, a) for a, b in steps])
    same = lax.all_to_all(sent, "gz", 0, 0, tiled=True)

    parent_packed, near, rim_near, leaf_at, parent_at = pl.pallas_call(
        functools.partial(mid_kernel, axes),
        name="mid",
        out_shape=[
            shape((parents, rank, many * rank), bf16),
            shape((pairs, sides, 2 * width), f32),
            shape((2, width, width), bf16),
            shape((many, leaves), jnp.int32),
            shape((parents, many), jnp.int32),
        ],
        in_specs=[VMEM] + [HBM] * 4,
        out_specs=[VMEM] * 5,
        scratch_shapes=[
            pltpu.VMEM(near_blocks.shape, bf16),
            pltpu.VMEM(parent_coupling.shape, bf16),
            dma(3 + parents // 4),
        ],
        compiler_params=params(12),
    )(live, *keep(near_blocks, parent_coupling, leaf_partners.T, parent_partners))

    other_own = lax.ppermute(parent_coef, "gp", [(0, 1), (1, 0)])
    piece = shape(((n // 2 - 1) * own // 2, sides, 2 * rank), bf16)
    pieces = pl.pallas_call(
        functools.partial(halves_kernel, "gz"),
        name="halves",
        out_shape=[piece, piece],
        in_specs=[VMEM, VMEM, VMEM],
        out_specs=[VMEM, VMEM],
        compiler_params=params(4),
    )(same, other_own, parent_at)
    other = [lax.ppermute(piece, "gp", [(0, 1), (1, 0)]) for piece in pieces]

    far, edge, transfer_in, basis_in = pl.pallas_call(
        functools.partial(leaf_kernel, axes),
        name="leaf",
        out_shape=[
            shape((pairs, sides, 2 * rank), f32),
            shape((2, sides, 2 * width), f32),
            shape(transfer.shape, bf16),
            shape((pairs, width, 2 * rank), bf16),
        ],
        in_specs=[VMEM] * 5 + [HBM] * 3,
        out_specs=[VMEM] * 4,
        scratch_shapes=[
            pltpu.VMEM((3 * leaves, sides, 2 * rank), bf16),
            pltpu.SMEM((many, leaves), jnp.int32),
            pltpu.VMEM(leaf_coupling.shape, bf16),
            pltpu.VMEM((leaves, rank, many * rank), bf16),
            pltpu.VMEM(basis.shape, bf16),
            dma(4 + leaves // 4),
        ],
        compiler_params=params(20),
    )(leaf_at, rim, even, odd, rim_near, *keep(leaf_coupling, transfer, basis))

    out = pl.pallas_call(
        functools.partial(down_kernel, axes[1:]),
        name="down",
        out_shape=pltpu.HBM((sides, leaves * width), bf16),
        in_specs=[VMEM, VMEM, VMEM, [VMEM] * 2, VMEM, HBM] + [VMEM] * 5,
        out_specs=HBM,
        scratch_shapes=[
            pltpu.VMEM((n * parents, sides, 2 * rank), bf16),
            pltpu.SMEM((parents, many), jnp.int32),
            pltpu.VMEM((pairs, sides, 2 * rank), bf16),
            pltpu.VMEM((parents, sides, rank), bf16),
            pltpu.SMEM((leaves,), jnp.int32),
            pltpu.VMEM((sides, leaves * width), bf16),
            dma(2),
            dma(parents // 4),
        ],
        compiler_params=params(12),
    )(parent_at, same, other_own, other, parent_packed, *keep(panel_counts), far, near, edge, transfer_in, basis_in)
    return out.T


def solution(mesh):
    outer, inner = mesh.devices.shape
    split = jax.sharding.Mesh(mesh.devices.reshape(outer, inner // 2, 2), ("gx", "gz", "gp"))
    leaves = ("gx", "gz", "gp")
    in_specs = (
        P(leaves, None),
        P(leaves),
        P(leaves, None, None),
        P(leaves, None, None),
        P(leaves, None, None, None),
        P(leaves, None),
        P(leaves, None, None, None),
        P(leaves, None, None, None),
        P(leaves, None),
    )
    return jax.shard_map(
        per_device, mesh=split, in_specs=in_specs, out_specs=P(leaves, None), check_vma=False
    )
```

```python
import functools

import jax
import jax.numpy as jnp
from jax import lax
from jax.experimental import pallas as pl
from jax.experimental.pallas import tpu as pltpu
from jax.sharding import PartitionSpec as P

VMEM = pl.BlockSpec(memory_space=pltpu.VMEM)
HBM = pl.BlockSpec(memory_space=pltpu.HBM)
NN = (((1,), (0,)), ((), ()))
NT = (((1,), (1,)), ((), ()))


def dot(a, b, dims):
    return lax.dot_general(a, b, dims, preferred_element_type=jnp.float32)


def left_half(sides, width):
    return lax.broadcasted_iota(jnp.int32, (sides, 2 * width), 1) < width


def pair_mask(counts_ref, pair, sides, width):
    lane = lax.broadcasted_iota(jnp.int32, (sides, 2 * width), 1)
    left = lane < width
    count = jnp.where(left, counts_ref[2 * pair], counts_ref[2 * pair + 1])
    return jnp.where(left, lane, lane - width) < count


def swap(pair, width):
    return jnp.concatenate([pair[:, width:], pair[:, :width]], axis=1)


def mod(x, m):
    return x & (m - 1) if m & (m - 1) == 0 else lax.rem(x, m)


def div(x, m):
    return x >> (m.bit_length() - 1) if m & (m - 1) == 0 else x // m


def position(axes):
    index = 0
    for axis in axes:
        index = index * lax.axis_size(axis) + lax.axis_index(axis)
    return index


def start_all(copies, sems):
    started = [pltpu.make_async_copy(src, dst, sems.at[i]) for i, (src, dst) in enumerate(copies)]
    for copy in started:
        copy.start()
    return started


def up_kernel(
    counts_hbm, charges_hbm, basis_hbm, transfer_hbm,
    rim_ref, even_rim_ref, live_ref, sent_hbm,
    counts_ref, charges_ref, basis_ref, transfer_ref, sems, sent_sems,
):
    counts_in, charges_in, basis_in, transfer_in = start_all(
        [
            (counts_hbm, counts_ref), (charges_hbm, charges_ref),
            (basis_hbm, basis_ref), (transfer_hbm, transfer_ref),
        ],
        sems,
    )
    sides = charges_ref.shape[0]
    leaves, width, rank = basis_ref.shape
    pairs = leaves // 2
    own = pairs // 2
    left = left_half(sides, width)
    counts_in.wait()
    charges_in.wait()
    lives = []
    for a in range(pairs):
        charge = charges_ref[:, 2 * width * a : 2 * width * (a + 1)]
        live = jnp.where(pair_mask(counts_ref, a, sides, width), charge, jnp.zeros_like(charge))
        live_ref[a] = live
        lives.append(live)
    for ref in (rim_ref, even_rim_ref):
        ref[pairs] = lives[0]
        ref[pairs + 1] = lives[-1]
    basis_in.wait()
    none = jnp.zeros_like(lives[0])
    coefs = []
    for a in range(pairs):
        live = lives[a]
        both = jnp.concatenate([jnp.where(left, live, none), jnp.where(left, none, live)], axis=0)
        coef = dot(both, basis_ref[2 * a : 2 * a + 2].reshape(2 * width, rank), NN)
        coef = jnp.concatenate([coef[:sides], coef[sides:]], axis=1).astype(jnp.bfloat16)
        rim_ref[a] = coef
        even_rim_ref[a] = coef
        coefs.append(coef)
    transfer_in.wait()
    sums = [
        dot(coefs[a], transfer_ref[2 * a : 2 * a + 2].reshape(2 * rank, rank), NN)
        for a in range(pairs)
    ]
    for a in range(own):
        even_rim_ref[pairs + 2 + a] = jnp.concatenate(sums[2 * a : 2 * a + 2], axis=1).astype(jnp.bfloat16)
    copies = sent_hbm.shape[0] // own
    block = even_rim_ref.at[pl.ds(pairs + 2, own)]
    for copy in start_all([(block, sent_hbm.at[pl.ds(own * c, own)]) for c in range(copies)], sent_sems):
        copy.wait()


def side_by_side(blocks_ref, g):
    return jnp.concatenate([blocks_ref[g, j] for j in range(blocks_ref.shape[1])], axis=1)


def mid_kernel(
    axes, live_ref, near_hbm, parent_hbm, leaf_partners_hbm, parent_partners_hbm,
    parent_packed_ref, near_out_ref, rim_near_ref, leaf_at_ref, parent_at_ref,
    near_ref, parent_ref, sems,
):
    parents, many, rank, _ = parent_ref.shape
    leaves = near_ref.shape[0]
    width = near_ref.shape[2]
    pairs = leaves // 2
    started = start_all(
        [(near_hbm, near_ref)]
        + [(parent_hbm.at[pl.ds(4 * i, 4)], parent_ref.at[pl.ds(4 * i, 4)]) for i in range(parents // 4)]
        + [(leaf_partners_hbm, leaf_at_ref), (parent_partners_hbm, parent_at_ref)],
        sems,
    )
    near_in = started[0]
    parent_in = started[1:-2]
    near_in.wait()
    rim_near_ref[0] = near_ref[0, 0]
    rim_near_ref[1] = near_ref[leaves - 1, 2]
    for a in range(pairs):
        here = live_ref[a]
        even = dot(here, jnp.concatenate([near_ref[2 * a, 1], near_ref[2 * a, 2]], axis=1), NT)
        odd = dot(here, jnp.concatenate([near_ref[2 * a + 1, 0], near_ref[2 * a + 1, 1]], axis=1), NT)
        if a > 0:
            even = even + dot(live_ref[a - 1][:, width:], near_ref[2 * a, 0], NT)
        if a < pairs - 1:
            odd = odd + dot(live_ref[a + 1][:, :width], near_ref[2 * a + 1, 2], NT)
        near_out_ref[a] = jnp.concatenate([even, odd], axis=1)

    for i, copy in enumerate(parent_in):
        copy.wait()
        for q in range(4 * i, 4 * i + 4):
            parent_packed_ref[q] = side_by_side(parent_ref, q)
    for copy in started[-2:]:
        copy.wait()
    wanted = leaf_at_ref[...] + (1 - position(axes)) * leaves
    leaf_at_ref[...] = wanted ^ (lax.broadcasted_iota(jnp.int32, wanted.shape, 0) & 1)
    inner = lax.axis_size(axes[2])
    outer = lax.axis_size(axes[1])
    wanted = mod(parent_at_ref[...], outer * inner * parents)
    source = div(wanted, parents)
    wanted = (mod(source, inner) * outer + div(source, inner)) * parents + mod(wanted, parents)
    parent_at_ref[...] = wanted ^ (lax.broadcasted_iota(jnp.int32, wanted.shape, 1) & 1)


def halves_kernel(axis, whole_ref, at_ref, first_ref, second_ref):
    del at_ref
    count, half = lax.axis_size(axis), first_ref.shape[0]
    own = whole_ref.shape[0] // count
    for t in range(2 * half):
        source = lax.rem(lax.axis_index(axis) + 1 + t // own, count) * own + t % own
        (first_ref if t < half else second_ref)[t % half] = whole_ref[source]


def spread_pair(table_ref, at, pair, width):
    table_ref[at] = pair
    table_ref[at + 1] = swap(pair, width)


def picked(table_ref, rows, left):
    return jnp.concatenate(
        [
            jnp.where(left, table_ref[rows[j]], table_ref[rows[j + 1]])
            for j in range(0, len(rows), 2)
        ],
        axis=1,
    )


def leaf_kernel(
    axes, at_vmem, rim_ref, even_ref, odd_ref, rim_near_ref, coupling_hbm, transfer_hbm, basis_hbm,
    far_ref, edge_ref, transfer_ref, basis_packed_ref, table_ref, at_ref, coupling_ref, packed_ref, basis_ref, sems,
):
    leaves, many, rank, _ = coupling_ref.shape
    chunks = [(at, 4) for at in range(0, leaves - 4, 4)] + [(leaves - 4, 2), (leaves - 2, 2)]
    at_in, *coupling_in, transfer_in, basis_in = start_all(
        [(at_vmem, at_ref)]
        + [(coupling_hbm.at[pl.ds(at, size)], coupling_ref.at[pl.ds(at, size)]) for at, size in chunks]
        + [(transfer_hbm, transfer_ref), (basis_hbm, basis_ref)],
        sems,
    )
    width = rim_near_ref.shape[1]
    pairs = leaves // 2
    sides = rim_ref.shape[1]
    left = left_half(sides, rank)
    parity = lax.rem(position(axes), 2)
    for ref, base in (
        (rim_ref, leaves), (even_ref, 2 * leaves * (1 - parity)), (odd_ref, 2 * leaves * parity),
    ):
        for a in range(pairs):
            spread_pair(table_ref, base + 2 * a, ref[a], rank)
    before = jnp.where(parity == 1, even_ref[pairs + 1], odd_ref[pairs + 1])
    after = jnp.where(parity == 1, odd_ref[pairs], even_ref[pairs])
    low = dot(before[:, width:], rim_near_ref[0], NT)
    high = dot(after[:, :width], rim_near_ref[1], NT)
    edge_ref[0] = jnp.concatenate([low, jnp.zeros_like(low)], axis=1)
    edge_ref[1] = jnp.concatenate([jnp.zeros_like(high), high], axis=1)
    at_in.wait()
    ready = []
    for i in range(len(chunks) + 1):
        now, ready = ready, []
        if i < len(chunks):
            coupling_in[i].wait()
            ready = range(chunks[i][0], sum(chunks[i]))
            for g in ready:
                packed_ref[g] = side_by_side(coupling_ref, g)
        fars = []
        for g in now:
            rows = [at_ref[j, g] for j in range(many)]
            fars.append(dot(picked(table_ref, rows, left), packed_ref[g], NT))
            if g % 2 == 1:
                far_ref[g // 2] = jnp.concatenate(fars[-2:], axis=1)
    basis_in.wait()
    for a in range(pairs):
        basis_packed_ref[a] = jnp.concatenate([basis_ref[2 * a], basis_ref[2 * a + 1]], axis=1)
    transfer_in.wait()


def down_kernel(
    axes, at_vmem, same_ref, even_ref, other_refs, packed_ref, counts_hbm,
    far_ref, near_ref, edge_ref, transfer_ref, basis_ref,
    out_hbm, table_ref, at_ref, local_ref, down_ref, counts_ref, out_ref, sems, out_sems,
):
    at_in, counts_in = start_all([(at_vmem, at_ref), (counts_hbm, counts_ref)], sems)
    parents, many = at_ref.shape
    rank = packed_ref.shape[1]
    width = basis_ref.shape[1]
    sides = same_ref.shape[1]
    half = 2 * same_ref.shape[0]
    left = left_half(sides, rank)
    parity, mine, count = lax.axis_index(axes[1]), lax.axis_index(axes[0]), lax.axis_size(axes[0])
    own, piece = same_ref.shape[0] // count, other_refs[0].shape[0]
    start = even_ref.shape[0] - own
    for t in range(count * own):
        spread_pair(table_ref, half * parity + 2 * t, same_ref[t], rank)
    for t in range(own):
        spread_pair(table_ref, half * (1 - parity) + 2 * (mine * own + t), even_ref[start + t], rank)
    for t in range(2 * piece):
        place = lax.rem(mine + 1 + t // own, count) * own + t % own
        spread_pair(table_ref, half * (1 - parity) + 2 * place, other_refs[t // piece][t % piece], rank)
    at_in.wait()
    for q in range(parents):
        rows = [at_ref[q, j] for j in range(many)]
        far = dot(picked(table_ref, rows, left), packed_ref[q], NT)
        down_ref[q] = far.astype(jnp.bfloat16)
    for q in range(parents):
        local = far_ref[q] + dot(down_ref[q], transfer_ref[2 * q : 2 * q + 2].reshape(2 * rank, rank), NT)
        local_ref[q] = local.astype(jnp.bfloat16)
    counts_in.wait()
    sent = []
    for q in range(parents):
        local = local_ref[q]
        none = jnp.zeros_like(local)
        both = jnp.concatenate([jnp.where(left, local, none), jnp.where(left, none, local)], axis=0)
        total = dot(both, basis_ref[q], NT)
        total = jnp.concatenate([total[:sides], total[sides:]], axis=1) + near_ref[q]
        if q == 0:
            total = total + edge_ref[0]
        if q == parents - 1:
            total = total + edge_ref[1]
        total = jnp.where(pair_mask(counts_ref, q, sides, width), total, jnp.zeros_like(total))
        out_ref[:, 2 * width * q : 2 * width * (q + 1)] = total.astype(out_ref.dtype)
        if (q + 1) % 4 == 0:
            lanes = pl.ds(2 * width * (q - 3), 8 * width)
            sent.append(pltpu.make_async_copy(out_ref.at[:, lanes], out_hbm.at[:, lanes], out_sems.at[q // 4]))
            sent[-1].start()
    for copy in sent:
        copy.wait()


def per_device(
    charges,
    panel_counts,
    basis,
    transfer,
    leaf_coupling,
    leaf_partners,
    near_blocks,
    parent_coupling,
    parent_partners,
):
    leaves, width, rank = basis.shape
    sides = charges.shape[1]
    parents, many = parent_partners.shape
    pairs = leaves // 2
    own = pairs // 2
    axes = ("gx", "gz", "gp")
    n = lax.axis_size("gz") * lax.axis_size("gp")
    total = n * lax.axis_size("gx")
    bf16, f32 = jnp.bfloat16, jnp.float32
    keep = lambda *arrays: [pltpu.with_memory_space_constraint(a, pltpu.HBM) for a in arrays]
    shape = pltpu.VMEM
    dma = lambda count: pltpu.SemaphoreType.DMA((count,))
    params = lambda mib: pltpu.CompilerParams(vmem_limit_bytes=mib * 2**20)

    rim, even_rim, live, sent = pl.pallas_call(
        up_kernel,
        name="up",
        out_shape=[
            shape((pairs + 2, sides, 2 * rank), bf16),
            shape((pairs + 2 + own, sides, 2 * rank), bf16),
            shape((pairs, sides, 2 * width), bf16),
            pltpu.HBM((n // 2 * own, sides, 2 * rank), bf16),
        ],
        in_specs=[HBM] * 4,
        out_specs=[VMEM, VMEM, VMEM, HBM],
        scratch_shapes=[
            pltpu.SMEM((leaves,), jnp.int32),
            pltpu.VMEM((sides, leaves * width), bf16),
            pltpu.VMEM((leaves, width, rank), bf16),
            pltpu.VMEM((leaves, rank, rank), bf16),
            dma(4),
            dma(n // 2),
        ],
        compiler_params=params(8),
    )(*keep(panel_counts, charges.T, basis, transfer))

    even = lax.ppermute(even_rim, axes, [(i, i ^ 1) for i in range(total)])
    steps = [(i, i + 1) for i in range(1, total - 1, 2)]
    odd = lax.ppermute(rim, axes, steps + [(b, a) for a, b in steps])
    same = lax.all_to_all(sent, "gz", 0, 0, tiled=True)

    parent_packed, near, rim_near, leaf_at, parent_at = pl.pallas_call(
        functools.partial(mid_kernel, axes),
        name="mid",
        out_shape=[
            shape((parents, rank, many * rank), bf16),
            shape((pairs, sides, 2 * width), f32),
            shape((2, width, width), bf16),
            shape((many, leaves), jnp.int32),
            shape((parents, many), jnp.int32),
        ],
        in_specs=[VMEM] + [HBM] * 4,
        out_specs=[VMEM] * 5,
        scratch_shapes=[
            pltpu.VMEM(near_blocks.shape, bf16),
            pltpu.VMEM(parent_coupling.shape, bf16),
            dma(3 + parents // 4),
        ],
        compiler_params=params(12),
    )(live, *keep(near_blocks, parent_coupling, leaf_partners.T, parent_partners))

    piece = shape(((n // 2 - 1) * own // 2, sides, 2 * rank), bf16)
    pieces = pl.pallas_call(
        functools.partial(halves_kernel, "gz"),
        name="halves",
        out_shape=[piece, piece],
        in_specs=[VMEM, VMEM],
        out_specs=[VMEM, VMEM],
        compiler_params=params(4),
    )(same, parent_at)
    other = [lax.ppermute(piece, "gp", [(0, 1), (1, 0)]) for piece in pieces]

    far, edge, transfer_in, basis_in = pl.pallas_call(
        functools.partial(leaf_kernel, axes),
        name="leaf",
        out_shape=[
            shape((pairs, sides, 2 * rank), f32),
            shape((2, sides, 2 * width), f32),
            shape(transfer.shape, bf16),
            shape((pairs, width, 2 * rank), bf16),
        ],
        in_specs=[VMEM] * 5 + [HBM] * 3,
        out_specs=[VMEM] * 4,
        scratch_shapes=[
            pltpu.VMEM((3 * leaves, sides, 2 * rank), bf16),
            pltpu.SMEM((many, leaves), jnp.int32),
            pltpu.VMEM(leaf_coupling.shape, bf16),
            pltpu.VMEM((leaves, rank, many * rank), bf16),
            pltpu.VMEM(basis.shape, bf16),
            dma(4 + leaves // 4),
        ],
        compiler_params=params(20),
    )(leaf_at, rim, even, odd, rim_near, *keep(leaf_coupling, transfer, basis))

    out = pl.pallas_call(
        functools.partial(down_kernel, axes[1:]),
        name="down",
        out_shape=pltpu.HBM((sides, leaves * width), bf16),
        in_specs=[VMEM, VMEM, VMEM, [VMEM] * 2, VMEM, HBM] + [VMEM] * 5,
        out_specs=HBM,
        scratch_shapes=[
            pltpu.VMEM((n * parents, sides, 2 * rank), bf16),
            pltpu.SMEM((parents, many), jnp.int32),
            pltpu.VMEM((pairs, sides, 2 * rank), bf16),
            pltpu.VMEM((parents, sides, rank), bf16),
            pltpu.SMEM((leaves,), jnp.int32),
            pltpu.VMEM((sides, leaves * width), bf16),
            dma(2),
            dma(parents // 4),
        ],
        compiler_params=params(12),
    )(parent_at, same, even, other, parent_packed, *keep(panel_counts), far, near, edge, transfer_in, basis_in)
    return out.T


def solution(mesh):
    outer, inner = mesh.devices.shape
    split = jax.sharding.Mesh(mesh.devices.reshape(outer, inner // 2, 2), ("gx", "gz", "gp"))
    leaves = ("gx", "gz", "gp")
    in_specs = (
        P(leaves, None),
        P(leaves),
        P(leaves, None, None),
        P(leaves, None, None),
        P(leaves, None, None, None),
        P(leaves, None),
        P(leaves, None, None, None),
        P(leaves, None, None, None),
        P(leaves, None),
    )
    return jax.shard_map(
        per_device, mesh=split, in_specs=in_specs, out_specs=P(leaves, None), check_vma=False
    )
```

```python
import functools

import jax
import jax.numpy as jnp
from jax import lax
from jax.experimental import pallas as pl
from jax.experimental.pallas import tpu as pltpu
from jax.sharding import PartitionSpec as P

VMEM = pl.BlockSpec(memory_space=pltpu.VMEM)
HBM = pl.BlockSpec(memory_space=pltpu.HBM)
NN = (((1,), (0,)), ((), ()))
NT = (((1,), (1,)), ((), ()))


def dot(a, b, dims):
    return lax.dot_general(a, b, dims, preferred_element_type=jnp.float32)


def left_half(sides, width):
    return lax.broadcasted_iota(jnp.int32, (sides, 2 * width), 1) < width


def pair_mask(counts_ref, pair, sides, width):
    lane = lax.broadcasted_iota(jnp.int32, (sides, 2 * width), 1)
    left = lane < width
    count = jnp.where(left, counts_ref[2 * pair], counts_ref[2 * pair + 1])
    return jnp.where(left, lane, lane - width) < count


def swap(pair, width):
    return jnp.concatenate([pair[:, width:], pair[:, :width]], axis=1)


def mod(x, m):
    return x & (m - 1) if m & (m - 1) == 0 else lax.rem(x, m)


def div(x, m):
    return x >> (m.bit_length() - 1) if m & (m - 1) == 0 else x // m


def position(axes):
    index = 0
    for axis in axes:
        index = index * lax.axis_size(axis) + lax.axis_index(axis)
    return index


def start_all(copies, sems):
    started = [pltpu.make_async_copy(src, dst, sems.at[i]) for i, (src, dst) in enumerate(copies)]
    for copy in started:
        copy.start()
    return started


def up_kernel(
    axes, counts_hbm, charges_hbm, basis_hbm, transfer_hbm,
    rim_ref, even_rim_ref, odd_rim_ref, live_ref, sent_hbm,
    counts_ref, charges_ref, basis_ref, transfer_ref, sems, sent_sems,
):
    counts_in, charges_in, basis_in, transfer_in = start_all(
        [
            (counts_hbm, counts_ref), (charges_hbm, charges_ref),
            (basis_hbm, basis_ref), (transfer_hbm, transfer_ref),
        ],
        sems,
    )
    sides = charges_ref.shape[0]
    leaves, width, rank = basis_ref.shape
    pairs = leaves // 2
    own = pairs // 2
    left = left_half(sides, width)
    counts_in.wait()
    charges_in.wait()
    lives = []
    for a in range(pairs):
        charge = charges_ref[:, 2 * width * a : 2 * width * (a + 1)]
        live = jnp.where(pair_mask(counts_ref, a, sides, width), charge, jnp.zeros_like(charge))
        live_ref[a] = live
        lives.append(live)
    for ref in (rim_ref, even_rim_ref):
        ref[pairs] = lives[0]
        ref[pairs + 1] = lives[-1]
    odd_rim_ref[pairs] = jnp.where(lax.rem(position(axes), 2) == 1, lives[-1], lives[0])
    basis_in.wait()
    none = jnp.zeros_like(lives[0])
    coefs = []
    for a in range(pairs):
        live = lives[a]
        both = jnp.concatenate([jnp.where(left, live, none), jnp.where(left, none, live)], axis=0)
        coef = dot(both, basis_ref[2 * a : 2 * a + 2].reshape(2 * width, rank), NN)
        coef = jnp.concatenate([coef[:sides], coef[sides:]], axis=1).astype(jnp.bfloat16)
        rim_ref[a] = coef
        even_rim_ref[a] = coef
        odd_rim_ref[a] = coef
        coefs.append(coef)
    transfer_in.wait()
    sums = [
        dot(coefs[a], transfer_ref[2 * a : 2 * a + 2].reshape(2 * rank, rank), NN)
        for a in range(pairs)
    ]
    for a in range(own):
        even_rim_ref[pairs + 2 + a] = jnp.concatenate(sums[2 * a : 2 * a + 2], axis=1).astype(jnp.bfloat16)
    copies = sent_hbm.shape[0] // own
    block = even_rim_ref.at[pl.ds(pairs + 2, own)]
    for copy in start_all([(block, sent_hbm.at[pl.ds(own * c, own)]) for c in range(copies)], sent_sems):
        copy.wait()


def side_by_side(blocks_ref, g):
    return jnp.concatenate([blocks_ref[g, j] for j in range(blocks_ref.shape[1])], axis=1)


def mid_kernel(
    axes, live_ref, near_hbm, parent_hbm, leaf_partners_hbm, parent_partners_hbm,
    parent_packed_ref, near_out_ref, rim_near_ref, leaf_at_ref, parent_at_ref,
    near_ref, parent_ref, sems,
):
    parents, many, rank, _ = parent_ref.shape
    leaves = near_ref.shape[0]
    width = near_ref.shape[2]
    pairs = leaves // 2
    started = start_all(
        [(near_hbm, near_ref)]
        + [(parent_hbm.at[pl.ds(4 * i, 4)], parent_ref.at[pl.ds(4 * i, 4)]) for i in range(parents // 4)]
        + [(leaf_partners_hbm, leaf_at_ref), (parent_partners_hbm, parent_at_ref)],
        sems,
    )
    near_in = started[0]
    parent_in = started[1:-2]
    near_in.wait()
    rim_near_ref[0] = near_ref[0, 0]
    rim_near_ref[1] = near_ref[leaves - 1, 2]
    for a in range(pairs):
        here = live_ref[a]
        even = dot(here, jnp.concatenate([near_ref[2 * a, 1], near_ref[2 * a, 2]], axis=1), NT)
        odd = dot(here, jnp.concatenate([near_ref[2 * a + 1, 0], near_ref[2 * a + 1, 1]], axis=1), NT)
        if a > 0:
            even = even + dot(live_ref[a - 1][:, width:], near_ref[2 * a, 0], NT)
        if a < pairs - 1:
            odd = odd + dot(live_ref[a + 1][:, :width], near_ref[2 * a + 1, 2], NT)
        near_out_ref[a] = jnp.concatenate([even, odd], axis=1)

    for i, copy in enumerate(parent_in):
        copy.wait()
        for q in range(4 * i, 4 * i + 4):
            parent_packed_ref[q] = side_by_side(parent_ref, q)
    for copy in started[-2:]:
        copy.wait()
    wanted = leaf_at_ref[...] + (1 - position(axes)) * leaves
    leaf_at_ref[...] = wanted ^ (lax.broadcasted_iota(jnp.int32, wanted.shape, 0) & 1)
    inner = lax.axis_size(axes[2])
    outer = lax.axis_size(axes[1])
    wanted = mod(parent_at_ref[...], outer * inner * parents)
    source = div(wanted, parents)
    wanted = (mod(source, inner) * outer + div(source, inner)) * parents + mod(wanted, parents)
    parent_at_ref[...] = wanted ^ (lax.broadcasted_iota(jnp.int32, wanted.shape, 1) & 1)


def halves_kernel(axis, whole_ref, at_ref, first_ref, second_ref):
    del at_ref
    count, half = lax.axis_size(axis), first_ref.shape[0]
    own = whole_ref.shape[0] // count
    for t in range(2 * half):
        source = lax.rem(lax.axis_index(axis) + 1 + t // own, count) * own + t % own
        (first_ref if t < half else second_ref)[t % half] = whole_ref[source]


def spread_pair(table_ref, at, pair, width):
    table_ref[at] = pair
    table_ref[at + 1] = swap(pair, width)


def picked(table_ref, rows, left):
    return jnp.concatenate(
        [
            jnp.where(left, table_ref[rows[j]], table_ref[rows[j + 1]])
            for j in range(0, len(rows), 2)
        ],
        axis=1,
    )


def leaf_kernel(
    axes, at_vmem, rim_ref, even_ref, ends_ref, odd_ref, rim_near_ref, coupling_hbm, transfer_hbm, basis_hbm,
    far_ref, edge_ref, transfer_ref, basis_packed_ref, table_ref, at_ref, coupling_ref, packed_ref, basis_ref, sems,
):
    leaves, many, rank, _ = coupling_ref.shape
    chunks = [(at, 4) for at in range(0, leaves, 4)]
    at_in, *coupling_in, transfer_in, basis_in = start_all(
        [(at_vmem, at_ref)]
        + [(coupling_hbm.at[pl.ds(at, size)], coupling_ref.at[pl.ds(at, size)]) for at, size in chunks]
        + [(transfer_hbm, transfer_ref), (basis_hbm, basis_ref)],
        sems,
    )
    width = rim_near_ref.shape[1]
    pairs = leaves // 2
    sides = rim_ref.shape[1]
    left = left_half(sides, rank)
    parity = lax.rem(position(axes), 2)
    row = lax.axis_size(axes[1]) * lax.axis_size(axes[2])
    at_end = lax.rem(position(axes) + 1, row) < 2
    for a in range(pairs):
        spread_pair(table_ref, leaves + 2 * a, rim_ref[a], rank)
        spread_pair(table_ref, 2 * leaves * (1 - parity) + 2 * a, even_ref[a], rank)
        odd = jnp.where(at_end, ends_ref[a], odd_ref[a])
        spread_pair(table_ref, 2 * leaves * parity + 2 * a, odd, rank)
    edge = jnp.where(at_end, jnp.where(parity == 1, ends_ref[pairs], ends_ref[pairs + 1]), odd_ref[pairs])
    before = jnp.where(parity == 1, even_ref[pairs + 1], edge)
    after = jnp.where(parity == 1, edge, even_ref[pairs])
    low = dot(before[:, width:], rim_near_ref[0], NT)
    high = dot(after[:, :width], rim_near_ref[1], NT)
    edge_ref[0] = jnp.concatenate([low, jnp.zeros_like(low)], axis=1)
    edge_ref[1] = jnp.concatenate([jnp.zeros_like(high), high], axis=1)
    at_in.wait()
    ready = []
    for i in range(len(chunks) + 1):
        now, ready = ready, []
        if i < len(chunks):
            coupling_in[i].wait()
            ready = range(chunks[i][0], sum(chunks[i]))
            for g in ready:
                packed_ref[g] = side_by_side(coupling_ref, g)
        fars = []
        for g in now:
            rows = [at_ref[j, g] for j in range(many)]
            fars.append(dot(picked(table_ref, rows, left), packed_ref[g], NT))
            if g % 2 == 1:
                far_ref[g // 2] = jnp.concatenate(fars[-2:], axis=1)
    basis_in.wait()
    for a in range(pairs):
        basis_packed_ref[a] = jnp.concatenate([basis_ref[2 * a], basis_ref[2 * a + 1]], axis=1)
    transfer_in.wait()


def down_kernel(
    axes, at_vmem, same_ref, even_ref, other_refs, packed_ref, counts_hbm,
    far_ref, near_ref, edge_ref, transfer_ref, basis_ref,
    out_ref, table_ref, at_ref, local_ref, down_ref, counts_ref, sems,
):
    at_in, counts_in = start_all([(at_vmem, at_ref), (counts_hbm, counts_ref)], sems)
    parents, many = at_ref.shape
    rank = packed_ref.shape[1]
    width = basis_ref.shape[1]
    sides = same_ref.shape[1]
    half = 2 * same_ref.shape[0]
    left = left_half(sides, rank)
    parity, mine, count = lax.axis_index(axes[1]), lax.axis_index(axes[0]), lax.axis_size(axes[0])
    own, piece = same_ref.shape[0] // count, other_refs[0].shape[0]
    start = even_ref.shape[0] - own
    for t in range(count * own):
        spread_pair(table_ref, half * parity + 2 * t, same_ref[t], rank)
    for t in range(own):
        spread_pair(table_ref, half * (1 - parity) + 2 * (mine * own + t), even_ref[start + t], rank)
    for t in range(2 * piece):
        place = lax.rem(mine + 1 + t // own, count) * own + t % own
        spread_pair(table_ref, half * (1 - parity) + 2 * place, other_refs[t // piece][t % piece], rank)
    at_in.wait()
    for q in range(parents):
        rows = [at_ref[q, j] for j in range(many)]
        far = dot(picked(table_ref, rows, left), packed_ref[q], NT)
        down_ref[q] = far.astype(jnp.bfloat16)
    for q in range(parents):
        local = far_ref[q] + dot(down_ref[q], transfer_ref[2 * q : 2 * q + 2].reshape(2 * rank, rank), NT)
        local_ref[q] = local.astype(jnp.bfloat16)
    counts_in.wait()
    for q in range(parents):
        local = local_ref[q]
        none = jnp.zeros_like(local)
        both = jnp.concatenate([jnp.where(left, local, none), jnp.where(left, none, local)], axis=0)
        total = dot(both, basis_ref[q], NT)
        total = jnp.concatenate([total[:sides], total[sides:]], axis=1) + near_ref[q]
        if q == 0:
            total = total + edge_ref[0]
        if q == parents - 1:
            total = total + edge_ref[1]
        total = jnp.where(pair_mask(counts_ref, q, sides, width), total, jnp.zeros_like(total))
        out_ref[:, 2 * width * q : 2 * width * (q + 1)] = total.astype(out_ref.dtype)


def per_device(
    charges,
    panel_counts,
    basis,
    transfer,
    leaf_coupling,
    leaf_partners,
    near_blocks,
    parent_coupling,
    parent_partners,
):
    leaves, width, rank = basis.shape
    sides = charges.shape[1]
    parents, many = parent_partners.shape
    pairs = leaves // 2
    own = pairs // 2
    axes = ("gx", "gz", "gp")
    n = lax.axis_size("gz") * lax.axis_size("gp")
    total = n * lax.axis_size("gx")
    bf16, f32 = jnp.bfloat16, jnp.float32
    keep = lambda *arrays: [pltpu.with_memory_space_constraint(a, pltpu.HBM) for a in arrays]
    shape = pltpu.VMEM
    dma = lambda count: pltpu.SemaphoreType.DMA((count,))
    params = lambda mib: pltpu.CompilerParams(vmem_limit_bytes=mib * 2**20)

    rim, even_rim, odd_rim, live, sent = pl.pallas_call(
        functools.partial(up_kernel, axes),
        name="up",
        out_shape=[
            shape((pairs + 2, sides, 2 * rank), bf16),
            shape((pairs + 2 + own, sides, 2 * rank), bf16),
            shape((pairs + 1, sides, 2 * rank), bf16),
            shape((pairs, sides, 2 * width), bf16),
            pltpu.HBM((n // 2 * own, sides, 2 * rank), bf16),
        ],
        in_specs=[HBM] * 4,
        out_specs=[VMEM] * 4 + [HBM],
        scratch_shapes=[
            pltpu.SMEM((leaves,), jnp.int32),
            pltpu.VMEM((sides, leaves * width), bf16),
            pltpu.VMEM((leaves, width, rank), bf16),
            pltpu.VMEM((leaves, rank, rank), bf16),
            dma(4),
            dma(n // 2),
        ],
        compiler_params=params(8),
    )(*keep(panel_counts, charges.T, basis, transfer))

    even = lax.ppermute(even_rim, axes, [(i, i ^ 1) for i in range(total)])
    steps = [(i, i + 1) for i in range(1, total - 1, 2)]
    both_ways = lambda pairs: pairs + [(b, a) for a, b in pairs]
    ends = lax.ppermute(rim, axes, both_ways([s for s in steps if s[1] % n == 0]))
    odd = lax.ppermute(odd_rim, axes, both_ways([s for s in steps if s[1] % n]))
    same = lax.all_to_all(sent, "gz", 0, 0, tiled=True)

    parent_packed, near, rim_near, leaf_at, parent_at = pl.pallas_call(
        functools.partial(mid_kernel, axes),
        name="mid",
        out_shape=[
            shape((parents, rank, many * rank), bf16),
            shape((pairs, sides, 2 * width), f32),
            shape((2, width, width), bf16),
            shape((many, leaves), jnp.int32),
            shape((parents, many), jnp.int32),
        ],
        in_specs=[VMEM] + [HBM] * 4,
        out_specs=[VMEM] * 5,
        scratch_shapes=[
            pltpu.VMEM(near_blocks.shape, bf16),
            pltpu.VMEM(parent_coupling.shape, bf16),
            dma(3 + parents // 4),
        ],
        compiler_params=params(12),
    )(live, *keep(near_blocks, parent_coupling, leaf_partners.T, parent_partners))

    piece = shape(((n // 2 - 1) * own // 2, sides, 2 * rank), bf16)
    pieces = pl.pallas_call(
        functools.partial(halves_kernel, "gz"),
        name="halves",
        out_shape=[piece, piece],
        in_specs=[VMEM, VMEM],
        out_specs=[VMEM, VMEM],
        compiler_params=params(4),
    )(same, parent_at)
    other = [lax.ppermute(piece, "gp", [(0, 1), (1, 0)]) for piece in pieces]

    far, edge, transfer_in, basis_in = pl.pallas_call(
        functools.partial(leaf_kernel, axes),
        name="leaf",
        out_shape=[
            shape((pairs, sides, 2 * rank), f32),
            shape((2, sides, 2 * width), f32),
            shape(transfer.shape, bf16),
            shape((pairs, width, 2 * rank), bf16),
        ],
        in_specs=[VMEM] * 6 + [HBM] * 3,
        out_specs=[VMEM] * 4,
        scratch_shapes=[
            pltpu.VMEM((3 * leaves, sides, 2 * rank), bf16),
            pltpu.SMEM((many, leaves), jnp.int32),
            pltpu.VMEM(leaf_coupling.shape, bf16),
            pltpu.VMEM((leaves, rank, many * rank), bf16),
            pltpu.VMEM(basis.shape, bf16),
            dma(3 + leaves // 4),
        ],
        compiler_params=params(20),
    )(leaf_at, rim, even, ends, odd, rim_near, *keep(leaf_coupling, transfer, basis))

    out = pl.pallas_call(
        functools.partial(down_kernel, axes[1:]),
        name="down",
        out_shape=jax.ShapeDtypeStruct((sides, leaves * width), bf16),
        in_specs=[VMEM, VMEM, VMEM, [VMEM] * 2, VMEM, HBM] + [VMEM] * 5,
        out_specs=VMEM,
        scratch_shapes=[
            pltpu.VMEM((n * parents, sides, 2 * rank), bf16),
            pltpu.SMEM((parents, many), jnp.int32),
            pltpu.VMEM((pairs, sides, 2 * rank), bf16),
            pltpu.VMEM((parents, sides, rank), bf16),
            pltpu.SMEM((leaves,), jnp.int32),
            dma(2),
        ],
        compiler_params=params(12),
    )(parent_at, same, even, other, parent_packed, *keep(panel_counts), far, near, edge, transfer_in, basis_in)
    return out.T


def solution(mesh):
    outer, inner = mesh.devices.shape
    split = jax.sharding.Mesh(mesh.devices.reshape(outer, inner // 2, 2), ("gx", "gz", "gp"))
    leaves = ("gx", "gz", "gp")
    in_specs = (
        P(leaves, None),
        P(leaves),
        P(leaves, None, None),
        P(leaves, None, None),
        P(leaves, None, None, None),
        P(leaves, None),
        P(leaves, None, None, None),
        P(leaves, None, None, None),
        P(leaves, None),
    )
    return jax.shard_map(
        per_device, mesh=split, in_specs=in_specs, out_specs=P(leaves, None), check_vma=False
    )
```

```python
import functools

import jax
import jax.numpy as jnp
from jax import lax
from jax.experimental import pallas as pl
from jax.experimental.pallas import tpu as pltpu
from jax.sharding import PartitionSpec as P

VMEM = pl.BlockSpec(memory_space=pltpu.VMEM)
HBM = pl.BlockSpec(memory_space=pltpu.HBM)
NN = (((1,), (0,)), ((), ()))
NT = (((1,), (1,)), ((), ()))


def dot(a, b, dims):
    return lax.dot_general(a, b, dims, preferred_element_type=jnp.float32)


def left_half(sides, width):
    return lax.broadcasted_iota(jnp.int32, (sides, 2 * width), 1) < width


def pair_mask(counts_ref, pair, sides, width):
    lane = lax.broadcasted_iota(jnp.int32, (sides, 2 * width), 1)
    left = lane < width
    count = jnp.where(left, counts_ref[2 * pair], counts_ref[2 * pair + 1])
    return jnp.where(left, lane, lane - width) < count


def swap(pair, width):
    return jnp.concatenate([pair[:, width:], pair[:, :width]], axis=1)


def mod(x, m):
    return x & (m - 1) if m & (m - 1) == 0 else lax.rem(x, m)


def div(x, m):
    return x >> (m.bit_length() - 1) if m & (m - 1) == 0 else x // m


def position(axes):
    index = 0
    for axis in axes:
        index = index * lax.axis_size(axis) + lax.axis_index(axis)
    return index


def start_all(copies, sems):
    started = [pltpu.make_async_copy(src, dst, sems.at[i]) for i, (src, dst) in enumerate(copies)]
    for copy in started:
        copy.start()
    return started


def up_kernel(
    counts_hbm, charges_hbm, basis_hbm, transfer_hbm,
    rim_ref, live_ref, parents_ref, sent_hbm,
    counts_ref, charges_ref, basis_ref, transfer_ref, sems, sent_sems,
):
    counts_in, charges_in, basis_in, transfer_in = start_all(
        [
            (counts_hbm, counts_ref), (charges_hbm, charges_ref),
            (basis_hbm, basis_ref), (transfer_hbm, transfer_ref),
        ],
        sems,
    )
    sides = charges_ref.shape[0]
    leaves, width, rank = basis_ref.shape
    pairs = leaves // 2
    own = pairs // 2
    left = left_half(sides, width)
    counts_in.wait()
    charges_in.wait()
    lives = []
    for a in range(pairs):
        charge = charges_ref[:, 2 * width * a : 2 * width * (a + 1)]
        live = jnp.where(pair_mask(counts_ref, a, sides, width), charge, jnp.zeros_like(charge))
        live_ref[a] = live
        lives.append(live)
    rim_ref[pairs] = lives[0]
    rim_ref[pairs + 1] = lives[-1]
    basis_in.wait()
    none = jnp.zeros_like(lives[0])
    coefs = []
    for a in range(pairs):
        live = lives[a]
        both = jnp.concatenate([jnp.where(left, live, none), jnp.where(left, none, live)], axis=0)
        coef = dot(both, basis_ref[2 * a : 2 * a + 2].reshape(2 * width, rank), NN)
        coef = jnp.concatenate([coef[:sides], coef[sides:]], axis=1).astype(jnp.bfloat16)
        rim_ref[a] = coef
        coefs.append(coef)
    transfer_in.wait()
    sums = [
        dot(coefs[a], transfer_ref[2 * a : 2 * a + 2].reshape(2 * rank, rank), NN)
        for a in range(pairs)
    ]
    for a in range(own):
        parents_ref[a] = jnp.concatenate(sums[2 * a : 2 * a + 2], axis=1).astype(jnp.bfloat16)
    copies = sent_hbm.shape[0] // own
    for copy in start_all([(parents_ref, sent_hbm.at[pl.ds(own * c, own)]) for c in range(copies)], sent_sems):
        copy.wait()


def side_by_side(blocks_ref, g):
    return jnp.concatenate([blocks_ref[g, j] for j in range(blocks_ref.shape[1])], axis=1)


def mid_kernel(
    axes, live_ref, near_hbm, parent_hbm, leaf_partners_hbm, parent_partners_hbm,
    parent_packed_ref, near_out_ref, rim_near_ref, leaf_at_ref, parent_at_ref,
    near_ref, parent_ref, sems,
):
    parents, many, rank, _ = parent_ref.shape
    leaves = near_ref.shape[0]
    width = near_ref.shape[2]
    pairs = leaves // 2
    started = start_all(
        [(near_hbm, near_ref)]
        + [(parent_hbm.at[pl.ds(4 * i, 4)], parent_ref.at[pl.ds(4 * i, 4)]) for i in range(parents // 4)]
        + [(leaf_partners_hbm, leaf_at_ref), (parent_partners_hbm, parent_at_ref)],
        sems,
    )
    near_in = started[0]
    parent_in = started[1:-2]
    near_in.wait()
    rim_near_ref[0] = near_ref[0, 0]
    rim_near_ref[1] = near_ref[leaves - 1, 2]
    for a in range(pairs):
        here = live_ref[a]
        even = dot(here, jnp.concatenate([near_ref[2 * a, 1], near_ref[2 * a, 2]], axis=1), NT)
        odd = dot(here, jnp.concatenate([near_ref[2 * a + 1, 0], near_ref[2 * a + 1, 1]], axis=1), NT)
        if a > 0:
            even = even + dot(live_ref[a - 1][:, width:], near_ref[2 * a, 0], NT)
        if a < pairs - 1:
            odd = odd + dot(live_ref[a + 1][:, :width], near_ref[2 * a + 1, 2], NT)
        near_out_ref[a] = jnp.concatenate([even, odd], axis=1)

    for i, copy in enumerate(parent_in):
        copy.wait()
        for q in range(4 * i, 4 * i + 4):
            parent_packed_ref[q] = side_by_side(parent_ref, q)
    for copy in started[-2:]:
        copy.wait()
    wanted = leaf_at_ref[...] + (1 - position(axes)) * leaves
    leaf_at_ref[...] = wanted ^ (lax.broadcasted_iota(jnp.int32, wanted.shape, 0) & 1)
    inner = lax.axis_size(axes[2])
    outer = lax.axis_size(axes[1])
    wanted = mod(parent_at_ref[...], outer * inner * parents)
    source = div(wanted, parents)
    wanted = (mod(source, inner) * outer + div(source, inner)) * parents + mod(wanted, parents)
    parent_at_ref[...] = wanted ^ (lax.broadcasted_iota(jnp.int32, wanted.shape, 1) & 1)


def halves_kernel(axis, whole_ref, own_ref, at_ref, first_ref, second_ref):
    del at_ref
    own, half = own_ref.shape[0], first_ref.shape[0]
    count = lax.axis_size(axis)
    for t in range(2 * half):
        source = lax.rem(lax.axis_index(axis) + 1 + t // own, count) * own + t % own
        (first_ref if t < half else second_ref)[t % half] = whole_ref[source]


def spread_pair(table_ref, at, pair, width):
    table_ref[at] = pair
    table_ref[at + 1] = swap(pair, width)


def picked(table_ref, rows, left):
    return jnp.concatenate(
        [
            jnp.where(left, table_ref[rows[j]], table_ref[rows[j + 1]])
            for j in range(0, len(rows), 2)
        ],
        axis=1,
    )


def leaf_kernel(
    axes, at_vmem, rim_ref, even_ref, odd_ref, rim_near_ref, coupling_hbm, transfer_hbm, basis_hbm,
    far_ref, edge_ref, transfer_ref, basis_packed_ref, table_ref, at_ref, coupling_ref, packed_ref, basis_ref, sems,
):
    leaves, many, rank, _ = coupling_ref.shape
    chunks = [(at, 4) for at in range(0, leaves, 4)]
    at_in, *coupling_in, transfer_in, basis_in = start_all(
        [(at_vmem, at_ref)]
        + [(coupling_hbm.at[pl.ds(at, size)], coupling_ref.at[pl.ds(at, size)]) for at, size in chunks]
        + [(transfer_hbm, transfer_ref), (basis_hbm, basis_ref)],
        sems,
    )
    width = rim_near_ref.shape[1]
    pairs = leaves // 2
    sides = rim_ref.shape[1]
    left = left_half(sides, rank)
    parity = lax.rem(position(axes), 2)
    for ref, base in (
        (rim_ref, leaves), (even_ref, 2 * leaves * (1 - parity)), (odd_ref, 2 * leaves * parity),
    ):
        for a in range(pairs):
            spread_pair(table_ref, base + 2 * a, ref[a], rank)
    before = jnp.where(parity == 1, even_ref[pairs + 1], odd_ref[pairs + 1])
    after = jnp.where(parity == 1, odd_ref[pairs], even_ref[pairs])
    low = dot(before[:, width:], rim_near_ref[0], NT)
    high = dot(after[:, :width], rim_near_ref[1], NT)
    edge_ref[0] = jnp.concatenate([low, jnp.zeros_like(low)], axis=1)
    edge_ref[1] = jnp.concatenate([jnp.zeros_like(high), high], axis=1)
    at_in.wait()
    ready = []
    for i in range(len(chunks) + 1):
        now, ready = ready, []
        if i < len(chunks):
            coupling_in[i].wait()
            ready = range(chunks[i][0], sum(chunks[i]))
            for g in ready:
                packed_ref[g] = side_by_side(coupling_ref, g)
        fars = []
        for g in now:
            rows = [at_ref[j, g] for j in range(many)]
            fars.append(dot(picked(table_ref, rows, left), packed_ref[g], NT))
            if g % 2 == 1:
                far_ref[g // 2] = jnp.concatenate(fars[-2:], axis=1)
    basis_in.wait()
    for a in range(pairs):
        basis_packed_ref[a] = jnp.concatenate([basis_ref[2 * a], basis_ref[2 * a + 1]], axis=1)
    transfer_in.wait()


def down_kernel(
    axes, at_vmem, same_ref, other_own_ref, other_refs, packed_ref, counts_hbm,
    far_ref, near_ref, edge_ref, transfer_ref, basis_ref,
    out_ref, table_ref, at_ref, local_ref, down_ref, counts_ref, sems,
):
    at_in, counts_in = start_all([(at_vmem, at_ref), (counts_hbm, counts_ref)], sems)
    parents, many = at_ref.shape
    rank = packed_ref.shape[1]
    width = basis_ref.shape[1]
    sides = same_ref.shape[1]
    half = 2 * same_ref.shape[0]
    left = left_half(sides, rank)
    parity, mine, count = lax.axis_index(axes[1]), lax.axis_index(axes[0]), lax.axis_size(axes[0])
    own, piece = other_own_ref.shape[0], other_refs[0].shape[0]
    for t in range(count * own):
        spread_pair(table_ref, half * parity + 2 * t, same_ref[t], rank)
    for t in range(own):
        spread_pair(table_ref, half * (1 - parity) + 2 * (mine * own + t), other_own_ref[t], rank)
    for t in range(2 * piece):
        place = lax.rem(mine + 1 + t // own, count) * own + t % own
        spread_pair(table_ref, half * (1 - parity) + 2 * place, other_refs[t // piece][t % piece], rank)
    at_in.wait()
    for q in range(parents):
        rows = [at_ref[q, j] for j in range(many)]
        far = dot(picked(table_ref, rows, left), packed_ref[q], NT)
        down_ref[q] = far.astype(jnp.bfloat16)
    for q in range(parents):
        local = far_ref[q] + dot(down_ref[q], transfer_ref[2 * q : 2 * q + 2].reshape(2 * rank, rank), NT)
        local_ref[q] = local.astype(jnp.bfloat16)
    counts_in.wait()
    for q in range(parents):
        local = local_ref[q]
        none = jnp.zeros_like(local)
        both = jnp.concatenate([jnp.where(left, local, none), jnp.where(left, none, local)], axis=0)
        total = dot(both, basis_ref[q], NT)
        total = jnp.concatenate([total[:sides], total[sides:]], axis=1) + near_ref[q]
        if q == 0:
            total = total + edge_ref[0]
        if q == parents - 1:
            total = total + edge_ref[1]
        total = jnp.where(pair_mask(counts_ref, q, sides, width), total, jnp.zeros_like(total))
        out_ref[:, 2 * width * q : 2 * width * (q + 1)] = total.astype(out_ref.dtype)


def per_device(
    charges,
    panel_counts,
    basis,
    transfer,
    leaf_coupling,
    leaf_partners,
    near_blocks,
    parent_coupling,
    parent_partners,
):
    leaves, width, rank = basis.shape
    sides = charges.shape[1]
    parents, many = parent_partners.shape
    pairs = leaves // 2
    own = pairs // 2
    axes = ("gx", "gz", "gp")
    n = lax.axis_size("gz") * lax.axis_size("gp")
    total = n * lax.axis_size("gx")
    bf16, f32 = jnp.bfloat16, jnp.float32
    keep = lambda *arrays: [pltpu.with_memory_space_constraint(a, pltpu.HBM) for a in arrays]
    shape = pltpu.VMEM
    dma = lambda count: pltpu.SemaphoreType.DMA((count,))
    params = lambda mib: pltpu.CompilerParams(vmem_limit_bytes=mib * 2**20)

    rim, live, parent_coef, sent = pl.pallas_call(
        up_kernel,
        name="up",
        out_shape=[
            shape((pairs + 2, sides, 2 * rank), bf16),
            shape((pairs, sides, 2 * width), bf16),
            shape((own, sides, 2 * rank), bf16),
            pltpu.HBM((n // 2 * own, sides, 2 * rank), bf16),
        ],
        in_specs=[HBM] * 4,
        out_specs=[VMEM, VMEM, VMEM, HBM],
        scratch_shapes=[
            pltpu.SMEM((leaves,), jnp.int32),
            pltpu.VMEM((sides, leaves * width), bf16),
            pltpu.VMEM((leaves, width, rank), bf16),
            pltpu.VMEM((leaves, rank, rank), bf16),
            dma(4),
            dma(n // 2),
        ],
        compiler_params=params(8),
    )(*keep(panel_counts, charges.T, basis, transfer))

    even = lax.ppermute(rim, axes, [(i, i ^ 1) for i in range(total)])
    steps = [(i, i + 1) for i in range(1, total - 1, 2)]
    odd = lax.ppermute(rim, axes, steps + [(b, a) for a, b in steps])
    same = lax.all_to_all(sent, "gz", 0, 0, tiled=True)

    parent_packed, near, rim_near, leaf_at, parent_at = pl.pallas_call(
        functools.partial(mid_kernel, axes),
        name="mid",
        out_shape=[
            shape((parents, rank, many * rank), bf16),
            shape((pairs, sides, 2 * width), f32),
            shape((2, width, width), bf16),
            shape((many, leaves), jnp.int32),
            shape((parents, many), jnp.int32),
        ],
        in_specs=[VMEM] + [HBM] * 4,
        out_specs=[VMEM] * 5,
        scratch_shapes=[
            pltpu.VMEM(near_blocks.shape, bf16),
            pltpu.VMEM(parent_coupling.shape, bf16),
            dma(3 + parents // 4),
        ],
        compiler_params=params(12),
    )(live, *keep(near_blocks, parent_coupling, leaf_partners.T, parent_partners))

    other_own = lax.ppermute(parent_coef, "gp", [(0, 1), (1, 0)])
    piece = shape(((n // 2 - 1) * own // 2, sides, 2 * rank), bf16)
    pieces = pl.pallas_call(
        functools.partial(halves_kernel, "gz"),
        name="halves",
        out_shape=[piece, piece],
        in_specs=[VMEM, VMEM, VMEM],
        out_specs=[VMEM, VMEM],
        compiler_params=params(4),
    )(same, other_own, parent_at)
    other = [lax.ppermute(piece, "gp", [(0, 1), (1, 0)]) for piece in pieces]

    far, edge, transfer_in, basis_in = pl.pallas_call(
        functools.partial(leaf_kernel, axes),
        name="leaf",
        out_shape=[
            shape((pairs, sides, 2 * rank), f32),
            shape((2, sides, 2 * width), f32),
            shape(transfer.shape, bf16),
            shape((pairs, width, 2 * rank), bf16),
        ],
        in_specs=[VMEM] * 5 + [HBM] * 3,
        out_specs=[VMEM] * 4,
        scratch_shapes=[
            pltpu.VMEM((3 * leaves, sides, 2 * rank), bf16),
            pltpu.SMEM((many, leaves), jnp.int32),
            pltpu.VMEM(leaf_coupling.shape, bf16),
            pltpu.VMEM((leaves, rank, many * rank), bf16),
            pltpu.VMEM(basis.shape, bf16),
            dma(3 + leaves // 4),
        ],
        compiler_params=params(20),
    )(leaf_at, rim, even, odd, rim_near, *keep(leaf_coupling, transfer, basis))

    out = pl.pallas_call(
        functools.partial(down_kernel, axes[1:]),
        name="down",
        out_shape=jax.ShapeDtypeStruct((sides, leaves * width), bf16),
        in_specs=[VMEM, VMEM, VMEM, [VMEM] * 2, VMEM, HBM] + [VMEM] * 5,
        out_specs=VMEM,
        scratch_shapes=[
            pltpu.VMEM((n * parents, sides, 2 * rank), bf16),
            pltpu.SMEM((parents, many), jnp.int32),
            pltpu.VMEM((pairs, sides, 2 * rank), bf16),
            pltpu.VMEM((parents, sides, rank), bf16),
            pltpu.SMEM((leaves,), jnp.int32),
            dma(2),
        ],
        compiler_params=params(12),
    )(parent_at, same, other_own, other, parent_packed, *keep(panel_counts), far, near, edge, transfer_in, basis_in)
    return out.T


def solution(mesh):
    outer, inner = mesh.devices.shape
    split = jax.sharding.Mesh(mesh.devices.reshape(outer, inner // 2, 2), ("gx", "gz", "gp"))
    leaves = ("gx", "gz", "gp")
    in_specs = (
        P(leaves, None),
        P(leaves),
        P(leaves, None, None),
        P(leaves, None, None),
        P(leaves, None, None, None),
        P(leaves, None),
        P(leaves, None, None, None),
        P(leaves, None, None, None),
        P(leaves, None),
    )
    return jax.shard_map(
        per_device, mesh=split, in_specs=in_specs, out_specs=P(leaves, None), check_vma=False
    )
```

```python
import functools

import jax
import jax.numpy as jnp
from jax import lax
from jax.experimental import pallas as pl
from jax.experimental.pallas import tpu as pltpu
from jax.sharding import PartitionSpec as P

VMEM = pl.BlockSpec(memory_space=pltpu.VMEM)
HBM = pl.BlockSpec(memory_space=pltpu.HBM)
NN = (((1,), (0,)), ((), ()))
NT = (((1,), (1,)), ((), ()))


def dot(a, b, dims):
    return lax.dot_general(a, b, dims, preferred_element_type=jnp.float32)


def left_half(sides, width):
    return lax.broadcasted_iota(jnp.int32, (sides, 2 * width), 1) < width


def pair_mask(counts_ref, pair, sides, width):
    lane = lax.broadcasted_iota(jnp.int32, (sides, 2 * width), 1)
    left = lane < width
    count = jnp.where(left, counts_ref[2 * pair], counts_ref[2 * pair + 1])
    return jnp.where(left, lane, lane - width) < count


def swap(pair, width):
    return jnp.concatenate([pair[:, width:], pair[:, :width]], axis=1)


def mod(x, m):
    return x & (m - 1) if m & (m - 1) == 0 else lax.rem(x, m)


def div(x, m):
    return x >> (m.bit_length() - 1) if m & (m - 1) == 0 else x // m


def position(axes):
    index = 0
    for axis in axes:
        index = index * lax.axis_size(axis) + lax.axis_index(axis)
    return index


def start_all(copies, sems):
    started = [pltpu.make_async_copy(src, dst, sems.at[i]) for i, (src, dst) in enumerate(copies)]
    for copy in started:
        copy.start()
    return started


def up_kernel(
    counts_hbm, charges_hbm, basis_hbm, transfer_hbm,
    rim_ref, live_ref, parents_ref, sent_hbm,
    counts_ref, charges_ref, basis_ref, transfer_ref, sems, sent_sems,
):
    counts_in, charges_in, basis_in, transfer_in = start_all(
        [
            (counts_hbm, counts_ref), (charges_hbm, charges_ref),
            (basis_hbm, basis_ref), (transfer_hbm, transfer_ref),
        ],
        sems,
    )
    sides = charges_ref.shape[0]
    leaves, width, rank = basis_ref.shape
    pairs = leaves // 2
    own = pairs // 2
    left = left_half(sides, width)
    counts_in.wait()
    charges_in.wait()
    lives = []
    for a in range(pairs):
        charge = charges_ref[:, 2 * width * a : 2 * width * (a + 1)]
        live = jnp.where(pair_mask(counts_ref, a, sides, width), charge, jnp.zeros_like(charge))
        live_ref[a] = live
        lives.append(live)
    rim_ref[pairs] = lives[0]
    rim_ref[pairs + 1] = lives[-1]
    basis_in.wait()
    none = jnp.zeros_like(lives[0])
    coefs = []
    for a in range(pairs):
        live = lives[a]
        both = jnp.concatenate([jnp.where(left, live, none), jnp.where(left, none, live)], axis=0)
        coef = dot(both, basis_ref[2 * a : 2 * a + 2].reshape(2 * width, rank), NN)
        coef = jnp.concatenate([coef[:sides], coef[sides:]], axis=1).astype(jnp.bfloat16)
        rim_ref[a] = coef
        coefs.append(coef)
    transfer_in.wait()
    sums = [
        dot(coefs[a], transfer_ref[2 * a : 2 * a + 2].reshape(2 * rank, rank), NN)
        for a in range(pairs)
    ]
    for a in range(own):
        parents_ref[a] = jnp.concatenate(sums[2 * a : 2 * a + 2], axis=1).astype(jnp.bfloat16)
    copies = sent_hbm.shape[0] // own
    for copy in start_all([(parents_ref, sent_hbm.at[pl.ds(own * c, own)]) for c in range(copies)], sent_sems):
        copy.wait()


def side_by_side(blocks_ref, g):
    return jnp.concatenate([blocks_ref[g, j] for j in range(blocks_ref.shape[1])], axis=1)


def mid_kernel(
    axes, live_ref, near_hbm, parent_hbm, leaf_partners_hbm, parent_partners_hbm,
    parent_packed_ref, near_out_ref, rim_near_ref, leaf_at_ref, parent_at_ref,
    near_ref, parent_ref, sems,
):
    parents, many, rank, _ = parent_ref.shape
    leaves = near_ref.shape[0]
    width = near_ref.shape[2]
    pairs = leaves // 2
    started = start_all(
        [(near_hbm, near_ref)]
        + [(parent_hbm.at[pl.ds(4 * i, 4)], parent_ref.at[pl.ds(4 * i, 4)]) for i in range(parents // 4)]
        + [(leaf_partners_hbm, leaf_at_ref), (parent_partners_hbm, parent_at_ref)],
        sems,
    )
    near_in = started[0]
    parent_in = started[1:-2]
    near_in.wait()
    rim_near_ref[0] = near_ref[0, 0]
    rim_near_ref[1] = near_ref[leaves - 1, 2]
    for a in range(pairs):
        here = live_ref[a]
        even = dot(here, jnp.concatenate([near_ref[2 * a, 1], near_ref[2 * a, 2]], axis=1), NT)
        odd = dot(here, jnp.concatenate([near_ref[2 * a + 1, 0], near_ref[2 * a + 1, 1]], axis=1), NT)
        if a > 0:
            even = even + dot(live_ref[a - 1][:, width:], near_ref[2 * a, 0], NT)
        if a < pairs - 1:
            odd = odd + dot(live_ref[a + 1][:, :width], near_ref[2 * a + 1, 2], NT)
        near_out_ref[a] = jnp.concatenate([even, odd], axis=1)

    for i, copy in enumerate(parent_in):
        copy.wait()
        for q in range(4 * i, 4 * i + 4):
            parent_packed_ref[q] = side_by_side(parent_ref, q)
    for copy in started[-2:]:
        copy.wait()
    wanted = leaf_at_ref[...] + (1 - position(axes)) * leaves
    leaf_at_ref[...] = wanted ^ (lax.broadcasted_iota(jnp.int32, wanted.shape, 0) & 1)
    inner = lax.axis_size(axes[2])
    outer = lax.axis_size(axes[1])
    wanted = mod(parent_at_ref[...], outer * inner * parents)
    source = div(wanted, parents)
    wanted = (mod(source, inner) * outer + div(source, inner)) * parents + mod(wanted, parents)
    parent_at_ref[...] = wanted ^ (lax.broadcasted_iota(jnp.int32, wanted.shape, 1) & 1)


def halves_kernel(axis, whole_ref, own_ref, at_ref, first_ref, second_ref):
    del at_ref
    own, half = own_ref.shape[0], first_ref.shape[0]
    count = lax.axis_size(axis)
    for t in range(2 * half):
        source = lax.rem(lax.axis_index(axis) + 1 + t // own, count) * own + t % own
        (first_ref if t < half else second_ref)[t % half] = whole_ref[source]


def spread_pair(table_ref, at, pair, width):
    table_ref[at] = pair
    table_ref[at + 1] = swap(pair, width)


def picked(table_ref, rows, left):
    return jnp.concatenate(
        [
            jnp.where(left, table_ref[rows[j]], table_ref[rows[j + 1]])
            for j in range(0, len(rows), 2)
        ],
        axis=1,
    )


def leaf_kernel(
    axes, at_vmem, rim_ref, even_ref, odd_ref, rim_near_ref, same_ref, other_own_ref,
    coupling_hbm, transfer_hbm, basis_hbm,
    far_ref, edge_ref, transfer_ref, basis_packed_ref, parent_table_ref, table_ref, at_ref, coupling_ref, packed_ref, basis_ref, sems,
):
    leaves, many, rank, _ = coupling_ref.shape
    chunks = [(at, 4) for at in range(0, leaves, 4)]
    at_in, *coupling_in, transfer_in, basis_in = start_all(
        [(at_vmem, at_ref)]
        + [(coupling_hbm.at[pl.ds(at, size)], coupling_ref.at[pl.ds(at, size)]) for at, size in chunks]
        + [(transfer_hbm, transfer_ref), (basis_hbm, basis_ref)],
        sems,
    )
    width = rim_near_ref.shape[1]
    pairs = leaves // 2
    sides = rim_ref.shape[1]
    left = left_half(sides, rank)
    parity = lax.rem(position(axes), 2)
    for ref, base in (
        (rim_ref, leaves), (even_ref, 2 * leaves * (1 - parity)), (odd_ref, 2 * leaves * parity),
    ):
        for a in range(pairs):
            spread_pair(table_ref, base + 2 * a, ref[a], rank)
    own, half = other_own_ref.shape[0], 2 * same_ref.shape[0]
    for t in range(same_ref.shape[0]):
        spread_pair(parent_table_ref, half * parity + 2 * t, same_ref[t], rank)
    for t in range(own):
        place = lax.axis_index(axes[1]) * own + t
        spread_pair(parent_table_ref, half * (1 - parity) + 2 * place, other_own_ref[t], rank)
    before = jnp.where(parity == 1, even_ref[pairs + 1], odd_ref[pairs + 1])
    after = jnp.where(parity == 1, odd_ref[pairs], even_ref[pairs])
    low = dot(before[:, width:], rim_near_ref[0], NT)
    high = dot(after[:, :width], rim_near_ref[1], NT)
    edge_ref[0] = jnp.concatenate([low, jnp.zeros_like(low)], axis=1)
    edge_ref[1] = jnp.concatenate([jnp.zeros_like(high), high], axis=1)
    at_in.wait()
    ready = []
    for i in range(len(chunks) + 1):
        now, ready = ready, []
        if i < len(chunks):
            coupling_in[i].wait()
            ready = range(chunks[i][0], sum(chunks[i]))
            for g in ready:
                packed_ref[g] = side_by_side(coupling_ref, g)
        fars = []
        for g in now:
            rows = [at_ref[j, g] for j in range(many)]
            fars.append(dot(picked(table_ref, rows, left), packed_ref[g], NT))
            if g % 2 == 1:
                far_ref[g // 2] = jnp.concatenate(fars[-2:], axis=1)
    basis_in.wait()
    for a in range(pairs):
        basis_packed_ref[a] = jnp.concatenate([basis_ref[2 * a], basis_ref[2 * a + 1]], axis=1)
    transfer_in.wait()


def down_kernel(
    axes, at_vmem, table_in, other_refs, packed_ref, counts_hbm,
    far_ref, near_ref, edge_ref, transfer_ref, basis_ref,
    out_ref, table_ref, at_ref, local_ref, down_ref, counts_ref, sems,
):
    del table_in
    at_in, counts_in = start_all([(at_vmem, at_ref), (counts_hbm, counts_ref)], sems)
    parents, many = at_ref.shape
    rank = packed_ref.shape[1]
    width = basis_ref.shape[1]
    sides = table_ref.shape[1]
    half = table_ref.shape[0] // 2
    left = left_half(sides, rank)
    parity, mine, count = lax.axis_index(axes[1]), lax.axis_index(axes[0]), lax.axis_size(axes[0])
    own, piece = half // 2 // count, other_refs[0].shape[0]
    for t in range(2 * piece):
        place = lax.rem(mine + 1 + t // own, count) * own + t % own
        spread_pair(table_ref, half * (1 - parity) + 2 * place, other_refs[t // piece][t % piece], rank)
    at_in.wait()
    for q in range(parents):
        rows = [at_ref[q, j] for j in range(many)]
        far = dot(picked(table_ref, rows, left), packed_ref[q], NT)
        down_ref[q] = far.astype(jnp.bfloat16)
    for q in range(parents):
        local = far_ref[q] + dot(down_ref[q], transfer_ref[2 * q : 2 * q + 2].reshape(2 * rank, rank), NT)
        local_ref[q] = local.astype(jnp.bfloat16)
    counts_in.wait()
    for q in range(parents):
        local = local_ref[q]
        none = jnp.zeros_like(local)
        both = jnp.concatenate([jnp.where(left, local, none), jnp.where(left, none, local)], axis=0)
        total = dot(both, basis_ref[q], NT)
        total = jnp.concatenate([total[:sides], total[sides:]], axis=1) + near_ref[q]
        if q == 0:
            total = total + edge_ref[0]
        if q == parents - 1:
            total = total + edge_ref[1]
        total = jnp.where(pair_mask(counts_ref, q, sides, width), total, jnp.zeros_like(total))
        out_ref[:, 2 * width * q : 2 * width * (q + 1)] = total.astype(out_ref.dtype)


def per_device(
    charges,
    panel_counts,
    basis,
    transfer,
    leaf_coupling,
    leaf_partners,
    near_blocks,
    parent_coupling,
    parent_partners,
):
    leaves, width, rank = basis.shape
    sides = charges.shape[1]
    parents, many = parent_partners.shape
    pairs = leaves // 2
    own = pairs // 2
    axes = ("gx", "gz", "gp")
    n = lax.axis_size("gz") * lax.axis_size("gp")
    total = n * lax.axis_size("gx")
    bf16, f32 = jnp.bfloat16, jnp.float32
    keep = lambda *arrays: [pltpu.with_memory_space_constraint(a, pltpu.HBM) for a in arrays]
    shape = pltpu.VMEM
    dma = lambda count: pltpu.SemaphoreType.DMA((count,))
    params = lambda mib: pltpu.CompilerParams(vmem_limit_bytes=mib * 2**20)

    rim, live, parent_coef, sent = pl.pallas_call(
        up_kernel,
        name="up",
        out_shape=[
            shape((pairs + 2, sides, 2 * rank), bf16),
            shape((pairs, sides, 2 * width), bf16),
            shape((own, sides, 2 * rank), bf16),
            pltpu.HBM((n // 2 * own, sides, 2 * rank), bf16),
        ],
        in_specs=[HBM] * 4,
        out_specs=[VMEM, VMEM, VMEM, HBM],
        scratch_shapes=[
            pltpu.SMEM((leaves,), jnp.int32),
            pltpu.VMEM((sides, leaves * width), bf16),
            pltpu.VMEM((leaves, width, rank), bf16),
            pltpu.VMEM((leaves, rank, rank), bf16),
            dma(4),
            dma(n // 2),
        ],
        compiler_params=params(8),
    )(*keep(panel_counts, charges.T, basis, transfer))

    even = lax.ppermute(rim, axes, [(i, i ^ 1) for i in range(total)])
    steps = [(i, i + 1) for i in range(1, total - 1, 2)]
    odd = lax.ppermute(rim, axes, steps + [(b, a) for a, b in steps])
    same = lax.all_to_all(sent, "gz", 0, 0, tiled=True)

    parent_packed, near, rim_near, leaf_at, parent_at = pl.pallas_call(
        functools.partial(mid_kernel, axes),
        name="mid",
        out_shape=[
            shape((parents, rank, many * rank), bf16),
            shape((pairs, sides, 2 * width), f32),
            shape((2, width, width), bf16),
            shape((many, leaves), jnp.int32),
            shape((parents, many), jnp.int32),
        ],
        in_specs=[VMEM] + [HBM] * 4,
        out_specs=[VMEM] * 5,
        scratch_shapes=[
            pltpu.VMEM(near_blocks.shape, bf16),
            pltpu.VMEM(parent_coupling.shape, bf16),
            dma(3 + parents // 4),
        ],
        compiler_params=params(12),
    )(live, *keep(near_blocks, parent_coupling, leaf_partners.T, parent_partners))

    other_own = lax.ppermute(parent_coef, "gp", [(0, 1), (1, 0)])
    piece = shape(((n // 2 - 1) * own // 2, sides, 2 * rank), bf16)
    pieces = pl.pallas_call(
        functools.partial(halves_kernel, "gz"),
        name="halves",
        out_shape=[piece, piece],
        in_specs=[VMEM, VMEM, VMEM],
        out_specs=[VMEM, VMEM],
        compiler_params=params(4),
    )(same, other_own, parent_at)
    other = [lax.ppermute(piece, "gp", [(0, 1), (1, 0)]) for piece in pieces]

    far, edge, transfer_in, basis_in, parent_table = pl.pallas_call(
        functools.partial(leaf_kernel, axes),
        name="leaf",
        out_shape=[
            shape((pairs, sides, 2 * rank), f32),
            shape((2, sides, 2 * width), f32),
            shape(transfer.shape, bf16),
            shape((pairs, width, 2 * rank), bf16),
            shape((n * parents, sides, 2 * rank), bf16),
        ],
        in_specs=[VMEM] * 7 + [HBM] * 3,
        out_specs=[VMEM] * 5,
        scratch_shapes=[
            pltpu.VMEM((3 * leaves, sides, 2 * rank), bf16),
            pltpu.SMEM((many, leaves), jnp.int32),
            pltpu.VMEM(leaf_coupling.shape, bf16),
            pltpu.VMEM((leaves, rank, many * rank), bf16),
            pltpu.VMEM(basis.shape, bf16),
            dma(3 + leaves // 4),
        ],
        compiler_params=params(20),
    )(leaf_at, rim, even, odd, rim_near, same, other_own, *keep(leaf_coupling, transfer, basis))

    out, _ = pl.pallas_call(
        functools.partial(down_kernel, axes[1:]),
        name="down",
        out_shape=[
            jax.ShapeDtypeStruct((sides, leaves * width), bf16),
            shape((n * parents, sides, 2 * rank), bf16),
        ],
        in_specs=[VMEM, VMEM, [VMEM] * 2, VMEM, HBM] + [VMEM] * 5,
        out_specs=[VMEM, VMEM],
        input_output_aliases={1: 1},
        scratch_shapes=[
            pltpu.SMEM((parents, many), jnp.int32),
            pltpu.VMEM((pairs, sides, 2 * rank), bf16),
            pltpu.VMEM((parents, sides, rank), bf16),
            pltpu.SMEM((leaves,), jnp.int32),
            dma(2),
        ],
        compiler_params=params(12),
    )(parent_at, parent_table, other, parent_packed, *keep(panel_counts), far, near, edge, transfer_in, basis_in)
    return out.T


def solution(mesh):
    outer, inner = mesh.devices.shape
    split = jax.sharding.Mesh(mesh.devices.reshape(outer, inner // 2, 2), ("gx", "gz", "gp"))
    leaves = ("gx", "gz", "gp")
    in_specs = (
        P(leaves, None),
        P(leaves),
        P(leaves, None, None),
        P(leaves, None, None),
        P(leaves, None, None, None),
        P(leaves, None),
        P(leaves, None, None, None),
        P(leaves, None, None, None),
        P(leaves, None),
    )
    return jax.shard_map(
        per_device, mesh=split, in_specs=in_specs, out_specs=P(leaves, None), check_vma=False
    )
```

```python
import functools

import jax
import jax.numpy as jnp
from jax import lax
from jax.experimental import pallas as pl
from jax.experimental.pallas import tpu as pltpu
from jax.sharding import PartitionSpec as P

VMEM = pl.BlockSpec(memory_space=pltpu.VMEM)
HBM = pl.BlockSpec(memory_space=pltpu.HBM)
NN = (((1,), (0,)), ((), ()))
NT = (((1,), (1,)), ((), ()))


def dot(a, b, dims):
    return lax.dot_general(a, b, dims, preferred_element_type=jnp.float32)


def left_half(sides, width):
    return lax.broadcasted_iota(jnp.int32, (sides, 2 * width), 1) < width


def pair_mask(counts_ref, pair, sides, width):
    lane = lax.broadcasted_iota(jnp.int32, (sides, 2 * width), 1)
    left = lane < width
    count = jnp.where(left, counts_ref[2 * pair], counts_ref[2 * pair + 1])
    return jnp.where(left, lane, lane - width) < count


def swap(pair, width):
    return jnp.concatenate([pair[:, width:], pair[:, :width]], axis=1)


def mod(x, m):
    return x & (m - 1) if m & (m - 1) == 0 else lax.rem(x, m)


def div(x, m):
    return x >> (m.bit_length() - 1) if m & (m - 1) == 0 else x // m


def position(axes):
    index = 0
    for axis in axes:
        index = index * lax.axis_size(axis) + lax.axis_index(axis)
    return index


def start_all(copies, sems):
    started = [pltpu.make_async_copy(src, dst, sems.at[i]) for i, (src, dst) in enumerate(copies)]
    for copy in started:
        copy.start()
    return started


def up_kernel(
    counts_hbm, charges_hbm, basis_hbm, transfer_hbm,
    rim_ref, live_ref, parents_ref, sent_hbm,
    counts_ref, charges_ref, basis_ref, transfer_ref, sems, sent_sems,
):
    sides = charges_ref.shape[0]
    leaves, width, rank = basis_ref.shape
    pairs = leaves // 2
    own = pairs // 2
    parts = [pl.ds(0, pairs), pl.ds(pairs, pairs)]
    counts_in, charges_in, *halves_in = start_all(
        [(counts_hbm, counts_ref), (charges_hbm, charges_ref)]
        + [(basis_hbm.at[part], basis_ref.at[part]) for part in parts]
        + [(transfer_hbm.at[part], transfer_ref.at[part]) for part in parts],
        sems,
    )
    left = left_half(sides, width)
    counts_in.wait()
    charges_in.wait()
    lives = []
    for a in range(pairs):
        charge = charges_ref[:, 2 * width * a : 2 * width * (a + 1)]
        live = jnp.where(pair_mask(counts_ref, a, sides, width), charge, jnp.zeros_like(charge))
        live_ref[a] = live
        lives.append(live)
    rim_ref[pairs] = lives[0]
    rim_ref[pairs + 1] = lives[-1]
    none = jnp.zeros_like(lives[0])
    coefs = []
    for a in range(pairs):
        if a % own == 0:
            halves_in[a // own].wait()
        live = lives[a]
        both = jnp.concatenate([jnp.where(left, live, none), jnp.where(left, none, live)], axis=0)
        coef = dot(both, basis_ref[2 * a : 2 * a + 2].reshape(2 * width, rank), NN)
        coef = jnp.concatenate([coef[:sides], coef[sides:]], axis=1).astype(jnp.bfloat16)
        rim_ref[a] = coef
        coefs.append(coef)
    copies = sent_hbm.shape[0] // own
    sent, few = [], own // 2
    for h in range(2):
        halves_in[2 + h].wait()
        sums = [
            dot(coefs[a], transfer_ref[2 * a : 2 * a + 2].reshape(2 * rank, rank), NN)
            for a in range(own * h, own * (h + 1))
        ]
        for a in range(few):
            parents_ref[few * h + a] = jnp.concatenate(sums[2 * a : 2 * a + 2], axis=1).astype(jnp.bfloat16)
        part = parents_ref.at[pl.ds(few * h, few)]
        sent += start_all(
            [(part, sent_hbm.at[pl.ds(own * c + few * h, few)]) for c in range(copies)], sent_sems.at[h]
        )
    for copy in sent:
        copy.wait()


def side_by_side(blocks_ref, g):
    return jnp.concatenate([blocks_ref[g, j] for j in range(blocks_ref.shape[1])], axis=1)


def mid_kernel(
    axes, live_ref, near_hbm, parent_hbm, leaf_partners_hbm, parent_partners_hbm,
    parent_packed_ref, near_out_ref, rim_near_ref, leaf_at_ref, parent_at_ref,
    near_ref, parent_ref, sems,
):
    parents, many, rank, _ = parent_ref.shape
    leaves = near_ref.shape[0]
    width = near_ref.shape[2]
    pairs = leaves // 2
    started = start_all(
        [(near_hbm, near_ref)]
        + [(parent_hbm.at[pl.ds(4 * i, 4)], parent_ref.at[pl.ds(4 * i, 4)]) for i in range(parents // 4)]
        + [(leaf_partners_hbm, leaf_at_ref), (parent_partners_hbm, parent_at_ref)],
        sems,
    )
    near_in = started[0]
    parent_in = started[1:-2]
    near_in.wait()
    rim_near_ref[0] = near_ref[0, 0]
    rim_near_ref[1] = near_ref[leaves - 1, 2]
    for a in range(pairs):
        here = live_ref[a]
        even = dot(here, jnp.concatenate([near_ref[2 * a, 1], near_ref[2 * a, 2]], axis=1), NT)
        odd = dot(here, jnp.concatenate([near_ref[2 * a + 1, 0], near_ref[2 * a + 1, 1]], axis=1), NT)
        if a > 0:
            even = even + dot(live_ref[a - 1][:, width:], near_ref[2 * a, 0], NT)
        if a < pairs - 1:
            odd = odd + dot(live_ref[a + 1][:, :width], near_ref[2 * a + 1, 2], NT)
        near_out_ref[a] = jnp.concatenate([even, odd], axis=1)

    for i, copy in enumerate(parent_in):
        copy.wait()
        for q in range(4 * i, 4 * i + 4):
            parent_packed_ref[q] = side_by_side(parent_ref, q)
    for copy in started[-2:]:
        copy.wait()
    wanted = leaf_at_ref[...] + (1 - position(axes)) * leaves
    leaf_at_ref[...] = wanted ^ (lax.broadcasted_iota(jnp.int32, wanted.shape, 0) & 1)
    inner = lax.axis_size(axes[2])
    outer = lax.axis_size(axes[1])
    wanted = mod(parent_at_ref[...], outer * inner * parents)
    source = div(wanted, parents)
    wanted = (mod(source, inner) * outer + div(source, inner)) * parents + mod(wanted, parents)
    parent_at_ref[...] = wanted ^ (lax.broadcasted_iota(jnp.int32, wanted.shape, 1) & 1)


def halves_kernel(axis, whole_ref, own_ref, at_ref, first_ref, second_ref):
    del at_ref
    own, half = own_ref.shape[0], first_ref.shape[0]
    count = lax.axis_size(axis)
    for t in range(2 * half):
        source = lax.rem(lax.axis_index(axis) + 1 + t // own, count) * own + t % own
        (first_ref if t < half else second_ref)[t % half] = whole_ref[source]


def spread_pair(table_ref, at, pair, width):
    table_ref[at] = pair
    table_ref[at + 1] = swap(pair, width)


def picked(table_ref, rows, left):
    return jnp.concatenate(
        [
            jnp.where(left, table_ref[rows[j]], table_ref[rows[j + 1]])
            for j in range(0, len(rows), 2)
        ],
        axis=1,
    )


def leaf_kernel(
    axes, at_vmem, rim_ref, even_ref, odd_ref, rim_near_ref, coupling_hbm, transfer_hbm, basis_hbm,
    far_ref, edge_ref, transfer_ref, basis_packed_ref, table_ref, at_ref, coupling_ref, packed_ref, basis_ref, sems,
):
    leaves, many, rank, _ = coupling_ref.shape
    chunks = [(at, 4) for at in range(0, leaves, 4)]
    at_in, *coupling_in, transfer_in, basis_in = start_all(
        [(at_vmem, at_ref)]
        + [(coupling_hbm.at[pl.ds(at, size)], coupling_ref.at[pl.ds(at, size)]) for at, size in chunks]
        + [(transfer_hbm, transfer_ref), (basis_hbm, basis_ref)],
        sems,
    )
    width = rim_near_ref.shape[1]
    pairs = leaves // 2
    sides = rim_ref.shape[1]
    left = left_half(sides, rank)
    parity = lax.rem(position(axes), 2)
    for ref, base in (
        (rim_ref, leaves), (even_ref, 2 * leaves * (1 - parity)), (odd_ref, 2 * leaves * parity),
    ):
        for a in range(pairs):
            spread_pair(table_ref, base + 2 * a, ref[a], rank)
    before = jnp.where(parity == 1, even_ref[pairs + 1], odd_ref[pairs + 1])
    after = jnp.where(parity == 1, odd_ref[pairs], even_ref[pairs])
    low = dot(before[:, width:], rim_near_ref[0], NT)
    high = dot(after[:, :width], rim_near_ref[1], NT)
    edge_ref[0] = jnp.concatenate([low, jnp.zeros_like(low)], axis=1)
    edge_ref[1] = jnp.concatenate([jnp.zeros_like(high), high], axis=1)
    at_in.wait()
    ready = []
    for i in range(len(chunks) + 1):
        now, ready = ready, []
        if i < len(chunks):
            coupling_in[i].wait()
            ready = range(chunks[i][0], sum(chunks[i]))
            for g in ready:
                packed_ref[g] = side_by_side(coupling_ref, g)
        fars = []
        for g in now:
            rows = [at_ref[j, g] for j in range(many)]
            fars.append(dot(picked(table_ref, rows, left), packed_ref[g], NT))
            if g % 2 == 1:
                far_ref[g // 2] = jnp.concatenate(fars[-2:], axis=1)
    basis_in.wait()
    for a in range(pairs):
        basis_packed_ref[a] = jnp.concatenate([basis_ref[2 * a], basis_ref[2 * a + 1]], axis=1)
    transfer_in.wait()


def down_kernel(
    axes, at_vmem, same_ref, other_own_ref, other_refs, packed_ref, counts_hbm,
    far_ref, near_ref, edge_ref, transfer_ref, basis_ref,
    out_ref, table_ref, at_ref, local_ref, down_ref, counts_ref, sems,
):
    at_in, counts_in = start_all([(at_vmem, at_ref), (counts_hbm, counts_ref)], sems)
    parents, many = at_ref.shape
    rank = packed_ref.shape[1]
    width = basis_ref.shape[1]
    sides = same_ref.shape[1]
    half = 2 * same_ref.shape[0]
    left = left_half(sides, rank)
    parity, mine, count = lax.axis_index(axes[1]), lax.axis_index(axes[0]), lax.axis_size(axes[0])
    own, piece = other_own_ref.shape[0], other_refs[0].shape[0]
    for t in range(count * own):
        spread_pair(table_ref, half * parity + 2 * t, same_ref[t], rank)
    for t in range(own):
        spread_pair(table_ref, half * (1 - parity) + 2 * (mine * own + t), other_own_ref[t], rank)
    for t in range(2 * piece):
        place = lax.rem(mine + 1 + t // own, count) * own + t % own
        spread_pair(table_ref, half * (1 - parity) + 2 * place, other_refs[t // piece][t % piece], rank)
    at_in.wait()
    for q in range(parents):
        rows = [at_ref[q, j] for j in range(many)]
        far = dot(picked(table_ref, rows, left), packed_ref[q], NT)
        down_ref[q] = far.astype(jnp.bfloat16)
    for q in range(parents):
        local = far_ref[q] + dot(down_ref[q], transfer_ref[2 * q : 2 * q + 2].reshape(2 * rank, rank), NT)
        local_ref[q] = local.astype(jnp.bfloat16)
    counts_in.wait()
    for q in range(parents):
        local = local_ref[q]
        none = jnp.zeros_like(local)
        both = jnp.concatenate([jnp.where(left, local, none), jnp.where(left, none, local)], axis=0)
        total = dot(both, basis_ref[q], NT)
        total = jnp.concatenate([total[:sides], total[sides:]], axis=1) + near_ref[q]
        if q == 0:
            total = total + edge_ref[0]
        if q == parents - 1:
            total = total + edge_ref[1]
        total = jnp.where(pair_mask(counts_ref, q, sides, width), total, jnp.zeros_like(total))
        out_ref[:, 2 * width * q : 2 * width * (q + 1)] = total.astype(out_ref.dtype)


def per_device(
    charges,
    panel_counts,
    basis,
    transfer,
    leaf_coupling,
    leaf_partners,
    near_blocks,
    parent_coupling,
    parent_partners,
):
    leaves, width, rank = basis.shape
    sides = charges.shape[1]
    parents, many = parent_partners.shape
    pairs = leaves // 2
    own = pairs // 2
    axes = ("gx", "gz", "gp")
    n = lax.axis_size("gz") * lax.axis_size("gp")
    total = n * lax.axis_size("gx")
    bf16, f32 = jnp.bfloat16, jnp.float32
    keep = lambda *arrays: [pltpu.with_memory_space_constraint(a, pltpu.HBM) for a in arrays]
    shape = pltpu.VMEM
    dma = lambda count: pltpu.SemaphoreType.DMA((count,))
    params = lambda mib: pltpu.CompilerParams(vmem_limit_bytes=mib * 2**20)

    rim, live, parent_coef, sent = pl.pallas_call(
        up_kernel,
        name="up",
        out_shape=[
            shape((pairs + 2, sides, 2 * rank), bf16),
            shape((pairs, sides, 2 * width), bf16),
            shape((own, sides, 2 * rank), bf16),
            pltpu.HBM((n // 2 * own, sides, 2 * rank), bf16),
        ],
        in_specs=[HBM] * 4,
        out_specs=[VMEM, VMEM, VMEM, HBM],
        scratch_shapes=[
            pltpu.SMEM((leaves,), jnp.int32),
            pltpu.VMEM((sides, leaves * width), bf16),
            pltpu.VMEM((leaves, width, rank), bf16),
            pltpu.VMEM((leaves, rank, rank), bf16),
            dma(6),
            pltpu.SemaphoreType.DMA((2, n // 2)),
        ],
        compiler_params=params(8),
    )(*keep(panel_counts, charges.T, basis, transfer))

    even = lax.ppermute(rim, axes, [(i, i ^ 1) for i in range(total)])
    steps = [(i, i + 1) for i in range(1, total - 1, 2)]
    odd = lax.ppermute(rim, axes, steps + [(b, a) for a, b in steps])
    same = lax.all_to_all(sent, "gz", 0, 0, tiled=True)

    parent_packed, near, rim_near, leaf_at, parent_at = pl.pallas_call(
        functools.partial(mid_kernel, axes),
        name="mid",
        out_shape=[
            shape((parents, rank, many * rank), bf16),
            shape((pairs, sides, 2 * width), f32),
            shape((2, width, width), bf16),
            shape((many, leaves), jnp.int32),
            shape((parents, many), jnp.int32),
        ],
        in_specs=[VMEM] + [HBM] * 4,
        out_specs=[VMEM] * 5,
        scratch_shapes=[
            pltpu.VMEM(near_blocks.shape, bf16),
            pltpu.VMEM(parent_coupling.shape, bf16),
            dma(3 + parents // 4),
        ],
        compiler_params=params(12),
    )(live, *keep(near_blocks, parent_coupling, leaf_partners.T, parent_partners))

    other_own = lax.ppermute(parent_coef, "gp", [(0, 1), (1, 0)])
    piece = shape(((n // 2 - 1) * own // 2, sides, 2 * rank), bf16)
    pieces = pl.pallas_call(
        functools.partial(halves_kernel, "gz"),
        name="halves",
        out_shape=[piece, piece],
        in_specs=[VMEM, VMEM, VMEM],
        out_specs=[VMEM, VMEM],
        compiler_params=params(4),
    )(same, other_own, parent_at)
    other = [lax.ppermute(piece, "gp", [(0, 1), (1, 0)]) for piece in pieces]

    far, edge, transfer_in, basis_in = pl.pallas_call(
        functools.partial(leaf_kernel, axes),
        name="leaf",
        out_shape=[
            shape((pairs, sides, 2 * rank), f32),
            shape((2, sides, 2 * width), f32),
            shape(transfer.shape, bf16),
            shape((pairs, width, 2 * rank), bf16),
        ],
        in_specs=[VMEM] * 5 + [HBM] * 3,
        out_specs=[VMEM] * 4,
        scratch_shapes=[
            pltpu.VMEM((3 * leaves, sides, 2 * rank), bf16),
            pltpu.SMEM((many, leaves), jnp.int32),
            pltpu.VMEM(leaf_coupling.shape, bf16),
            pltpu.VMEM((leaves, rank, many * rank), bf16),
            pltpu.VMEM(basis.shape, bf16),
            dma(3 + leaves // 4),
        ],
        compiler_params=params(20),
    )(leaf_at, rim, even, odd, rim_near, *keep(leaf_coupling, transfer, basis))

    out = pl.pallas_call(
        functools.partial(down_kernel, axes[1:]),
        name="down",
        out_shape=jax.ShapeDtypeStruct((sides, leaves * width), bf16),
        in_specs=[VMEM, VMEM, VMEM, [VMEM] * 2, VMEM, HBM] + [VMEM] * 5,
        out_specs=VMEM,
        scratch_shapes=[
            pltpu.VMEM((n * parents, sides, 2 * rank), bf16),
            pltpu.SMEM((parents, many), jnp.int32),
            pltpu.VMEM((pairs, sides, 2 * rank), bf16),
            pltpu.VMEM((parents, sides, rank), bf16),
            pltpu.SMEM((leaves,), jnp.int32),
            dma(2),
        ],
        compiler_params=params(12),
    )(parent_at, same, other_own, other, parent_packed, *keep(panel_counts), far, near, edge, transfer_in, basis_in)
    return out.T


def solution(mesh):
    outer, inner = mesh.devices.shape
    split = jax.sharding.Mesh(mesh.devices.reshape(outer, inner // 2, 2), ("gx", "gz", "gp"))
    leaves = ("gx", "gz", "gp")
    in_specs = (
        P(leaves, None),
        P(leaves),
        P(leaves, None, None),
        P(leaves, None, None),
        P(leaves, None, None, None),
        P(leaves, None),
        P(leaves, None, None, None),
        P(leaves, None, None, None),
        P(leaves, None),
    )
    return jax.shard_map(
        per_device, mesh=split, in_specs=in_specs, out_specs=P(leaves, None), check_vma=False
    )
```

```python
import functools

import jax
import jax.numpy as jnp
from jax import lax
from jax.experimental import pallas as pl
from jax.experimental.pallas import tpu as pltpu
from jax.sharding import PartitionSpec as P

VMEM = pl.BlockSpec(memory_space=pltpu.VMEM)
HBM = pl.BlockSpec(memory_space=pltpu.HBM)
NN = (((1,), (0,)), ((), ()))
NT = (((1,), (1,)), ((), ()))


def dot(a, b, dims):
    return lax.dot_general(a, b, dims, preferred_element_type=jnp.float32)


def left_half(sides, width):
    return lax.broadcasted_iota(jnp.int32, (sides, 2 * width), 1) < width


def pair_mask(counts_ref, pair, sides, width):
    lane = lax.broadcasted_iota(jnp.int32, (sides, 2 * width), 1)
    left = lane < width
    count = jnp.where(left, counts_ref[2 * pair], counts_ref[2 * pair + 1])
    return jnp.where(left, lane, lane - width) < count


def swap(pair, width):
    return jnp.concatenate([pair[:, width:], pair[:, :width]], axis=1)


def mod(x, m):
    return x & (m - 1) if m & (m - 1) == 0 else lax.rem(x, m)


def div(x, m):
    return x >> (m.bit_length() - 1) if m & (m - 1) == 0 else x // m


def position(axes):
    index = 0
    for axis in axes:
        index = index * lax.axis_size(axis) + lax.axis_index(axis)
    return index


def start_all(copies, sems):
    started = [pltpu.make_async_copy(src, dst, sems.at[i]) for i, (src, dst) in enumerate(copies)]
    for copy in started:
        copy.start()
    return started


def up_kernel(
    counts_hbm, charges_hbm, basis_hbm, transfer_hbm,
    rim_ref, live_ref, parents_ref, sent_hbm,
    counts_ref, charges_ref, basis_ref, transfer_ref, sems, sent_sems,
):
    counts_in, charges_in, basis_in, transfer_in = start_all(
        [
            (counts_hbm, counts_ref), (charges_hbm, charges_ref),
            (basis_hbm, basis_ref), (transfer_hbm, transfer_ref),
        ],
        sems,
    )
    sides = charges_ref.shape[0]
    leaves, width, rank = basis_ref.shape
    pairs = leaves // 2
    own = pairs // 2
    left = left_half(sides, width)
    counts_in.wait()
    charges_in.wait()
    lives = []
    for a in range(pairs):
        charge = charges_ref[:, 2 * width * a : 2 * width * (a + 1)]
        live = jnp.where(pair_mask(counts_ref, a, sides, width), charge, jnp.zeros_like(charge))
        live_ref[a] = live
        lives.append(live)
    rim_ref[pairs] = lives[0]
    rim_ref[pairs + 1] = lives[-1]
    basis_in.wait()
    transfer_in.wait()
    none = jnp.zeros_like(lives[0])
    coefs = []
    for a in range(pairs):
        live = lives[a]
        both = jnp.concatenate([jnp.where(left, live, none), jnp.where(left, none, live)], axis=0)
        coef = dot(both, basis_ref[2 * a : 2 * a + 2].reshape(2 * width, rank), NN)
        coef = jnp.concatenate([coef[:sides], coef[sides:]], axis=1).astype(jnp.bfloat16)
        rim_ref[a] = coef
        coefs.append(coef)
    sums = [
        dot(coefs[a], transfer_ref[2 * a : 2 * a + 2].reshape(2 * rank, rank), NN)
        for a in range(pairs)
    ]
    for a in range(own):
        parents_ref[a] = jnp.concatenate(sums[2 * a : 2 * a + 2], axis=1).astype(jnp.bfloat16)
    copies = sent_hbm.shape[0] // own
    for copy in start_all([(parents_ref, sent_hbm.at[pl.ds(own * c, own)]) for c in range(copies)], sent_sems):
        copy.wait()


def side_by_side(blocks_ref, g):
    return jnp.concatenate([blocks_ref[g, j] for j in range(blocks_ref.shape[1])], axis=1)


def mid_kernel(
    axes, live_ref, near_hbm, parent_hbm, leaf_partners_hbm, parent_partners_hbm,
    parent_packed_ref, near_out_ref, rim_near_ref, leaf_at_ref, parent_at_ref,
    near_ref, parent_ref, sems,
):
    parents, many, rank, _ = parent_ref.shape
    leaves = near_ref.shape[0]
    width = near_ref.shape[2]
    pairs = leaves // 2
    started = start_all(
        [(near_hbm, near_ref)]
        + [(parent_hbm.at[pl.ds(8 * i, 8)], parent_ref.at[pl.ds(8 * i, 8)]) for i in range(parents // 8)]
        + [(leaf_partners_hbm, leaf_at_ref), (parent_partners_hbm, parent_at_ref)],
        sems,
    )
    near_in = started[0]
    parent_in = started[1:-2]
    near_in.wait()
    rim_near_ref[0] = near_ref[0, 0]
    rim_near_ref[1] = near_ref[leaves - 1, 2]
    for a in range(pairs):
        here = live_ref[a]
        even = dot(here, jnp.concatenate([near_ref[2 * a, 1], near_ref[2 * a, 2]], axis=1), NT)
        odd = dot(here, jnp.concatenate([near_ref[2 * a + 1, 0], near_ref[2 * a + 1, 1]], axis=1), NT)
        if a > 0:
            even = even + dot(live_ref[a - 1][:, width:], near_ref[2 * a, 0], NT)
        if a < pairs - 1:
            odd = odd + dot(live_ref[a + 1][:, :width], near_ref[2 * a + 1, 2], NT)
        near_out_ref[a] = jnp.concatenate([even, odd], axis=1)

    for i, copy in enumerate(parent_in):
        copy.wait()
        for q in range(8 * i, 8 * i + 8):
            parent_packed_ref[q] = side_by_side(parent_ref, q)
    for copy in started[-2:]:
        copy.wait()
    wanted = leaf_at_ref[...] + (1 - position(axes)) * leaves
    leaf_at_ref[...] = wanted ^ (lax.broadcasted_iota(jnp.int32, wanted.shape, 0) & 1)
    inner = lax.axis_size(axes[2])
    outer = lax.axis_size(axes[1])
    wanted = mod(parent_at_ref[...], outer * inner * parents)
    source = div(wanted, parents)
    wanted = (mod(source, inner) * outer + div(source, inner)) * parents + mod(wanted, parents)
    parent_at_ref[...] = wanted ^ (lax.broadcasted_iota(jnp.int32, wanted.shape, 1) & 1)


def halves_kernel(axis, whole_ref, own_ref, at_ref, first_ref, second_ref):
    del at_ref
    own, half = own_ref.shape[0], first_ref.shape[0]
    count = lax.axis_size(axis)
    for t in range(2 * half):
        source = lax.rem(lax.axis_index(axis) + 1 + t // own, count) * own + t % own
        (first_ref if t < half else second_ref)[t % half] = whole_ref[source]


def spread_pair(table_ref, at, pair, width):
    table_ref[at] = pair
    table_ref[at + 1] = swap(pair, width)


def picked(table_ref, rows, left):
    return jnp.concatenate(
        [
            jnp.where(left, table_ref[rows[j]], table_ref[rows[j + 1]])
            for j in range(0, len(rows), 2)
        ],
        axis=1,
    )


def leaf_kernel(
    axes, at_vmem, rim_ref, even_ref, odd_ref, rim_near_ref, coupling_hbm, transfer_hbm, basis_hbm,
    far_ref, edge_ref, transfer_ref, basis_packed_ref, table_ref, at_ref, coupling_ref, packed_ref, basis_ref, sems,
):
    leaves, many, rank, _ = coupling_ref.shape
    chunks = [(at, 4) for at in range(0, leaves, 4)]
    at_in, *coupling_in, transfer_in, basis_in = start_all(
        [(at_vmem, at_ref)]
        + [(coupling_hbm.at[pl.ds(at, size)], coupling_ref.at[pl.ds(at, size)]) for at, size in chunks]
        + [(transfer_hbm, transfer_ref), (basis_hbm, basis_ref)],
        sems,
    )
    width = rim_near_ref.shape[1]
    pairs = leaves // 2
    sides = rim_ref.shape[1]
    left = left_half(sides, rank)
    parity = lax.rem(position(axes), 2)
    for ref, base in (
        (rim_ref, leaves), (even_ref, 2 * leaves * (1 - parity)), (odd_ref, 2 * leaves * parity),
    ):
        for a in range(pairs):
            spread_pair(table_ref, base + 2 * a, ref[a], rank)
    before = jnp.where(parity == 1, even_ref[pairs + 1], odd_ref[pairs + 1])
    after = jnp.where(parity == 1, odd_ref[pairs], even_ref[pairs])
    low = dot(before[:, width:], rim_near_ref[0], NT)
    high = dot(after[:, :width], rim_near_ref[1], NT)
    edge_ref[0] = jnp.concatenate([low, jnp.zeros_like(low)], axis=1)
    edge_ref[1] = jnp.concatenate([jnp.zeros_like(high), high], axis=1)
    at_in.wait()
    ready = []
    for i in range(len(chunks) + 1):
        now, ready = ready, []
        if i < len(chunks):
            coupling_in[i].wait()
            ready = range(chunks[i][0], sum(chunks[i]))
            for g in ready:
                packed_ref[g] = side_by_side(coupling_ref, g)
        fars = []
        for g in now:
            rows = [at_ref[j, g] for j in range(many)]
            fars.append(dot(picked(table_ref, rows, left), packed_ref[g], NT))
            if g % 2 == 1:
                far_ref[g // 2] = jnp.concatenate(fars[-2:], axis=1)
    basis_in.wait()
    for a in range(pairs):
        basis_packed_ref[a] = jnp.concatenate([basis_ref[2 * a], basis_ref[2 * a + 1]], axis=1)
    transfer_in.wait()


def down_kernel(
    axes, at_vmem, same_ref, other_own_ref, other_refs, packed_ref, counts_hbm,
    far_ref, near_ref, edge_ref, transfer_ref, basis_ref,
    out_ref, table_ref, at_ref, local_ref, down_ref, counts_ref, sems,
):
    at_in, counts_in = start_all([(at_vmem, at_ref), (counts_hbm, counts_ref)], sems)
    parents, many = at_ref.shape
    rank = packed_ref.shape[1]
    width = basis_ref.shape[1]
    sides = same_ref.shape[1]
    half = 2 * same_ref.shape[0]
    left = left_half(sides, rank)
    parity, mine, count = lax.axis_index(axes[1]), lax.axis_index(axes[0]), lax.axis_size(axes[0])
    own, piece = other_own_ref.shape[0], other_refs[0].shape[0]
    for t in range(count * own):
        spread_pair(table_ref, half * parity + 2 * t, same_ref[t], rank)
    for t in range(own):
        spread_pair(table_ref, half * (1 - parity) + 2 * (mine * own + t), other_own_ref[t], rank)
    for t in range(2 * piece):
        place = lax.rem(mine + 1 + t // own, count) * own + t % own
        spread_pair(table_ref, half * (1 - parity) + 2 * place, other_refs[t // piece][t % piece], rank)
    at_in.wait()
    for q in range(parents):
        rows = [at_ref[q, j] for j in range(many)]
        far = dot(picked(table_ref, rows, left), packed_ref[q], NT)
        down_ref[q] = far.astype(jnp.bfloat16)
    for q in range(parents):
        local = far_ref[q] + dot(down_ref[q], transfer_ref[2 * q : 2 * q + 2].reshape(2 * rank, rank), NT)
        local_ref[q] = local.astype(jnp.bfloat16)
    counts_in.wait()
    for q in range(parents):
        local = local_ref[q]
        none = jnp.zeros_like(local)
        both = jnp.concatenate([jnp.where(left, local, none), jnp.where(left, none, local)], axis=0)
        total = dot(both, basis_ref[q], NT)
        total = jnp.concatenate([total[:sides], total[sides:]], axis=1) + near_ref[q]
        if q == 0:
            total = total + edge_ref[0]
        if q == parents - 1:
            total = total + edge_ref[1]
        total = jnp.where(pair_mask(counts_ref, q, sides, width), total, jnp.zeros_like(total))
        out_ref[:, 2 * width * q : 2 * width * (q + 1)] = total.astype(out_ref.dtype)


def per_device(
    charges,
    panel_counts,
    basis,
    transfer,
    leaf_coupling,
    leaf_partners,
    near_blocks,
    parent_coupling,
    parent_partners,
):
    leaves, width, rank = basis.shape
    sides = charges.shape[1]
    parents, many = parent_partners.shape
    pairs = leaves // 2
    own = pairs // 2
    axes = ("gx", "gz", "gp")
    n = lax.axis_size("gz") * lax.axis_size("gp")
    total = n * lax.axis_size("gx")
    bf16, f32 = jnp.bfloat16, jnp.float32
    keep = lambda *arrays: [pltpu.with_memory_space_constraint(a, pltpu.HBM) for a in arrays]
    shape = pltpu.VMEM
    dma = lambda count: pltpu.SemaphoreType.DMA((count,))
    params = lambda mib: pltpu.CompilerParams(vmem_limit_bytes=mib * 2**20)

    rim, live, parent_coef, sent = pl.pallas_call(
        up_kernel,
        name="up",
        out_shape=[
            shape((pairs + 2, sides, 2 * rank), bf16),
            shape((pairs, sides, 2 * width), bf16),
            shape((own, sides, 2 * rank), bf16),
            pltpu.HBM((n // 2 * own, sides, 2 * rank), bf16),
        ],
        in_specs=[HBM] * 4,
        out_specs=[VMEM, VMEM, VMEM, HBM],
        scratch_shapes=[
            pltpu.SMEM((leaves,), jnp.int32),
            pltpu.VMEM((sides, leaves * width), bf16),
            pltpu.VMEM((leaves, width, rank), bf16),
            pltpu.VMEM((leaves, rank, rank), bf16),
            dma(4),
            dma(n // 2),
        ],
        compiler_params=params(8),
    )(*keep(panel_counts, charges.T, basis, transfer))

    even = lax.ppermute(rim, axes, [(i, i ^ 1) for i in range(total)])
    steps = [(i, i + 1) for i in range(1, total - 1, 2)]
    odd = lax.ppermute(rim, axes, steps + [(b, a) for a, b in steps])
    same = lax.all_to_all(sent, "gz", 0, 0, tiled=True)

    parent_packed, near, rim_near, leaf_at, parent_at = pl.pallas_call(
        functools.partial(mid_kernel, axes),
        name="mid",
        out_shape=[
            shape((parents, rank, many * rank), bf16),
            shape((pairs, sides, 2 * width), f32),
            shape((2, width, width), bf16),
            shape((many, leaves), jnp.int32),
            shape((parents, many), jnp.int32),
        ],
        in_specs=[VMEM] + [HBM] * 4,
        out_specs=[VMEM] * 5,
        scratch_shapes=[
            pltpu.VMEM(near_blocks.shape, bf16),
            pltpu.VMEM(parent_coupling.shape, bf16),
            dma(3 + parents // 8),
        ],
        compiler_params=params(12),
    )(live, *keep(near_blocks, parent_coupling, leaf_partners.T, parent_partners))

    other_own = lax.ppermute(parent_coef, "gp", [(0, 1), (1, 0)])
    piece = shape(((n // 2 - 1) * own // 2, sides, 2 * rank), bf16)
    pieces = pl.pallas_call(
        functools.partial(halves_kernel, "gz"),
        name="halves",
        out_shape=[piece, piece],
        in_specs=[VMEM, VMEM, VMEM],
        out_specs=[VMEM, VMEM],
        compiler_params=params(4),
    )(same, other_own, parent_at)
    other = [lax.ppermute(piece, "gp", [(0, 1), (1, 0)]) for piece in pieces]

    far, edge, transfer_in, basis_in = pl.pallas_call(
        functools.partial(leaf_kernel, axes),
        name="leaf",
        out_shape=[
            shape((pairs, sides, 2 * rank), f32),
            shape((2, sides, 2 * width), f32),
            shape(transfer.shape, bf16),
            shape((pairs, width, 2 * rank), bf16),
        ],
        in_specs=[VMEM] * 5 + [HBM] * 3,
        out_specs=[VMEM] * 4,
        scratch_shapes=[
            pltpu.VMEM((3 * leaves, sides, 2 * rank), bf16),
            pltpu.SMEM((many, leaves), jnp.int32),
            pltpu.VMEM(leaf_coupling.shape, bf16),
            pltpu.VMEM((leaves, rank, many * rank), bf16),
            pltpu.VMEM(basis.shape, bf16),
            dma(3 + leaves // 4),
        ],
        compiler_params=params(20),
    )(leaf_at, rim, even, odd, rim_near, *keep(leaf_coupling, transfer, basis))

    out = pl.pallas_call(
        functools.partial(down_kernel, axes[1:]),
        name="down",
        out_shape=jax.ShapeDtypeStruct((sides, leaves * width), bf16),
        in_specs=[VMEM, VMEM, VMEM, [VMEM] * 2, VMEM, HBM] + [VMEM] * 5,
        out_specs=VMEM,
        scratch_shapes=[
            pltpu.VMEM((n * parents, sides, 2 * rank), bf16),
            pltpu.SMEM((parents, many), jnp.int32),
            pltpu.VMEM((pairs, sides, 2 * rank), bf16),
            pltpu.VMEM((parents, sides, rank), bf16),
            pltpu.SMEM((leaves,), jnp.int32),
            dma(2),
        ],
        compiler_params=params(12),
    )(parent_at, same, other_own, other, parent_packed, *keep(panel_counts), far, near, edge, transfer_in, basis_in)
    return out.T


def solution(mesh):
    outer, inner = mesh.devices.shape
    split = jax.sharding.Mesh(mesh.devices.reshape(outer, inner // 2, 2), ("gx", "gz", "gp"))
    leaves = ("gx", "gz", "gp")
    in_specs = (
        P(leaves, None),
        P(leaves),
        P(leaves, None, None),
        P(leaves, None, None),
        P(leaves, None, None, None),
        P(leaves, None),
        P(leaves, None, None, None),
        P(leaves, None, None, None),
        P(leaves, None),
    )
    return jax.shard_map(
        per_device, mesh=split, in_specs=in_specs, out_specs=P(leaves, None), check_vma=False
    )
```

```python
import functools

import jax
import jax.numpy as jnp
from jax import lax
from jax.experimental import pallas as pl
from jax.experimental.pallas import tpu as pltpu
from jax.sharding import PartitionSpec as P

VMEM = pl.BlockSpec(memory_space=pltpu.VMEM)
HBM = pl.BlockSpec(memory_space=pltpu.HBM)
NN = (((1,), (0,)), ((), ()))
NT = (((1,), (1,)), ((), ()))


def dot(a, b, dims):
    return lax.dot_general(a, b, dims, preferred_element_type=jnp.float32)


def left_half(sides, width):
    return lax.broadcasted_iota(jnp.int32, (sides, 2 * width), 1) < width


def pair_mask(counts_ref, pair, sides, width):
    lane = lax.broadcasted_iota(jnp.int32, (sides, 2 * width), 1)
    left = lane < width
    count = jnp.where(left, counts_ref[2 * pair], counts_ref[2 * pair + 1])
    return jnp.where(left, lane, lane - width) < count


def swap(pair, width):
    return jnp.concatenate([pair[:, width:], pair[:, :width]], axis=1)


def mod(x, m):
    return x & (m - 1) if m & (m - 1) == 0 else lax.rem(x, m)


def div(x, m):
    return x >> (m.bit_length() - 1) if m & (m - 1) == 0 else x // m


def position(axes):
    index = 0
    for axis in axes:
        index = index * lax.axis_size(axis) + lax.axis_index(axis)
    return index


def start_all(copies, sems):
    started = [pltpu.make_async_copy(src, dst, sems.at[i]) for i, (src, dst) in enumerate(copies)]
    for copy in started:
        copy.start()
    return started


def up_kernel(
    counts_hbm, charges_hbm, basis_hbm, transfer_hbm,
    rim_ref, live_ref, parents_ref, sent_hbm,
    counts_ref, charges_ref, basis_ref, transfer_ref, sems, sent_sems,
):
    counts_in, charges_in, basis_in, transfer_in = start_all(
        [
            (counts_hbm, counts_ref), (charges_hbm, charges_ref),
            (basis_hbm, basis_ref), (transfer_hbm, transfer_ref),
        ],
        sems,
    )
    sides = charges_ref.shape[0]
    leaves, width, rank = basis_ref.shape
    pairs = leaves // 2
    own = pairs // 2
    left = left_half(sides, width)
    counts_in.wait()
    charges_in.wait()
    lives = []
    for a in range(pairs):
        charge = charges_ref[:, 2 * width * a : 2 * width * (a + 1)]
        live = jnp.where(pair_mask(counts_ref, a, sides, width), charge, jnp.zeros_like(charge))
        live_ref[a] = live
        lives.append(live)
    rim_ref[pairs] = lives[0]
    rim_ref[pairs + 1] = lives[-1]
    basis_in.wait()
    none = jnp.zeros_like(lives[0])
    coefs = []
    for a in range(pairs):
        live = lives[a]
        both = jnp.concatenate([jnp.where(left, live, none), jnp.where(left, none, live)], axis=0)
        coef = dot(both, basis_ref[2 * a : 2 * a + 2].reshape(2 * width, rank), NN)
        coef = jnp.concatenate([coef[:sides], coef[sides:]], axis=1).astype(jnp.bfloat16)
        rim_ref[a] = coef
        coefs.append(coef)
    transfer_in.wait()
    sums = [
        dot(coefs[a], transfer_ref[2 * a : 2 * a + 2].reshape(2 * rank, rank), NN)
        for a in range(pairs)
    ]
    for a in range(own):
        parents_ref[a] = jnp.concatenate(sums[2 * a : 2 * a + 2], axis=1).astype(jnp.bfloat16)
    copies = sent_hbm.shape[0] // own
    for copy in start_all([(parents_ref, sent_hbm.at[pl.ds(own * c, own)]) for c in range(copies)], sent_sems):
        copy.wait()


def side_by_side(blocks_ref, g):
    return jnp.concatenate([blocks_ref[g, j] for j in range(blocks_ref.shape[1])], axis=1)


def mid_kernel(
    axes, live_ref, near_hbm, parent_hbm, leaf_partners_hbm, parent_partners_hbm,
    parent_packed_ref, near_out_ref, rim_near_ref, leaf_at_ref, parent_at_ref,
    near_ref, parent_ref, sems,
):
    parents, many, rank, _ = parent_ref.shape
    leaves = near_ref.shape[0]
    width = near_ref.shape[2]
    pairs = leaves // 2
    started = start_all(
        [(near_hbm, near_ref)]
        + [(parent_hbm.at[pl.ds(4 * i, 4)], parent_ref.at[pl.ds(4 * i, 4)]) for i in range(parents // 4)]
        + [(leaf_partners_hbm, leaf_at_ref), (parent_partners_hbm, parent_at_ref)],
        sems,
    )
    near_in = started[0]
    parent_in = started[1:-2]
    near_in.wait()
    rim_near_ref[0] = near_ref[0, 0]
    rim_near_ref[1] = near_ref[leaves - 1, 2]
    for a in range(pairs):
        here = live_ref[a]
        even = dot(here, jnp.concatenate([near_ref[2 * a, 1], near_ref[2 * a, 2]], axis=1), NT)
        odd = dot(here, jnp.concatenate([near_ref[2 * a + 1, 0], near_ref[2 * a + 1, 1]], axis=1), NT)
        if a > 0:
            even = even + dot(live_ref[a - 1][:, width:], near_ref[2 * a, 0], NT)
        if a < pairs - 1:
            odd = odd + dot(live_ref[a + 1][:, :width], near_ref[2 * a + 1, 2], NT)
        near_out_ref[a] = jnp.concatenate([even, odd], axis=1)

    for i, copy in enumerate(parent_in):
        copy.wait()
        for q in range(4 * i, 4 * i + 4):
            parent_packed_ref[q] = side_by_side(parent_ref, q)
    for copy in started[-2:]:
        copy.wait()
    wanted = leaf_at_ref[...] + (1 - position(axes)) * leaves
    leaf_at_ref[...] = wanted ^ (lax.broadcasted_iota(jnp.int32, wanted.shape, 0) & 1)
    inner = lax.axis_size(axes[2])
    outer = lax.axis_size(axes[1])
    wanted = mod(parent_at_ref[...], outer * inner * parents)
    source = div(wanted, parents)
    wanted = (mod(source, inner) * outer + div(source, inner)) * parents + mod(wanted, parents)
    parent_at_ref[...] = wanted ^ (lax.broadcasted_iota(jnp.int32, wanted.shape, 1) & 1)


def halves_kernel(axis, whole_ref, own_ref, at_ref, first_ref, second_ref):
    del at_ref
    own, half = own_ref.shape[0], first_ref.shape[0]
    count = lax.axis_size(axis)
    for t in range(2 * half):
        source = lax.rem(lax.axis_index(axis) + 1 + t // own, count) * own + t % own
        (first_ref if t < half else second_ref)[t % half] = whole_ref[source]


def spread_pair(table_ref, at, pair, width):
    table_ref[at] = pair
    table_ref[at + 1] = swap(pair, width)


def picked(table_ref, rows, left):
    return jnp.concatenate(
        [
            jnp.where(left, table_ref[rows[j]], table_ref[rows[j + 1]])
            for j in range(0, len(rows), 2)
        ],
        axis=1,
    )


def leaf_kernel(
    axes, at_vmem, rim_ref, even_ref, odd_ref, rim_near_ref, coupling_hbm, transfer_hbm, basis_hbm,
    far_ref, edge_ref, transfer_ref, basis_packed_ref, table_ref, at_ref, coupling_ref, packed_ref, basis_ref, sems,
):
    leaves, many, rank, _ = coupling_ref.shape
    chunks = [(at, 4) for at in range(0, leaves, 4)]
    fetches = [(at, 2) for at in range(0, leaves, 2)]
    at_in, *coupling_in, transfer_in, basis_in = start_all(
        [(at_vmem, at_ref)]
        + [(coupling_hbm.at[pl.ds(at, size)], coupling_ref.at[pl.ds(at, size)]) for at, size in fetches]
        + [(transfer_hbm, transfer_ref), (basis_hbm, basis_ref)],
        sems,
    )
    width = rim_near_ref.shape[1]
    pairs = leaves // 2
    sides = rim_ref.shape[1]
    left = left_half(sides, rank)
    parity = lax.rem(position(axes), 2)
    for ref, base in (
        (rim_ref, leaves), (even_ref, 2 * leaves * (1 - parity)), (odd_ref, 2 * leaves * parity),
    ):
        for a in range(pairs):
            spread_pair(table_ref, base + 2 * a, ref[a], rank)
    before = jnp.where(parity == 1, even_ref[pairs + 1], odd_ref[pairs + 1])
    after = jnp.where(parity == 1, odd_ref[pairs], even_ref[pairs])
    low = dot(before[:, width:], rim_near_ref[0], NT)
    high = dot(after[:, :width], rim_near_ref[1], NT)
    edge_ref[0] = jnp.concatenate([low, jnp.zeros_like(low)], axis=1)
    edge_ref[1] = jnp.concatenate([jnp.zeros_like(high), high], axis=1)
    at_in.wait()
    ready = []
    for i in range(len(chunks) + 1):
        now, ready = ready, []
        if i < len(chunks):
            coupling_in[2 * i].wait()
            coupling_in[2 * i + 1].wait()
            ready = range(chunks[i][0], sum(chunks[i]))
            for g in ready:
                packed_ref[g] = side_by_side(coupling_ref, g)
        fars = []
        for g in now:
            rows = [at_ref[j, g] for j in range(many)]
            fars.append(dot(picked(table_ref, rows, left), packed_ref[g], NT))
            if g % 2 == 1:
                far_ref[g // 2] = jnp.concatenate(fars[-2:], axis=1)
    basis_in.wait()
    for a in range(pairs):
        basis_packed_ref[a] = jnp.concatenate([basis_ref[2 * a], basis_ref[2 * a + 1]], axis=1)
    transfer_in.wait()


def down_kernel(
    axes, at_vmem, same_ref, other_own_ref, other_refs, packed_ref, counts_hbm,
    far_ref, near_ref, edge_ref, transfer_ref, basis_ref,
    out_ref, table_ref, at_ref, local_ref, down_ref, counts_ref, sems,
):
    at_in, counts_in = start_all([(at_vmem, at_ref), (counts_hbm, counts_ref)], sems)
    parents, many = at_ref.shape
    rank = packed_ref.shape[1]
    width = basis_ref.shape[1]
    sides = same_ref.shape[1]
    half = 2 * same_ref.shape[0]
    left = left_half(sides, rank)
    parity, mine, count = lax.axis_index(axes[1]), lax.axis_index(axes[0]), lax.axis_size(axes[0])
    own, piece = other_own_ref.shape[0], other_refs[0].shape[0]
    for t in range(count * own):
        spread_pair(table_ref, half * parity + 2 * t, same_ref[t], rank)
    for t in range(own):
        spread_pair(table_ref, half * (1 - parity) + 2 * (mine * own + t), other_own_ref[t], rank)
    for t in range(2 * piece):
        place = lax.rem(mine + 1 + t // own, count) * own + t % own
        spread_pair(table_ref, half * (1 - parity) + 2 * place, other_refs[t // piece][t % piece], rank)
    at_in.wait()
    for q in range(parents):
        rows = [at_ref[q, j] for j in range(many)]
        far = dot(picked(table_ref, rows, left), packed_ref[q], NT)
        down_ref[q] = far.astype(jnp.bfloat16)
    for q in range(parents):
        local = far_ref[q] + dot(down_ref[q], transfer_ref[2 * q : 2 * q + 2].reshape(2 * rank, rank), NT)
        local_ref[q] = local.astype(jnp.bfloat16)
    counts_in.wait()
    for q in range(parents):
        local = local_ref[q]
        none = jnp.zeros_like(local)
        both = jnp.concatenate([jnp.where(left, local, none), jnp.where(left, none, local)], axis=0)
        total = dot(both, basis_ref[q], NT)
        total = jnp.concatenate([total[:sides], total[sides:]], axis=1) + near_ref[q]
        if q == 0:
            total = total + edge_ref[0]
        if q == parents - 1:
            total = total + edge_ref[1]
        total = jnp.where(pair_mask(counts_ref, q, sides, width), total, jnp.zeros_like(total))
        out_ref[:, 2 * width * q : 2 * width * (q + 1)] = total.astype(out_ref.dtype)


def per_device(
    charges,
    panel_counts,
    basis,
    transfer,
    leaf_coupling,
    leaf_partners,
    near_blocks,
    parent_coupling,
    parent_partners,
):
    leaves, width, rank = basis.shape
    sides = charges.shape[1]
    parents, many = parent_partners.shape
    pairs = leaves // 2
    own = pairs // 2
    axes = ("gx", "gz", "gp")
    n = lax.axis_size("gz") * lax.axis_size("gp")
    total = n * lax.axis_size("gx")
    bf16, f32 = jnp.bfloat16, jnp.float32
    keep = lambda *arrays: [pltpu.with_memory_space_constraint(a, pltpu.HBM) for a in arrays]
    shape = pltpu.VMEM
    dma = lambda count: pltpu.SemaphoreType.DMA((count,))
    params = lambda mib: pltpu.CompilerParams(vmem_limit_bytes=mib * 2**20)

    rim, live, parent_coef, sent = pl.pallas_call(
        up_kernel,
        name="up",
        out_shape=[
            shape((pairs + 2, sides, 2 * rank), bf16),
            shape((pairs, sides, 2 * width), bf16),
            shape((own, sides, 2 * rank), bf16),
            pltpu.HBM((n // 2 * own, sides, 2 * rank), bf16),
        ],
        in_specs=[HBM] * 4,
        out_specs=[VMEM, VMEM, VMEM, HBM],
        scratch_shapes=[
            pltpu.SMEM((leaves,), jnp.int32),
            pltpu.VMEM((sides, leaves * width), bf16),
            pltpu.VMEM((leaves, width, rank), bf16),
            pltpu.VMEM((leaves, rank, rank), bf16),
            dma(4),
            dma(n // 2),
        ],
        compiler_params=params(8),
    )(*keep(panel_counts, charges.T, basis, transfer))

    even = lax.ppermute(rim, axes, [(i, i ^ 1) for i in range(total)])
    steps = [(i, i + 1) for i in range(1, total - 1, 2)]
    odd = lax.ppermute(rim, axes, steps + [(b, a) for a, b in steps])
    same = lax.all_to_all(sent, "gz", 0, 0, tiled=True)

    parent_packed, near, rim_near, leaf_at, parent_at = pl.pallas_call(
        functools.partial(mid_kernel, axes),
        name="mid",
        out_shape=[
            shape((parents, rank, many * rank), bf16),
            shape((pairs, sides, 2 * width), f32),
            shape((2, width, width), bf16),
            shape((many, leaves), jnp.int32),
            shape((parents, many), jnp.int32),
        ],
        in_specs=[VMEM] + [HBM] * 4,
        out_specs=[VMEM] * 5,
        scratch_shapes=[
            pltpu.VMEM(near_blocks.shape, bf16),
            pltpu.VMEM(parent_coupling.shape, bf16),
            dma(3 + parents // 4),
        ],
        compiler_params=params(12),
    )(live, *keep(near_blocks, parent_coupling, leaf_partners.T, parent_partners))

    other_own = lax.ppermute(parent_coef, "gp", [(0, 1), (1, 0)])
    piece = shape(((n // 2 - 1) * own // 2, sides, 2 * rank), bf16)
    pieces = pl.pallas_call(
        functools.partial(halves_kernel, "gz"),
        name="halves",
        out_shape=[piece, piece],
        in_specs=[VMEM, VMEM, VMEM],
        out_specs=[VMEM, VMEM],
        compiler_params=params(4),
    )(same, other_own, parent_at)
    other = [lax.ppermute(piece, "gp", [(0, 1), (1, 0)]) for piece in pieces]

    far, edge, transfer_in, basis_in = pl.pallas_call(
        functools.partial(leaf_kernel, axes),
        name="leaf",
        out_shape=[
            shape((pairs, sides, 2 * rank), f32),
            shape((2, sides, 2 * width), f32),
            shape(transfer.shape, bf16),
            shape((pairs, width, 2 * rank), bf16),
        ],
        in_specs=[VMEM] * 5 + [HBM] * 3,
        out_specs=[VMEM] * 4,
        scratch_shapes=[
            pltpu.VMEM((3 * leaves, sides, 2 * rank), bf16),
            pltpu.SMEM((many, leaves), jnp.int32),
            pltpu.VMEM(leaf_coupling.shape, bf16),
            pltpu.VMEM((leaves, rank, many * rank), bf16),
            pltpu.VMEM(basis.shape, bf16),
            dma(3 + leaves // 2),
        ],
        compiler_params=params(20),
    )(leaf_at, rim, even, odd, rim_near, *keep(leaf_coupling, transfer, basis))

    out = pl.pallas_call(
        functools.partial(down_kernel, axes[1:]),
        name="down",
        out_shape=jax.ShapeDtypeStruct((sides, leaves * width), bf16),
        in_specs=[VMEM, VMEM, VMEM, [VMEM] * 2, VMEM, HBM] + [VMEM] * 5,
        out_specs=VMEM,
        scratch_shapes=[
            pltpu.VMEM((n * parents, sides, 2 * rank), bf16),
            pltpu.SMEM((parents, many), jnp.int32),
            pltpu.VMEM((pairs, sides, 2 * rank), bf16),
            pltpu.VMEM((parents, sides, rank), bf16),
            pltpu.SMEM((leaves,), jnp.int32),
            dma(2),
        ],
        compiler_params=params(12),
    )(parent_at, same, other_own, other, parent_packed, *keep(panel_counts), far, near, edge, transfer_in, basis_in)
    return out.T


def solution(mesh):
    outer, inner = mesh.devices.shape
    split = jax.sharding.Mesh(mesh.devices.reshape(outer, inner // 2, 2), ("gx", "gz", "gp"))
    leaves = ("gx", "gz", "gp")
    in_specs = (
        P(leaves, None),
        P(leaves),
        P(leaves, None, None),
        P(leaves, None, None),
        P(leaves, None, None, None),
        P(leaves, None),
        P(leaves, None, None, None),
        P(leaves, None, None, None),
        P(leaves, None),
    )
    return jax.shard_map(
        per_device, mesh=split, in_specs=in_specs, out_specs=P(leaves, None), check_vma=False
    )
```

```python
import functools

import jax
import jax.numpy as jnp
from jax import lax
from jax.experimental import pallas as pl
from jax.experimental.pallas import tpu as pltpu
from jax.sharding import PartitionSpec as P

VMEM = pl.BlockSpec(memory_space=pltpu.VMEM)
HBM = pl.BlockSpec(memory_space=pltpu.HBM)
NN = (((1,), (0,)), ((), ()))
NT = (((1,), (1,)), ((), ()))


def dot(a, b, dims):
    return lax.dot_general(a, b, dims, preferred_element_type=jnp.float32)


def left_half(sides, width):
    return lax.broadcasted_iota(jnp.int32, (sides, 2 * width), 1) < width


def pair_mask(counts_ref, pair, sides, width):
    lane = lax.broadcasted_iota(jnp.int32, (sides, 2 * width), 1)
    left = lane < width
    count = jnp.where(left, counts_ref[2 * pair], counts_ref[2 * pair + 1])
    return jnp.where(left, lane, lane - width) < count


def swap(pair, width):
    return jnp.concatenate([pair[:, width:], pair[:, :width]], axis=1)


def mod(x, m):
    return x & (m - 1) if m & (m - 1) == 0 else lax.rem(x, m)


def div(x, m):
    return x >> (m.bit_length() - 1) if m & (m - 1) == 0 else x // m


def position(axes):
    index = 0
    for axis in axes:
        index = index * lax.axis_size(axis) + lax.axis_index(axis)
    return index


def start_all(copies, sems):
    started = [pltpu.make_async_copy(src, dst, sems.at[i]) for i, (src, dst) in enumerate(copies)]
    for copy in started:
        copy.start()
    return started


def up_kernel(
    counts_hbm, charges_hbm, basis_hbm, transfer_hbm,
    rim_ref, live_ref, parents_ref, sent_hbm,
    counts_ref, charges_ref, basis_ref, transfer_ref, sems, sent_sems,
):
    counts_in, charges_in, basis_in, transfer_in = start_all(
        [
            (counts_hbm, counts_ref), (charges_hbm, charges_ref),
            (basis_hbm, basis_ref), (transfer_hbm, transfer_ref),
        ],
        sems,
    )
    sides = charges_ref.shape[0]
    leaves, width, rank = basis_ref.shape
    pairs = leaves // 2
    own = pairs // 2
    left = left_half(sides, width)
    counts_in.wait()
    charges_in.wait()
    lives = []
    for a in range(pairs):
        charge = charges_ref[:, 2 * width * a : 2 * width * (a + 1)]
        live = jnp.where(pair_mask(counts_ref, a, sides, width), charge, jnp.zeros_like(charge))
        live_ref[a] = live
        lives.append(live)
    rim_ref[pairs] = lives[0]
    rim_ref[pairs + 1] = lives[-1]
    basis_in.wait()
    none = jnp.zeros_like(lives[0])
    coefs = []
    for a in range(pairs):
        live = lives[a]
        both = jnp.concatenate([jnp.where(left, live, none), jnp.where(left, none, live)], axis=0)
        coef = dot(both, basis_ref[2 * a : 2 * a + 2].reshape(2 * width, rank), NN)
        coef = jnp.concatenate([coef[:sides], coef[sides:]], axis=1).astype(jnp.bfloat16)
        rim_ref[a] = coef
        coefs.append(coef)
    transfer_in.wait()
    sums = [
        dot(coefs[a], transfer_ref[2 * a : 2 * a + 2].reshape(2 * rank, rank), NN)
        for a in range(pairs)
    ]
    for a in range(own):
        parents_ref[a] = jnp.concatenate(sums[2 * a : 2 * a + 2], axis=1).astype(jnp.bfloat16)
    copies = sent_hbm.shape[0] // own
    for copy in start_all([(parents_ref, sent_hbm.at[pl.ds(own * c, own)]) for c in range(copies)], sent_sems):
        copy.wait()


def side_by_side(blocks_ref, g):
    return jnp.concatenate([blocks_ref[g, j] for j in range(blocks_ref.shape[1])], axis=1)


def mid_kernel(
    axes, live_ref, near_hbm, parent_hbm, leaf_partners_hbm, parent_partners_hbm,
    parent_packed_ref, near_out_ref, rim_near_ref, leaf_at_ref, parent_at_ref,
    near_ref, parent_ref, sems,
):
    parents, many, rank, _ = parent_ref.shape
    leaves = near_ref.shape[0]
    width = near_ref.shape[2]
    pairs = leaves // 2
    started = start_all(
        [(near_hbm, near_ref)]
        + [(parent_hbm.at[pl.ds(4 * i, 4)], parent_ref.at[pl.ds(4 * i, 4)]) for i in range(parents // 4)]
        + [(leaf_partners_hbm, leaf_at_ref), (parent_partners_hbm, parent_at_ref)],
        sems,
    )
    near_in = started[0]
    parent_in = started[1:-2]
    near_in.wait()
    rim_near_ref[0] = near_ref[0, 0]
    rim_near_ref[1] = near_ref[leaves - 1, 2]
    for a in range(pairs):
        here = live_ref[a]
        even = dot(here, jnp.concatenate([near_ref[2 * a, 1], near_ref[2 * a, 2]], axis=1), NT)
        odd = dot(here, jnp.concatenate([near_ref[2 * a + 1, 0], near_ref[2 * a + 1, 1]], axis=1), NT)
        if a > 0:
            even = even + dot(live_ref[a - 1][:, width:], near_ref[2 * a, 0], NT)
        if a < pairs - 1:
            odd = odd + dot(live_ref[a + 1][:, :width], near_ref[2 * a + 1, 2], NT)
        near_out_ref[a] = jnp.concatenate([even, odd], axis=1)

    for i, copy in enumerate(parent_in):
        copy.wait()
        for q in range(4 * i, 4 * i + 4):
            parent_packed_ref[q] = side_by_side(parent_ref, q)
    for copy in started[-2:]:
        copy.wait()
    wanted = leaf_at_ref[...] + (1 - position(axes)) * leaves
    leaf_at_ref[...] = wanted ^ (lax.broadcasted_iota(jnp.int32, wanted.shape, 0) & 1)
    inner = lax.axis_size(axes[2])
    outer = lax.axis_size(axes[1])
    wanted = mod(parent_at_ref[...], outer * inner * parents)
    source = div(wanted, parents)
    wanted = (mod(source, inner) * outer + div(source, inner)) * parents + mod(wanted, parents)
    parent_at_ref[...] = wanted ^ (lax.broadcasted_iota(jnp.int32, wanted.shape, 1) & 1)


def halves_kernel(axis, whole_ref, own_ref, at_ref, first_ref, second_ref):
    del at_ref
    own, half = own_ref.shape[0], first_ref.shape[0]
    count = lax.axis_size(axis)
    for t in range(2 * half):
        source = lax.rem(lax.axis_index(axis) + 1 + t // own, count) * own + t % own
        (first_ref if t < half else second_ref)[t % half] = whole_ref[source]


def spread_pair(table_ref, at, pair, width):
    table_ref[at] = pair
    table_ref[at + 1] = swap(pair, width)


def picked(table_ref, rows, left):
    return jnp.concatenate(
        [
            jnp.where(left, table_ref[rows[j]], table_ref[rows[j + 1]])
            for j in range(0, len(rows), 2)
        ],
        axis=1,
    )


def leaf_kernel(
    axes, at_vmem, rim_ref, even_ref, odd_ref, rim_near_ref, coupling_hbm, transfer_hbm, basis_hbm,
    far_ref, edge_ref, transfer_ref, basis_packed_ref, table_ref, at_ref, coupling_ref, packed_ref, basis_ref, sems,
):
    leaves, many, rank, _ = coupling_ref.shape
    chunks = [(at, 8) for at in range(0, leaves, 8)]
    at_in, *coupling_in, transfer_in, basis_in = start_all(
        [(at_vmem, at_ref)]
        + [(coupling_hbm.at[pl.ds(at, size)], coupling_ref.at[pl.ds(at, size)]) for at, size in chunks]
        + [(transfer_hbm, transfer_ref), (basis_hbm, basis_ref)],
        sems,
    )
    width = rim_near_ref.shape[1]
    pairs = leaves // 2
    sides = rim_ref.shape[1]
    left = left_half(sides, rank)
    parity = lax.rem(position(axes), 2)
    for ref, base in (
        (rim_ref, leaves), (even_ref, 2 * leaves * (1 - parity)), (odd_ref, 2 * leaves * parity),
    ):
        for a in range(pairs):
            spread_pair(table_ref, base + 2 * a, ref[a], rank)
    before = jnp.where(parity == 1, even_ref[pairs + 1], odd_ref[pairs + 1])
    after = jnp.where(parity == 1, odd_ref[pairs], even_ref[pairs])
    low = dot(before[:, width:], rim_near_ref[0], NT)
    high = dot(after[:, :width], rim_near_ref[1], NT)
    edge_ref[0] = jnp.concatenate([low, jnp.zeros_like(low)], axis=1)
    edge_ref[1] = jnp.concatenate([jnp.zeros_like(high), high], axis=1)
    at_in.wait()
    ready = []
    for i in range(len(chunks) + 1):
        now, ready = ready, []
        if i < len(chunks):
            coupling_in[i].wait()
            ready = range(chunks[i][0], sum(chunks[i]))
            for g in ready:
                packed_ref[g] = side_by_side(coupling_ref, g)
        fars = []
        for g in now:
            rows = [at_ref[j, g] for j in range(many)]
            fars.append(dot(picked(table_ref, rows, left), packed_ref[g], NT))
            if g % 2 == 1:
                far_ref[g // 2] = jnp.concatenate(fars[-2:], axis=1)
    basis_in.wait()
    for a in range(pairs):
        basis_packed_ref[a] = jnp.concatenate([basis_ref[2 * a], basis_ref[2 * a + 1]], axis=1)
    transfer_in.wait()


def down_kernel(
    axes, at_vmem, same_ref, other_own_ref, other_refs, packed_ref, counts_hbm,
    far_ref, near_ref, edge_ref, transfer_ref, basis_ref,
    out_ref, table_ref, at_ref, local_ref, down_ref, counts_ref, sems,
):
    at_in, counts_in = start_all([(at_vmem, at_ref), (counts_hbm, counts_ref)], sems)
    parents, many = at_ref.shape
    rank = packed_ref.shape[1]
    width = basis_ref.shape[1]
    sides = same_ref.shape[1]
    half = 2 * same_ref.shape[0]
    left = left_half(sides, rank)
    parity, mine, count = lax.axis_index(axes[1]), lax.axis_index(axes[0]), lax.axis_size(axes[0])
    own, piece = other_own_ref.shape[0], other_refs[0].shape[0]
    for t in range(count * own):
        spread_pair(table_ref, half * parity + 2 * t, same_ref[t], rank)
    for t in range(own):
        spread_pair(table_ref, half * (1 - parity) + 2 * (mine * own + t), other_own_ref[t], rank)
    for t in range(2 * piece):
        place = lax.rem(mine + 1 + t // own, count) * own + t % own
        spread_pair(table_ref, half * (1 - parity) + 2 * place, other_refs[t // piece][t % piece], rank)
    at_in.wait()
    for q in range(parents):
        rows = [at_ref[q, j] for j in range(many)]
        far = dot(picked(table_ref, rows, left), packed_ref[q], NT)
        down_ref[q] = far.astype(jnp.bfloat16)
    for q in range(parents):
        local = far_ref[q] + dot(down_ref[q], transfer_ref[2 * q : 2 * q + 2].reshape(2 * rank, rank), NT)
        local_ref[q] = local.astype(jnp.bfloat16)
    counts_in.wait()
    for q in range(parents):
        local = local_ref[q]
        none = jnp.zeros_like(local)
        both = jnp.concatenate([jnp.where(left, local, none), jnp.where(left, none, local)], axis=0)
        total = dot(both, basis_ref[q], NT)
        total = jnp.concatenate([total[:sides], total[sides:]], axis=1) + near_ref[q]
        if q == 0:
            total = total + edge_ref[0]
        if q == parents - 1:
            total = total + edge_ref[1]
        total = jnp.where(pair_mask(counts_ref, q, sides, width), total, jnp.zeros_like(total))
        out_ref[:, 2 * width * q : 2 * width * (q + 1)] = total.astype(out_ref.dtype)


def per_device(
    charges,
    panel_counts,
    basis,
    transfer,
    leaf_coupling,
    leaf_partners,
    near_blocks,
    parent_coupling,
    parent_partners,
):
    leaves, width, rank = basis.shape
    sides = charges.shape[1]
    parents, many = parent_partners.shape
    pairs = leaves // 2
    own = pairs // 2
    axes = ("gx", "gz", "gp")
    n = lax.axis_size("gz") * lax.axis_size("gp")
    total = n * lax.axis_size("gx")
    bf16, f32 = jnp.bfloat16, jnp.float32
    keep = lambda *arrays: [pltpu.with_memory_space_constraint(a, pltpu.HBM) for a in arrays]
    shape = pltpu.VMEM
    dma = lambda count: pltpu.SemaphoreType.DMA((count,))
    params = lambda mib: pltpu.CompilerParams(vmem_limit_bytes=mib * 2**20)

    rim, live, parent_coef, sent = pl.pallas_call(
        up_kernel,
        name="up",
        out_shape=[
            shape((pairs + 2, sides, 2 * rank), bf16),
            shape((pairs, sides, 2 * width), bf16),
            shape((own, sides, 2 * rank), bf16),
            pltpu.HBM((n // 2 * own, sides, 2 * rank), bf16),
        ],
        in_specs=[HBM] * 4,
        out_specs=[VMEM, VMEM, VMEM, HBM],
        scratch_shapes=[
            pltpu.SMEM((leaves,), jnp.int32),
            pltpu.VMEM((sides, leaves * width), bf16),
            pltpu.VMEM((leaves, width, rank), bf16),
            pltpu.VMEM((leaves, rank, rank), bf16),
            dma(4),
            dma(n // 2),
        ],
        compiler_params=params(8),
    )(*keep(panel_counts, charges.T, basis, transfer))

    even = lax.ppermute(rim, axes, [(i, i ^ 1) for i in range(total)])
    steps = [(i, i + 1) for i in range(1, total - 1, 2)]
    odd = lax.ppermute(rim, axes, steps + [(b, a) for a, b in steps])
    same = lax.all_to_all(sent, "gz", 0, 0, tiled=True)

    parent_packed, near, rim_near, leaf_at, parent_at = pl.pallas_call(
        functools.partial(mid_kernel, axes),
        name="mid",
        out_shape=[
            shape((parents, rank, many * rank), bf16),
            shape((pairs, sides, 2 * width), f32),
            shape((2, width, width), bf16),
            shape((many, leaves), jnp.int32),
            shape((parents, many), jnp.int32),
        ],
        in_specs=[VMEM] + [HBM] * 4,
        out_specs=[VMEM] * 5,
        scratch_shapes=[
            pltpu.VMEM(near_blocks.shape, bf16),
            pltpu.VMEM(parent_coupling.shape, bf16),
            dma(3 + parents // 4),
        ],
        compiler_params=params(12),
    )(live, *keep(near_blocks, parent_coupling, leaf_partners.T, parent_partners))

    other_own = lax.ppermute(parent_coef, "gp", [(0, 1), (1, 0)])
    piece = shape(((n // 2 - 1) * own // 2, sides, 2 * rank), bf16)
    pieces = pl.pallas_call(
        functools.partial(halves_kernel, "gz"),
        name="halves",
        out_shape=[piece, piece],
        in_specs=[VMEM, VMEM, VMEM],
        out_specs=[VMEM, VMEM],
        compiler_params=params(4),
    )(same, other_own, parent_at)
    other = [lax.ppermute(piece, "gp", [(0, 1), (1, 0)]) for piece in pieces]

    far, edge, transfer_in, basis_in = pl.pallas_call(
        functools.partial(leaf_kernel, axes),
        name="leaf",
        out_shape=[
            shape((pairs, sides, 2 * rank), f32),
            shape((2, sides, 2 * width), f32),
            shape(transfer.shape, bf16),
            shape((pairs, width, 2 * rank), bf16),
        ],
        in_specs=[VMEM] * 5 + [HBM] * 3,
        out_specs=[VMEM] * 4,
        scratch_shapes=[
            pltpu.VMEM((3 * leaves, sides, 2 * rank), bf16),
            pltpu.SMEM((many, leaves), jnp.int32),
            pltpu.VMEM(leaf_coupling.shape, bf16),
            pltpu.VMEM((leaves, rank, many * rank), bf16),
            pltpu.VMEM(basis.shape, bf16),
            dma(3 + leaves // 8),
        ],
        compiler_params=params(20),
    )(leaf_at, rim, even, odd, rim_near, *keep(leaf_coupling, transfer, basis))

    out = pl.pallas_call(
        functools.partial(down_kernel, axes[1:]),
        name="down",
        out_shape=jax.ShapeDtypeStruct((sides, leaves * width), bf16),
        in_specs=[VMEM, VMEM, VMEM, [VMEM] * 2, VMEM, HBM] + [VMEM] * 5,
        out_specs=VMEM,
        scratch_shapes=[
            pltpu.VMEM((n * parents, sides, 2 * rank), bf16),
            pltpu.SMEM((parents, many), jnp.int32),
            pltpu.VMEM((pairs, sides, 2 * rank), bf16),
            pltpu.VMEM((parents, sides, rank), bf16),
            pltpu.SMEM((leaves,), jnp.int32),
            dma(2),
        ],
        compiler_params=params(12),
    )(parent_at, same, other_own, other, parent_packed, *keep(panel_counts), far, near, edge, transfer_in, basis_in)
    return out.T


def solution(mesh):
    outer, inner = mesh.devices.shape
    split = jax.sharding.Mesh(mesh.devices.reshape(outer, inner // 2, 2), ("gx", "gz", "gp"))
    leaves = ("gx", "gz", "gp")
    in_specs = (
        P(leaves, None),
        P(leaves),
        P(leaves, None, None),
        P(leaves, None, None),
        P(leaves, None, None, None),
        P(leaves, None),
        P(leaves, None, None, None),
        P(leaves, None, None, None),
        P(leaves, None),
    )
    return jax.shard_map(
        per_device, mesh=split, in_specs=in_specs, out_specs=P(leaves, None), check_vma=False
    )
```
